32 devices in a mesh: dp: 8 (over z, x), mix: 4 (over y, core).
Axes of the slice: x: 2, y: 2, z: 4, core: 2. Of those that a mesh axis runs over, the one named last changes fastest.
Arguments:
- tokens: bfloat16 [64, 512, 768], P('dp', 'mix'), may hold values from -6 to 6
- cotangent: bfloat16 [64, 512, 768], P('dp', 'mix'), may hold values from -6 to 6
- pair_lengths: int32 [64, 4], P('dp'), may hold values from 2 to 505, as said below
- labels: int32 [64, 4], P('dp'), may hold values from 0 to 2
- w_qkv: bfloat16 [768, 2304], replicated, may hold values from -0.21875 to 0.21875
- b_query: float32 [768], replicated, may hold values from -1.75 to 1.75
- b_value: float32 [768], replicated, may hold values from -0.625 to 0.625
- w_attn: bfloat16 [768, 768], replicated, may hold values from -0.625 to 0.625
- b_attn: float32 [768], replicated, may hold values from -1.75 to 1.75
- gain_one: float32 [768], replicated, may hold values from 0.25 to 1.75
- shift_one: float32 [768], replicated, may hold values from -1.75 to 1.75
- w_in: bfloat16 [768, 3072], replicated, may hold values from -0.21875 to 0.21875
- b_in: float32 [3072], replicated, may hold values from -1.75 to 1.75
- w_out: bfloat16 [3072, 768], replicated, may hold values from -0.109375 to 0.109375
- b_out: float32 [768], replicated, may hold values from -1.75 to 1.75
- gain_two: float32 [768], replicated, may hold values from 0.25 to 1.75
- shift_two: float32 [768], replicated, may hold values from -1.75 to 1.75
- w_pool: float32 [768, 768], replicated, may hold values from -0.21875 to 0.21875
- b_pool: float32 [768], replicated, may hold values from -1.75 to 1.75
- w_class: float32 [768, 3], replicated, may hold values from -0.75 to 0.75
- b_class: float32 [3], replicated, may hold values from -3 to 3
Outputs:
- output: bfloat16 [64, 512, 768], P('dp', 'mix')
- pair_loss: float32 [64, 4], P('dp')
- grad_tokens: bfloat16 [64, 512, 768], P('dp', 'mix')
- grad_w_qkv: float32 [768, 2304], P('dp')
- grad_b_query: float32 [768], P('dp')
- grad_b_value: float32 [768], P('dp')
- grad_w_attn: float32 [768, 768], P('dp')
- grad_b_attn: float32 [768], P('dp')
- grad_gain_one: float32 [768], P('dp')
- grad_shift_one: float32 [768], P('dp')
- grad_w_in: float32 [768, 3072], P('dp')
- grad_b_in: float32 [3072], P('dp')
- grad_w_out: float32 [3072, 768], P('dp')
- grad_b_out: float32 [768], P('dp')
- grad_gain_two: float32 [768], P('dp')
- grad_shift_two: float32 [768], P('dp')
- grad_w_pool: float32 [768, 768], P('dp')
- grad_b_pool: float32 [768], P('dp')
- grad_w_class: float32 [768, 3], P('dp')
- grad_b_class: float32 [3], replicated
The draws below stay inside these ranges and needn't reach their ends.
Inputs may be any that keep to these rules, and one draw needn't show every extreme that they name: `pair_lengths`: each row holds 4 sentence pairs laid from its first token on, each of 2 or more tokens, followed by 1 or more tokens of padding, so a row's lengths sum to at most 511; some row has pairs of exactly the least and the most length.
All inputs are finite; a program needn't handle non-finite values.
Results may differ from the reference program's by a relative error of at most 0.015.
Values may be sent and summed in bfloat16 or wider, within the bound.
No kernel may reach another device: no remote copies, remote signals or barrier semaphores. Data moves between devices by JAX's collectives and lax.ppermute only.
A program may use at most 192 MiB of HBM per device.

```python
import jax
import jax.numpy as jnp
from jax import lax

D = 768
HEADS = 12
FF = 3072
CLASSES = 3
SEQ_LEN = 512
PAIRS = 4
ROW_DEV = 8
ROWS = 64


def draw_pair_lengths(key, part):
    key = jax.random.fold_in(key, 11)
    short_key, pad_key, long_key, row_key, cut_key, span_key = jax.random.split(key, 6)
    padding = jax.random.randint(pad_key, (ROWS, 1), 1, SEQ_LEN // 32 + 1)
    chosen_row = jax.random.randint(row_key, (), 0, ROWS)
    row_ids = jnp.arange(ROWS, dtype=jnp.int32)
    is_chosen = (row_ids == chosen_row)[:, None]
    even_row = (chosen_row + 1) % ROWS
    is_even = (row_ids == even_row)[:, None]
    padding = jnp.where(is_chosen, 1, padding)
    spare = SEQ_LEN - padding - 2 * PAIRS
    cuts = jax.random.randint(cut_key, (ROWS, PAIRS - 1), 0, spare + 1)
    cuts = jnp.sort(cuts, axis=1)
    bounds = jnp.concatenate([jnp.zeros((ROWS, 1), jnp.int32), cuts.astype(jnp.int32), spare.astype(jnp.int32)], axis=1)
    spread_lengths = bounds[:, 1:] - bounds[:, :-1] + 2
    shorts = jax.random.randint(short_key, (ROWS, PAIRS), 2, SEQ_LEN // 16 + 1)
    shorts = jnp.where(is_chosen, 2, shorts)
    long_index = jax.random.randint(long_key, (ROWS, 1), 0, PAIRS)
    is_long = jnp.arange(PAIRS, dtype=jnp.int32)[None, :] == long_index
    others = jnp.sum(jnp.where(is_long, 0, shorts), axis=1, keepdims=True)
    long_len = SEQ_LEN - padding - others
    spanning_lengths = jnp.where(is_long, long_len, shorts)
    block_pick = jax.random.randint(span_key, (ROWS // ROW_DEV, 1), 0, ROW_DEV)
    within = jnp.arange(ROW_DEV, dtype=jnp.int32)[None, :]
    is_span = (within == block_pick).reshape(ROWS, 1)
    use_span = jnp.logical_or(is_span, is_chosen)
    lengths = jnp.where(use_span, spanning_lengths, spread_lengths).astype(jnp.int32)
    pair_ids = jnp.arange(PAIRS, dtype=jnp.int32)[None, :]
    even_lengths = jnp.where(pair_ids == PAIRS - 1, SEQ_LEN - (PAIRS - 1) * (SEQ_LEN // PAIRS) - 1, SEQ_LEN // PAIRS)
    even_lengths = jnp.broadcast_to(even_lengths, (ROWS, PAIRS)).astype(jnp.int32)
    return jnp.where(jnp.logical_and(is_even, jnp.logical_not(is_chosen)), even_lengths, lengths).astype(jnp.int32)


def set_ends(drawn, own_key, smallest, top_value):
    shape = drawn.shape
    place = [jax.random.randint(jax.random.fold_in(own_key, axis), (), 0, shape[axis]) for axis in range(len(shape))]
    drawn = drawn.at[tuple(place)].set(smallest)
    longest = shape.index(max(shape))
    place[longest] = (place[longest] + 1) % shape[longest]
    return drawn.at[tuple(place)].set(top_value)


def spiked(drawn, own_key, source, target, parts, factor):
    def block_of(axis_at):
        return (jnp.arange(drawn.shape[axis_at]) // (drawn.shape[axis_at] // parts)).reshape((-1,) + (1,) * (drawn.ndim - 1 - axis_at))

    near = jax.random.permutation(own_key, parts)[block_of(target)]
    far = (block_of(target) + parts // 2) % parts
    return jnp.where((block_of(source) == near) | (block_of(source) == far), factor * drawn, drawn)


def steps_of(own_key, extent, cuts, low, largest):
    level = 1.0
    for dim, blocks in cuts:
        heights = jax.random.uniform(jax.random.fold_in(jax.random.fold_in(own_key, 6), dim), (blocks,), jnp.float32, low / len(cuts), largest / len(cuts))
        level = level * jnp.repeat(jnp.exp(heights), extent[dim] // blocks).reshape((-1,) + (1,) * (len(extent) - 1 - dim))
    return level


def bell_draw(rng, shape, width, reach, cuts=(), kind=jnp.bfloat16):
    array = width * jax.random.normal(rng, shape, jnp.float32)
    if cuts:
        array = array * steps_of(rng, shape, cuts, -0.22, 0.18)
    return jnp.clip(array, -reach, reach).astype(kind)


def noise_with(rng, dims, deviation, reach, cuts, heavy, kind=jnp.bfloat16):
    drawn = deviation * jax.random.normal(rng, dims, jnp.float32)
    if cuts:
        drawn = drawn * steps_of(rng, dims, cuts, -0.22, 0.18)
    return jnp.clip(spiked(drawn, jax.random.fold_in(rng, 3), *heavy), -reach, reach).astype(kind)


def setup_inputs(seed: int = 0) -> dict:
    keys = jax.random.split(jax.random.key(seed), 22)
    return {
        "tokens": noise_with(keys[0], (ROWS, SEQ_LEN, D), 1.0, 6.0, ((0, 8), (1, 4)), (0, 2, 8, 2.0)),
        "cotangent": noise_with(keys[1], (ROWS, SEQ_LEN, D), 1.0, 6.0, ((0, 8), (1, 4)), (0, 2, 8, 2.0)),
        "pair_lengths": draw_pair_lengths(jax.random.fold_in(keys[21], 71), 0),
        "labels": set_ends(jax.random.randint(keys[3], (ROWS, PAIRS), 0, CLASSES), jax.random.fold_in(keys[3], 1), 0, CLASSES - 1).astype(jnp.int32),
        "w_qkv": bell_draw(keys[4], (D, 3 * D), D ** -0.5, 0.21875),
        "b_query": bell_draw(keys[5], (D,), 0.3, 1.75, (), jnp.float32),
        "b_value": bell_draw(keys[6], (D,), 0.1, 0.625, (), jnp.float32),
        "w_attn": bell_draw(keys[7], (D, D), (D // 8) ** -0.5, 0.625),
        "b_attn": bell_draw(keys[8], (D,), 0.3, 1.75, (), jnp.float32),
        "gain_one": jnp.clip(1.0 + 0.15 * jax.random.normal(keys[9], (D,), jnp.float32), 0.25, 1.75),
        "shift_one": bell_draw(keys[10], (D,), 0.3, 1.75, (), jnp.float32),
        "w_in": bell_draw(keys[11], (D, FF), D ** -0.5, 0.21875),
        "b_in": bell_draw(keys[12], (FF,), 0.3, 1.75, (), jnp.float32),
        "w_out": bell_draw(keys[13], (FF, D), FF ** -0.5, 0.109375),
        "b_out": bell_draw(keys[14], (D,), 0.3, 1.75, (), jnp.float32),
        "gain_two": jnp.clip(1.0 + 0.15 * jax.random.normal(keys[15], (D,), jnp.float32), 0.25, 1.75),
        "shift_two": bell_draw(keys[16], (D,), 0.3, 1.75, (), jnp.float32),
        "w_pool": bell_draw(keys[17], (D, D), D ** -0.5, 0.21875, (), jnp.float32),
        "b_pool": bell_draw(keys[18], (D,), 0.3, 1.75, (), jnp.float32),
        "w_class": bell_draw(keys[19], (D, CLASSES), 0.12, 0.75, (), jnp.float32),
        "b_class": bell_draw(keys[20], (CLASSES,), 0.5, 3.0, (), jnp.float32),
    }


@jax.custom_vjp
def low(v):
    return lax.optimization_barrier(v.astype(jnp.bfloat16)).astype(jnp.float32)

@jax.custom_vjp
def low_back(v):
    return v

def low_keep(v):
    return (low(v), None)

def low_pass(kept, grad):
    return (grad,)

def back_keep(v):
    return (v, None)

def back_low(kept, grad):
    return (low(grad),)
low.defvjp(low_keep, low_pass)
low_back.defvjp(back_keep, back_low)
norm_eps = 1e-06
masked_score = -1000000000.0
highest = lax.Precision.HIGHEST
inv_root_two = 0.7071067811865476

def layer_norm(values, gain_vec, shift_vec):
    centre = values - lax.optimization_barrier(jnp.mean(values, axis=-1, keepdims=True))
    spread = lax.optimization_barrier(jnp.mean(centre * centre, axis=-1, keepdims=True))
    return centre * lax.rsqrt(spread + norm_eps) * gain_vec + shift_vec

def gelu_exact(values):
    return 0.5 * values * (1.0 + jax.scipy.special.erf(values * inv_root_two))

def group_forward(params, group_tokens, group_lengths, group_labels):
    w_qkv, b_query, b_value, w_attn, b_attn, gain_one, shift_one, w_in, b_in, w_out, b_out, gain_two, shift_two, w_pool, b_pool, w_class, b_class = params
    group_rows, seq_len, model_width = group_tokens.shape
    head_size = model_width // HEADS
    pair_ends = jnp.cumsum(group_lengths, axis=1)
    starts = pair_ends - group_lengths
    places = jnp.arange(seq_len, dtype=jnp.int32)
    pair_of = lax.optimization_barrier(jnp.sum((places[None, :, None] >= pair_ends[:, None, :]).astype(jnp.int32), axis=2))
    same_pair = (pair_of[:, :, None] == pair_of[:, None, :])[:, None]
    qkv_bias = jnp.concatenate([b_query, jnp.zeros_like(b_query), b_value])
    qkv = jnp.einsum('gtd,de->gte', group_tokens, w_qkv, precision=highest) + qkv_bias
    qkv = low(low_back(qkv)).reshape(group_rows, seq_len, 3, HEADS, head_size)
    queries = qkv[:, :, 0]
    key_part = qkv[:, :, 1]
    values = qkv[:, :, 2]
    scores = low_back(jnp.einsum('gqhe,gkhe->ghqk', queries, key_part, precision=highest) * head_size ** (-0.5))
    scores = jnp.where(same_pair, scores, masked_score)
    row_top = lax.optimization_barrier(jnp.max(scores, axis=-1, keepdims=True))
    exponent = jnp.exp(scores - row_top)
    attn_probs = exponent / lax.optimization_barrier(jnp.sum(exponent, axis=-1, keepdims=True))
    mixture = jnp.einsum('ghqk,gkhe->gqhe', low(attn_probs), values, precision=highest)
    mixture = low(low_back(mixture)).reshape(group_rows, seq_len, model_width)
    attended = low_back(jnp.einsum('gtd,de->gte', mixture, w_attn, precision=highest) + b_attn)
    hidden = layer_norm(group_tokens + attended, gain_one, shift_one)
    upward = low_back(jnp.einsum('gtd,df->gtf', low(hidden), w_in, precision=highest) + b_in)
    active = gelu_exact(upward)
    feed_out = low_back(jnp.einsum('gtf,fd->gtd', low(active), w_out, precision=highest) + b_out)
    output = layer_norm(hidden + feed_out, gain_two, shift_two)
    firsts = jnp.take_along_axis(output, starts[:, :, None], axis=1)
    pooled = jnp.tanh(jnp.einsum('gpd,de->gpe', firsts, w_pool, precision=highest) + b_pool)
    logits = jnp.einsum('gpd,dc->gpc', pooled, w_class, precision=highest) + b_class
    logit_top = lax.optimization_barrier(jnp.max(logits, axis=-1, keepdims=True))
    log_total = logit_top[..., 0] + jnp.log(lax.optimization_barrier(jnp.sum(jnp.exp(logits - logit_top), axis=-1)))
    chosen = (group_labels[:, :, None] == jnp.arange(logits.shape[-1], dtype=jnp.int32)).astype(jnp.float32)
    losses = log_total - lax.optimization_barrier(jnp.sum(logits * chosen, axis=-1))
    return (output, losses)

def reference(tokens, cotangent, pair_lengths, labels, w_qkv, b_query, b_value, w_attn, b_attn, gain_one, shift_one, w_in, b_in, w_out, b_out, gain_two, shift_two, w_pool, b_pool, w_class, b_class):
    params = (w_qkv.astype(jnp.float32), b_query, b_value, w_attn.astype(jnp.float32), b_attn, gain_one, shift_one, w_in.astype(jnp.float32), b_in, w_out.astype(jnp.float32), b_out, gain_two, shift_two, w_pool, b_pool, w_class, b_class)
    row_count, seq_len, model_width = tokens.shape
    block_rows = 4
    blocks = row_count // block_rows

    def forward(weights_all, inputs):

        def single(pieces):
            return jax.checkpoint(group_forward)(weights_all, pieces[0], pieces[1], pieces[2])
        outputs, losses = lax.map(single, (inputs.reshape(blocks, block_rows, seq_len, model_width), pair_lengths.reshape(blocks, block_rows, -1), labels.reshape(blocks, block_rows, -1)))
        return (outputs.reshape(row_count, seq_len, model_width), losses.reshape(row_count, -1))
    (output, losses), pullback = jax.vjp(forward, params, tokens.astype(jnp.float32))
    grads, tok_grad = pullback((cotangent.astype(jnp.float32), jnp.ones_like(losses)))
    return (output.astype(jnp.bfloat16), losses, tok_grad.astype(jnp.bfloat16), grads[0], grads[1], grads[2], grads[3], grads[4], grads[5], grads[6], grads[7], grads[8], grads[9], grads[10], grads[11], grads[12], grads[13], grads[14], grads[15], grads[16])
```

```python
import functools

import jax
import jax.numpy as jnp
from jax import lax
from jax.experimental import pallas as pl
from jax.experimental.pallas import tpu as pltpu
from jax.sharding import PartitionSpec as P

HEADS = 12
GROUP = 4
CHUNK = 512
norm_eps = 1e-06
masked_score = -1000000000.0
inv_root_two = 0.7071067811865476
inv_root_tau = 0.3989422804014327
f32 = jnp.float32
bf16 = jnp.bfloat16
VMEM_LIMIT = 56 * 1024 * 1024
SMEM_SPEC = pl.BlockSpec(memory_space=pltpu.SMEM)


def whole(shape):
    return pl.BlockSpec(shape, lambda *_: (0,) * len(shape))


def nn(left, right):
    return jnp.dot(left, right, preferred_element_type=f32)


def nt(left, right):
    return lax.dot_general(left, right, (((1,), (1,)), ((), ())), preferred_element_type=f32)


def params():
    return pltpu.CompilerParams(vmem_limit_bytes=VMEM_LIMIT)


def cost(flops, nbytes, trans=0):
    return pl.CostEstimate(flops=int(flops), bytes_accessed=int(nbytes), transcendentals=int(trans))


def mean_of(values):
    return jnp.mean(values, axis=-1, keepdims=True)


def col_sum(values):
    return jnp.sum(values, axis=0, keepdims=True)


def segments(places, lengths, row):
    total = jnp.int32(0)
    seg = jnp.zeros(places.shape, jnp.int32)
    for k in range(4):
        total = total + lengths[row, k]
        seg = seg + (places >= total).astype(jnp.int32)
    return seg


def forward_kernel(
    row, rows_here, part_len, mixers, head_size,
    me, lengths, *refs,
):
    pieces, refs = refs[:mixers], refs[mixers:]
    (wq, wk, wv, bq, bv, wa, ba, g1, s1,
     q_o, k_o, v_o, probs_o, mix_t_o, tok_t_o, hid_o, hid_t_o, n1_o, rho_o,
     tok_s, att_s, bias_s) = refs
    step = pl.program_id(0)
    seq = part_len * mixers
    shift = part_len.bit_length() - 1

    @pl.when(step == 0)
    def _():
        for i, piece in enumerate(pieces):
            tok_s[i * part_len : (i + 1) * part_len, :] = piece[...]
        tok_t_o[...] = tok_s[...].T
        mine = me[0]
        down = lax.broadcasted_iota(jnp.int32, (seq, 1), 0)
        across = lax.broadcasted_iota(jnp.int32, (1, seq), 1)

        def place(i):
            return (((i >> shift) ^ mine) << shift) + (i & (part_len - 1))

        number = mine * rows_here + row
        same = segments(place(down), lengths, number) == segments(place(across), lengths, number)
        bias_s[...] = jnp.where(same, 0.0, masked_score)

    tok = tok_s[...]
    qs = (nn(tok, wq[...]) + bq[...]).astype(bf16) * bf16(head_size ** (-0.5))
    keys = nn(tok, wk[...]).astype(bf16)
    values = (nn(tok, wv[...]) + bv[...]).astype(bf16)
    q_o[...] = qs
    k_o[...] = keys
    v_o[...] = values
    values_t = values.T
    lane = lax.broadcasted_iota(jnp.int32, (1, GROUP * head_size), 1) // head_size
    outs = []
    for h in range(GROUP):
        scores = nt(keys, jnp.where(lane == h, qs, bf16(0))) + bias_s[...]
        top = jnp.max(scores, axis=0, keepdims=True)
        expo = jnp.exp(scores - top)
        total = jnp.sum(expo, axis=0, keepdims=True)
        probs = (expo * (1.0 / total)).astype(bf16)
        probs_o[h] = probs
        outs.append(nn(values_t[h * head_size : (h + 1) * head_size], probs))
    mix_t = jnp.concatenate(outs, axis=0).astype(bf16)
    mix_t_o[...] = mix_t
    part = nn(mix_t.T, wa[...])

    @pl.when(step == 0)
    def _():
        att_s[...] = part

    @pl.when(step > 0)
    def _():
        att_s[...] += part

    @pl.when(step == pl.num_programs(0) - 1)
    def _():
        full = tok_s[...].astype(f32) + (att_s[...] + ba[...])
        centre = full - mean_of(full)
        rho = lax.rsqrt(mean_of(centre * centre) + norm_eps)
        normed = centre * rho
        hidden = normed * g1[...] + s1[...]
        hid_o[...] = hidden
        hid_t_o[...] = hidden.astype(bf16).T
        n1_o[...] = normed.astype(bf16)
        rho_o[...] = jnp.broadcast_to(rho, rho_o.shape)


def forward_row(row, rows_here, me, lengths, pieces, w_qkv, b_query, b_value, w_attn, b_attn, gain, shift):
    part_len, width = pieces[0].shape
    mixers = len(pieces)
    seq = part_len * mixers
    head_size = width // HEADS
    span = GROUP * head_size
    steps = width // span

    def col(block):
        return pl.BlockSpec((seq, span), lambda g: (0, g))

    def weight(which):
        return pl.BlockSpec((width, span), lambda g: (0, which * steps + g))

    vec = pl.BlockSpec((1, span), lambda g: (0, g))
    kernel = functools.partial(forward_kernel, row, rows_here, part_len, mixers, head_size)
    macs = seq * width * width * 4 + 8 * seq * seq * width
    return pl.pallas_call(
        kernel,
        grid=(steps,),
        in_specs=[SMEM_SPEC, SMEM_SPEC]
        + [whole((part_len, width))] * mixers
        + [weight(0), weight(1), weight(2), vec, vec,
           pl.BlockSpec((span, width), lambda g: (g, 0)),
           whole((1, width)), whole((1, width)), whole((1, width))],
        out_specs=[col(0), col(1), col(2),
                   pl.BlockSpec((GROUP, seq, seq), lambda g: (g, 0, 0)),
                   pl.BlockSpec((span, seq), lambda g: (g, 0)),
                   whole((width, seq)), whole((seq, width)), whole((width, seq)),
                   whole((seq, width)), whole((seq, 128))],
        out_shape=[jax.ShapeDtypeStruct((seq, width), bf16)] * 3
        + [jax.ShapeDtypeStruct((HEADS, seq, seq), bf16),
           jax.ShapeDtypeStruct((width, seq), bf16),
           jax.ShapeDtypeStruct((width, seq), bf16),
           jax.ShapeDtypeStruct((seq, width), f32),
           jax.ShapeDtypeStruct((width, seq), bf16),
           jax.ShapeDtypeStruct((seq, width), bf16),
           jax.ShapeDtypeStruct((seq, 128), f32)],
        scratch_shapes=[pltpu.VMEM((seq, width), bf16), pltpu.VMEM((seq, width), f32), pltpu.VMEM((seq, seq), f32)],
        compiler_params=params(),
        cost_estimate=cost(2 * macs, 16e6, HEADS * seq * seq),
        name="forward_row",
    )(me, lengths, *pieces, w_qkv, w_qkv, w_qkv, b_query, b_value, w_attn, b_attn, gain, shift)


def feed_kernel(rows_here, part_len, pairs, me, lengths, *refs):
    hid = refs[:rows_here]
    (w_in, b_in, w_out, b_out, g2, s2,
     act_t_o, slope_o, out_o, n2_o, rho_o, first_o,
     low_s, feed_s, full_s) = refs[rows_here:]
    step = pl.program_id(0)
    last = pl.num_programs(0) - 1
    seq = hid[0].shape[0]
    tile = 256
    count = rows_here * seq // tile

    @pl.when(step == 0)
    def _():
        for r in range(rows_here):
            low_s[r * seq : (r + 1) * seq, :] = hid[r][...].astype(bf16)
        feed_s[...] = jnp.broadcast_to(b_out[...], feed_s.shape)

    for i in range(count):
        at = slice(i * tile, (i + 1) * tile)
        up = nn(low_s[at, :], w_in[...]) + b_in[...]
        half = 0.5 * (1.0 + lax.erf(up * inv_root_two))
        act = (up * half).astype(bf16)
        slope = half + up * jnp.exp(-0.5 * up * up) * inv_root_tau
        act_t_o[:, at] = act.T
        slope_o[at, :] = slope.astype(bf16)
        feed_s[at, :] += nn(act, w_out[...])

    @pl.when(step == last)
    def _():
        for r in range(rows_here):
            at = slice(r * seq, (r + 1) * seq)
            full = hid[r][...] + feed_s[at, :]
            centre = full - mean_of(full)
            rho = lax.rsqrt(mean_of(centre * centre) + norm_eps)
            normed = centre * rho
            out = normed * g2[...] + s2[...]
            full_s[at, :] = out
            out_o[at, :] = out.astype(bf16)
            n2_o[at, :] = normed.astype(bf16)
            rho_o[at, :] = jnp.broadcast_to(rho, (seq, 128))
        for r in range(rows_here):
            for k, spot in enumerate(start_spots(me, lengths, r, rows_here, part_len, pairs, seq)):
                first_o[r * pairs + k : r * pairs + k + 1, :] = full_s[pl.ds(spot, 1), :]


def start_spots(me, lengths, r, rows_here, part_len, pairs, seq):
    shift = part_len.bit_length() - 1
    spots = []
    start = jnp.int32(0)
    for k in range(pairs):
        spots.append(r * seq + (((start >> shift) ^ me[0]) << shift) + (start & (part_len - 1)))
        start = start + lengths[me[0] * rows_here + r, k]
    return spots


def feed_forward(part_len, me, lengths, hids, w_in, b_in, w_out, b_out, gain, shift):
    rows_here = len(hids)
    seq, width = hids[0].shape
    pairs = lengths.shape[1]
    units = w_in.shape[1]
    count = rows_here * seq
    steps = units // CHUNK
    return pl.pallas_call(
        functools.partial(feed_kernel, rows_here, part_len, pairs),
        grid=(steps,),
        in_specs=[SMEM_SPEC, SMEM_SPEC]
        + [whole((seq, width))] * rows_here
        + [pl.BlockSpec((width, CHUNK), lambda c: (0, c)), pl.BlockSpec((1, CHUNK), lambda c: (0, c)),
           pl.BlockSpec((CHUNK, width), lambda c: (c, 0)),
           whole((1, width)), whole((1, width)), whole((1, width))],
        out_specs=[pl.BlockSpec((CHUNK, count), lambda c: (c, 0)), pl.BlockSpec((count, CHUNK), lambda c: (0, c)),
                   whole((count, width)), whole((count, width)), whole((count, 128)), whole((rows_here * pairs, width))],
        out_shape=[jax.ShapeDtypeStruct((units, count), bf16), jax.ShapeDtypeStruct((count, units), bf16),
                   jax.ShapeDtypeStruct((count, width), bf16), jax.ShapeDtypeStruct((count, width), bf16),
                   jax.ShapeDtypeStruct((count, 128), f32), jax.ShapeDtypeStruct((rows_here * pairs, width), f32)],
        scratch_shapes=[pltpu.VMEM((count, width), bf16), pltpu.VMEM((count, width), f32), pltpu.VMEM((count, width), f32)],
        compiler_params=params(),
        cost_estimate=cost(4 * count * width * units, 35e6, 2 * count * units),
        name="feed_forward",
    )(me, lengths, *hids, w_in, b_in, w_out, b_out, gain, shift)


def dot_high(left, right, dims):
    return lax.dot_general(left, right, (dims, ((), ())), precision=lax.Precision.HIGHEST, preferred_element_type=f32)


def ramp_kernel(
    rows_here, part_len, pairs, mixers, classes,
    me, lengths, labels, first, w_pool, b_pool, w_class_t, b_class, *refs,
):
    cots, refs = refs[:mixers], refs[mixers:]
    n2, rho, g2, loss_o, vec_o, first_t_o, pre_o, sum_o, low_o, e_s, gf_s, tmp_s = refs
    seq = part_len * mixers
    here = rows_here * pairs
    width = first.shape[1]
    firsts = first[...]
    pooled = jnp.tanh(dot_high(firsts, w_pool[...], ((1,), (0,))) + b_pool[...])
    lane = lax.broadcasted_iota(jnp.int32, (here, 128), 1)
    logits = dot_high(pooled, w_class_t[...], ((1,), (1,))) + b_class[...]
    logits = jnp.where(lane < classes, logits, -jnp.inf)
    top = jnp.max(logits, axis=-1, keepdims=True)
    expo = jnp.exp(logits - top)
    total = jnp.sum(expo, axis=-1, keepdims=True)
    log_total = top + jnp.log(total)
    sub = lax.broadcasted_iota(jnp.int32, (here, 128), 0)
    label = jnp.zeros((here, 128), jnp.int32)
    for r in range(rows_here):
        for k in range(pairs):
            label = jnp.where(sub == r * pairs + k, labels[me[0] * rows_here + r, k], label)
    chosen = lane == label
    loss_o[...] = jnp.broadcast_to(
        log_total - jnp.sum(jnp.where(chosen, logits, 0.0), axis=-1, keepdims=True), loss_o.shape)
    grad_logits = expo / total - chosen.astype(f32)
    grad_pre = dot_high(grad_logits, w_class_t[...], ((1,), (0,))) * (1.0 - pooled * pooled)
    gf_s[...] = dot_high(grad_pre, w_pool[...], ((1,), (1,)))
    rows = [None] * 8
    rows[3] = col_sum(grad_pre)
    for c in range(classes):
        rows[4 + c] = col_sum(pooled * grad_logits[:, c : c + 1])
    rows[7] = jnp.concatenate([col_sum(grad_logits), jnp.zeros((1, width - 128), f32)], axis=1)
    pad = jnp.zeros((128 - here, width), f32)
    first_t_o[...] = jnp.concatenate([firsts, pad], axis=0).T.astype(bf16)
    pre_o[...] = jnp.concatenate([grad_pre, pad], axis=0).astype(bf16)
    for r in range(rows_here):
        for i, cot in enumerate(cots):
            at = r * seq + i * part_len
            e_s[at : at + part_len, :] = cot[r].astype(f32)
        for k, spot in enumerate(start_spots(me, lengths, r, rows_here, part_len, pairs, seq)):
            e_s[pl.ds(spot, 1), :] = e_s[pl.ds(spot, 1), :] + gf_s[r * pairs + k : r * pairs + k + 1, :]
    sums = [jnp.zeros((1, width), f32)] * 3
    tile = 256
    for i in range(rows_here * seq // tile):
        at = slice(i * tile, (i + 1) * tile)
        e = e_s[at, :]
        normed = n2[at, :].astype(f32)
        eg = e * g2[...]
        grad = rho[at, 0:1] * (eg - mean_of(eg) - normed * mean_of(eg * normed))
        sum_o[at, :] = grad
        low = grad.astype(bf16)
        low_o[at, :] = low
        sums = [sums[0] + col_sum(low.astype(f32)), sums[1] + col_sum(e * normed), sums[2] + col_sum(e)]
    rows[0:3] = sums
    for i, value in enumerate(rows):
        vec_o[i : i + 1, :] = value


def off_ramp(part_len, me, lengths, labels, firsts, w_pool, b_pool, w_class_t, b_class, cots, n2, rho, gain):
    rows_here = cots[0].shape[0]
    mixers = len(cots)
    width = firsts.shape[1]
    pairs = lengths.shape[1]
    classes = 3
    here = rows_here * pairs
    count = n2.shape[0]
    return pl.pallas_call(
        functools.partial(ramp_kernel, rows_here, part_len, pairs, mixers, classes),
        in_specs=[SMEM_SPEC] * 3 + [pl.BlockSpec(memory_space=pltpu.VMEM)] * (5 + mixers + 3),
        out_specs=[pl.BlockSpec(memory_space=pltpu.VMEM)] * 6,
        out_shape=[jax.ShapeDtypeStruct((here, 128), f32), jax.ShapeDtypeStruct((8, width), f32),
                   jax.ShapeDtypeStruct((width, 128), bf16), jax.ShapeDtypeStruct((128, width), bf16),
                   jax.ShapeDtypeStruct((count, width), f32), jax.ShapeDtypeStruct((count, width), bf16)],
        scratch_shapes=[pltpu.VMEM((count, width), f32), pltpu.VMEM((here, width), f32), pltpu.VMEM((here, width), f32)],
        compiler_params=params(),
        cost_estimate=cost(2e8, 12e6, 1e4),
        name="off_ramp",
    )(me, lengths, labels, firsts, w_pool, b_pool, w_class_t, b_class, *cots, n2, rho, gain)


def back_kernel(rows_here, *refs):
    low, slope, w_out, w_in, sum_two = refs[:5]
    refs = refs[5:]
    n1, refs = refs[:rows_here], refs[rows_here:]
    rho, refs = refs[:rows_here], refs[rows_here:]
    g1, w_attn = refs[:2]
    up_o, bin_o, vec_o, att_o = refs[2:6]
    refs = refs[6:]
    sum_o, refs = refs[:rows_here], refs[rows_here:]
    mix_o, refs = refs[:rows_here], refs[rows_here:]
    (hid_s,) = refs
    step = pl.program_id(0)
    last = pl.num_programs(0) - 1
    seq = n1[0].shape[0]
    tile = 256

    @pl.when(step == 0)
    def _():
        hid_s[...] = sum_two[...]

    total = jnp.zeros((1, bin_o.shape[1]), f32)
    for i in range(rows_here * seq // tile):
        at = slice(i * tile, (i + 1) * tile)
        up = (nt(low[at, :], w_out[...]) * slope[at, :].astype(f32)).astype(bf16)
        up_o[at, :] = up
        total = total + col_sum(up.astype(f32))
        hid_s[at, :] += nt(up, w_in[...])
    bin_o[...] = total

    @pl.when(step == last)
    def _():
        width = g1.shape[1]
        sums = [jnp.zeros((1, width), f32)] * 3
        for r in range(rows_here):
            for i in range(seq // tile):
                at = slice(i * tile, (i + 1) * tile)
                there = slice(r * seq + i * tile, r * seq + (i + 1) * tile)
                e = hid_s[there, :]
                normed = n1[r][at, :].astype(f32)
                eg = e * g1[...]
                grad = rho[r][at, 0:1] * (eg - mean_of(eg) - normed * mean_of(eg * normed))
                sum_o[r][at, :] = grad
                att = grad.astype(bf16)
                att_o[there, :] = att
                mix_o[r][at, :] = nt(att, w_attn[...]).astype(bf16)
                sums = [sums[0] + col_sum(e * normed), sums[1] + col_sum(e), sums[2] + col_sum(att.astype(f32))]
        for i in range(3):
            vec_o[i : i + 1, :] = sums[i]
        vec_o[3:8, :] = jnp.zeros((5, width), f32)


def feed_backward(low, slope, w_out, w_in, sum_two, n1, rho, gain, w_attn):
    rows_here = len(n1)
    seq, width = n1[0].shape
    count, units = slope.shape
    steps = units // CHUNK
    return pl.pallas_call(
        functools.partial(back_kernel, rows_here),
        grid=(steps,),
        in_specs=[whole((count, width)), pl.BlockSpec((count, CHUNK), lambda c: (0, c)),
                  pl.BlockSpec((CHUNK, width), lambda c: (c, 0)), pl.BlockSpec((width, CHUNK), lambda c: (0, c)),
                  whole((count, width))]
        + [whole((seq, width))] * rows_here + [whole((seq, 128))] * rows_here
        + [whole((1, width)), whole((width, width))],
        out_specs=[pl.BlockSpec((count, CHUNK), lambda c: (0, c)), pl.BlockSpec((1, CHUNK), lambda c: (0, c)),
                   whole((8, width)), whole((count, width))]
        + [whole((seq, width))] * (2 * rows_here),
        out_shape=[jax.ShapeDtypeStruct((count, units), bf16), jax.ShapeDtypeStruct((1, units), f32),
                   jax.ShapeDtypeStruct((8, width), f32), jax.ShapeDtypeStruct((count, width), bf16)]
        + [jax.ShapeDtypeStruct((seq, width), f32)] * rows_here
        + [jax.ShapeDtypeStruct((seq, width), bf16)] * rows_here,
        scratch_shapes=[pltpu.VMEM((count, width), f32)],
        compiler_params=params(),
        cost_estimate=cost(2 * count * width * (2 * units + width), 35e6),
        name="feed_backward",
    )(low, slope, w_out, w_in, sum_two, *n1, *rho, gain, w_attn)


def attention_back_kernel(
    head_size, qs_r, k_r, v_r, probs_r, mix_t, grad_r, wq, wk, wv, sum_one,
    dq_o, dk_o, dv_o, bq_o, bv_o, tok_o, acc_s,
):
    step = pl.program_id(0)
    last = pl.num_programs(0) - 1
    qs, keys, values, grad = qs_r[...], k_r[...], v_r[...], grad_r[...]
    keys_t = keys.T
    prod = grad.T.astype(f32) * mix_t[...].astype(f32)
    lane = lax.broadcasted_iota(jnp.int32, (1, GROUP * head_size), 1) // head_size
    dk = dv = None
    dq_t = []
    for h in range(GROUP):
        rows = slice(h * head_size, (h + 1) * head_size)
        inner = col_sum(prod[rows])
        grad_h = jnp.where(lane == h, grad, bf16(0))
        grad_probs = nt(values, grad_h)
        probs = probs_r[h]
        grad_scores = (probs.astype(f32) * (grad_probs - inner)).astype(bf16)
        dv_h = nn(probs, grad_h)
        dk_h = nn(grad_scores, jnp.where(lane == h, qs, bf16(0)))
        dv = dv_h if dv is None else dv + dv_h
        dk = dk_h if dk is None else dk + dk_h
        dq_t.append(nn(keys_t[rows], grad_scores))
    dq = (jnp.concatenate(dq_t, axis=0) * (head_size ** (-0.5))).astype(bf16).T
    dk = dk.astype(bf16)
    dv = dv.astype(bf16)
    dq_o[...] = dq
    dk_o[...] = dk
    dv_o[...] = dv
    bq_o[...] = col_sum(dq.astype(f32))
    bv_o[...] = col_sum(dv.astype(f32))
    part = nt(dq, wq[...]) + nt(dk, wk[...]) + nt(dv, wv[...])

    @pl.when(step == 0)
    def _():
        acc_s[...] = sum_one[...] + part

    @pl.when(step > 0)
    def _():
        acc_s[...] += part

    @pl.when(step == last)
    def _():
        tok_o[...] = acc_s[...].astype(bf16)


def attention_backward(qs, keys, values, probs, mix_t, grad_mix, w_qkv, sum_one):
    seq, width = qs.shape
    head_size = width // HEADS
    span = GROUP * head_size
    steps = width // span
    col = pl.BlockSpec((seq, span), lambda g: (0, g))
    vec = pl.BlockSpec((1, span), lambda g: (0, g))

    def weight(which):
        return pl.BlockSpec((width, span), lambda g: (0, which * steps + g))

    return pl.pallas_call(
        functools.partial(attention_back_kernel, head_size),
        grid=(steps,),
        in_specs=[col, col, col, pl.BlockSpec((GROUP, seq, seq), lambda g: (g, 0, 0)),
                  pl.BlockSpec((span, seq), lambda g: (g, 0)), col,
                  weight(0), weight(1), weight(2), whole((seq, width))],
        out_specs=[col, col, col, vec, vec, whole((seq, width))],
        out_shape=[jax.ShapeDtypeStruct((seq, width), bf16)] * 3
        + [jax.ShapeDtypeStruct((1, width), f32)] * 2
        + [jax.ShapeDtypeStruct((seq, width), bf16)],
        scratch_shapes=[pltpu.VMEM((seq, width), f32)],
        compiler_params=params(),
        cost_estimate=cost(2 * seq * width * width * 3 + 32 * seq * seq * width, 18e6),
        name="attention_backward",
    )(qs, keys, values, probs, mix_t, grad_mix, w_qkv, w_qkv, w_qkv, sum_one)


UNIT_ROWS = 48


def unit_kernel(parts, keep, here, *refs):
    recv = None
    lefts, refs = refs[:parts], refs[parts:]
    rights, refs = refs[:parts], refs[parts:]
    if keep:
        recv, refs = refs[0], refs[1:]
    outs, (left_s,) = refs[:-1], refs[-1:]
    dp = here[1]
    blocks = 8
    acc = None
    at = 0
    for left, right in zip(lefts, rights):
        depth = left.shape[-1]
        for p in range(blocks):
            left_s[p * UNIT_ROWS : (p + 1) * UNIT_ROWS, at : at + depth] = left[p ^ dp].reshape(UNIT_ROWS, depth)
        term = nn(left_s[:, at : at + depth], right[...])
        acc = term if acc is None else acc + term
        at += depth
    width = acc.shape[1]
    acc = acc.reshape(blocks, UNIT_ROWS, width)
    if not keep:
        outs[0][...] = acc.astype(bf16).reshape(outs[0].shape)
        return
    acc = acc + recv[...].reshape(acc.shape).astype(f32)
    low = acc.astype(bf16)
    half = width // 2
    upper = (here[0] >> 1) & 1
    first = jnp.where(upper == 0, low[:, :, :half], low[:, :, half:])
    second = jnp.where(upper == 0, low[:, :, half:], low[:, :, :half])
    xk, xs, yk, ys = outs
    for z2 in range(2):
        for x, out in ((0, xk), (1, xs)):
            out[0, z2, :, :half] = first[z2 * 4 + x]
            out[0, z2, :, half:] = second[z2 * 4 + x]
        for x in range(2):
            yk[0, x, z2] = first[z2 * 4 + 2 + x]
            ys[0, x, z2] = second[z2 * 4 + 2 + x]


def unit_products(here, keep, units, left_specs, lefts, right_specs, rights, recv=None, width=768):
    parts = len(lefts)
    depth = sum(a.shape[-1] for a in lefts)
    half = width // 2
    if keep:
        shapes = [(units, 2, UNIT_ROWS, width)] * 2 + [(units, 2, 2, UNIT_ROWS, half)] * 2
    else:
        shapes = [(units, 8, UNIT_ROWS, width)]
    extra_specs, extra = [], []
    if keep:
        extra_specs = [pl.BlockSpec((1, 8, UNIT_ROWS, width), lambda j, s: (j, 0, 0, 0))]
        extra = [recv]
    return pl.pallas_call(
        functools.partial(unit_kernel, parts, keep),
        grid_spec=pltpu.PrefetchScalarGridSpec(
            num_scalar_prefetch=1,
            grid=(units,),
            in_specs=left_specs + right_specs + extra_specs,
            out_specs=[pl.BlockSpec((1,) + s[1:], lambda j, s, n=len(s): (j,) + (0,) * (n - 1)) for s in shapes],
            scratch_shapes=[pltpu.VMEM((8 * UNIT_ROWS, depth), bf16)],
        ),
        out_shape=[jax.ShapeDtypeStruct(s, bf16) for s in shapes],
        compiler_params=params(),
        cost_estimate=cost(2 * units * 384 * depth * width, units * (384 * depth * 2 + 384 * width * 4) + depth * width * 2),
        name="unit_keep" if keep else "unit_send",
    )(here, *lefts, *rights, *extra)


def vmem_call(kernel, shapes, name, *args):
    return pl.pallas_call(
        kernel,
        in_specs=[pl.BlockSpec(memory_space=pltpu.VMEM)] * len(args),
        out_specs=[pl.BlockSpec(memory_space=pltpu.VMEM)] * len(shapes),
        out_shape=[jax.ShapeDtypeStruct(s, bf16) for s in shapes],
        compiler_params=params(),
        cost_estimate=cost(sum(a.size for a in args), 2 * sum(a.size for a in args) * 2),
        name=name,
    )(*args)


def second_kernel(xk, xr, yk, yr, x2k, x2s, y2k, y2s):
    half = x2k.shape[-1]
    x = (xk[...].astype(f32) + xr[...].astype(f32)).astype(bf16)
    x2k[...] = x[..., :half]
    x2s[...] = x[..., half:]
    y = (yk[...].astype(f32) + yr[...].astype(f32)).astype(bf16)
    y2k[...] = y[:, 0]
    y2s[...] = y[:, 1]


def third_kernel(xk, xr, yk, yr, x3, y3):
    x3[...] = (xk[...].astype(f32) + xr[...].astype(f32)).astype(bf16)
    y3[...] = (yk[...].astype(f32) + yr[...].astype(f32)).astype(bf16)


def fourth_kernel(x, r, keep, send):
    z = (x[...].astype(f32) + r[...].astype(f32)).astype(bf16)
    keep[...] = z[:, 0]
    send[...] = z[:, 1]


def fifth_kernel(z, r, out):
    out[...] = (z[...].astype(f32) + r[...].astype(f32)).astype(bf16)


def swap(value, axis, bit):
    size = lax.axis_size(axis)
    return lax.ppermute(value, axis, [(i, i ^ bit) for i in range(size)])


def reduce_units(xk, xs, yk, ys):
    units, _, rows, width = xk.shape
    half = width // 2
    xr, yr = swap(xs, "dp", 1), swap(ys, "mix", 2)
    small = (units, 2, rows, half)
    x2k, x2s, y2k, y2s = vmem_call(second_kernel, [small] * 4, "stage_two", xk, xr, yk, yr)
    xr, yr = swap(x2s, "mix", 2), swap(y2s, "dp", 1)
    x3, y3 = vmem_call(third_kernel, [small] * 2, "stage_three", x2k, xr, y2k, yr)
    yr = swap(y3, "dp", 2)
    tiny = (units, rows, half)
    keep, send = vmem_call(fourth_kernel, [tiny] * 2, "stage_four", x3, yr)
    zr = swap(send, "dp", 4)
    (final,) = vmem_call(fifth_kernel, [tiny], "stage_five", keep, zr)
    other = swap(final, "mix", 2)
    both = jnp.stack([final, other])
    return both, swap(both, "mix", 1)


def place_kernel(plan, here, own, far, *outs):
    core = here[0] & 1
    upper = (here[0] >> 1) & 1
    half = own.shape[-1]
    rows = own.shape[-2]
    for u, (which, row, col, step) in enumerate(plan):
        for c, ref in enumerate((own, far)):
            for y in range(2):
                r0 = pl.multiple_of(row + (core ^ c) * step, 8)
                c0 = pl.multiple_of(col + (upper ^ y) * half, 128)
                outs[which][pl.ds(r0, rows), pl.ds(c0, half)] = ref[y, u].astype(f32)


def place_units(here, plan, shapes, own, far):
    vm = pl.BlockSpec(memory_space=pltpu.VMEM)
    return pl.pallas_call(
        functools.partial(place_kernel, plan),
        in_specs=[SMEM_SPEC, vm, vm],
        out_specs=[vm] * len(shapes),
        out_shape=[jax.ShapeDtypeStruct(s, f32) for s in shapes],
        compiler_params=params(),
        cost_estimate=cost(own.size, own.size * 12),
        name="place_units",
    )(here, own, far)


def on_device(
    tokens, cotangent, pair_lengths, labels, w_qkv, b_query, b_value, w_attn, b_attn, gain_one, shift_one,
    w_in, b_in, w_out, b_out, gain_two, shift_two, w_pool, b_pool, w_class, b_class,
):
    row_count, part_len, width = tokens.shape
    mixers = lax.axis_size("mix")
    dps = lax.axis_size("dp")
    rows_here = row_count // mixers
    seq = part_len * mixers
    units_in = w_in.shape[1]
    mix = lax.axis_index("mix").astype(jnp.int32)
    dp = lax.axis_index("dp").astype(jnp.int32)
    here = jnp.stack([mix, dp])
    pairs = pair_lengths.shape[1]

    def gather_rows(array):
        chunks = array.reshape(mixers, rows_here, part_len, width)
        sent = [lax.dynamic_index_in_dim(chunks, mix ^ k, 0, keepdims=False) for k in range(mixers)]
        return sent

    tok_sent = gather_rows(tokens)
    tok_rows = [
        [tok_sent[0][r]] + [swap(tok_sent[k][r], "mix", k) for k in range(1, mixers)] for r in range(rows_here)
    ]
    cot_sent = gather_rows(cotangent)
    cots = [cot_sent[0]] + [swap(cot_sent[k], "mix", k) for k in range(1, mixers)]

    def row_vec(v):
        return v.reshape(1, -1)

    state = [
        forward_row(r, rows_here, here, pair_lengths, tok_rows[r], w_qkv, row_vec(b_query), row_vec(b_value),
                    w_attn, row_vec(b_attn), row_vec(gain_one), row_vec(shift_one))
        for r in range(rows_here)
    ]
    qs, keys, values, probs, mix_t, tok_t, hids, hid_t, n1, rho1 = zip(*state)
    act_t, slope, output, n2, rho2, firsts = feed_forward(
        part_len, here, pair_lengths, hids, w_in, row_vec(b_in), w_out, row_vec(b_out), row_vec(gain_two), row_vec(shift_two))
    w_class_t = jnp.zeros((128, width), f32).at[: w_class.shape[1]].set(w_class.T)
    b_class_row = jnp.zeros((1, 128), f32).at[0, : w_class.shape[1]].set(b_class)
    loss, vec_ramp, first_t, grad_pre, sum_two, grad_feed = off_ramp(
        part_len, here, pair_lengths, labels, firsts, w_pool, row_vec(b_pool), w_class_t, b_class_row, cots, n2, rho2,
        row_vec(gain_two))

    def give_back(blocks):
        got = [blocks[0]] + [swap(blocks[k], "mix", k) for k in range(1, mixers)]
        full = jnp.zeros((mixers,) + got[0].shape, got[0].dtype)
        for k in range(mixers):
            full = lax.dynamic_update_index_in_dim(full, got[k], mix ^ k, 0)
        return full.reshape(row_count, part_len, width)

    out_view = output.reshape(rows_here, mixers, part_len, width)
    output_back = give_back([out_view[:, k] for k in range(mixers)])
    loss_pairs = loss[:, 0].reshape(rows_here, pairs)
    loss_back = jnp.zeros((mixers, rows_here, pairs), f32)
    for k in range(mixers):
        got = loss_pairs if k == 0 else swap(loss_pairs, "mix", k)
        loss_back = lax.dynamic_update_index_in_dim(loss_back, got, mix ^ k, 0)
    loss_back = loss_back.reshape(row_count, pairs)

    back = feed_backward(grad_feed, slope, w_out, w_in, sum_two, n1, rho1, row_vec(gain_one), w_attn)
    grad_up, bin_sum, vec_back, grad_att = back[:4]
    sum_one, grad_mix = back[4 : 4 + rows_here], back[4 + rows_here :]
    tail = [
        attention_backward(qs[r], keys[r], values[r], probs[r], mix_t[r], grad_mix[r], w_qkv, sum_one[r])
        for r in range(rows_here)
    ]
    dq, dk, dv, bq, bv, grad_tok = zip(*tail)
    tok_view = jnp.stack([g.reshape(mixers, part_len, width) for g in grad_tok], axis=1)
    tokens_back = give_back([tok_view[k] for k in range(mixers)])

    vecs = jnp.concatenate(
        [vec_ramp, vec_back[:3], bin_sum.reshape(-1, width), sum(bq), sum(bv)], axis=0)
    for axis in ("mix", "dp"):
        bit = 1
        while bit < lax.axis_size(axis):
            vecs = vecs + swap(vecs, axis, bit)
            bit *= 2
    share = width // dps
    vec_rows = lax.dynamic_slice_in_dim(vecs, dp * share, share, axis=1)
    bin_total = vecs[11 : 11 + units_in // width].reshape(-1)
    bin_share = lax.dynamic_slice_in_dim(bin_total, dp * (units_in // dps), units_in // dps)
    late = 11 + units_in // width

    if dps == 8 and mixers == 4 and width == 768 and units_in == 3072 and seq * rows_here == 1024:
        grads = quick_grads(
            here, act_t, grad_feed, first_t, grad_pre, hid_t, grad_up, mix_t, grad_att, tok_t, dq, dk, dv)
    else:
        grads = plain_grads(
            rows_here, act_t, grad_feed, first_t, grad_pre, hid_t, grad_up, mix_t, grad_att, tok_t, dq, dk, dv)
    grad_w_qkv, grad_w_attn, grad_w_in, grad_w_out, grad_w_pool = grads
    return (
        output_back, loss_back, tokens_back,
        grad_w_qkv, vec_rows[late], vec_rows[late + 1],
        grad_w_attn, vec_rows[10], vec_rows[8], vec_rows[9],
        grad_w_in, bin_share, grad_w_out, vec_rows[0], vec_rows[1], vec_rows[2],
        grad_w_pool, vec_rows[3], vec_rows[4:7].T, vecs[7, :3],
    )


def quick_grads(here, act_t, grad_feed, first_t, grad_pre, hid_t, grad_up, mix_t, grad_att, tok_t, dq, dk, dv):
    width = 768
    seq = hid_t[0].shape[1]

    def split_rows(array):
        return array.reshape(8, 2, UNIT_ROWS, array.shape[-1])

    def core_rows(flip, depth):
        return pl.BlockSpec((8, 1, UNIT_ROWS, depth), lambda j, s: (0, (s[0] & 1) ^ flip, 0, 0))

    def both(units, left_spec, lefts, right_specs, rights):
        (send,) = unit_products(here, False, units, left_spec(1), lefts, right_specs, rights)
        recv = swap(send, "mix", 1)
        return unit_products(here, True, units, left_spec(0), lefts, right_specs, rights, recv)

    def fixed(shape):
        return pl.BlockSpec(shape, lambda j, s: (0,) * len(shape))

    def bundle(*kinds):
        return [jnp.concatenate(items, axis=0) if len(items) > 1 else items[0] for items in zip(*kinds)]

    count = grad_feed.shape[0]
    out_left = act_t.reshape(8, 2, 4, UNIT_ROWS, count)
    kind_out = both(
        4, lambda flip: [pl.BlockSpec((8, 1, 1, UNIT_ROWS, count), lambda j, s: (0, (s[0] & 1) ^ flip, j, 0, 0))],
        [out_left], [fixed((count, width))], [grad_feed])
    kind_pool = both(
        1, lambda flip: [core_rows(flip, 128)], [split_rows(first_t)], [fixed((128, width))], [grad_pre])
    own, far = reduce_units(*bundle(kind_out, kind_pool))
    grad_w_out, grad_w_pool = place_units(
        here, [(0, j * UNIT_ROWS, 0, 192) for j in range(4)] + [(1, 0, 0, UNIT_ROWS)],
        [(384, width), (96, width)], own, far)

    rows_here = len(hid_t)
    kind_in = both(
        4, lambda flip: [core_rows(flip, seq)] * rows_here, [split_rows(a) for a in hid_t],
        [pl.BlockSpec((seq, width), lambda j, s, r=r: (r, j)) for r in range(rows_here)], [grad_up] * rows_here)
    kind_att = both(
        1, lambda flip: [core_rows(flip, seq)] * rows_here, [split_rows(a) for a in mix_t],
        [pl.BlockSpec((seq, width), lambda j, s, r=r: (r, 0)) for r in range(rows_here)], [grad_att] * rows_here)
    own, far = reduce_units(*bundle(kind_in, kind_att))
    grad_w_in, grad_w_attn = place_units(
        here, [(0, 0, j * width, UNIT_ROWS) for j in range(4)] + [(1, 0, 0, UNIT_ROWS)],
        [(96, 4 * width), (96, width)], own, far)

    grads = [jnp.concatenate([a, b, c], axis=1) for a, b, c in zip(dq, dk, dv)]
    kind_qkv = both(
        3, lambda flip: [core_rows(flip, seq)] * rows_here, [split_rows(a) for a in tok_t],
        [pl.BlockSpec((seq, width), lambda j, s: (0, j))] * rows_here, grads)
    own, far = reduce_units(*kind_qkv)
    (grad_w_qkv,) = place_units(
        here, [(0, 0, j * width, UNIT_ROWS) for j in range(3)], [(96, 3 * width)], own, far)
    return grad_w_qkv, grad_w_attn, grad_w_in, grad_w_out, grad_w_pool


def plain_grads(rows_here, act_t, grad_feed, first_t, grad_pre, hid_t, grad_up, mix_t, grad_att, tok_t, dq, dk, dv):
    seq = hid_t[0].shape[1]

    def over_rows(lefts, right):
        return sum(nn(lefts[r], right[r * seq : (r + 1) * seq]) for r in range(rows_here))

    grad_qkv = jnp.concatenate(
        [jnp.concatenate(parts, axis=1) for parts in zip(dq, dk, dv)], axis=0)
    grads = (
        over_rows(tok_t, grad_qkv), over_rows(mix_t, grad_att), over_rows(hid_t, grad_up), nn(act_t, grad_feed),
        nn(first_t, grad_pre),
    )
    shards = [lax.psum_scatter(g, "dp", scatter_dimension=0, tiled=True) for g in grads]
    return [lax.psum(s.astype(bf16), "mix").astype(f32) for s in shards]


def solution(mesh):
    wide = P("dp", "mix", None)
    split = P("dp", None)
    in_specs = (wide, wide, split, split) + (P(),) * 17
    out_specs = (
        wide, split, wide,
        split, P("dp"), P("dp"), split, P("dp"), P("dp"), P("dp"),
        split, P("dp"), split, P("dp"), P("dp"), P("dp"),
        split, P("dp"), split, P(),
    )
    return jax.shard_map(on_device, mesh=mesh, in_specs=in_specs, out_specs=out_specs, check_vma=False)
```

```python
import functools

import jax
import jax.numpy as jnp
from jax import lax
from jax.experimental import pallas as pl
from jax.experimental.pallas import tpu as pltpu
from jax.sharding import PartitionSpec as P

HEADS = 12
SCALE = 1.0
STAGE = (0, 20e6, 0)
GROUP = 4
CHUNK = 768
TILE = 256
UNIT = 48
HALF = 384
norm_eps = 1e-06
masked_score = -1000000000.0
inv_root_two = 0.7071067811865476
inv_root_tau = 0.3989422804014327
f32 = jnp.float32
bf16 = jnp.bfloat16
VMEM_LIMIT = 56 * 1024 * 1024
SMEM_SPEC = pl.BlockSpec(memory_space=pltpu.SMEM)
B_QUERY, B_VALUE, B_ATTN, GAIN_ONE, SHIFT_ONE, B_OUT, GAIN_TWO, SHIFT_TWO, B_POOL, B_IN, B_CLASS = 0, 1, 2, 3, 4, 5, 6, 7, 8, 9, 13


def whole(shape):
    return pl.BlockSpec(shape, lambda *_: (0,) * len(shape))


def sds(shape, dtype):
    return jax.ShapeDtypeStruct(shape, dtype)


def nn(left, right):
    return jnp.dot(left, right, preferred_element_type=f32)


def nt(left, right):
    return lax.dot_general(left, right, (((1,), (1,)), ((), ())), preferred_element_type=f32)


def tn(left, right):
    return lax.dot_general(left, right, (((0,), (0,)), ((), ())), preferred_element_type=f32)


def call(kernel, name, grid, in_specs, out_specs, out_shape, scratch, work, *args, prefetch=0):
    work = work or (0, 8 * sum(a.size for a in args), 0)
    common = dict(
        out_shape=out_shape,
        compiler_params=pltpu.CompilerParams(vmem_limit_bytes=VMEM_LIMIT),
        cost_estimate=pl.CostEstimate(flops=int(2 * work[0] * SCALE), bytes_accessed=int(work[1] * SCALE), transcendentals=0),
        name=name,
    )
    if prefetch:
        spec = pltpu.PrefetchScalarGridSpec(
            num_scalar_prefetch=prefetch, grid=grid, in_specs=in_specs, out_specs=out_specs, scratch_shapes=scratch)
        return pl.pallas_call(kernel, grid_spec=spec, **common)(*args)
    return pl.pallas_call(
        kernel, grid=grid, in_specs=in_specs, out_specs=out_specs, scratch_shapes=scratch, **common)(*args)


def after(value, *earlier):
    return lax.optimization_barrier((value,) + earlier)[0]


def mean_of(values):
    return jnp.mean(values, axis=-1, keepdims=True)


def col_sum(values):
    return jnp.sum(values, axis=0, keepdims=True)


def head_only(values, head, size):
    lane = lax.broadcasted_iota(jnp.int32, (1, values.shape[1]), 1) // size
    return jnp.where(lane == head, values, jnp.zeros((), values.dtype))


def per_head(values, size):
    return jnp.concatenate([head_only(values, h, size) for h in range(GROUP)], axis=0)


def fold_heads(stacked, size):
    rows = stacked.shape[0] // GROUP
    return sum(head_only(stacked[h * rows : (h + 1) * rows], h, size) for h in range(GROUP))


def segments(places, lengths, row):
    total = jnp.int32(0)
    seg = jnp.zeros(places.shape, jnp.int32)
    for k in range(lengths.shape[1]):
        total = total + lengths[row, k]
        seg = seg + (places >= total).astype(jnp.int32)
    return seg


def forward_kernel(row, rows_here, part_len, mixers, head_size, here, lengths, *refs):
    pieces, refs = refs[:mixers], refs[mixers:]
    (pack, packq, packv, wq, wk, wv, wa,
     qkv_o, probs_o, left_o, hid_o, n1_o, rho_o,
     tok_s, mix_s, bias_s, w_s) = refs
    step = pl.program_id(0)
    seq = part_len * mixers
    shift = part_len.bit_length() - 1
    span = GROUP * head_size

    @pl.when(step == 0)
    def _():
        for i, piece in enumerate(pieces):
            tok_s[i * part_len : (i + 1) * part_len, :] = piece[...]
        mine = here[0]
        down = lax.broadcasted_iota(jnp.int32, (seq, 1), 0)
        across = lax.broadcasted_iota(jnp.int32, (1, seq), 1)

        def place(i):
            return (((i >> shift) ^ mine) << shift) + (i & (part_len - 1))

        number = mine * rows_here + row
        same = segments(place(down), lengths, number) == segments(place(across), lengths, number)
        bias_s[...] = jnp.where(same, 0.0, masked_score)

    for i, weight in enumerate((wq, wk, wv)):
        w_s[:, i * span : (i + 1) * span] = weight[...]
    qkv = nn(tok_s[...], w_s[...])
    qs = (qkv[:, :span] + packq[B_QUERY : B_QUERY + 1]).astype(bf16) * bf16(head_size ** (-0.5))
    keys = qkv[:, span : 2 * span].astype(bf16)
    values = (qkv[:, 2 * span :] + packv[B_VALUE : B_VALUE + 1]).astype(bf16)
    qkv_o[0, :, :span] = qs
    qkv_o[0, :, span : 2 * span] = keys
    qkv_o[0, :, 2 * span :] = values
    scores = nt(qs, per_head(keys, head_size))
    probs = []
    for h in range(GROUP):
        part = scores[:, h * seq : (h + 1) * seq] + bias_s[...]
        expo = jnp.exp(part - jnp.max(part, axis=1, keepdims=True))
        probs.append((expo * (1.0 / jnp.sum(expo, axis=1, keepdims=True))).astype(bf16))
    probs = jnp.concatenate(probs, axis=1)
    probs_o[0] = probs
    mix_s[step] = nn(probs, per_head(values, head_size)).astype(bf16)

    @pl.when(step == pl.num_programs(0) - 1)
    def _():
        mix = jnp.concatenate([mix_s[g] for g in range(mix_s.shape[0])], axis=1)
        left_o[0] = tok_s[...]
        left_o[2] = mix
        full = tok_s[...].astype(f32) + (nn(mix, wa[...]) + pack[B_ATTN : B_ATTN + 1])
        centre = full - mean_of(full)
        rho = lax.rsqrt(mean_of(centre * centre) + norm_eps)
        normed = centre * rho
        hidden = normed * pack[GAIN_ONE : GAIN_ONE + 1] + pack[SHIFT_ONE : SHIFT_ONE + 1]
        hid_o[...] = hidden
        left_o[1] = hidden.astype(bf16)
        n1_o[...] = normed.astype(bf16)
        rho_o[...] = jnp.broadcast_to(rho, rho_o.shape)


def forward_row(row, rows_here, here, lengths, pieces, pack, w_qkv, w_attn):
    part_len, width = pieces[0].shape
    mixers = len(pieces)
    seq = part_len * mixers
    head_size = width // HEADS
    span = GROUP * head_size
    steps = width // span

    def weight(which):
        return pl.BlockSpec((width, span), lambda g: (0, which * steps + g))

    rows = pack.shape[0]
    column = pl.BlockSpec((rows, span), lambda g: (0, g))
    return call(
        functools.partial(forward_kernel, row, rows_here, part_len, mixers, head_size), "forward_row", (steps,),
        [SMEM_SPEC, SMEM_SPEC] + [whole((part_len, width))] * mixers
        + [whole((rows, width)), column, column, weight(0), weight(1), weight(2), whole((width, width))],
        [pl.BlockSpec((1, seq, 3 * span), lambda g: (g, 0, 0)), pl.BlockSpec((1, seq, GROUP * seq), lambda g: (g, 0, 0)),
         whole((3, seq, width)), whole((seq, width)), whole((seq, width)), whole((seq, 128))],
        [sds((steps, seq, 3 * span), bf16), sds((steps, seq, GROUP * seq), bf16),
         sds((3, seq, width), bf16), sds((seq, width), f32), sds((seq, width), bf16), sds((seq, 128), f32)],
        [pltpu.VMEM((seq, width), bf16), pltpu.VMEM((steps, seq, span), bf16), pltpu.VMEM((seq, seq), f32),
         pltpu.VMEM((width, 3 * span), bf16)],
        (seq * width * width * 4 + 8 * seq * seq * width, 16e6, HEADS * seq * seq),
        here, lengths, *pieces, pack, pack, pack, w_qkv, w_qkv, w_qkv, w_attn)


def start_spots(here, lengths, r, rows_here, part_len, pairs, seq):
    shift = part_len.bit_length() - 1
    spots = []
    start = jnp.int32(0)
    for k in range(pairs):
        spots.append(r * seq + (((start >> shift) ^ here[0]) << shift) + (start & (part_len - 1)))
        start = start + lengths[here[0] * rows_here + r, k]
    return spots


def feed_kernel(rows_here, part_len, pairs, mixers, here, lengths, *refs):
    hid, refs = refs[:rows_here], refs[rows_here:]
    pack, w_in, w_out = refs[:3]
    act_o, slope_o, out_o, n2_o, rho_o, first_o, low_s, feed_s, full_s = refs[3:]
    step = pl.program_id(0)
    last = pl.num_programs(0) - 1
    seq = hid[0].shape[0]
    count = rows_here * seq // TILE

    @pl.when(step == 0)
    def _():
        for r in range(rows_here):
            low_s[r * seq : (r + 1) * seq, :] = hid[r][...].astype(bf16)
        feed_s[...] = jnp.broadcast_to(pack[B_OUT : B_OUT + 1], feed_s.shape)

    bias = pack[pl.ds(B_IN + step, 1), :]

    def rows(i):
        return slice(i * TILE, (i + 1) * TILE)

    up = nn(low_s[rows(0), :], w_in[...])
    before = None
    for i in range(count):
        following = nn(low_s[rows(i + 1), :], w_in[...]) if i + 1 < count else None
        up = up + bias
        half = 0.5 * (1.0 + lax.erf(up * inv_root_two))
        act = (up * half).astype(bf16)
        slope_o[rows(i), :] = (half + up * jnp.exp(-0.5 * up * up) * inv_root_tau).astype(bf16)
        act_o[:, rows(i)] = act.T
        if before is not None:
            feed_s[rows(i - 1), :] += nn(before, w_out[...])
        before, up = act, following
    feed_s[rows(count - 1), :] += nn(before, w_out[...])

    @pl.when(step == last)
    def _():
        for r in range(rows_here):
            for k in range(mixers):
                at = slice(r * seq + k * part_len, r * seq + (k + 1) * part_len)
                full = hid[r][k * part_len : (k + 1) * part_len, :] + feed_s[at, :]
                centre = full - mean_of(full)
                rho = lax.rsqrt(mean_of(centre * centre) + norm_eps)
                normed = centre * rho
                out = normed * pack[GAIN_TWO : GAIN_TWO + 1] + pack[SHIFT_TWO : SHIFT_TWO + 1]
                full_s[at, :] = out
                out_o[here[0] ^ k, r] = out.astype(bf16)
                n2_o[at, :] = normed.astype(bf16)
                rho_o[at, :] = jnp.broadcast_to(rho, (part_len, 128))
        for r in range(rows_here):
            for k, spot in enumerate(start_spots(here, lengths, r, rows_here, part_len, pairs, seq)):
                first_o[r * pairs + k : r * pairs + k + 1, :] = full_s[pl.ds(spot, 1), :]


def feed_forward(part_len, here, lengths, hids, pack, w_in, w_out):
    rows_here = len(hids)
    seq, width = hids[0].shape
    mixers = seq // part_len
    pairs = lengths.shape[1]
    units = w_in.shape[1]
    count = rows_here * seq
    steps = units // CHUNK
    return call(
        functools.partial(feed_kernel, rows_here, part_len, pairs, mixers), "feed_forward", (steps,),
        [SMEM_SPEC, SMEM_SPEC] + [whole((seq, width))] * rows_here
        + [whole(pack.shape), pl.BlockSpec((width, CHUNK), lambda c: (0, c)), pl.BlockSpec((CHUNK, width), lambda c: (c, 0))],
        [pl.BlockSpec((CHUNK, count), lambda c: (c, 0)), pl.BlockSpec((count, CHUNK), lambda c: (0, c))] + [whole((mixers, rows_here, part_len, width))]
        + [whole((count, width)), whole((count, 128)), whole((rows_here * pairs, width))],
        [sds((units, count), bf16), sds((count, units), bf16)] + [sds((mixers, rows_here, part_len, width), bf16)]
        + [sds((count, width), bf16), sds((count, 128), f32), sds((rows_here * pairs, width), f32)],
        [pltpu.VMEM((count, width), bf16), pltpu.VMEM((count, width), f32), pltpu.VMEM((count, width), f32)],
        (2 * count * width * units, 35e6, 2 * count * units),
        here, lengths, *hids, pack, w_in, w_out)


def ramp_kernel(rows_here, part_len, pairs, mixers, here, lengths, labels, first, pack, w_pool, w_class, *refs):
    cots, n2, rho, vec_o, sum_o, low_o, e_s, gf_s, sums_s = refs
    step = pl.program_id(0)
    last = pl.num_programs(0) - 1
    seq = part_len * mixers
    count = rows_here * pairs
    width = first.shape[1]
    classes = w_class.shape[1]

    @pl.when(step == 0)
    def _():
        firsts = first[...]
        pool = w_pool[...]
        pool_high = pool.astype(bf16)
        pool_rest = (pool - pool_high.astype(f32)).astype(bf16)
        first_high = firsts.astype(bf16)
        first_rest = (firsts - first_high.astype(f32)).astype(bf16)
        pre = nn(first_high, pool_high) + nn(first_rest, pool_high) + nn(first_high, pool_rest)
        pooled = jnp.tanh(pre + pack[B_POOL : B_POOL + 1])
        class_t = jnp.concatenate([w_class[...], jnp.zeros((width, 128 - classes), f32)], axis=1).T
        lane = lax.broadcasted_iota(jnp.int32, (count, 128), 1)
        logits = jnp.full((count, 128), -jnp.inf, f32)
        for c in range(classes):
            logits = jnp.where(lane == c, jnp.sum(pooled * class_t[c : c + 1], axis=1, keepdims=True), logits)
        logits = logits + pack[B_CLASS : B_CLASS + 1, :128]
        top = jnp.max(logits, axis=-1, keepdims=True)
        expo = jnp.exp(logits - top)
        total = jnp.sum(expo, axis=-1, keepdims=True)
        log_total = top + jnp.log(total)
        sub = lax.broadcasted_iota(jnp.int32, (count, 128), 0)
        label = jnp.zeros((count, 128), jnp.int32)
        for r in range(rows_here):
            for k in range(pairs):
                label = jnp.where(sub == r * pairs + k, labels[here[0] * rows_here + r, k], label)
        chosen = lane == label
        loss = log_total - jnp.sum(jnp.where(chosen, logits, 0.0), axis=-1, keepdims=True)
        grad_logits = expo / total - chosen.astype(f32)
        grad_pooled = jnp.zeros((count, width), f32)
        for c in range(classes):
            grad_pooled = grad_pooled + grad_logits[:, c : c + 1] * class_t[c : c + 1]
        grad_pre = grad_pooled * (1.0 - pooled * pooled)
        gf_s[...] = nt(grad_pre.astype(bf16), pool_high)
        vec_o[3:4, :] = col_sum(grad_pre)
        for c in range(classes):
            vec_o[4 + c : 5 + c, :] = col_sum(pooled * grad_logits[:, c : c + 1])
        spread = jnp.where(lane == here[0] * count + sub, loss, 0.0)
        vec_o[7:8, :] = jnp.concatenate(
            [col_sum(grad_logits), col_sum(spread), jnp.zeros((1, width - 256), f32)], axis=1)
        none = jnp.zeros((16 - count, width), f32)
        base = seq * rows_here
        low_o[base : base + 16, :] = jnp.concatenate([firsts, none], axis=0).astype(bf16)
        low_o[base + 16 :, :] = jnp.concatenate([grad_pre, none], axis=0).astype(bf16)
        for r in range(rows_here):
            for i in range(mixers):
                at = r * seq + i * part_len
                e_s[at : at + part_len, :] = cots[here[0] ^ i, r].astype(f32)
            for k, spot in enumerate(start_spots(here, lengths, r, rows_here, part_len, pairs, seq)):
                e_s[pl.ds(spot, 1), :] = e_s[pl.ds(spot, 1), :] + gf_s[r * pairs + k : r * pairs + k + 1, :]
        sums_s[...] = jnp.zeros(sums_s.shape, f32)

    e = e_s[pl.ds(pl.multiple_of(step * TILE, TILE), TILE), :]
    normed = n2[...].astype(f32)
    eg = e * pack[GAIN_TWO : GAIN_TWO + 1]
    grad = rho[:, 0:1] * (eg - mean_of(eg) - normed * mean_of(eg * normed))
    sum_o[...] = grad
    low = grad.astype(bf16)
    low_o[pl.ds(pl.multiple_of(step * TILE, TILE), TILE), :] = low
    for i, term in enumerate((low.astype(f32), e * normed, e)):
        sums_s[i : i + 1, :] += col_sum(term)

    @pl.when(step == last)
    def _():
        vec_o[0:3, :] = sums_s[0:3, :]


def off_ramp(part_len, here, lengths, labels, firsts, pack, w_pool, w_class, cots, n2, rho):
    mixers, rows_here = cots.shape[:2]
    width = firsts.shape[1]
    pairs = lengths.shape[1]
    tokens = n2.shape[0]
    tile = pl.BlockSpec((TILE, width), lambda t: (t, 0))
    return call(
        functools.partial(ramp_kernel, rows_here, part_len, pairs, mixers), "off_ramp", (tokens // TILE,),
        [SMEM_SPEC] * 3 + [whole(firsts.shape), whole(pack.shape), whole(w_pool.shape), whole(w_class.shape)]
        + [whole(cots.shape), tile, pl.BlockSpec((TILE, 128), lambda t: (t, 0))],
        [whole((8, width)), tile, whole((tokens + 32, width))],
        [sds((8, width), f32), sds((tokens, width), f32), sds((tokens + 32, width), bf16)],
        [pltpu.VMEM((tokens, width), f32), pltpu.VMEM(firsts.shape, f32), pltpu.VMEM((8, width), f32)],
        (1e8, 14e6, 1e4),
        here, lengths, labels, firsts, pack, w_pool, w_class, cots, n2, rho)


def back_kernel(rows_here, low, slope, w_out, w_in, sum_two, ramp, pack, w_attn, *refs):
    n1, refs = refs[:rows_here], refs[rows_here:]
    rho, refs = refs[:rows_here], refs[rows_here:]
    up_o, vec_o, att_o = refs[:3]
    refs = refs[3:]
    sum_o, refs = refs[:rows_here], refs[rows_here:]
    mix_o, refs = refs[:rows_here], refs[rows_here:]
    (hid_s,) = refs
    step = pl.program_id(0)
    last = pl.num_programs(0) - 1
    seq = n1[0].shape[0]
    count = slope.shape[0] // TILE

    def rows(i):
        return slice(i * TILE, (i + 1) * TILE)

    @pl.when(step == 0)
    def _():
        hid_s[...] = sum_two[...]
        vec_o[7:8, :] = jnp.zeros((1, vec_o.shape[1]), f32)
        vec_o[8:16, :] = ramp[...]

    total = jnp.zeros((1, slope.shape[1]), f32)
    act = nt(low[rows(0), :], w_out[...])
    before = None
    for i in range(count):
        following = nt(low[rows(i + 1), :], w_out[...]) if i + 1 < count else None
        up = (act * slope[rows(i), :].astype(f32)).astype(bf16)
        up_o[rows(i), :] = up
        total = total + col_sum(up.astype(f32))
        if before is not None:
            hid_s[rows(i - 1), :] += nt(before, w_in[...])
        before, act = up, following
    hid_s[rows(count - 1), :] += nt(before, w_in[...])
    vec_o[pl.ds(3 + step, 1), :] = total

    @pl.when(step == last)
    def _():
        width = pack.shape[1]
        sums = [jnp.zeros((1, width), f32)] * 3
        for r in range(rows_here):
            for i in range(seq // TILE):
                at = rows(i)
                there = slice(r * seq + i * TILE, r * seq + (i + 1) * TILE)
                e = hid_s[there, :]
                normed = n1[r][at, :].astype(f32)
                eg = e * pack[GAIN_ONE : GAIN_ONE + 1]
                grad = rho[r][at, 0:1] * (eg - mean_of(eg) - normed * mean_of(eg * normed))
                sum_o[r][at, :] = grad
                att = grad.astype(bf16)
                att_o[there, :] = att
                mix_o[r][at, :] = nt(att, w_attn[...]).astype(bf16)
                sums = [sums[0] + col_sum(e * normed), sums[1] + col_sum(e), sums[2] + col_sum(att.astype(f32))]
        for i in range(3):
            vec_o[i : i + 1, :] = sums[i]


def feed_backward(low, slope, w_out, w_in, sum_two, n1, rho, ramp, pack, w_attn):
    rows_here = len(n1)
    seq, width = n1[0].shape
    count, units = slope.shape
    block = pl.BlockSpec((count, CHUNK), lambda j: (0, j))
    result = call(
        functools.partial(back_kernel, rows_here), "feed_backward", (units // CHUNK,),
        [whole(low.shape), block, pl.BlockSpec((CHUNK, width), lambda j: (j, 0)), pl.BlockSpec((width, CHUNK), lambda j: (0, j)),
         whole((count, width)), whole((8, width)), whole(pack.shape), whole((width, width))]
        + [whole((seq, width))] * rows_here + [whole((seq, 128))] * rows_here,
        [block, whole((16, width)), whole((count, width))] + [whole((seq, width))] * (2 * rows_here),
        [sds((count, units), bf16), sds((16, width), f32), sds((count, width), bf16)]
        + [sds((seq, width), f32)] * rows_here + [sds((seq, width), bf16)] * rows_here,
        [pltpu.VMEM((count, width), f32)],
        (2 * count * width * units + count * width * width, 40e6, 0),
        low, slope, w_out, w_in, sum_two, ramp, pack, w_attn, *n1, *rho)
    return result[0], result[1], result[2], result[3 : 3 + rows_here], result[3 + rows_here :]


def attention_back_kernel(
    head_size, part_len, mixers, here, qkv_r, probs_r, left_r, grad_r, wq, wk, wv, sum_one, vec_in, *refs,
):
    d_o, vec_o, tok_o, acc_s, w_s, vec_s = refs
    step = pl.program_id(0)
    last = pl.num_programs(0) - 1
    span = GROUP * head_size
    seq = qkv_r.shape[1]
    qs, keys, values = qkv_r[0, :, :span], qkv_r[0, :, span : 2 * span], qkv_r[0, :, 2 * span :]
    grad = grad_r[...]
    for i, weight in enumerate((wq, wk, wv)):
        w_s[:, i * span : (i + 1) * span] = weight[...]
    prod = grad.astype(f32) * left_r[0].astype(f32)
    grad_probs = nt(grad, per_head(values, head_size))
    parts = []
    for h in range(GROUP):
        inner = jnp.sum(head_only(prod, h, head_size), axis=1, keepdims=True)
        at = slice(h * seq, (h + 1) * seq)
        parts.append((probs_r[0, :, at].astype(f32) * (grad_probs[:, at] - inner)).astype(bf16))
    grad_scores = jnp.concatenate(parts, axis=1)
    dv = fold_heads(tn(probs_r[0], grad), head_size).astype(bf16)
    dq = (nn(grad_scores, per_head(keys, head_size)) * (head_size ** (-0.5))).astype(bf16)
    dk = fold_heads(tn(grad_scores, qs), head_size).astype(bf16)
    all_three = jnp.concatenate([dq, dk, dv], axis=1)
    half = span // 2
    for c in range(2):
        at = slice(c * half, (c + 1) * half)
        d_o[c] = jnp.concatenate([dq[:, at], dk[:, at], dv[:, at]], axis=1)
    vec_s[step] = jnp.concatenate(
        [col_sum(dq.astype(f32)), col_sum(dv.astype(f32)), jnp.zeros((6, span), f32)], axis=0)
    part = nt(all_three, w_s[...])

    @pl.when(step == 0)
    def _():
        acc_s[...] = sum_one[...] + part

    @pl.when(step > 0)
    def _():
        acc_s[...] += part

    @pl.when(step == last)
    def _():
        steps = vec_s.shape[0]
        for k in range(mixers):
            tok_o[here[0] ^ k] = acc_s[k * part_len : (k + 1) * part_len, :].astype(bf16)
        vec_o[...] = vec_in[...] + jnp.concatenate([vec_s[g] for g in range(steps)], axis=1)


def attention_backward(here, part_len, qkv, probs, left, grad_mix, w_qkv, sum_one, vec_in):
    steps, seq, _ = qkv.shape
    width = grad_mix.shape[1]
    head_size = width // HEADS
    span = GROUP * head_size
    mixers = seq // part_len

    def weight(which):
        return pl.BlockSpec((width, span), lambda g: (0, which * steps + g))

    return call(
        functools.partial(attention_back_kernel, head_size, part_len, mixers), "attention_backward", (steps,),
        [SMEM_SPEC, pl.BlockSpec((1, seq, 3 * span), lambda g: (g, 0, 0)), pl.BlockSpec((1, seq, GROUP * seq), lambda g: (g, 0, 0)),
         pl.BlockSpec((1, seq, span), lambda g: (2, 0, g)), pl.BlockSpec((seq, span), lambda g: (0, g)),
         weight(0), weight(1), weight(2), whole((seq, width)), whole((8, width))],
        [pl.BlockSpec((2, seq, 3 * span // 2), lambda g: (0, 0, g)), whole((8, width)), whole((mixers, part_len, width))],
        [sds((2, seq, 3 * width // 2), bf16), sds((8, width), f32), sds((mixers, part_len, width), bf16)],
        [pltpu.VMEM((seq, width), f32), pltpu.VMEM((width, 3 * span), bf16), pltpu.VMEM((steps, 8, span), f32)],
        (3 * seq * width * width + 16 * seq * seq * width, 18e6, 0),
        here, qkv, probs, left, grad_mix, w_qkv, w_qkv, w_qkv, sum_one, vec_in)


def block_rows(ref, p, y, dp, upper):
    return ref[pl.ds(pl.multiple_of((p ^ dp) * 2 * UNIT + (y ^ upper) * UNIT, 16), UNIT), :]


def store_blocks(out, rows, read):
    for p in range(8):
        for y in range(2):
            out[p * 2 + y, rows, :] = read(p, y).astype(bf16)


def out_units_kernel(flip, here, act, low, out, left_s, acc_s, wide_s):
    step = pl.program_id(0)
    last = pl.num_programs(0) - 1
    dp = here[1]
    core, upper = (here[0] & 1) ^ flip, (here[0] >> 1) & 1
    count = act.shape[-1]

    @pl.when(step < last)
    def _():
        for p in range(8):
            left_s[p * UNIT : (p + 1) * UNIT, :] = act[p ^ dp, 0, 0]
        acc_s[...] = nn(left_s[...], low[:count])
        at = [pl.multiple_of((upper ^ y) * HALF, 128) for y in range(2)]
        store_blocks(out, slice(None), lambda p, y: acc_s[p * UNIT : (p + 1) * UNIT, pl.ds(at[y], HALF)])

    @pl.when(step == last)
    def _():
        right = low[count + 16 :]
        wide_s[...] = tn(low[count : count + 16], jnp.where(core == 0, right[:, :HALF], right[:, HALF:]))
        store_blocks(out, slice(None), lambda p, y: block_rows(wide_s, p, y, dp, upper))


def out_units(here, flip, act, low):
    width = low.shape[1]
    count = act.shape[-1]
    return call(
        functools.partial(out_units_kernel, flip), "units_out", (5,),
        [pl.BlockSpec((8, 1, 1, UNIT, count), lambda j, s: (0, (s[0] & 1) ^ flip, jnp.minimum(j, 3), 0, 0)), whole(low.shape)],
        [pl.BlockSpec((16, UNIT, HALF), lambda j, s: (0, j, 0))], [sds((16, 5 * UNIT, HALF), bf16)],
        [pltpu.VMEM((8 * UNIT, count), bf16), pltpu.VMEM((8 * UNIT, width), f32), pltpu.VMEM((width, HALF), f32)],
        (4 * 8 * UNIT * count * width, 10e6, 0), here, act, low, prefetch=1)[0]


def in_units_kernel(flip, parts, here, *refs):
    hids, refs = refs[:parts], refs[parts:]
    mixes, refs = refs[:parts], refs[parts:]
    up, att, out, acc_s = refs
    step = pl.program_id(0)
    dp = here[1]
    core, upper = (here[0] & 1) ^ flip, (here[0] >> 1) & 1
    seq = hids[0].shape[1]

    def product(lefts, right):
        return sum(tn(left[0], right[i * seq : (i + 1) * seq, :]) for i, left in enumerate(lefts))

    def store(unit, columns):
        rows = pl.ds(pl.multiple_of(unit * UNIT, 16), UNIT)
        at = pl.multiple_of(columns * HALF, 128)

        def read(p, y):
            return acc_s[pl.ds(pl.multiple_of((p ^ dp) * 2 * UNIT + (y ^ upper) * UNIT, 16), UNIT), pl.ds(at, HALF)]

        store_blocks(out, rows, read)

    @pl.when(step < 2)
    def _():
        acc_s[...] = product(hids, up)
        for i in range(2):
            store(2 * step + i, i)

    @pl.when(step == 2)
    def _():
        right = jnp.where(core == 0, att[:, :HALF], att[:, HALF:])
        acc_s[:, :HALF] = product(mixes, right)
        store(4, 0)


def in_units(here, flip, lefts, up, att):
    parts = len(lefts)
    _, seq, width = lefts[0].shape
    count = up.shape[0]
    rows = 5 * UNIT

    def left(which):
        return [pl.BlockSpec((1, seq, width), lambda j, s: (which, 0, 0))] * parts

    return call(
        functools.partial(in_units_kernel, flip, parts), "units_in", (3,),
        left(1) + left(2) + [pl.BlockSpec((count, 2 * HALF), lambda j, s: (0, ((s[0] & 1) ^ flip) * 2 + jnp.minimum(j, 1))),
                             whole((count, width))],
        [whole((16, rows, HALF))], [sds((16, rows, HALF), bf16)], [pltpu.VMEM((width, 2 * HALF), f32)],
        (5 * width * HALF * count, 12e6, 0), here, *lefts, *lefts, up, att, prefetch=1)[0]


VEC_ROWS = 16


def qkv_units_kernel(flip, parts, here, *refs):
    lefts, refs = refs[:parts], refs[parts:]
    grads, refs = refs[:parts], refs[parts:]
    back, late, out, acc_s, tab_s = refs
    dp, upper = here[1], (here[0] >> 1) & 1
    acc_s[...] = sum(tn(left[0], grad[0]) for left, grad in zip(lefts, grads))
    for u in range(3):
        def read(p, y):
            rows = pl.ds(pl.multiple_of((p ^ dp) * 2 * UNIT + (y ^ upper) * UNIT, 16), UNIT)
            return acc_s[rows, u * HALF : (u + 1) * HALF]

        store_blocks(out, slice(u * UNIT, (u + 1) * UNIT), read)
    ramp = back[8:16, :]
    units = jnp.concatenate([back[3 + i : 4 + i, :] for i in range(4)], axis=1)
    short = jnp.concatenate(
        [ramp[0:7], back[0:3, :], late[0:2, :], jnp.zeros((4, ramp.shape[1]), f32)], axis=0)
    share = short.shape[1] // 8
    fill = jnp.zeros((16, 128 - share), f32)
    blank = jnp.zeros((VEC_ROWS - 3, HALF), f32)
    for b in range(8):
        slots = jnp.concatenate([short[:, b * share : (b + 1) * share], fill], axis=1)
        slots = [slots[i : i + 1] for i in range(12)]
        slots += [units[:, b * HALF + i * 128 : b * HALF + (i + 1) * 128] for i in range(3)]
        slots += [ramp[7:8, :128], jnp.where(dp == b, ramp[7:8, 128:256], 0.0), jnp.zeros((1, 128), f32)]
        lines = [jnp.concatenate(slots[i * 3 : i * 3 + 3], axis=1) for i in range(6)]
        for y in range(2):
            tab_s[b, y] = jnp.concatenate(lines[y * 3 : y * 3 + 3] + [blank], axis=0)
    store_blocks(out, slice(3 * UNIT, 3 * UNIT + VEC_ROWS), lambda p, y: tab_s[p ^ dp, y ^ upper])


def qkv_units(here, flip, lefts, grads, back, late):
    parts = len(lefts)
    _, seq, width = lefts[0].shape
    rows = 3 * UNIT + VEC_ROWS
    wide = 3 * HALF
    return call(
        functools.partial(qkv_units_kernel, flip, parts), "units_qkv", (1,),
        [pl.BlockSpec((1, seq, width), lambda j, s: (0, 0, 0))] * parts
        + [pl.BlockSpec((1, seq, wide), lambda j, s: ((s[0] & 1) ^ flip, 0, 0))] * parts
        + [whole((16, width)), whole((8, width))],
        [whole((16, rows, HALF))], [sds((16, rows, HALF), bf16)],
        [pltpu.VMEM((width, wide), f32), pltpu.VMEM((8, 2, VEC_ROWS, HALF), f32)],
        (width * wide * parts * seq, 10e6, 0), here, *lefts, *grads, back, late, prefetch=1)[0]


def first_kernel(mine, got, xk, xs, yk, ys):
    def total(*at):
        return (mine[at].astype(f32) + got[at].astype(f32)).astype(bf16)

    for z2 in range(2):
        for other in range(2):
            xk[z2, other] = total(z2, 0, 0, other)
            xs[z2, other] = total(z2, 0, 1, other)
            yk[z2, other] = total(z2, 1, other, 0)
            ys[z2, other] = total(z2, 1, other, 1)


def first_stage(mine, got):
    rows = mine.shape[1]
    step = 80
    block = pl.BlockSpec((2, 2, 2, 2, step, HALF), lambda j: (0, 0, 0, 0, j, 0))
    out = pl.BlockSpec((2, 2, step, HALF), lambda j: (0, 0, j, 0))
    view = (2, 2, 2, 2, rows, HALF)
    return call(first_kernel, "stage_one", (rows // step,), [block] * 2, [out] * 4, [sds((2, 2, rows, HALF), bf16)] * 4, [],
                STAGE, mine.reshape(view), got.reshape(view))


def second_kernel(xk, xr, yk, yr, x2k, x2s, y2k, y2s):
    x = xk[0].astype(f32) + xr[0].astype(f32)
    x2k[0] = x[0].astype(bf16)
    x2s[0] = x[1].astype(bf16)
    y = yk[0].astype(f32) + yr[0].astype(f32)
    y2k[0] = y[0].astype(bf16)
    y2s[0] = y[1].astype(bf16)


def third_kernel(xk, xr, yk, yr, keep, send):
    keep[...] = (xk[...].astype(f32) + xr[...].astype(f32)).astype(bf16)
    send[...] = (yk[...].astype(f32) + yr[...].astype(f32)).astype(bf16)


def fourth_kernel(mine, got, keep, send):
    keep[...] = (mine[0].astype(f32) + got[0].astype(f32)).astype(bf16)
    send[...] = (mine[1].astype(f32) + got[1].astype(f32)).astype(bf16)


def fifth_kernel(mine, got, out):
    out[...] = (mine[...].astype(f32) + got[...].astype(f32)).astype(bf16)


def swap(value, axis, bit):
    size = lax.axis_size(axis)
    return lax.ppermute(value, axis, [(i, i ^ bit) for i in range(size)])


def first_swap(stage):
    xk, xs, yk, ys = stage
    return xk, swap(xs, "dp", 1), yk, swap(ys, "mix", 2)


def second_stage(stage):
    rows = stage[0].shape[2]
    block = pl.BlockSpec((1, 2, rows, HALF), lambda z: (z, 0, 0, 0))
    out = pl.BlockSpec((1, rows, HALF), lambda z: (z, 0, 0))
    return call(second_kernel, "stage_two", (2,), [block] * 4, [out] * 4, [sds((2, rows, HALF), bf16)] * 4, [],
                STAGE, *stage)


def second_swap(stage):
    xk, xs, yk, ys = stage
    return xk, swap(xs, "mix", 2), yk, swap(ys, "dp", 1)


def third_stage(stage):
    shape = stage[0].shape
    return call(third_kernel, "stage_three", (), [whole(shape)] * 4, [whole(shape)] * 2, [sds(shape, bf16)] * 2, [], STAGE, *stage)


def third_swap(stage):
    return stage[0], swap(stage[1], "dp", 2)


def fourth_stage(stage):
    shape = stage[0].shape
    return call(fourth_kernel, "stage_four", (), [whole(shape)] * 2, [whole(shape[1:])] * 2, [sds(shape[1:], bf16)] * 2, [],
                STAGE, *stage)


def fourth_swap(stage):
    return stage[0], swap(stage[1], "dp", 4)


def fifth_stage(stage):
    shape = stage[0].shape
    return call(fifth_kernel, "stage_five", (), [whole(shape)] * 2, [whole(shape)], [sds(shape, bf16)], [], STAGE, *stage)[0]


def spread(final):
    other = swap(final, "mix", 2)
    return final, other, swap(final, "mix", 1), swap(other, "mix", 1)


def place_kernel(plan, vec, here, *refs):
    parts, outs = refs[:4], refs[4:]
    core, upper = here[0] & 1, (here[0] >> 1) & 1
    for i, part in enumerate(parts):
        c, y = core ^ (i // 2), upper ^ (i % 2)
        for u, (which, row, row_core, row_y, col_core, col_y, pieces) in enumerate(plan):
            r0 = pl.multiple_of(row + c * row_core + y * row_y, 8)
            at = 0
            for col, size in pieces:
                c0 = pl.multiple_of(col + c * col_core + y * col_y, 128)
                outs[which][pl.ds(r0, UNIT), pl.ds(c0, size)] = part[u * UNIT : (u + 1) * UNIT, at : at + size].astype(f32)
                at += size
    if vec:
        base = len(plan) * UNIT
        mine, other = parts[0][base : base + 8, :].astype(f32), parts[1][base : base + 8, :].astype(f32)
        lines = [jnp.where(upper == 0, mine, other), jnp.where(upper == 0, other, mine)]

        def slot(i):
            return lines[i // 9][i % 9 // 3 : i % 9 // 3 + 1, (i % 3) * 128 : (i % 3 + 1) * 128]

        vec_outs = outs[-13:]
        share = 96
        for i, target in zip((0, 1, 2, 3, 7, 8, 9, 10, 11), vec_outs[:9]):
            target[...] = slot(i)[0, :share]
        vec_outs[9][...] = jnp.concatenate([slot(12), slot(13), slot(14)], axis=1)[0]
        grad_class = jnp.concatenate([slot(4), slot(5), slot(6), jnp.zeros((125, 128), f32)], axis=0).T
        vec_outs[10][...] = grad_class[:share, :3]
        vec_outs[11][...] = slot(15)[0, :3]
        losses = slot(16)
        pairs = vec_outs[12].shape[1]
        for r in range(vec_outs[12].shape[0]):
            vec_outs[12][r : r + 1, :] = losses[:, r * pairs : (r + 1) * pairs]


def place_units(here, plan, shapes, parts, vec_shapes=()):
    shape = parts[0].shape
    vm = [whole(s) for s in list(shapes) + list(vec_shapes)]
    return call(
        functools.partial(place_kernel, plan, bool(vec_shapes)), "place_units", (),
        [SMEM_SPEC] + [whole(shape)] * 4, vm, [sds(s, f32) for s in list(shapes) + list(vec_shapes)], [],
        STAGE, here, *parts)


def weave_kernel(*refs):
    for r, piece in enumerate(refs[:-1]):
        refs[-1][:, r] = piece[...]


def weave(pieces):
    mixers, part_len, width = pieces[0].shape
    shape = (mixers, len(pieces), part_len, width)
    (out,) = call(
        weave_kernel, "weave", (mixers,), [pl.BlockSpec((1, part_len, width), lambda k: (k, 0, 0))] * len(pieces),
        [pl.BlockSpec((1,) + shape[1:], lambda k: (k, 0, 0, 0))], [sds(shape, bf16)], [], STAGE, *pieces)
    return out.reshape(mixers * len(pieces), part_len, width)


def between(value):
    return lax.all_to_all(value, "mix", split_axis=0, concat_axis=0, tiled=True)


def on_device(
    tokens, cotangent, pair_lengths, labels, w_qkv, b_query, b_value, w_attn, b_attn, gain_one, shift_one,
    w_in, b_in, w_out, b_out, gain_two, shift_two, w_pool, b_pool, w_class, b_class,
):
    row_count, part_len, width = tokens.shape
    mixers = lax.axis_size("mix")
    dps = lax.axis_size("dp")
    rows_here = row_count // mixers
    seq = part_len * mixers
    units = w_in.shape[1]
    mix = lax.axis_index("mix").astype(jnp.int32)
    dp = lax.axis_index("dp").astype(jnp.int32)
    here = jnp.stack([mix, dp])
    pairs = pair_lengths.shape[1]
    quick = dps == 8 and mixers == 4 and width == 768 and units == 3072 and seq * rows_here == 1024 and rows_here == 2

    def for_device(array, k):
        return lax.dynamic_index_in_dim(array.reshape(mixers, rows_here, part_len, width), mix ^ k, 0, keepdims=False)

    order = sorted(range(1, mixers), reverse=True)

    def exchange(blocks):
        got = {0: blocks[0]}
        for k in order:
            got[k] = swap(blocks[k], "mix", k)
        return [got[k] for k in range(mixers)]

    sent = [for_device(tokens, k) for k in range(mixers)]
    pack = jnp.concatenate(
        [b_query, b_value, b_attn, gain_one, shift_one, b_out, gain_two, shift_two, b_pool, b_in, b_class,
         jnp.zeros((3 * width - b_class.shape[0],), f32)]).reshape(16, width)

    def tie(first, second):
        return lax.optimization_barrier((first, second))

    blocks = [[s[r] for s in sent] for r in range(rows_here)]
    cot = cotangent.reshape(mixers, rows_here, part_len, width)
    rows, lefts_sib = [], []
    got = exchange(blocks[0])
    for r in range(rows_here):
        if r + 1 < rows_here:
            got, blocks[r + 1] = tie(got, blocks[r + 1])
            following = exchange(blocks[r + 1])
        else:
            got, cot = tie(got, cot)
            cots = between(cot)
        rows.append(forward_row(r, rows_here, here, pair_lengths, got, pack, w_qkv, w_attn))
        if r + 1 < rows_here:
            rows[r], got = tie(rows[r], following)
    qkvs, probs, lefts, hids, n1, rho1 = zip(*rows)
    act, slope, outs, n2, rho2, firsts = feed_forward(part_len, here, pair_lengths, hids, pack, w_in, w_out)
    outs = between(outs)
    vec_ramp, sum_two, low = off_ramp(
        part_len, here, pair_lengths, labels, firsts, pack, w_pool, w_class, cots, n2, rho2)

    if not quick:
        return plain_rest(
            here, part_len, act, slope, outs, low, sum_two, vec_ramp, qkvs, probs, lefts, n1, rho1, pack,
            w_qkv, w_attn, w_in, w_out, mix, dp, row_count, units)

    def both_cores(make, *args):
        send = make(here, 1, *args)
        got = swap(send, "mix", 1)
        args = tie(send, args)[1]
        return first_swap(first_stage(make(here, 0, *args), got))

    one = both_cores(out_units, act.reshape(8, 2, 4, UNIT, rows_here * seq), low)
    _, sum_two = tie(one[0], sum_two)
    grad_up, vec_back, grad_att, sum_one, grad_mix = feed_backward(
        low, slope, w_out, w_in, sum_two, n1, rho1, vec_ramp, pack, w_attn)
    _, one = tie(grad_up, one)
    one, outs = tie(one, outs)
    one = second_swap(second_stage(one))
    _, grad_up = tie(one[0], grad_up)
    two = both_cores(in_units, list(lefts), grad_up, grad_att)
    _, one = tie(two[0], one)
    one = third_swap(third_stage(one))
    _, grad_mix = tie(one[0], grad_mix)

    vec_late = jnp.zeros((8, width), f32)
    grads, toks = [], []
    for r in range(rows_here):
        dqkv, vec_late, tok = attention_backward(
            here, part_len, qkvs[r], probs[r], lefts[r], grad_mix[r], w_qkv, sum_one[r], vec_late)
        grads.append(dqkv)
        toks.append(between(tok))
        if r == 0:
            _, one = tie(dqkv, one)
            one = fourth_swap(fourth_stage(one))
            _, two = tie(one[0], two)
            two = second_swap(second_stage(two))
            _, grad_mix = tie(two[0], grad_mix)
    _, one = tie(grads[1], one)
    one = spread(fifth_stage(one))
    _, two = tie(one[0], two)
    two = third_swap(third_stage(two))
    _, grads = tie(two[0], grads)
    three = both_cores(qkv_units, list(lefts), grads, vec_back, vec_late)
    _, two = tie(three[0], two)
    two = fourth_swap(fourth_stage(two))
    _, one = tie(two[0], one)
    grad_w_out, grad_w_pool = place_units(
        here, [(0, j * UNIT, 192, 0, 0, HALF, ((0, HALF),)) for j in range(4)] + [(1, 0, 0, UNIT, HALF, 0, ((0, HALF),))],
        [(384, width), (96, width)], one)
    _, three = tie(grad_w_out, three)
    three = second_swap(second_stage(three))
    _, two = tie(three[0], two)
    two = spread(fifth_stage(two))
    _, three = tie(two[0], three)
    three = third_swap(third_stage(three))
    _, two = tie(three[0], two)
    grad_w_in, grad_w_attn = place_units(
        here, [(0, 0, 0, UNIT, 4 * HALF, 0, ((j * HALF, HALF),)) for j in range(4)] + [(1, 0, 0, UNIT, HALF, 0, ((0, HALF),))],
        [(96, units), (96, width)], two)
    _, three = tie(grad_w_in, three)
    three = fourth_swap(fourth_stage(three))
    _, toks = tie(three[0], toks)
    grad_tokens = weave(toks)
    _, three = tie(grad_tokens, three)
    three = spread(fifth_stage(three))
    output = outs.reshape(row_count, part_len, width)
    share = width // dps
    last = place_units(
        here, [(0, 0, 0, UNIT, 128, 0, tuple((w * width + g * 256, 128) for w in range(3))) for g in range(3)],
        [(96, 3 * width)], three,
        [(share,)] * 9 + [(units // dps,), (share, w_class.shape[1]), b_class.shape, (row_count, pairs)])
    (grad_w_qkv, grad_b_out, grad_gain_two, grad_shift_two, grad_b_pool, grad_gain_one, grad_shift_one, grad_b_attn,
     grad_b_query, grad_b_value, grad_b_in, grad_w_class, grad_b_class, pair_loss) = last
    return (
        output, pair_loss, grad_tokens, grad_w_qkv, grad_b_query, grad_b_value, grad_w_attn, grad_b_attn,
        grad_gain_one, grad_shift_one, grad_w_in, grad_b_in, grad_w_out, grad_b_out, grad_gain_two, grad_shift_two,
        grad_w_pool, grad_b_pool, grad_w_class, grad_b_class,
    )


def plain_rest(
    here, part_len, act, slope, outs, low, sum_two, vec_ramp, qkvs, probs, lefts, n1, rho1, pack,
    w_qkv, w_attn, w_in, w_out, mix, dp, row_count, units,
):
    rows_here = len(n1)
    seq, width = n1[0].shape
    dps = lax.axis_size("dp")
    pairs = vec_ramp.shape[0] // rows_here
    grad_up, vec_back, grad_att, sum_one, grad_mix = feed_backward(
        low, slope, w_out, w_in, sum_two, n1, rho1, vec_ramp, pack, w_attn)
    vec_late = jnp.zeros((8, width), f32)
    dqkv, toks = [], []
    for r in range(rows_here):
        grad, vec_late, tok = attention_backward(
            here, part_len, qkvs[r], probs[r], lefts[r], grad_mix[r], w_qkv, sum_one[r], vec_late)
        parts = grad.reshape(2, seq, width // 256, 3, 128).transpose(1, 3, 2, 0, 4)
        dqkv.append(parts.reshape(seq, 3 * width))
        toks.append(between(tok))
    output = outs.reshape(row_count, part_len, width)
    grad_tokens = weave(toks)
    low, pool = low[: seq * rows_here], low[seq * rows_here :]
    left = [jnp.concatenate([l[i] for l in lefts], axis=0) for i in range(3)]
    grads = (
        tn(left[0], jnp.concatenate(dqkv, axis=0)), tn(left[2], grad_att), tn(left[1], grad_up), nn(act, low),
        tn(pool[:16], pool[16:]),
    )
    shards = [lax.psum_scatter(g, "dp", scatter_dimension=0, tiled=True) for g in grads]
    shards = [lax.psum(s.astype(bf16), "mix").astype(f32) for s in shards]
    bins = vec_back[3:7]
    vecs = jnp.concatenate([vec_ramp[:7], vec_back[:3], vec_late[:2], bins], axis=0)
    vecs = lax.psum(vecs, ("dp", "mix"))
    class_total = lax.psum(vec_ramp[7, :3], ("dp", "mix"))
    loss = lax.psum(vec_ramp[7, 128 : 128 + row_count * pairs], "mix").reshape(row_count, pairs)
    share = width // dps
    v = lax.dynamic_slice_in_dim(vecs, dp * share, share, axis=1)
    bin_share = lax.dynamic_slice_in_dim(vecs[12:].reshape(-1), dp * (units // dps), units // dps)
    return (
        output, loss, grad_tokens, shards[0], v[10], v[11], shards[1], v[9], v[7], v[8], shards[2], bin_share,
        shards[3], v[0], v[1], v[2], shards[4], v[3], v[4:7].T, class_total,
    )


def solution(mesh):
    wide = P("dp", "mix", None)
    split = P("dp", None)
    in_specs = (wide, wide, split, split) + (P(),) * 17
    out_specs = (
        wide, split, wide,
        split, P("dp"), P("dp"), split, P("dp"), P("dp"), P("dp"),
        split, P("dp"), split, P("dp"), P("dp"), P("dp"),
        split, P("dp"), split, P(),
    )
    return jax.shard_map(on_device, mesh=mesh, in_specs=in_specs, out_specs=out_specs, check_vma=False)
```

```python
import functools

import jax
import jax.numpy as jnp
from jax import lax
from jax.experimental import pallas as pl
from jax.experimental.pallas import tpu as pltpu
from jax.sharding import PartitionSpec as P

HEADS = 12
SCALE = 1.0
STAGE = (0, 700e6, 0)
GROUP = 4
CHUNK = 768
TILE = 256
UNIT = 48
HALF = 384
norm_eps = 1e-06
masked_score = -1000000000.0
inv_root_two = 0.7071067811865476
inv_root_tau = 0.3989422804014327
f32 = jnp.float32
bf16 = jnp.bfloat16
VMEM_LIMIT = 62 * 1024 * 1024
SMEM_SPEC = pl.BlockSpec(memory_space=pltpu.SMEM)
B_QUERY, B_VALUE, B_ATTN, GAIN_ONE, SHIFT_ONE, B_OUT, GAIN_TWO, SHIFT_TWO, B_POOL, B_IN, B_CLASS = 0, 1, 2, 3, 4, 5, 6, 7, 8, 9, 13


def whole(shape):
    return pl.BlockSpec(shape, lambda *_: (0,) * len(shape))


def sds(shape, dtype):
    return jax.ShapeDtypeStruct(shape, dtype)


def nn(left, right):
    return jnp.dot(left, right, preferred_element_type=f32)


def nt(left, right):
    return lax.dot_general(left, right, (((1,), (1,)), ((), ())), preferred_element_type=f32)


def tn(left, right):
    return lax.dot_general(left, right, (((0,), (0,)), ((), ())), preferred_element_type=f32)


def call(kernel, name, grid, in_specs, out_specs, out_shape, scratch, work, *args, prefetch=0):
    work = work or (0, 8 * sum(a.size for a in args), 0)
    common = dict(
        out_shape=out_shape,
        compiler_params=pltpu.CompilerParams(vmem_limit_bytes=VMEM_LIMIT),
        cost_estimate=pl.CostEstimate(flops=int(2 * work[0] * SCALE), bytes_accessed=int(work[1] * SCALE), transcendentals=0),
        name=name,
    )
    if prefetch:
        spec = pltpu.PrefetchScalarGridSpec(
            num_scalar_prefetch=prefetch, grid=grid, in_specs=in_specs, out_specs=out_specs, scratch_shapes=scratch)
        return pl.pallas_call(kernel, grid_spec=spec, **common)(*args)
    return pl.pallas_call(
        kernel, grid=grid, in_specs=in_specs, out_specs=out_specs, scratch_shapes=scratch, **common)(*args)


def after(value, *earlier):
    return lax.optimization_barrier((value,) + earlier)[0]


def mean_of(values):
    return jnp.mean(values, axis=-1, keepdims=True)


def col_sum(values):
    return jnp.sum(values, axis=0, keepdims=True)


def head_only(values, head, size):
    lane = lax.broadcasted_iota(jnp.int32, (1, values.shape[1]), 1) // size
    return jnp.where(lane == head, values, jnp.zeros((), values.dtype))


def per_head(values, size):
    return jnp.concatenate([head_only(values, h, size) for h in range(GROUP)], axis=0)


def segments(places, lengths, row):
    total = jnp.int32(0)
    seg = jnp.zeros(places.shape, jnp.int32)
    for k in range(lengths.shape[1]):
        total = total + lengths[row, k]
        seg = seg + (places >= total).astype(jnp.int32)
    return seg


def forward_kernel(row, rows_here, part_len, mixers, head_size, here, lengths, *refs):
    pieces, refs = refs[:mixers], refs[mixers:]
    (pack, packq, packv, wq, wk, wv, wa,
     qkv_o, probs_o, tok_o, mix_o, hid_o, n1_o, rho_o,
     tok_s, mix_s, bias_s, w_s) = refs
    step = pl.program_id(0)
    seq = part_len * mixers
    shift = part_len.bit_length() - 1
    span = GROUP * head_size

    @pl.when(step == 0)
    def _():
        for i, piece in enumerate(pieces):
            tok_s[i * part_len : (i + 1) * part_len, :] = piece[...]
        mine = here[0]
        down = lax.broadcasted_iota(jnp.int32, (seq, 1), 0)
        across = lax.broadcasted_iota(jnp.int32, (1, seq), 1)

        def place(i):
            return (((i >> shift) ^ mine) << shift) + (i & (part_len - 1))

        number = mine * rows_here + row
        same = segments(place(down), lengths, number) == segments(place(across), lengths, number)
        bias_s[...] = jnp.where(same, 0.0, masked_score)

    for i, weight in enumerate((wq, wk, wv)):
        w_s[:, i * span : (i + 1) * span] = weight[...]
    qkv = nn(tok_s[...], w_s[...])
    qs = (qkv[:, :span] + packq[B_QUERY : B_QUERY + 1]).astype(bf16) * bf16(head_size ** (-0.5))
    keys = qkv[:, span : 2 * span].astype(bf16)
    values = (qkv[:, 2 * span :] + packv[B_VALUE : B_VALUE + 1]).astype(bf16)
    qkv_o[0, :, :span] = qs
    qkv_o[0, :, span : 2 * span] = keys
    qkv_o[0, :, 2 * span :] = values
    scores = nt(keys, per_head(qs, head_size))
    values_t = values.T
    mixed = []
    for h in range(GROUP):
        at = slice(h * seq, (h + 1) * seq)
        part = scores[:, at] + bias_s[...]
        expo = jnp.exp(part - jnp.max(part, axis=0, keepdims=True))
        probs = (expo * (1.0 / col_sum(expo))).astype(bf16)
        probs_o[0, :, at] = probs
        mixed.append(nn(values_t[h * head_size : (h + 1) * head_size], probs))
    mixed = jnp.concatenate(mixed, axis=0).astype(bf16).T
    mix_s[step] = mixed
    mix_o[...] = mixed
    tok_o[...] = tok_s[:, pl.ds(pl.multiple_of(step * span, 128), span)]

    @pl.when(step == pl.num_programs(0) - 1)
    def _():
        mix = jnp.concatenate([mix_s[g] for g in range(mix_s.shape[0])], axis=1)
        full = tok_s[...].astype(f32) + (nn(mix, wa[...]) + pack[B_ATTN : B_ATTN + 1])
        centre = full - mean_of(full)
        rho = lax.rsqrt(mean_of(centre * centre) + norm_eps)
        normed = centre * rho
        hidden = normed * pack[GAIN_ONE : GAIN_ONE + 1] + pack[SHIFT_ONE : SHIFT_ONE + 1]
        hid_o[...] = hidden.astype(bf16)
        n1_o[...] = normed.astype(bf16)
        rho_o[...] = jnp.broadcast_to(rho, rho_o.shape)


def forward_row(row, rows_here, here, lengths, pieces, pack, w_qkv, w_attn):
    part_len, width = pieces[0].shape
    mixers = len(pieces)
    seq = part_len * mixers
    head_size = width // HEADS
    span = GROUP * head_size
    steps = width // span

    def weight(which):
        return pl.BlockSpec((width, span), lambda g: (0, which * steps + g))

    rows = pack.shape[0]
    column = pl.BlockSpec((rows, span), lambda g: (0, g))
    return call(
        functools.partial(forward_kernel, row, rows_here, part_len, mixers, head_size), "forward_row", (steps,),
        [SMEM_SPEC, SMEM_SPEC] + [whole((part_len, width))] * mixers
        + [whole((rows, width)), column, column, weight(0), weight(1), weight(2), whole((width, width))],
        [pl.BlockSpec((1, seq, 3 * span), lambda g: (g, 0, 0)), pl.BlockSpec((1, seq, GROUP * seq), lambda g: (g, 0, 0)),
         pl.BlockSpec((seq, span), lambda g: (0, g)), pl.BlockSpec((seq, span), lambda g: (0, g)),
         whole((seq, width)), whole((seq, width)), whole((seq, 128))],
        [sds((steps, seq, 3 * span), bf16), sds((steps, seq, GROUP * seq), bf16),
         sds((seq, width), bf16), sds((seq, width), bf16), sds((seq, width), bf16), sds((seq, width), bf16), sds((seq, 128), f32)],
        [pltpu.VMEM((seq, width), bf16), pltpu.VMEM((steps, seq, span), bf16), pltpu.VMEM((seq, seq), f32),
         pltpu.VMEM((width, 3 * span), bf16)],
        (seq * width * width * 4 + 8 * seq * seq * width, 16e6, HEADS * seq * seq),
        here, lengths, *pieces, pack, pack, pack, w_qkv, w_qkv, w_qkv, w_attn)


def start_spots(here, lengths, r, rows_here, part_len, pairs, seq):
    shift = part_len.bit_length() - 1
    spots = []
    start = jnp.int32(0)
    for k in range(pairs):
        spots.append(r * seq + (((start >> shift) ^ here[0]) << shift) + (start & (part_len - 1)))
        start = start + lengths[here[0] * rows_here + r, k]
    return spots


def feed_kernel(rows_here, part_len, pairs, mixers, here, lengths, *refs):
    hid, refs = refs[:rows_here], refs[rows_here:]
    pack, w_in, w_out = refs[:3]
    act_o, slope_o, out_o, n2_o, rho_o, first_o, low_s, feed_s, full_s = refs[3:]
    step = pl.program_id(0)
    last = pl.num_programs(0) - 1
    seq = hid[0].shape[0]
    count = rows_here * seq // TILE

    @pl.when(step == 0)
    def _():
        for r in range(rows_here):
            low_s[r * seq : (r + 1) * seq, :] = hid[r][...]
        feed_s[...] = jnp.broadcast_to(pack[B_OUT : B_OUT + 1], feed_s.shape)

    bias = pack[pl.ds(B_IN + step, 1), :]

    def rows(i):
        return slice(i * TILE, (i + 1) * TILE)

    up = nn(low_s[rows(0), :], w_in[...])
    before = None
    for i in range(count):
        following = nn(low_s[rows(i + 1), :], w_in[...]) if i + 1 < count else None
        up = up + bias
        half = 0.5 * (1.0 + lax.erf(up * inv_root_two))
        act = (up * half).astype(bf16)
        slope_o[rows(i), :] = (half + up * jnp.exp(-0.5 * up * up) * inv_root_tau).astype(bf16)
        act_o[:, rows(i)] = act.T
        if before is not None:
            feed_s[rows(i - 1), :] += nn(before, w_out[...])
        before, up = act, following
    feed_s[rows(count - 1), :] += nn(before, w_out[...])

    @pl.when(step == last)
    def _():
        for r in range(rows_here):
            for k in range(mixers):
                at = slice(r * seq + k * part_len, r * seq + (k + 1) * part_len)
                full = hid[r][k * part_len : (k + 1) * part_len, :].astype(f32) + feed_s[at, :]
                centre = full - mean_of(full)
                rho = lax.rsqrt(mean_of(centre * centre) + norm_eps)
                normed = centre * rho
                out = normed * pack[GAIN_TWO : GAIN_TWO + 1] + pack[SHIFT_TWO : SHIFT_TWO + 1]
                full_s[at, :] = out
                out_o[here[0] ^ k, r] = out.astype(bf16)
                n2_o[at, :] = normed.astype(bf16)
                rho_o[at, :] = jnp.broadcast_to(rho, (part_len, 128))
        for r in range(rows_here):
            for k, spot in enumerate(start_spots(here, lengths, r, rows_here, part_len, pairs, seq)):
                first_o[r * pairs + k : r * pairs + k + 1, :] = full_s[pl.ds(spot, 1), :]


def feed_forward(part_len, here, lengths, hids, pack, w_in, w_out):
    rows_here = len(hids)
    seq, width = hids[0].shape
    mixers = seq // part_len
    pairs = lengths.shape[1]
    units = w_in.shape[1]
    count = rows_here * seq
    steps = units // CHUNK
    return call(
        functools.partial(feed_kernel, rows_here, part_len, pairs, mixers), "feed_forward", (steps,),
        [SMEM_SPEC, SMEM_SPEC] + [whole((seq, width))] * rows_here
        + [whole(pack.shape), pl.BlockSpec((width, CHUNK), lambda c: (0, c)), pl.BlockSpec((CHUNK, width), lambda c: (c, 0))],
        [pl.BlockSpec((CHUNK, count), lambda c: (c, 0)), pl.BlockSpec((count, CHUNK), lambda c: (0, c))] + [whole((mixers, rows_here, part_len, width))]
        + [whole((count, width)), whole((count, 128)), whole((rows_here * pairs, width))],
        [sds((units, count), bf16), sds((count, units), bf16)] + [sds((mixers, rows_here, part_len, width), bf16)]
        + [sds((count, width), bf16), sds((count, 128), f32), sds((rows_here * pairs, width), f32)],
        [pltpu.VMEM((count, width), bf16), pltpu.VMEM((count, width), f32), pltpu.VMEM((count, width), f32)],
        (2 * count * width * units, 35e6, 2 * count * units),
        here, lengths, *hids, pack, w_in, w_out)


def ramp_kernel(rows_here, part_len, pairs, mixers, here, lengths, labels, first, pack, w_pool, w_class, *refs):
    cots, n2, rho, vec_o, sum_o, low_o, e_s, gf_s, sums_s = refs
    step = pl.program_id(0)
    last = pl.num_programs(0) - 1
    seq = part_len * mixers
    count = rows_here * pairs
    width = first.shape[1]
    classes = w_class.shape[1]

    @pl.when(step == 0)
    def _():
        firsts = first[...]
        pool = w_pool[...]
        pool_high = pool.astype(bf16)
        pool_rest = (pool - pool_high.astype(f32)).astype(bf16)
        first_high = firsts.astype(bf16)
        first_rest = (firsts - first_high.astype(f32)).astype(bf16)
        pre = nn(first_high, pool_high) + nn(first_rest, pool_high) + nn(first_high, pool_rest)
        pooled = jnp.tanh(pre + pack[B_POOL : B_POOL + 1])
        class_t = jnp.concatenate([w_class[...], jnp.zeros((width, 128 - classes), f32)], axis=1).T
        lane = lax.broadcasted_iota(jnp.int32, (count, 128), 1)
        logits = jnp.full((count, 128), -jnp.inf, f32)
        for c in range(classes):
            logits = jnp.where(lane == c, jnp.sum(pooled * class_t[c : c + 1], axis=1, keepdims=True), logits)
        logits = logits + pack[B_CLASS : B_CLASS + 1, :128]
        top = jnp.max(logits, axis=-1, keepdims=True)
        expo = jnp.exp(logits - top)
        total = jnp.sum(expo, axis=-1, keepdims=True)
        log_total = top + jnp.log(total)
        sub = lax.broadcasted_iota(jnp.int32, (count, 128), 0)
        label = jnp.zeros((count, 128), jnp.int32)
        for r in range(rows_here):
            for k in range(pairs):
                label = jnp.where(sub == r * pairs + k, labels[here[0] * rows_here + r, k], label)
        chosen = lane == label
        loss = log_total - jnp.sum(jnp.where(chosen, logits, 0.0), axis=-1, keepdims=True)
        grad_logits = expo / total - chosen.astype(f32)
        grad_pooled = jnp.zeros((count, width), f32)
        for c in range(classes):
            grad_pooled = grad_pooled + grad_logits[:, c : c + 1] * class_t[c : c + 1]
        grad_pre = grad_pooled * (1.0 - pooled * pooled)
        gf_s[...] = nt(grad_pre.astype(bf16), pool_high)
        vec_o[3:4, :] = col_sum(grad_pre)
        for c in range(classes):
            vec_o[4 + c : 5 + c, :] = col_sum(pooled * grad_logits[:, c : c + 1])
        spread = jnp.where(lane == here[0] * count + sub, loss, 0.0)
        vec_o[7:8, :] = jnp.concatenate(
            [col_sum(grad_logits), col_sum(spread), jnp.zeros((1, width - 256), f32)], axis=1)
        none = jnp.zeros((16 - count, width), f32)
        base = seq * rows_here
        low_o[base : base + 16, :] = jnp.concatenate([firsts, none], axis=0).astype(bf16)
        low_o[base + 16 :, :] = jnp.concatenate([grad_pre, none], axis=0).astype(bf16)
        for r in range(rows_here):
            for i in range(mixers):
                at = r * seq + i * part_len
                e_s[at : at + part_len, :] = cots[here[0] ^ i, r].astype(f32)
            for k, spot in enumerate(start_spots(here, lengths, r, rows_here, part_len, pairs, seq)):
                e_s[pl.ds(spot, 1), :] = e_s[pl.ds(spot, 1), :] + gf_s[r * pairs + k : r * pairs + k + 1, :]
        sums_s[...] = jnp.zeros(sums_s.shape, f32)

    e = e_s[pl.ds(pl.multiple_of(step * TILE, TILE), TILE), :]
    normed = n2[...].astype(f32)
    eg = e * pack[GAIN_TWO : GAIN_TWO + 1]
    grad = rho[:, 0:1] * (eg - mean_of(eg) - normed * mean_of(eg * normed))
    sum_o[...] = grad
    low = grad.astype(bf16)
    low_o[pl.ds(pl.multiple_of(step * TILE, TILE), TILE), :] = low
    for i, term in enumerate((low.astype(f32), e * normed, e)):
        sums_s[i : i + 1, :] += col_sum(term)

    @pl.when(step == last)
    def _():
        vec_o[0:3, :] = sums_s[0:3, :]


def off_ramp(part_len, here, lengths, labels, firsts, pack, w_pool, w_class, cots, n2, rho):
    mixers, rows_here = cots.shape[:2]
    width = firsts.shape[1]
    pairs = lengths.shape[1]
    tokens = n2.shape[0]
    tile = pl.BlockSpec((TILE, width), lambda t: (t, 0))
    return call(
        functools.partial(ramp_kernel, rows_here, part_len, pairs, mixers), "off_ramp", (tokens // TILE,),
        [SMEM_SPEC] * 3 + [whole(firsts.shape), whole(pack.shape), whole(w_pool.shape), whole(w_class.shape)]
        + [whole(cots.shape), tile, pl.BlockSpec((TILE, 128), lambda t: (t, 0))],
        [whole((8, width)), tile, whole((tokens + 32, width))],
        [sds((8, width), f32), sds((tokens, width), f32), sds((tokens + 32, width), bf16)],
        [pltpu.VMEM((tokens, width), f32), pltpu.VMEM(firsts.shape, f32), pltpu.VMEM((8, width), f32)],
        (1e8, 14e6, 1e4),
        here, lengths, labels, firsts, pack, w_pool, w_class, cots, n2, rho)


def back_kernel(rows_here, low, slope, w_out, w_in, sum_two, ramp, pack, w_attn, *refs):
    n1, refs = refs[:rows_here], refs[rows_here:]
    rho, refs = refs[:rows_here], refs[rows_here:]
    up_o, vec_o, att_o = refs[:3]
    refs = refs[3:]
    sum_o, refs = refs[:rows_here], refs[rows_here:]
    mix_o, refs = refs[:rows_here], refs[rows_here:]
    (hid_s,) = refs
    step = pl.program_id(0)
    last = pl.num_programs(0) - 1
    seq = n1[0].shape[0]
    count = slope.shape[0] // TILE

    def rows(i):
        return slice(i * TILE, (i + 1) * TILE)

    @pl.when(step == 0)
    def _():
        hid_s[...] = sum_two[...]
        vec_o[7:8, :] = jnp.zeros((1, vec_o.shape[1]), f32)
        vec_o[8:16, :] = ramp[...]

    total = jnp.zeros((1, slope.shape[1]), f32)
    act = nt(low[rows(0), :], w_out[...])
    before = None
    for i in range(count):
        following = nt(low[rows(i + 1), :], w_out[...]) if i + 1 < count else None
        up = (act * slope[rows(i), :].astype(f32)).astype(bf16)
        up_o[rows(i), :] = up
        total = total + col_sum(up.astype(f32))
        if before is not None:
            hid_s[rows(i - 1), :] += nt(before, w_in[...])
        before, act = up, following
    hid_s[rows(count - 1), :] += nt(before, w_in[...])
    vec_o[pl.ds(3 + step, 1), :] = total

    @pl.when(step == last)
    def _():
        width = pack.shape[1]
        sums = [jnp.zeros((1, width), f32)] * 3
        for r in range(rows_here):
            for i in range(seq // TILE):
                at = rows(i)
                there = slice(r * seq + i * TILE, r * seq + (i + 1) * TILE)
                e = hid_s[there, :]
                normed = n1[r][at, :].astype(f32)
                eg = e * pack[GAIN_ONE : GAIN_ONE + 1]
                grad = rho[r][at, 0:1] * (eg - mean_of(eg) - normed * mean_of(eg * normed))
                sum_o[r][at, :] = grad
                att = grad.astype(bf16)
                att_o[there, :] = att
                mix_o[r][at, :] = nt(att, w_attn[...]).astype(bf16)
                sums = [sums[0] + col_sum(e * normed), sums[1] + col_sum(e), sums[2] + col_sum(att.astype(f32))]
        for i in range(3):
            vec_o[i : i + 1, :] = sums[i]


def feed_backward(low, slope, w_out, w_in, sum_two, n1, rho, ramp, pack, w_attn):
    rows_here = len(n1)
    seq, width = n1[0].shape
    count, units = slope.shape
    block = pl.BlockSpec((count, CHUNK), lambda j: (0, j))
    result = call(
        functools.partial(back_kernel, rows_here), "feed_backward", (units // CHUNK,),
        [whole(low.shape), block, pl.BlockSpec((CHUNK, width), lambda j: (j, 0)), pl.BlockSpec((width, CHUNK), lambda j: (0, j)),
         whole((count, width)), whole((8, width)), whole(pack.shape), whole((width, width))]
        + [whole((seq, width))] * rows_here + [whole((seq, 128))] * rows_here,
        [block, whole((16, width)), whole((count, width))] + [whole((seq, width))] * (2 * rows_here),
        [sds((count, units), bf16), sds((16, width), f32), sds((count, width), bf16)]
        + [sds((seq, width), f32)] * rows_here + [sds((seq, width), bf16)] * rows_here,
        [pltpu.VMEM((count, width), f32)],
        (2 * count * width * units + count * width * width, 40e6, 0),
        low, slope, w_out, w_in, sum_two, ramp, pack, w_attn, *n1, *rho)
    return result[0], result[1], result[2], result[3 : 3 + rows_here], result[3 + rows_here :]


def attention_back_kernel(
    head_size, part_len, mixers, here, qkv_r, probs_r, mix_r, grad_r, wq, wk, wv, sum_one, vec_in, *refs,
):
    d_o, vec_o, tok_o, acc_s, w_s, vec_s = refs
    step = pl.program_id(0)
    last = pl.num_programs(0) - 1
    span = GROUP * head_size
    seq = qkv_r.shape[1]
    qs, keys, values = qkv_r[0, :, :span], qkv_r[0, :, span : 2 * span], qkv_r[0, :, 2 * span :]
    grad = grad_r[...]
    for i, weight in enumerate((wq, wk, wv)):
        w_s[:, i * span : (i + 1) * span] = weight[...]
    prod = grad.T.astype(f32) * mix_r[...].T.astype(f32)
    keys_t = keys.T
    grad_heads = per_head(grad, head_size)
    grad_probs = nt(values, grad_heads)
    parts, dq_t = [], []
    for h in range(GROUP):
        rows = slice(h * head_size, (h + 1) * head_size)
        at = slice(h * seq, (h + 1) * seq)
        part = (probs_r[0, :, at].astype(f32) * (grad_probs[:, at] - col_sum(prod[rows]))).astype(bf16)
        parts.append(part)
        dq_t.append(nn(keys_t[rows], part))
    grad_scores = jnp.concatenate(parts, axis=1)
    dv = nn(probs_r[0], grad_heads).astype(bf16)
    dk = nn(grad_scores, per_head(qs, head_size)).astype(bf16)
    dq = (jnp.concatenate(dq_t, axis=0) * (head_size ** (-0.5))).astype(bf16).T
    all_three = jnp.concatenate([dq, dk, dv], axis=1)
    half = span // 2
    for c in range(2):
        at = slice(c * half, (c + 1) * half)
        d_o[c] = jnp.concatenate([dq[:, at], dk[:, at], dv[:, at]], axis=1)
    vec_s[step] = jnp.concatenate(
        [col_sum(dq.astype(f32)), col_sum(dv.astype(f32)), jnp.zeros((6, span), f32)], axis=0)
    part = nt(all_three, w_s[...])

    @pl.when(step == 0)
    def _():
        acc_s[...] = sum_one[...] + part

    @pl.when(step > 0)
    def _():
        acc_s[...] += part

    @pl.when(step == last)
    def _():
        steps = vec_s.shape[0]
        for k in range(mixers):
            tok_o[here[0] ^ k] = acc_s[k * part_len : (k + 1) * part_len, :].astype(bf16)
        vec_o[...] = vec_in[...] + jnp.concatenate([vec_s[g] for g in range(steps)], axis=1)


def attention_backward(here, part_len, qkv, probs, mix, grad_mix, w_qkv, sum_one, vec_in):
    steps, seq, _ = qkv.shape
    width = grad_mix.shape[1]
    head_size = width // HEADS
    span = GROUP * head_size
    mixers = seq // part_len

    def weight(which):
        return pl.BlockSpec((width, span), lambda g: (0, which * steps + g))

    return call(
        functools.partial(attention_back_kernel, head_size, part_len, mixers), "attention_backward", (steps,),
        [SMEM_SPEC, pl.BlockSpec((1, seq, 3 * span), lambda g: (g, 0, 0)), pl.BlockSpec((1, seq, GROUP * seq), lambda g: (g, 0, 0)),
         pl.BlockSpec((seq, span), lambda g: (0, g)), pl.BlockSpec((seq, span), lambda g: (0, g)),
         weight(0), weight(1), weight(2), whole((seq, width)), whole((8, width))],
        [pl.BlockSpec((2, seq, 3 * span // 2), lambda g: (0, 0, g)), whole((8, width)), whole((mixers, part_len, width))],
        [sds((2, seq, 3 * width // 2), bf16), sds((8, width), f32), sds((mixers, part_len, width), bf16)],
        [pltpu.VMEM((seq, width), f32), pltpu.VMEM((width, 3 * span), bf16), pltpu.VMEM((steps, 8, span), f32)],
        (3 * seq * width * width + 16 * seq * seq * width, 18e6, 0),
        here, qkv, probs, mix, grad_mix, w_qkv, w_qkv, w_qkv, sum_one, vec_in)


def store_sums(outs, got, rows, read):
    for p in range(8):
        for y in range(2):
            value = read(p, y)
            if got is None:
                outs[0][p * 2 + y, rows, :] = value.astype(bf16)
                continue
            value = (value + got[p * 2 + y, rows, :].astype(f32)).astype(bf16)
            xk, xs, yk, ys = outs
            z2, z1, x = p // 4, p // 2 % 2, p % 2
            if z1 == 0:
                (xk, xs)[x][z2, y, rows, :] = value
            else:
                (yk, ys)[y][z2, x, rows, :] = value


def natural(acc, p, y, dp, upper, columns):
    return acc[pl.ds(pl.multiple_of((p ^ dp) * 2 * UNIT + (y ^ upper) * UNIT, 16), UNIT), columns]


def split_refs(flip, refs):
    return (refs[0], None, refs[1:]) if flip else (refs[1:5], refs[0], refs[5:])


def unit_call(kernel, name, flip, grid, in_specs, rows, step_rows, scratch, work, here, *args, got=None):
    if flip:
        specs, shapes = [pl.BlockSpec((16, step_rows, HALF), lambda j, s: (0, j, 0))], [sds((16, rows, HALF), bf16)]
    else:
        in_specs = in_specs + [pl.BlockSpec((16, step_rows, HALF), lambda j, s: (0, j, 0))]
        args = args + (got,)
        specs = [pl.BlockSpec((2, 2, step_rows, HALF), lambda j, s: (0, 0, j, 0))] * 4
        shapes = [sds((2, 2, rows, HALF), bf16)] * 4
    out = call(kernel, name, (grid,), in_specs, specs, shapes, scratch, work, here, *args, prefetch=1)
    return out[0] if flip else out


def out_units_kernel(flip, here, act, low, *refs):
    outs, got, (acc_s,) = split_refs(flip, refs)
    outs = [outs] if flip else outs
    dp, upper = here[1], (here[0] >> 1) & 1
    count = act.shape[-1]
    acc_s[...] = nn(act[...].reshape(16 * UNIT, count), low[:count])
    at = [pl.multiple_of((upper ^ y) * HALF, 128) for y in range(2)]
    store_sums(outs, got, slice(None), lambda p, y: acc_s[
        pl.ds(pl.multiple_of((p ^ dp) * 2 * UNIT, 16), 2 * UNIT), pl.ds(at[y], HALF)])


def out_units(here, flip, got, act, low):
    width = low.shape[1]
    count = act.shape[-1]
    return unit_call(
        functools.partial(out_units_kernel, flip), "units_out", flip, 2,
        [pl.BlockSpec((8, 1, 2, UNIT, count), lambda j, s: (0, (s[0] & 1) ^ flip, j, 0, 0)), whole(low.shape)],
        4 * UNIT, 2 * UNIT, [pltpu.VMEM((16 * UNIT, width), f32)], (4 * 8 * UNIT * count * width, 5e6, 0),
        here, act, low, got=got)


def in_units_kernel(flip, parts, here, *refs):
    hids, refs = refs[:parts], refs[parts:]
    mixes, refs = refs[:parts], refs[parts:]
    up, att, low = refs[:3]
    outs, got, (acc_s,) = split_refs(flip, refs[3:])
    outs = [outs] if flip else outs
    step = pl.program_id(0)
    dp = here[1]
    core, upper = (here[0] & 1) ^ flip, (here[0] >> 1) & 1
    seq = hids[0].shape[0]

    def product(lefts, right):
        return sum(tn(left[...], right[i * seq : (i + 1) * seq, :]) for i, left in enumerate(lefts))

    @pl.when(step < 2)
    def _():
        acc_s[...] = product(hids, up)

    @pl.when(step == 2)
    def _():
        acc_s[:, :HALF] = product(mixes, att)
        right = low[16:32, :]
        acc_s[:, HALF:] = tn(low[:16, :], jnp.where(core == 0, right[:, :HALF], right[:, HALF:]))

    for u in range(2):
        store_sums(outs, got, slice(u * UNIT, (u + 1) * UNIT), lambda p, y: natural(
            acc_s, p, y, dp, upper, slice(u * HALF, (u + 1) * HALF)))


def in_units(here, flip, got, hids, mixes, up, att, low):
    parts = len(hids)
    seq, width = hids[0].shape
    count = up.shape[0]
    return unit_call(
        functools.partial(in_units_kernel, flip, parts), "units_in", flip, 3,
        [whole((seq, width))] * (2 * parts)
        + [pl.BlockSpec((count, 2 * HALF), lambda j, s: (0, ((s[0] & 1) ^ flip) * 2 + jnp.minimum(j, 1))),
           pl.BlockSpec((count, HALF), lambda j, s: (0, (s[0] & 1) ^ flip)),
           pl.BlockSpec((32, width), lambda j, s: (count // 32, 0))],
        6 * UNIT, 2 * UNIT, [pltpu.VMEM((width, 2 * HALF), f32)], (5 * width * HALF * count, 5e6, 0),
        here, *hids, *mixes, up, att, low, got=got)


VEC_ROWS = 16


def qkv_units_kernel(flip, parts, here, *refs):
    toks, refs = refs[:parts], refs[parts:]
    grads, refs = refs[:parts], refs[parts:]
    back, late = refs[:2]
    outs, got, (acc_s, tab_s) = split_refs(flip, refs[2:])
    outs = [outs] if flip else outs
    dp, upper = here[1], (here[0] >> 1) & 1
    acc_s[...] = sum(tn(tok[...], grad[0]) for tok, grad in zip(toks, grads))
    for u in range(3):
        store_sums(outs, got, slice(u * UNIT, (u + 1) * UNIT), lambda p, y: natural(
            acc_s, p, y, dp, upper, slice(u * HALF, (u + 1) * HALF)))
    ramp = back[8:16, :]
    units = jnp.concatenate([back[3 + i : 4 + i, :] for i in range(4)], axis=1)
    short = jnp.concatenate(
        [ramp[0:7], back[0:3, :], late[0:2, :], jnp.zeros((4, ramp.shape[1]), f32)], axis=0)
    share = short.shape[1] // 8
    fill = jnp.zeros((16, 128 - share), f32)
    blank = jnp.zeros((VEC_ROWS - 3, HALF), f32)
    for b in range(8):
        slots = jnp.concatenate([short[:, b * share : (b + 1) * share], fill], axis=1)
        slots = [slots[i : i + 1] for i in range(12)]
        slots += [units[:, b * HALF + i * 128 : b * HALF + (i + 1) * 128] for i in range(3)]
        slots += [ramp[7:8, :128], jnp.where(dp == b, ramp[7:8, 128:256], 0.0), jnp.zeros((1, 128), f32)]
        lines = [jnp.concatenate(slots[i * 3 : i * 3 + 3], axis=1) for i in range(6)]
        for y in range(2):
            tab_s[b, y] = jnp.concatenate(lines[y * 3 : y * 3 + 3] + [blank], axis=0)
    store_sums(outs, got, slice(3 * UNIT, 3 * UNIT + VEC_ROWS), lambda p, y: tab_s[p ^ dp, y ^ upper])


def qkv_units(here, flip, got, toks, grads, back, late):
    parts = len(toks)
    seq, width = toks[0].shape
    rows = 3 * UNIT + VEC_ROWS
    wide = 3 * HALF
    return unit_call(
        functools.partial(qkv_units_kernel, flip, parts), "units_qkv", flip, 1,
        [whole((seq, width))] * parts + [pl.BlockSpec((1, seq, wide), lambda j, s: ((s[0] & 1) ^ flip, 0, 0))] * parts
        + [whole((16, width)), whole((8, width))],
        rows, rows, [pltpu.VMEM((width, wide), f32), pltpu.VMEM((8, 2, VEC_ROWS, HALF), f32)],
        (width * wide * parts * seq, 5e6, 0), here, *toks, *grads, back, late, got=got)


def second_kernel(xk, xr, yk, yr, x2k, x2s, y2k, y2s):
    x = xk[0].astype(f32) + xr[0].astype(f32)
    x2k[0] = x[0].astype(bf16)
    x2s[0] = x[1].astype(bf16)
    y = yk[0].astype(f32) + yr[0].astype(f32)
    y2k[0] = y[0].astype(bf16)
    y2s[0] = y[1].astype(bf16)


def add(left, right):
    return (left.astype(f32) + right.astype(f32)).astype(bf16)


def swap(value, axis, bit):
    size = lax.axis_size(axis)
    return lax.ppermute(value, axis, [(i, i ^ bit) for i in range(size)])


def first_swap(stage):
    xk, xs, yk, ys = stage
    return xk, swap(xs, "dp", 1), yk, swap(ys, "mix", 2)


def second_stage(stage):
    rows = stage[0].shape[2]
    block = pl.BlockSpec((1, 2, rows, HALF), lambda z: (z, 0, 0, 0))
    out = pl.BlockSpec((1, rows, HALF), lambda z: (z, 0, 0))
    return call(second_kernel, "stage_two", (2,), [block] * 4, [out] * 4, [sds((2, rows, HALF), bf16)] * 4, [],
                STAGE, *stage)


def second_swap(stage):
    xk, xs, yk, ys = stage
    return xk, swap(xs, "mix", 2), yk, swap(ys, "dp", 1)


def third_stage(stage):
    xk, xr, yk, yr = stage
    return add(xk, xr), add(yk, yr)


def third_swap(stage):
    return stage[0], swap(stage[1], "dp", 2)


def fourth_stage(stage):
    mine, got = stage
    return add(mine[0], got[0]), add(mine[1], got[1])


def fourth_swap(stage):
    return stage[0], swap(stage[1], "dp", 4)


def fifth_stage(stage):
    return add(*stage)


def spread(final):
    other = swap(final, "mix", 2)
    return final, other, swap(final, "mix", 1), swap(other, "mix", 1)


def place_kernel(plan, vec, here, *refs):
    parts, outs = refs[:4], refs[4:]
    core, upper = here[0] & 1, (here[0] >> 1) & 1
    for i, part in enumerate(parts):
        c, y = core ^ (i // 2), upper ^ (i % 2)
        for u, (which, row, row_core, row_y, col_core, col_y, pieces) in enumerate(plan):
            r0 = pl.multiple_of(row + c * row_core + y * row_y, 8)
            at = 0
            for col, size in pieces:
                c0 = pl.multiple_of(col + c * col_core + y * col_y, 128)
                outs[which][pl.ds(r0, UNIT), pl.ds(c0, size)] = part[u * UNIT : (u + 1) * UNIT, at : at + size].astype(f32)
                at += size
    if vec:
        base = len(plan) * UNIT
        mine, other = parts[0][base : base + 8, :].astype(f32), parts[1][base : base + 8, :].astype(f32)
        lines = [jnp.where(upper == 0, mine, other), jnp.where(upper == 0, other, mine)]

        def slot(i):
            return lines[i // 9][i % 9 // 3 : i % 9 // 3 + 1, (i % 3) * 128 : (i % 3 + 1) * 128]

        vec_outs = outs[-13:]
        share = 96
        for i, target in zip((0, 1, 2, 3, 7, 8, 9, 10, 11), vec_outs[:9]):
            target[...] = slot(i)[0, :share]
        vec_outs[9][...] = jnp.concatenate([slot(12), slot(13), slot(14)], axis=1)[0]
        vec_outs[10][...] = jnp.concatenate([slot(4), slot(5), slot(6)], axis=0)[:, :share]
        vec_outs[11][...] = slot(15)[0, :3]
        losses = slot(16)
        pairs, count = vec_outs[12].shape
        lines = [losses[:, r * pairs : (r + 1) * pairs] for r in range(count)]
        lines = jnp.concatenate(lines + [jnp.zeros((8 - count % 8, pairs), f32)] if count % 8 else lines, axis=0)
        vec_outs[12][...] = jnp.concatenate([lines, jnp.zeros((lines.shape[0], 128 - pairs), f32)], axis=1).T[:pairs, :count]


def place_units(here, plan, shapes, parts, vec_shapes=()):
    shape = parts[0].shape
    vm = [whole(s) for s in list(shapes) + list(vec_shapes)]
    return call(
        functools.partial(place_kernel, plan, bool(vec_shapes)), "place_units", (),
        [SMEM_SPEC] + [whole(shape)] * 4, vm, [sds(s, f32) for s in list(shapes) + list(vec_shapes)], [],
        STAGE, here, *parts)


def weave_kernel(*refs):
    for r, piece in enumerate(refs[:-1]):
        refs[-1][:, r] = piece[...]


def weave(pieces):
    mixers, part_len, width = pieces[0].shape
    shape = (mixers, len(pieces), part_len, width)
    (out,) = call(
        weave_kernel, "weave", (mixers,), [pl.BlockSpec((1, part_len, width), lambda k: (k, 0, 0))] * len(pieces),
        [pl.BlockSpec((1,) + shape[1:], lambda k: (k, 0, 0, 0))], [sds(shape, bf16)], [], STAGE, *pieces)
    return out.reshape(mixers * len(pieces), part_len, width)


def between(value):
    return lax.all_to_all(value, "mix", split_axis=0, concat_axis=0, tiled=True)


def on_device(
    tokens, cotangent, pair_lengths, labels, w_qkv, b_query, b_value, w_attn, b_attn, gain_one, shift_one,
    w_in, b_in, w_out, b_out, gain_two, shift_two, w_pool, b_pool, w_class, b_class,
):
    row_count, part_len, width = tokens.shape
    mixers = lax.axis_size("mix")
    dps = lax.axis_size("dp")
    rows_here = row_count // mixers
    seq = part_len * mixers
    units = w_in.shape[1]
    mix = lax.axis_index("mix").astype(jnp.int32)
    dp = lax.axis_index("dp").astype(jnp.int32)
    here = jnp.stack([mix, dp])
    pairs = pair_lengths.shape[1]
    quick = dps == 8 and mixers == 4 and width == 768 and units == 3072 and seq * rows_here == 1024 and rows_here == 2

    order = sorted(range(1, mixers), reverse=True)

    def exchange(blocks):
        got = {0: blocks[0]}
        for k in order:
            got[k] = swap(blocks[k], "mix", k)
        return [got[k] for k in range(mixers)]

    pack = jnp.concatenate(
        [b_query, b_value, b_attn, gain_one, shift_one, b_out, gain_two, shift_two, b_pool, b_in, b_class,
         jnp.zeros((3 * width - b_class.shape[0],), f32)]).reshape(16, width)

    def tie(first, second):
        return lax.optimization_barrier((first, second))

    cot = cotangent.reshape(mixers, rows_here, part_len, width)
    rows = []
    def pieces(array, r):
        view = array.reshape(mixers, rows_here, part_len, width)
        return [lax.dynamic_index_in_dim(view[:, r], mix ^ k, 0, keepdims=False) for k in range(mixers)]

    first = pieces(tokens, 0)
    got = exchange(first)
    _, later = tie(first[0], tokens)
    for r in range(rows_here):
        if r + 1 < rows_here:
            blocks = pieces(later, r + 1)
            got, blocks = tie(got, blocks)
            following = exchange(blocks)
        else:
            got, cot = tie(got, cot)
            cots = between(cot)
        rows.append(forward_row(r, rows_here, here, pair_lengths, got, pack, w_qkv, w_attn))
        if r + 1 < rows_here:
            rows[r], got = tie(rows[r], following)
    qkvs, probs, toks_in, mixes, hids, n1, rho1 = zip(*rows)
    act, slope, outs, n2, rho2, firsts = feed_forward(part_len, here, pair_lengths, hids, pack, w_in, w_out)
    outs = between(outs)
    vec_ramp, sum_two, low = off_ramp(
        part_len, here, pair_lengths, labels, firsts, pack, w_pool, w_class, cots, n2, rho2)

    if not quick:
        return plain_rest(
            here, part_len, act, slope, outs, low, sum_two, vec_ramp, qkvs, probs, toks_in, mixes, hids, n1, rho1, pack,
            w_qkv, w_attn, w_in, w_out, mix, dp, row_count, units)

    def both_cores(make, args, meanwhile):
        send = make(here, 1, None, *args)
        got = swap(send, "mix", 1)
        _, meanwhile = tie(send, meanwhile)
        meanwhile = second_swap(second_stage(meanwhile)) if meanwhile is not None else None
        if meanwhile is not None:
            _, args = tie(meanwhile[0], args)
        return first_swap(make(here, 0, got, *args)), meanwhile

    one, _ = both_cores(out_units, (act.reshape(8, 2, 4, UNIT, rows_here * seq), low), None)
    _, sum_two = tie(one[0], sum_two)
    grad_up, vec_back, grad_att, sum_one, grad_mix = feed_backward(
        low, slope, w_out, w_in, sum_two, n1, rho1, vec_ramp, pack, w_attn)
    (outs, one), grad_up = tie((outs, one), grad_up)
    two, one = both_cores(in_units, (hids, mixes, grad_up, grad_att, low), one)
    _, one = tie(two[0], one)
    one = third_swap(third_stage(one))
    _, grad_mix = tie(one[0], grad_mix)

    vec_late = jnp.zeros((8, width), f32)
    grads, toks = [], []
    for r in range(rows_here):
        dqkv, vec_late, tok = attention_backward(
            here, part_len, qkvs[r], probs[r], mixes[r], grad_mix[r], w_qkv, sum_one[r], vec_late)
        grads.append(dqkv)
        toks.append(between(tok))
        if r == 0:
            _, one = tie(dqkv, one)
            one = fourth_swap(fourth_stage(one))
            _, two = tie(one[0], two)
            two = second_swap(second_stage(two))
            _, grad_mix = tie(two[0], grad_mix)
    toks[0], one, two, grads = lax.optimization_barrier((toks[0], one, two, grads))
    send = qkv_units(here, 1, None, toks_in, grads, vec_back, vec_late)
    got = swap(send, "mix", 1)
    _, two = tie(send, two)
    two = third_swap(third_stage(two))
    _, one = tie(two[0], one)
    final = fifth_stage(one)
    _, grads = tie(final, grads)
    three = first_swap(qkv_units(here, 0, got, toks_in, grads, vec_back, vec_late))
    _, two = tie(three[0], two)
    two = fourth_swap(fourth_stage(two))
    _, three = tie(two[0], three)
    three = second_swap(second_stage(three))
    _, two = tie(three[0], two)
    final = jnp.concatenate([final, fifth_stage(two)], axis=0)
    other = swap(final, "mix", 2)
    _, three = tie(final, three)
    three = third_swap(third_stage(three))
    _, toks = tie(three[0], toks)
    grad_tokens = weave(toks)
    _, three = tie(grad_tokens, three)
    three = fourth_swap(fourth_stage(three))
    _, other = tie(three[0], other)
    final = (final, other, swap(final, "mix", 1), swap(other, "mix", 1))
    other, three = tie(other, three)
    three = spread(fifth_stage(three))
    _, final = tie(three[0], final)
    grad_w_out, grad_w_in, grad_w_attn, grad_w_pool = place_units(
        here, [(0, j * UNIT, 192, 0, 0, HALF, ((0, HALF),)) for j in range(4)]
        + [(1, 0, 0, UNIT, 4 * HALF, 0, ((j * HALF, HALF),)) for j in range(4)]
        + [(2, 0, 0, UNIT, HALF, 0, ((0, HALF),)), (3, 0, 0, UNIT, HALF, 0, ((0, HALF),))],
        [(384, width), (96, units), (96, width), (96, width)], final)
    _, three = tie(grad_w_in, three)
    output = outs.reshape(row_count, part_len, width)
    share = width // dps
    last = place_units(
        here, [(0, 0, 0, UNIT, 128, 0, tuple((w * width + g * 256, 128) for w in range(3))) for g in range(3)],
        [(96, 3 * width)], three,
        [(share,)] * 9 + [(units // dps,), (w_class.shape[1], share), b_class.shape, (pairs, row_count)])
    (grad_w_qkv, grad_b_out, grad_gain_two, grad_shift_two, grad_b_pool, grad_gain_one, grad_shift_one, grad_b_attn,
     grad_b_query, grad_b_value, grad_b_in, grad_w_class, grad_b_class, pair_loss) = last
    return (
        output, pair_loss.T, grad_tokens, grad_w_qkv, grad_b_query, grad_b_value, grad_w_attn, grad_b_attn,
        grad_gain_one, grad_shift_one, grad_w_in, grad_b_in, grad_w_out, grad_b_out, grad_gain_two, grad_shift_two,
        grad_w_pool, grad_b_pool, grad_w_class.T, grad_b_class,
    )


def plain_rest(
    here, part_len, act, slope, outs, low, sum_two, vec_ramp, qkvs, probs, toks_in, mixes, hids, n1, rho1, pack,
    w_qkv, w_attn, w_in, w_out, mix, dp, row_count, units,
):
    rows_here = len(n1)
    seq, width = n1[0].shape
    dps = lax.axis_size("dp")
    pairs = vec_ramp.shape[0] // rows_here
    grad_up, vec_back, grad_att, sum_one, grad_mix = feed_backward(
        low, slope, w_out, w_in, sum_two, n1, rho1, vec_ramp, pack, w_attn)
    vec_late = jnp.zeros((8, width), f32)
    dqkv, toks = [], []
    for r in range(rows_here):
        grad, vec_late, tok = attention_backward(
            here, part_len, qkvs[r], probs[r], mixes[r], grad_mix[r], w_qkv, sum_one[r], vec_late)
        parts = grad.reshape(2, seq, width // 256, 3, 128).transpose(1, 3, 2, 0, 4)
        dqkv.append(parts.reshape(seq, 3 * width))
        toks.append(between(tok))
    output = outs.reshape(row_count, part_len, width)
    grad_tokens = weave(toks)
    low, pool = low[: seq * rows_here], low[seq * rows_here :]
    left = [jnp.concatenate(arrays, axis=0) for arrays in (toks_in, hids, mixes)]
    grads = (
        tn(left[0], jnp.concatenate(dqkv, axis=0)), tn(left[2], grad_att), tn(left[1], grad_up), nn(act, low),
        tn(pool[:16], pool[16:]),
    )
    shards = [lax.psum_scatter(g, "dp", scatter_dimension=0, tiled=True) for g in grads]
    shards = [lax.psum(s.astype(bf16), "mix").astype(f32) for s in shards]
    bins = vec_back[3:7]
    vecs = jnp.concatenate([vec_ramp[:7], vec_back[:3], vec_late[:2], bins], axis=0)
    vecs = lax.psum(vecs, ("dp", "mix"))
    class_total = lax.psum(vec_ramp[7, :3], ("dp", "mix"))
    loss = lax.psum(vec_ramp[7, 128 : 128 + row_count * pairs], "mix").reshape(row_count, pairs)
    share = width // dps
    v = lax.dynamic_slice_in_dim(vecs, dp * share, share, axis=1)
    bin_share = lax.dynamic_slice_in_dim(vecs[12:].reshape(-1), dp * (units // dps), units // dps)
    return (
        output, loss, grad_tokens, shards[0], v[10], v[11], shards[1], v[9], v[7], v[8], shards[2], bin_share,
        shards[3], v[0], v[1], v[2], shards[4], v[3], v[4:7].T, class_total,
    )


def solution(mesh):
    wide = P("dp", "mix", None)
    split = P("dp", None)
    in_specs = (wide, wide, split, split) + (P(),) * 17
    out_specs = (
        wide, split, wide,
        split, P("dp"), P("dp"), split, P("dp"), P("dp"), P("dp"),
        split, P("dp"), split, P("dp"), P("dp"), P("dp"),
        split, P("dp"), split, P(),
    )
    return jax.shard_map(on_device, mesh=mesh, in_specs=in_specs, out_specs=out_specs, check_vma=False)
```

```python
import functools

import jax
import jax.numpy as jnp
from jax import lax
from jax.experimental import pallas as pl
from jax.experimental.pallas import tpu as pltpu
from jax.sharding import PartitionSpec as P

HEADS = 12
SCALE = 1.0
WORK = 5.8e8
GROUP = 4
CHUNK = 768
TILE = 256
UNIT = 48
HALF = 384
norm_eps = 1e-06
masked_score = -1000000000.0
inv_root_two = 0.7071067811865476
inv_root_tau = 0.3989422804014327
f32 = jnp.float32
bf16 = jnp.bfloat16
VMEM_LIMIT = 62 * 1024 * 1024
SMEM_SPEC = pl.BlockSpec(memory_space=pltpu.SMEM)
B_QUERY, B_VALUE, B_ATTN, GAIN_ONE, SHIFT_ONE, B_OUT, GAIN_TWO, SHIFT_TWO, B_POOL, B_IN, B_CLASS = 0, 1, 2, 3, 4, 5, 6, 7, 8, 9, 13


def whole(shape):
    return pl.BlockSpec(shape, lambda *_: (0,) * len(shape))


def sds(shape, dtype):
    return jax.ShapeDtypeStruct(shape, dtype)


def nn(left, right):
    return jnp.dot(left, right, preferred_element_type=f32)


def nt(left, right):
    return lax.dot_general(left, right, (((1,), (1,)), ((), ())), preferred_element_type=f32)


def tn(left, right):
    return lax.dot_general(left, right, (((0,), (0,)), ((), ())), preferred_element_type=f32)


def call(kernel, name, grid, in_specs, out_specs, out_shape, scratch, work, *args, prefetch=0, aliases=None):
    common = dict(
        out_shape=out_shape,
        compiler_params=pltpu.CompilerParams(vmem_limit_bytes=VMEM_LIMIT),
        cost_estimate=pl.CostEstimate(flops=int(2 * work[0] * SCALE), bytes_accessed=int(work[1] * SCALE), transcendentals=0),
        name=name,
        input_output_aliases=aliases or {},
    )
    if prefetch:
        spec = pltpu.PrefetchScalarGridSpec(
            num_scalar_prefetch=prefetch, grid=grid, in_specs=in_specs, out_specs=out_specs, scratch_shapes=scratch)
        return pl.pallas_call(kernel, grid_spec=spec, **common)(*args)
    return pl.pallas_call(
        kernel, grid=grid, in_specs=in_specs, out_specs=out_specs, scratch_shapes=scratch, **common)(*args)


def after(value, *earlier):
    return lax.optimization_barrier((value,) + earlier)[0]


def mean_of(values):
    return jnp.mean(values, axis=-1, keepdims=True)


def col_sum(values):
    return jnp.sum(values, axis=0, keepdims=True)


def head_only(values, head, size):
    lane = lax.broadcasted_iota(jnp.int32, (1, values.shape[1]), 1) // size
    return jnp.where(lane == head, values, jnp.zeros((), values.dtype))


def per_head(values, size):
    return jnp.concatenate([head_only(values, h, size) for h in range(GROUP)], axis=0)


def segments(places, lengths, row):
    total = jnp.int32(0)
    seg = jnp.zeros(places.shape, jnp.int32)
    for k in range(lengths.shape[1]):
        total = total + lengths[row, k]
        seg = seg + (places >= total).astype(jnp.int32)
    return seg


def forward_kernel(row, rows_here, part_len, mixers, head_size, here, lengths, *refs):
    pieces, refs = refs[:mixers], refs[mixers:]
    pack, packq, packv, wq, wk, wv, wa = refs[:7]
    (qkv_o, probs_o, tok_o, mix_o, hid_o, n1_o, rho_o,
     tok_s, mix_s, bias_s, w_s) = refs[-11:]
    step = pl.program_id(0)
    seq = part_len * mixers
    shift = part_len.bit_length() - 1
    span = GROUP * head_size

    @pl.when(step == 0)
    def _():
        for i, piece in enumerate(pieces):
            tok_s[i * part_len : (i + 1) * part_len, :] = piece[...]
        mine = here[0]
        down = lax.broadcasted_iota(jnp.int32, (seq, 1), 0)
        across = lax.broadcasted_iota(jnp.int32, (1, seq), 1)

        def place(i):
            return (((i >> shift) ^ mine) << shift) + (i & (part_len - 1))

        number = mine * rows_here + row
        same = segments(place(down), lengths, number) == segments(place(across), lengths, number)
        bias_s[...] = jnp.where(same, 0.0, masked_score)

    for i, weight in enumerate((wq, wk, wv)):
        w_s[:, i * span : (i + 1) * span] = weight[...]
    qkv = nn(tok_s[...], w_s[...])
    qs = (qkv[:, :span] + packq[B_QUERY : B_QUERY + 1]).astype(bf16) * bf16(head_size ** (-0.5))
    keys = qkv[:, span : 2 * span].astype(bf16)
    values = (qkv[:, 2 * span :] + packv[B_VALUE : B_VALUE + 1]).astype(bf16)
    qkv_o[0, 0, :, :span] = qs
    qkv_o[0, 0, :, span : 2 * span] = keys
    qkv_o[0, 0, :, 2 * span :] = values
    scores = nt(keys, per_head(qs, head_size))
    values_t = values.T
    mixed = []
    for h in range(GROUP):
        at = slice(h * seq, (h + 1) * seq)
        part = scores[:, at] + bias_s[...]
        expo = jnp.exp(part - jnp.max(part, axis=0, keepdims=True))
        probs = (expo * (1.0 / col_sum(expo))).astype(bf16)
        probs_o[0, 0, :, at] = probs
        mixed.append(nn(values_t[h * head_size : (h + 1) * head_size], probs))
    mixed = jnp.concatenate(mixed, axis=0).astype(bf16).T
    here_columns = pl.ds(pl.multiple_of(step * span, 128), span)
    mix_s[:, here_columns] = mixed
    mix_o[...] = mixed
    tok_o[...] = tok_s[:, here_columns]

    @pl.when(step == pl.num_programs(0) - 1)
    def _():
        full = tok_s[...].astype(f32) + (nn(mix_s[...], wa[...]) + pack[B_ATTN : B_ATTN + 1])
        centre = full - mean_of(full)
        rho = lax.rsqrt(mean_of(centre * centre) + norm_eps)
        normed = centre * rho
        hidden = normed * pack[GAIN_ONE : GAIN_ONE + 1] + pack[SHIFT_ONE : SHIFT_ONE + 1]
        hid_o[...] = hidden.astype(bf16)
        n1_o[...] = normed.astype(bf16)
        rho_o[...] = jnp.broadcast_to(rho, rho_o.shape)


def forward_row(row, rows_here, here, lengths, pieces, pack, w_qkv, w_attn, earlier):
    part_len, width = pieces[0].shape
    mixers = len(pieces)
    seq = part_len * mixers
    head_size = width // HEADS
    span = GROUP * head_size
    steps = width // span

    def weight(which):
        return pl.BlockSpec((width, span), lambda g: (0, which * steps + g))

    rows = pack.shape[0]
    column = pl.BlockSpec((rows, span), lambda g: (0, g))
    part = pl.BlockSpec((seq, span), lambda g: (row, g))
    wide = pl.BlockSpec((seq, width), lambda g: (row, 0))
    total = rows_here * seq
    specs = [SMEM_SPEC, SMEM_SPEC] + [whole((part_len, width))] * mixers
    specs += [whole((rows, width)), column, column, weight(0), weight(1), weight(2), whole((width, width))]
    return call(
        functools.partial(forward_kernel, row, rows_here, part_len, mixers, head_size), "forward_row", (steps,),
        specs + [pl.BlockSpec(memory_space=pl.ANY)] * len(earlier),
        [pl.BlockSpec((1, 1, seq, 3 * span), lambda g: (row, g, 0, 0)),
         pl.BlockSpec((1, 1, seq, GROUP * seq), lambda g: (row, g, 0, 0)),
         part, part, wide, wide, pl.BlockSpec((seq, 128), lambda g: (row, 0))],
        [sds((rows_here, steps, seq, 3 * span), bf16), sds((rows_here, steps, seq, GROUP * seq), bf16)]
        + [sds((total, width), bf16)] * 4 + [sds((total, 128), f32)],
        [pltpu.VMEM((seq, width), bf16), pltpu.VMEM((seq, width), bf16), pltpu.VMEM((seq, seq), f32),
         pltpu.VMEM((width, 3 * span), bf16)],
        (seq * width * width * 4 + 8 * seq * seq * width, 16e6, HEADS * seq * seq),
        here, lengths, *pieces, pack, pack, pack, w_qkv, w_qkv, w_qkv, w_attn, *earlier,
        aliases={len(specs) + i: i for i in range(len(earlier))})


def start_spots(here, lengths, r, rows_here, part_len, pairs, seq):
    shift = part_len.bit_length() - 1
    spots = []
    start = jnp.int32(0)
    for k in range(pairs):
        spots.append(r * seq + (((start >> shift) ^ here[0]) << shift) + (start & (part_len - 1)))
        start = start + lengths[here[0] * rows_here + r, k]
    return spots


def feed_kernel(rows_here, part_len, pairs, mixers, send, here, lengths, labels, *refs):
    hid, pack, w_in, w_out, w_pool, w_class, cots = refs[:7]
    act_o, slope_o, out_o, vec_o, sum_o, low_o, send_o = refs[7:14]
    feed_s, normed_s, rho_s, act_s, acc_s = refs[14:]
    step = pl.program_id(0)
    last = pl.num_programs(0) - 1
    tokens, width = hid.shape
    seq = part_len * mixers
    count = tokens // TILE

    @pl.when(step == 0)
    def _():
        feed_s[...] = hid[...].astype(f32) + pack[B_OUT : B_OUT + 1]

    bias = pack[pl.ds(B_IN + step, 1), :]

    def rows(i):
        return slice(i * TILE, (i + 1) * TILE)

    up = nn(hid[rows(0), :], w_in[...])
    before = None
    for i in range(count):
        following = nn(hid[rows(i + 1), :], w_in[...]) if i + 1 < count else None
        up = up + bias
        half = 0.5 * (1.0 + lax.erf(up * inv_root_two))
        act = (up * half).astype(bf16)
        slope_o[rows(i), :] = (half + up * jnp.exp(-0.5 * up * up) * inv_root_tau).astype(bf16)
        turned = act.T
        act_o[:, rows(i)] = turned
        if send:
            blocks = CHUNK // (8 * UNIT)
            act_s[pl.ds(step * blocks, blocks), :, :, :, rows(i)] = turned.reshape(blocks, 2, 2, 2 * UNIT, TILE)
        if before is not None:
            feed_s[rows(i - 1), :] += nn(before, w_out[...])
        before, up = act, following
    feed_s[rows(count - 1), :] += nn(before, w_out[...])

    @pl.when(step == last)
    def _():
        gain = pack[GAIN_TWO : GAIN_TWO + 1]
        for r in range(rows_here):
            for k in range(mixers):
                at = slice(r * seq + k * part_len, r * seq + (k + 1) * part_len)
                full = feed_s[at, :]
                centre = full - mean_of(full)
                rho = lax.rsqrt(mean_of(centre * centre) + norm_eps)
                normed = centre * rho
                out = normed * gain + pack[SHIFT_TWO : SHIFT_TWO + 1]
                feed_s[at, :] = out
                out_o[here[0] ^ k, r] = out.astype(bf16)
                normed_s[at, :] = normed
                rho_s[at, :] = jnp.broadcast_to(rho, (part_len, 128))
        spots = []
        for r in range(rows_here):
            spots += start_spots(here, lengths, r, rows_here, part_len, pairs, seq)
        firsts = jnp.concatenate([feed_s[pl.ds(spot, 1), :] for spot in spots], axis=0)
        sums = [jnp.zeros((1, width), f32)] * 2

        def backward(i, sums):
            r, k = i // mixers, i % mixers
            at = slice(i * part_len, (i + 1) * part_len)
            e = cots[here[0] ^ k, r].astype(f32)
            normed = normed_s[at, :]
            eg = e * gain
            sum_o[at, :] = rho_s[at, 0:1] * (eg - mean_of(eg) - normed * mean_of(eg * normed))
            return [sums[0] + col_sum(e * normed), sums[1] + col_sum(e)]

        tiles = rows_here * mixers
        pool = w_pool[...]
        pool_high = pool.astype(bf16)
        pool_rest = (pool - pool_high.astype(f32)).astype(bf16)
        first_high = firsts.astype(bf16)
        first_rest = (firsts - first_high.astype(f32)).astype(bf16)
        pre = nn(first_high, pool_high) + nn(first_rest, pool_high) + nn(first_high, pool_rest)
        for i in range(tiles // 2):
            sums = backward(i, sums)
        pooled = jnp.tanh(pre + pack[B_POOL : B_POOL + 1])
        classes = w_class.shape[1]
        here_pairs = rows_here * pairs
        class_t = jnp.concatenate([w_class[...], jnp.zeros((width, 128 - classes), f32)], axis=1).T
        lane = lax.broadcasted_iota(jnp.int32, (here_pairs, 128), 1)
        logits = jnp.full((here_pairs, 128), -jnp.inf, f32)
        for c in range(classes):
            logits = jnp.where(lane == c, jnp.sum(pooled * class_t[c : c + 1], axis=1, keepdims=True), logits)
        logits = logits + pack[B_CLASS : B_CLASS + 1, :128]
        top = jnp.max(logits, axis=-1, keepdims=True)
        expo = jnp.exp(logits - top)
        total = jnp.sum(expo, axis=-1, keepdims=True)
        log_total = top + jnp.log(total)
        sub = lax.broadcasted_iota(jnp.int32, (here_pairs, 128), 0)
        label = jnp.zeros((here_pairs, 128), jnp.int32)
        for r in range(rows_here):
            for k in range(pairs):
                label = jnp.where(sub == r * pairs + k, labels[here[0] * rows_here + r, k], label)
        chosen = lane == label
        loss = log_total - jnp.sum(jnp.where(chosen, logits, 0.0), axis=-1, keepdims=True)
        grad_logits = expo / total - chosen.astype(f32)
        grad_pooled = jnp.zeros((here_pairs, width), f32)
        for c in range(classes):
            grad_pooled = grad_pooled + grad_logits[:, c : c + 1] * class_t[c : c + 1]
        grad_pre = grad_pooled * (1.0 - pooled * pooled)
        grad_firsts = nt(grad_pre.astype(bf16), pool_high)
        for i in range(tiles // 2, tiles):
            sums = backward(i, sums)
        normed = jnp.concatenate([normed_s[pl.ds(spot, 1), :] for spot in spots], axis=0)
        rho = jnp.concatenate([rho_s[pl.ds(spot, 1), :] for spot in spots], axis=0)[:, 0:1]
        eg = grad_firsts * gain
        more = rho * (eg - mean_of(eg) - normed * mean_of(eg * normed))
        for i, spot in enumerate(spots):
            sum_o[pl.ds(spot, 1), :] = sum_o[pl.ds(spot, 1), :] + more[i : i + 1, :]
        vec_o[1:2, :] = sums[0] + col_sum(grad_firsts * normed)
        vec_o[2:3, :] = sums[1] + col_sum(grad_firsts)
        vec_o[3:4, :] = col_sum(grad_pre)
        for c in range(classes):
            vec_o[4 + c : 5 + c, :] = col_sum(pooled * grad_logits[:, c : c + 1])
        spread_loss = jnp.where(lane == here[0] * here_pairs + sub, loss, 0.0)
        vec_o[7:8, :] = jnp.concatenate(
            [col_sum(grad_logits), col_sum(spread_loss), jnp.zeros((1, width - 256), f32)], axis=1)
        none = jnp.zeros((16 - here_pairs, width), f32)
        low_o[tokens : tokens + 16, :] = jnp.concatenate([firsts, none], axis=0).astype(bf16)
        low_o[tokens + 16 :, :] = jnp.concatenate([grad_pre, none], axis=0).astype(bf16)
        bias_sum = jnp.zeros((1, width), f32)
        for i in range(count):
            low = sum_o[rows(i), :].astype(bf16)
            low_o[rows(i), :] = low
            bias_sum = bias_sum + col_sum(low.astype(f32))
        vec_o[0:1, :] = bias_sum
        if send:
            dp, upper = here[1], (here[0] >> 1) & 1
            other = 1 - (here[0] & 1)
            for j in range(2):
                acc_s[...] = nn(act_s[:, other, j].reshape(16 * UNIT, tokens), low_o[:tokens, :])
                store_sums([send_o], None, slice(j * 2 * UNIT, (j + 1) * 2 * UNIT), lambda p, y: acc_s[
                    pl.ds(pl.multiple_of((p ^ dp) * 2 * UNIT, 16), 2 * UNIT),
                    pl.ds(pl.multiple_of((upper ^ y) * HALF, 128), HALF)])
        else:
            send_o[...] = jnp.zeros(send_o.shape, bf16)


def feed_forward(part_len, here, lengths, labels, hid, pack, w_in, w_out, w_pool, w_class, cots, send):
    mixers, rows_here = cots.shape[:2]
    tokens, width = hid.shape
    pairs = lengths.shape[1]
    units = w_in.shape[1]
    steps = units // CHUNK
    sent = (16, 4 * UNIT, HALF) if send else (16, 128)
    act_shape = (units // (8 * UNIT), 2, 2, 2 * UNIT, tokens) if send else (8, 128)
    acc_shape = (16 * UNIT, width) if send else (8, 128)
    return call(
        functools.partial(feed_kernel, rows_here, part_len, pairs, mixers, send), "feed_forward", (steps,),
        [SMEM_SPEC] * 3
        + [whole(hid.shape), whole(pack.shape), pl.BlockSpec((width, CHUNK), lambda c: (0, c)),
           pl.BlockSpec((CHUNK, width), lambda c: (c, 0)), whole(w_pool.shape), whole(w_class.shape), whole(cots.shape)],
        [pl.BlockSpec((CHUNK, tokens), lambda c: (c, 0)), pl.BlockSpec((tokens, CHUNK), lambda c: (0, c)),
         whole(cots.shape), whole((8, width)), whole((tokens, width)), whole((tokens + 32, width)), whole(sent)],
        [sds((units, tokens), bf16), sds((tokens, units), bf16), sds(cots.shape, bf16), sds((8, width), f32),
         sds((tokens, width), f32), sds((tokens + 32, width), bf16), sds(sent, bf16)],
        [pltpu.VMEM((tokens, width), f32), pltpu.VMEM((tokens, width), f32), pltpu.VMEM((tokens, 128), f32),
         pltpu.VMEM(act_shape, bf16), pltpu.VMEM(acc_shape, f32)],
        (2 * tokens * width * units, 35e6, 0),
        here, lengths, labels, hid, pack, w_in, w_out, w_pool, w_class, cots)


def back_kernel(low, slope, w_out, w_in, sum_two, ramp, pack, w_attn, n1, rho, up_o, vec_o, att_o, sum_o, mix_o, hid_s):
    step = pl.program_id(0)
    last = pl.num_programs(0) - 1
    count = slope.shape[0] // TILE

    def rows(i):
        return slice(i * TILE, (i + 1) * TILE)

    @pl.when(step == 0)
    def _():
        hid_s[...] = sum_two[...]
        vec_o[7:8, :] = jnp.zeros((1, vec_o.shape[1]), f32)
        vec_o[8:16, :] = ramp[...]

    total = jnp.zeros((1, slope.shape[1]), f32)
    act = nt(low[rows(0), :], w_out[...])
    before = None
    for i in range(count):
        following = nt(low[rows(i + 1), :], w_out[...]) if i + 1 < count else None
        up = (act * slope[rows(i), :].astype(f32)).astype(bf16)
        up_o[rows(i), :] = up
        total = total + col_sum(up.astype(f32))
        if before is not None:
            hid_s[rows(i - 1), :] += nt(before, w_in[...])
        before, act = up, following
    hid_s[rows(count - 1), :] += nt(before, w_in[...])
    vec_o[pl.ds(3 + step, 1), :] = total

    @pl.when(step == last)
    def _():
        width = pack.shape[1]
        sums = [jnp.zeros((1, width), f32)] * 3
        for i in range(count):
            at = rows(i)
            e = hid_s[at, :]
            normed = n1[at, :].astype(f32)
            eg = e * pack[GAIN_ONE : GAIN_ONE + 1]
            grad = rho[at, 0:1] * (eg - mean_of(eg) - normed * mean_of(eg * normed))
            sum_o[at, :] = grad
            att = grad.astype(bf16)
            att_o[at, :] = att
            mix_o[at, :] = nt(att, w_attn[...]).astype(bf16)
            sums = [sums[0] + col_sum(e * normed), sums[1] + col_sum(e), sums[2] + col_sum(att.astype(f32))]
        for i in range(3):
            vec_o[i : i + 1, :] = sums[i]


def feed_backward(low, slope, w_out, w_in, sum_two, n1, rho, ramp, pack, w_attn):
    count, width = n1.shape
    units = slope.shape[1]
    block = pl.BlockSpec((count, CHUNK), lambda j: (0, j))
    return call(
        back_kernel, "feed_backward", (units // CHUNK,),
        [whole(low.shape), block, pl.BlockSpec((CHUNK, width), lambda j: (j, 0)), pl.BlockSpec((width, CHUNK), lambda j: (0, j)),
         whole((count, width)), whole((8, width)), whole(pack.shape), whole((width, width)), whole((count, width)),
         whole((count, 128))],
        [block, whole((16, width))] + [whole((count, width))] * 3,
        [sds((count, units), bf16), sds((16, width), f32), sds((count, width), bf16), sds((count, width), f32),
         sds((count, width), bf16)],
        [pltpu.VMEM((count, width), f32)],
        (2 * count * width * units + count * width * width, 40e6, 0),
        low, slope, w_out, w_in, sum_two, ramp, pack, w_attn, n1, rho)


def attention_back_kernel(
    head_size, part_len, mixers, here, qkv_r, probs_r, mix_r, grad_r, wq, wk, wv, sum_one,
    d_o, vec_o, tok_o, acc_s, w_s, vec_s,
):
    row = pl.program_id(0)
    step = pl.program_id(1)
    last = pl.num_programs(1) - 1
    span = GROUP * head_size
    seq = qkv_r.shape[2]
    qs, keys, values = qkv_r[0, 0, :, :span], qkv_r[0, 0, :, span : 2 * span], qkv_r[0, 0, :, 2 * span :]
    grad = grad_r[...]
    for i, weight in enumerate((wq, wk, wv)):
        w_s[:, i * span : (i + 1) * span] = weight[...]
    prod = grad.T.astype(f32) * mix_r[...].T.astype(f32)
    keys_t = keys.T
    grad_heads = per_head(grad, head_size)
    grad_probs = nt(values, grad_heads)
    parts, dq_t = [], []
    for h in range(GROUP):
        rows = slice(h * head_size, (h + 1) * head_size)
        at = slice(h * seq, (h + 1) * seq)
        part = (probs_r[0, 0, :, at].astype(f32) * (grad_probs[:, at] - col_sum(prod[rows]))).astype(bf16)
        parts.append(part)
        dq_t.append(nn(keys_t[rows], part))
    grad_scores = jnp.concatenate(parts, axis=1)
    dv = nn(probs_r[0, 0], grad_heads).astype(bf16)
    dk = nn(grad_scores, per_head(qs, head_size)).astype(bf16)
    dq = (jnp.concatenate(dq_t, axis=0) * (head_size ** (-0.5))).astype(bf16).T
    all_three = jnp.concatenate([dq, dk, dv], axis=1)
    half = span // 2
    for c in range(2):
        at = slice(c * half, (c + 1) * half)
        d_o[c] = jnp.concatenate([dq[:, at], dk[:, at], dv[:, at]], axis=1)
    vec = jnp.concatenate([col_sum(dq.astype(f32)), col_sum(dv.astype(f32)), jnp.zeros((6, span), f32)], axis=0)

    @pl.when(row == 0)
    def _():
        vec_s[step] = vec

    @pl.when(row > 0)
    def _():
        vec_s[step] += vec

    part = nt(all_three, w_s[...])

    @pl.when(step == 0)
    def _():
        acc_s[...] = sum_one[...] + part

    @pl.when(step > 0)
    def _():
        acc_s[...] += part

    @pl.when(step == last)
    def _():
        steps = vec_s.shape[0]
        for k in range(mixers):
            tok_o[here[0] ^ k, 0] = acc_s[k * part_len : (k + 1) * part_len, :].astype(bf16)
        vec_o[...] = jnp.concatenate([vec_s[g] for g in range(steps)], axis=1)


def attention_backward(here, part_len, qkv, probs, mix, grad_mix, w_qkv, sum_one):
    rows_here, steps, seq, _ = qkv.shape
    total, width = grad_mix.shape
    head_size = width // HEADS
    span = GROUP * head_size
    mixers = seq // part_len
    part = pl.BlockSpec((seq, span), lambda r, g: (r, g))

    def weight(which):
        return pl.BlockSpec((width, span), lambda r, g: (0, which * steps + g))

    return call(
        functools.partial(attention_back_kernel, head_size, part_len, mixers), "attention_backward", (rows_here, steps),
        [SMEM_SPEC, pl.BlockSpec((1, 1, seq, 3 * span), lambda r, g: (r, g, 0, 0)),
         pl.BlockSpec((1, 1, seq, GROUP * seq), lambda r, g: (r, g, 0, 0)), part, part,
         weight(0), weight(1), weight(2), pl.BlockSpec((seq, width), lambda r, g: (r, 0))],
        [pl.BlockSpec((2, seq, 3 * span // 2), lambda r, g: (0, r, g)), whole((8, width)),
         pl.BlockSpec((mixers, 1, part_len, width), lambda r, g: (0, r, 0, 0))],
        [sds((2, total, 3 * width // 2), bf16), sds((8, width), f32), sds((mixers, rows_here, part_len, width), bf16)],
        [pltpu.VMEM((seq, width), f32), pltpu.VMEM((width, 3 * span), bf16), pltpu.VMEM((steps, 8, span), f32)],
        (rows_here * (3 * seq * width * width + 16 * seq * seq * width), 18e6, 0),
        here, qkv, probs, mix, grad_mix, w_qkv, w_qkv, w_qkv, sum_one)


def store_sums(outs, got, rows, read):
    for p in range(8):
        for y in range(2):
            value = read(p, y)
            if got is None:
                outs[0][p * 2 + y, rows, :] = value.astype(bf16)
                continue
            value = (value + got[p * 2 + y, rows, :].astype(f32)).astype(bf16)
            xk, xs, yk, ys = outs
            z2, z1, x = p // 4, p // 2 % 2, p % 2
            if z1 == 0:
                (xk, xs)[x][z2, y, rows, :] = value
            else:
                (yk, ys)[y][z2, x, rows, :] = value


def natural(acc, p, y, dp, upper, columns):
    return acc[pl.ds(pl.multiple_of((p ^ dp) * 2 * UNIT + (y ^ upper) * UNIT, 16), UNIT), columns]


def split_refs(flip, refs):
    return (refs[0], None, refs[1:]) if flip else (refs[1:5], refs[0], refs[5:])


def unit_call(kernel, name, flip, grid, in_specs, rows, step_rows, scratch, work, here, *args, got=None):
    if flip:
        specs, shapes = [pl.BlockSpec((16, step_rows, HALF), lambda j, s: (0, j, 0))], [sds((16, rows, HALF), bf16)]
    else:
        in_specs = in_specs + [pl.BlockSpec((16, step_rows, HALF), lambda j, s: (0, j, 0))]
        args = args + (got,)
        specs = [pl.BlockSpec((2, 2, step_rows, HALF), lambda j, s: (0, 0, j, 0))] * 4
        shapes = [sds((2, 2, rows, HALF), bf16)] * 4
    out = call(kernel, name, (grid,), in_specs, specs, shapes, scratch, work, here, *args, prefetch=1)
    return out[0] if flip else out


def out_units_kernel(flip, here, act, low, *refs):
    outs, got, (acc_s,) = split_refs(flip, refs)
    outs = [outs] if flip else outs
    dp, upper = here[1], (here[0] >> 1) & 1
    count = act.shape[-1]
    acc_s[...] = nn(act[...].reshape(16 * UNIT, count), low[:count])
    at = [pl.multiple_of((upper ^ y) * HALF, 128) for y in range(2)]
    store_sums(outs, got, slice(None), lambda p, y: acc_s[
        pl.ds(pl.multiple_of((p ^ dp) * 2 * UNIT, 16), 2 * UNIT), pl.ds(at[y], HALF)])


def out_units(here, flip, got, act, low):
    width = low.shape[1]
    count = act.shape[-1]
    return unit_call(
        functools.partial(out_units_kernel, flip), "units_out", flip, 2,
        [pl.BlockSpec((8, 1, 2, UNIT, count), lambda j, s: (0, (s[0] & 1) ^ flip, j, 0, 0)), whole(low.shape)],
        4 * UNIT, 2 * UNIT, [pltpu.VMEM((16 * UNIT, width), f32)], (4 * 8 * UNIT * count * width, 5e6, 0),
        here, act, low, got=got)


def in_units_kernel(flip, here, hid, mix, up, att, low, *refs):
    outs, got, (acc_s,) = split_refs(flip, refs)
    outs = [outs] if flip else outs
    step = pl.program_id(0)
    dp = here[1]
    core, upper = (here[0] & 1) ^ flip, (here[0] >> 1) & 1

    @pl.when(step < 2)
    def _():
        acc_s[...] = tn(hid[...], up[...])

    @pl.when(step == 2)
    def _():
        acc_s[:, :HALF] = tn(mix[...], att[...])
        right = low[16:32, :]
        acc_s[:, HALF:] = tn(low[:16, :], jnp.where(core == 0, right[:, :HALF], right[:, HALF:]))

    for u in range(2):
        store_sums(outs, got, slice(u * UNIT, (u + 1) * UNIT), lambda p, y: natural(
            acc_s, p, y, dp, upper, slice(u * HALF, (u + 1) * HALF)))


def in_units(here, flip, got, hid, mix, up, att, low):
    count, width = hid.shape
    return unit_call(
        functools.partial(in_units_kernel, flip), "units_in", flip, 3,
        [whole((count, width))] * 2
        + [pl.BlockSpec((count, 2 * HALF), lambda j, s: (0, ((s[0] & 1) ^ flip) * 2 + jnp.minimum(j, 1))),
           pl.BlockSpec((count, HALF), lambda j, s: (0, (s[0] & 1) ^ flip)),
           pl.BlockSpec((32, width), lambda j, s: (count // 32, 0))],
        6 * UNIT, 2 * UNIT, [pltpu.VMEM((width, 2 * HALF), f32)], (5 * width * HALF * count, 5e6, 0),
        here, hid, mix, up, att, low, got=got)


VEC_ROWS = 16


def qkv_units_kernel(flip, here, tok, grad, back, late, *refs):
    outs, got, (acc_s, tab_s) = split_refs(flip, refs)
    outs = [outs] if flip else outs
    dp, upper = here[1], (here[0] >> 1) & 1
    acc_s[...] = tn(tok[...], grad[0])
    for u in range(3):
        store_sums(outs, got, slice(u * UNIT, (u + 1) * UNIT), lambda p, y: natural(
            acc_s, p, y, dp, upper, slice(u * HALF, (u + 1) * HALF)))
    ramp = back[8:16, :]
    units = jnp.concatenate([back[3 + i : 4 + i, :] for i in range(4)], axis=1)
    short = jnp.concatenate(
        [ramp[0:7], back[0:3, :], late[0:2, :], jnp.zeros((4, ramp.shape[1]), f32)], axis=0)
    share = short.shape[1] // 8
    fill = jnp.zeros((16, 128 - share), f32)
    blank = jnp.zeros((VEC_ROWS - 3, HALF), f32)
    for b in range(8):
        slots = jnp.concatenate([short[:, b * share : (b + 1) * share], fill], axis=1)
        slots = [slots[i : i + 1] for i in range(12)]
        slots += [units[:, b * HALF + i * 128 : b * HALF + (i + 1) * 128] for i in range(3)]
        slots += [ramp[7:8, :128], jnp.where(dp == b, ramp[7:8, 128:256], 0.0), jnp.zeros((1, 128), f32)]
        lines = [jnp.concatenate(slots[i * 3 : i * 3 + 3], axis=1) for i in range(6)]
        for y in range(2):
            tab_s[b, y] = jnp.concatenate(lines[y * 3 : y * 3 + 3] + [blank], axis=0)
    store_sums(outs, got, slice(3 * UNIT, 3 * UNIT + VEC_ROWS), lambda p, y: tab_s[p ^ dp, y ^ upper])


def qkv_units(here, flip, got, tok, grad, back, late):
    count, width = tok.shape
    rows = 3 * UNIT + VEC_ROWS
    wide = 3 * HALF
    return unit_call(
        functools.partial(qkv_units_kernel, flip), "units_qkv", flip, 1,
        [whole((count, width)), pl.BlockSpec((1, count, wide), lambda j, s: ((s[0] & 1) ^ flip, 0, 0)),
         whole((16, width)), whole((8, width))],
        rows, rows, [pltpu.VMEM((width, wide), f32), pltpu.VMEM((8, 2, VEC_ROWS, HALF), f32)],
        (width * wide * count, 5e6, 0), here, tok, grad, back, late, got=got)


def second_kernel(xk, xr, yk, yr, x2k, x2s, y2k, y2s):
    x = xk[0].astype(f32) + xr[0].astype(f32)
    x2k[0] = x[0].astype(bf16)
    x2s[0] = x[1].astype(bf16)
    y = yk[0].astype(f32) + yr[0].astype(f32)
    y2k[0] = y[0].astype(bf16)
    y2s[0] = y[1].astype(bf16)


def add(left, right):
    return (left.astype(f32) + right.astype(f32)).astype(bf16)


def swap(value, axis, bit):
    size = lax.axis_size(axis)
    return lax.ppermute(value, axis, [(i, i ^ bit) for i in range(size)])


def first_swap(stage):
    xk, xs, yk, ys = stage
    return xk, swap(xs, "dp", 1), yk, swap(ys, "mix", 2)


def second_stage(stage, weight):
    rows = stage[0].shape[2]
    block = pl.BlockSpec((1, 2, rows, HALF), lambda z: (z, 0, 0, 0))
    out = pl.BlockSpec((1, rows, HALF), lambda z: (z, 0, 0))
    return call(second_kernel, "stage_two", (2,), [block] * 4, [out] * 4, [sds((2, rows, HALF), bf16)] * 4, [],
                (weight * WORK, 0, 0), *stage)


def second_swap(stage):
    xk, xs, yk, ys = stage
    return xk, swap(xs, "mix", 2), yk, swap(ys, "dp", 1)


def third_stage(stage):
    xk, xr, yk, yr = stage
    return add(xk, xr), add(yk, yr)


def third_kernel(xk, xr, yk, yr, keep, send):
    keep[...] = add(xk[...], xr[...])
    send[...] = add(yk[...], yr[...])


def third_stage_kernel(stage, weight):
    shape = stage[0].shape
    block = pl.BlockSpec((1,) + shape[1:], lambda z: (z, 0, 0))
    return call(third_kernel, "stage_three", (2,), [block] * 4, [block] * 2, [sds(shape, bf16)] * 2, [],
                (weight * WORK, 0, 0), *stage)


def third_swap(stage):
    return stage[0], swap(stage[1], "dp", 2)


def fourth_stage(stage):
    mine, got = stage
    return add(mine[0], got[0]), add(mine[1], got[1])


def fourth_swap(stage):
    return stage[0], swap(stage[1], "dp", 4)


def fifth_stage(stage):
    return add(*stage)


def spread(final):
    other = swap(final, "mix", 2)
    return final, other, swap(final, "mix", 1), swap(other, "mix", 1)


def place_kernel(plan, vec, here, *refs):
    parts, outs = refs[:4], refs[4:]
    core, upper = here[0] & 1, (here[0] >> 1) & 1
    for i, part in enumerate(parts):
        c, y = core ^ (i // 2), upper ^ (i % 2)
        for u, (which, row, row_core, row_y, col_core, col_y, pieces) in enumerate(plan):
            r0 = pl.multiple_of(row + c * row_core + y * row_y, 8)
            at = 0
            for col, size in pieces:
                c0 = pl.multiple_of(col + c * col_core + y * col_y, 128)
                outs[which][pl.ds(r0, UNIT), pl.ds(c0, size)] = part[u * UNIT : (u + 1) * UNIT, at : at + size].astype(f32)
                at += size
    if vec:
        base = len(plan) * UNIT
        mine, other = parts[0][base : base + 8, :].astype(f32), parts[1][base : base + 8, :].astype(f32)
        lines = [jnp.where(upper == 0, mine, other), jnp.where(upper == 0, other, mine)]

        def slot(i):
            return lines[i // 9][i % 9 // 3 : i % 9 // 3 + 1, (i % 3) * 128 : (i % 3 + 1) * 128]

        vec_outs = outs[-13:]
        share = 96
        for i, target in zip((0, 1, 2, 3, 7, 8, 9, 10, 11), vec_outs[:9]):
            target[...] = slot(i)[0, :share]
        vec_outs[9][...] = jnp.concatenate([slot(12), slot(13), slot(14)], axis=1)[0]
        vec_outs[10][...] = jnp.concatenate([slot(4), slot(5), slot(6)], axis=0)[:, :share]
        vec_outs[11][...] = slot(15)[0, :3]
        losses = slot(16)
        pairs, count = vec_outs[12].shape
        lines = [losses[:, r * pairs : (r + 1) * pairs] for r in range(count)]
        lines = jnp.concatenate(lines + [jnp.zeros((8 - count % 8, pairs), f32)] if count % 8 else lines, axis=0)
        vec_outs[12][...] = jnp.concatenate([lines, jnp.zeros((lines.shape[0], 128 - pairs), f32)], axis=1).T[:pairs, :count]


def place_units(here, plan, shapes, parts, vec_shapes=()):
    shape = parts[0].shape
    vm = [whole(s) for s in list(shapes) + list(vec_shapes)]
    return call(
        functools.partial(place_kernel, plan, bool(vec_shapes)), "place_units", (),
        [SMEM_SPEC] + [whole(shape)] * 4, vm, [sds(s, f32) for s in list(shapes) + list(vec_shapes)], [],
        (0.5 * WORK, 0, 0), here, *parts)


def settle_kernel(value, out):
    out[...] = value[...]


def settle(value, weight):
    shape = value.shape
    block = pl.BlockSpec((shape[0] // 2,) + shape[1:], lambda k: (k, 0, 0, 0))
    (out,) = call(settle_kernel, "settle", (2,), [block], [block], [sds(shape, value.dtype)], [], (weight * WORK, 0, 0), value)
    return out.reshape(shape[0] * shape[1], *shape[2:])


def between(value):
    return lax.all_to_all(value, "mix", split_axis=0, concat_axis=0, tiled=True)


def on_device(
    tokens, cotangent, pair_lengths, labels, w_qkv, b_query, b_value, w_attn, b_attn, gain_one, shift_one,
    w_in, b_in, w_out, b_out, gain_two, shift_two, w_pool, b_pool, w_class, b_class,
):
    row_count, part_len, width = tokens.shape
    mixers = lax.axis_size("mix")
    dps = lax.axis_size("dp")
    rows_here = row_count // mixers
    seq = part_len * mixers
    units = w_in.shape[1]
    mix = lax.axis_index("mix").astype(jnp.int32)
    dp = lax.axis_index("dp").astype(jnp.int32)
    here = jnp.stack([mix, dp])
    pairs = pair_lengths.shape[1]
    quick = dps == 8 and mixers == 4 and width == 768 and units == 3072 and seq * rows_here == 1024 and rows_here == 2

    order = sorted(range(1, mixers), reverse=True)

    def exchange(blocks):
        got = {0: blocks[0]}
        for k in order:
            got[k] = swap(blocks[k], "mix", k)
        return [got[k] for k in range(mixers)]

    pack = jnp.concatenate(
        [b_query, b_value, b_attn, gain_one, shift_one, b_out, gain_two, shift_two, b_pool, b_in, b_class,
         jnp.zeros((3 * width - b_class.shape[0],), f32)]).reshape(16, width)

    def tie(first, second):
        return lax.optimization_barrier((first, second))

    cot = cotangent.reshape(mixers, rows_here, part_len, width)
    rows = ()
    def pieces(array, r):
        view = array.reshape(mixers, rows_here, part_len, width)
        return [lax.dynamic_index_in_dim(view[:, r], mix ^ k, 0, keepdims=False) for k in range(mixers)]

    first = pieces(tokens, 0)
    got = exchange(first)
    _, later = tie(first[0], tokens)
    for r in range(rows_here):
        if r + 1 < rows_here:
            blocks = pieces(later, r + 1)
            got, blocks = tie(got, blocks)
            following = exchange(blocks)
        else:
            got, cot = tie(got, cot)
            cots = between(cot)
        rows = forward_row(r, rows_here, here, pair_lengths, got, pack, w_qkv, w_attn, rows)
        if r + 1 < rows_here:
            rows, got = tie(rows, following)
    qkv, probs, tok, mixture, hid, n1, rho1 = rows
    act, slope, outs, vec_ramp, sum_two, low, send = feed_forward(
        part_len, here, pair_lengths, labels, hid, pack, w_in, w_out, w_pool, w_class, cots, quick)
    outs = between(outs)

    if not quick:
        return plain_rest(
            here, part_len, act, slope, outs, low, sum_two, vec_ramp, qkv, probs, tok, mixture, hid, n1, rho1, pack,
            w_qkv, w_attn, w_in, w_out, mix, dp, row_count, units)

    one = first_swap(out_units(here, 0, swap(send, "mix", 1), act.reshape(8, 2, 4, UNIT, rows_here * seq), low))
    _, sum_two = tie(one[0], sum_two)
    grad_up, vec_back, grad_att, sum_one, grad_mix = feed_backward(
        low, slope, w_out, w_in, sum_two, n1, rho1, vec_ramp, pack, w_attn)
    (outs, one), grad_up = tie((outs, one), grad_up)
    args = (hid, mixture, grad_up, grad_att, low)
    send = in_units(here, 1, None, *args)
    _, one = tie(send, one)
    one = second_swap(second_stage(one, 60))
    _, args = tie(one[0], args)
    two = first_swap(in_units(here, 0, swap(send, "mix", 1), *args))
    _, one = tie(two[0], one)
    one = third_swap(third_stage(one))
    _, grad_mix = tie(one[0], grad_mix)

    grad, vec_late, grad_tokens = attention_backward(here, part_len, qkv, probs, mixture, grad_mix, w_qkv, sum_one)
    grad_tokens = between(grad_tokens)
    (one, two), grad = tie((one, two), grad)
    send = qkv_units(here, 1, None, tok, grad, vec_back, vec_late)
    _, two = tie(send, two)
    two = second_swap(second_stage(two, 60))
    _, one = tie(two[0], one)
    one = fourth_swap(fourth_stage(one))
    _, grad = tie(one[0], grad)
    three = first_swap(qkv_units(here, 0, swap(send, "mix", 1), tok, grad, vec_back, vec_late))
    _, outs = tie(three[0], outs)
    output = settle(outs, 1)
    _, one = tie(output, one)
    final = fifth_stage(one)
    _, two = tie(final, two)
    two = third_swap(third_stage_kernel(two, 2))
    (_, grad_tokens), three = tie((two[0], grad_tokens), three)
    three = second_swap(second_stage(three, 60))
    _, two = tie(three[0], two)
    two = fourth_swap(fourth_stage(two))
    _, three = tie(two[0], three)
    three = third_swap(third_stage_kernel(three, 0.2))
    _, grad_tokens = tie(three[0], grad_tokens)
    grad_tokens = settle(grad_tokens, 0.5)
    _, two = tie(grad_tokens, two)
    final = jnp.concatenate([final, fifth_stage(two)], axis=0)
    _, three = tie(final, three)
    three = fourth_swap(fourth_stage(three))
    other = swap(final, "mix", 2)
    final = (final, other, swap(final, "mix", 1), swap(other, "mix", 1))
    other, three = tie(other, three)
    mine = fifth_stage(three)
    other = swap(mine, "mix", 2)
    far = swap(mine, "mix", 1)
    _, final = tie(mine, final)
    grad_w_out, grad_w_in, grad_w_attn, grad_w_pool = place_units(
        here, [(0, j * UNIT, 192, 0, 0, HALF, ((0, HALF),)) for j in range(4)]
        + [(1, 0, 0, UNIT, 4 * HALF, 0, ((j * HALF, HALF),)) for j in range(4)]
        + [(2, 0, 0, UNIT, HALF, 0, ((0, HALF),)), (3, 0, 0, UNIT, HALF, 0, ((0, HALF),))],
        [(384, width), (96, units), (96, width), (96, width)], final)
    _, other = tie(grad_w_in, other)
    three = (mine, other, far, swap(other, "mix", 1))
    share = width // dps
    last = place_units(
        here, [(0, 0, 0, UNIT, 128, 0, tuple((w * width + g * 256, 128) for w in range(3))) for g in range(3)],
        [(96, 3 * width)], three,
        [(share,)] * 9 + [(units // dps,), (w_class.shape[1], share), b_class.shape, (pairs, row_count)])
    (grad_w_qkv, grad_b_out, grad_gain_two, grad_shift_two, grad_b_pool, grad_gain_one, grad_shift_one, grad_b_attn,
     grad_b_query, grad_b_value, grad_b_in, grad_w_class, grad_b_class, pair_loss) = last
    return (
        output, pair_loss.T, grad_tokens, grad_w_qkv, grad_b_query, grad_b_value, grad_w_attn, grad_b_attn,
        grad_gain_one, grad_shift_one, grad_w_in, grad_b_in, grad_w_out, grad_b_out, grad_gain_two, grad_shift_two,
        grad_w_pool, grad_b_pool, grad_w_class.T, grad_b_class,
    )


def plain_rest(
    here, part_len, act, slope, outs, low, sum_two, vec_ramp, qkv, probs, tok, mixture, hid, n1, rho1, pack,
    w_qkv, w_attn, w_in, w_out, mix, dp, row_count, units,
):
    rows_here, _, seq, _ = qkv.shape
    total, width = n1.shape
    dps = lax.axis_size("dp")
    pairs = vec_ramp.shape[0] // rows_here
    grad_up, vec_back, grad_att, sum_one, grad_mix = feed_backward(
        low, slope, w_out, w_in, sum_two, n1, rho1, vec_ramp, pack, w_attn)
    grad, vec_late, grad_tokens = attention_backward(here, part_len, qkv, probs, mixture, grad_mix, w_qkv, sum_one)
    dqkv = grad.reshape(2, total, width // 256, 3, 128).transpose(1, 3, 2, 0, 4).reshape(total, 3 * width)
    output = outs.reshape(row_count, part_len, width)
    grad_tokens = between(grad_tokens).reshape(row_count, part_len, width)
    low, pool = low[:total], low[total:]
    grads = (tn(tok, dqkv), tn(mixture, grad_att), tn(hid, grad_up), nn(act, low), tn(pool[:16], pool[16:]))
    shards = [lax.psum_scatter(g, "dp", scatter_dimension=0, tiled=True) for g in grads]
    shards = [lax.psum(s.astype(bf16), "mix").astype(f32) for s in shards]
    bins = vec_back[3:7]
    vecs = jnp.concatenate([vec_ramp[:7], vec_back[:3], vec_late[:2], bins], axis=0)
    vecs = lax.psum(vecs, ("dp", "mix"))
    class_total = lax.psum(vec_ramp[7, :3], ("dp", "mix"))
    loss = lax.psum(vec_ramp[7, 128 : 128 + row_count * pairs], "mix").reshape(row_count, pairs)
    share = width // dps
    v = lax.dynamic_slice_in_dim(vecs, dp * share, share, axis=1)
    bin_share = lax.dynamic_slice_in_dim(vecs[12:].reshape(-1), dp * (units // dps), units // dps)
    return (
        output, loss, grad_tokens, shards[0], v[10], v[11], shards[1], v[9], v[7], v[8], shards[2], bin_share,
        shards[3], v[0], v[1], v[2], shards[4], v[3], v[4:7].T, class_total,
    )


def solution(mesh):
    wide = P("dp", "mix", None)
    split = P("dp", None)
    in_specs = (wide, wide, split, split) + (P(),) * 17
    out_specs = (
        wide, split, wide,
        split, P("dp"), P("dp"), split, P("dp"), P("dp"), P("dp"),
        split, P("dp"), split, P("dp"), P("dp"), P("dp"),
        split, P("dp"), split, P(),
    )
    return jax.shard_map(on_device, mesh=mesh, in_specs=in_specs, out_specs=out_specs, check_vma=False)
```

```python
import functools

import jax
import jax.numpy as jnp
from jax import lax
from jax.experimental import pallas as pl
from jax.experimental.pallas import tpu as pltpu
from jax.sharding import PartitionSpec as P

HEADS = 12
SCALE = 1.0
WORK = 5.8e8
GROUP = 4
CHUNK = 768
TILE = 256
UNIT = 48
HALF = 384
norm_eps = 1e-06
masked_score = -1000000000.0
inv_root_two = 0.7071067811865476
inv_root_tau = 0.3989422804014327
f32 = jnp.float32
bf16 = jnp.bfloat16
VMEM_LIMIT = 62 * 1024 * 1024
SMEM_SPEC = pl.BlockSpec(memory_space=pltpu.SMEM)
B_QUERY, B_VALUE, B_ATTN, GAIN_ONE, SHIFT_ONE, B_OUT, GAIN_TWO, SHIFT_TWO, B_POOL, B_IN, B_CLASS = 0, 1, 2, 3, 4, 5, 6, 7, 8, 9, 13


def whole(shape):
    return pl.BlockSpec(shape, lambda *_: (0,) * len(shape))


def sds(shape, dtype):
    return jax.ShapeDtypeStruct(shape, dtype)


def nn(left, right):
    return jnp.dot(left, right, preferred_element_type=f32)


def nt(left, right):
    return lax.dot_general(left, right, (((1,), (1,)), ((), ())), preferred_element_type=f32)


def tn(left, right):
    return lax.dot_general(left, right, (((0,), (0,)), ((), ())), preferred_element_type=f32)


def call(kernel, name, grid, in_specs, out_specs, out_shape, scratch, work, *args, prefetch=0, aliases=None):
    common = dict(
        out_shape=out_shape,
        compiler_params=pltpu.CompilerParams(vmem_limit_bytes=VMEM_LIMIT),
        cost_estimate=pl.CostEstimate(flops=int(2 * work[0] * SCALE), bytes_accessed=int(work[1] * SCALE), transcendentals=0),
        name=name,
        input_output_aliases=aliases or {},
    )
    if prefetch:
        spec = pltpu.PrefetchScalarGridSpec(
            num_scalar_prefetch=prefetch, grid=grid, in_specs=in_specs, out_specs=out_specs, scratch_shapes=scratch)
        return pl.pallas_call(kernel, grid_spec=spec, **common)(*args)
    return pl.pallas_call(
        kernel, grid=grid, in_specs=in_specs, out_specs=out_specs, scratch_shapes=scratch, **common)(*args)


def after(value, *earlier):
    return lax.optimization_barrier((value,) + earlier)[0]


def mean_of(values):
    return jnp.mean(values, axis=-1, keepdims=True)


def col_sum(values):
    return jnp.sum(values, axis=0, keepdims=True)


def head_only(values, head, size):
    lane = lax.broadcasted_iota(jnp.int32, (1, values.shape[1]), 1) // size
    return jnp.where(lane == head, values, jnp.zeros((), values.dtype))


def per_head(values, size):
    return jnp.concatenate([head_only(values, h, size) for h in range(GROUP)], axis=0)


def segments(places, lengths, row):
    total = jnp.int32(0)
    seg = jnp.zeros(places.shape, jnp.int32)
    for k in range(lengths.shape[0]):
        total = total + lengths[k, row]
        seg = seg + (places >= total).astype(jnp.int32)
    return seg


def forward_kernel(row, rows_here, part_len, mixers, head_size, here, lengths, *refs):
    pieces, refs = refs[:mixers], refs[mixers:]
    pack, packq, packv, wq, wk, wv, wa = refs[:7]
    (qkv_o, probs_o, tok_o, mix_o, hid_o, n1_o, rho_o,
     tok_s, mix_s, bias_s, w_s) = refs[-11:]
    step = pl.program_id(0)
    seq = part_len * mixers
    shift = part_len.bit_length() - 1
    span = GROUP * head_size

    @pl.when(step == 0)
    def _():
        for i, piece in enumerate(pieces):
            tok_s[i * part_len : (i + 1) * part_len, :] = piece[...]
        mine = here[0]
        down = lax.broadcasted_iota(jnp.int32, (seq, 1), 0)
        across = lax.broadcasted_iota(jnp.int32, (1, seq), 1)

        def place(i):
            return (((i >> shift) ^ mine) << shift) + (i & (part_len - 1))

        number = mine * rows_here + row
        same = segments(place(down), lengths, number) == segments(place(across), lengths, number)
        bias_s[...] = jnp.where(same, 0.0, masked_score)

    for i, weight in enumerate((wq, wk, wv)):
        w_s[:, i * span : (i + 1) * span] = weight[...]
    qkv = nn(tok_s[...], w_s[...])
    qs = (qkv[:, :span] + packq[B_QUERY : B_QUERY + 1]).astype(bf16) * bf16(head_size ** (-0.5))
    keys = qkv[:, span : 2 * span].astype(bf16)
    values = (qkv[:, 2 * span :] + packv[B_VALUE : B_VALUE + 1]).astype(bf16)
    qkv_o[0, 0, :, :span] = qs
    qkv_o[0, 0, :, span : 2 * span] = keys
    qkv_o[0, 0, :, 2 * span :] = values
    scores = nt(keys, per_head(qs, head_size))
    values_t = values.T
    mixed = []
    for h in range(GROUP):
        at = slice(h * seq, (h + 1) * seq)
        part = scores[:, at] + bias_s[...]
        expo = jnp.exp(part - jnp.max(part, axis=0, keepdims=True))
        probs = (expo * (1.0 / col_sum(expo))).astype(bf16)
        probs_o[0, 0, :, at] = probs
        mixed.append(nn(values_t[h * head_size : (h + 1) * head_size], probs))
    mixed = jnp.concatenate(mixed, axis=0).astype(bf16).T
    here_columns = pl.ds(pl.multiple_of(step * span, 128), span)
    mix_s[:, here_columns] = mixed
    mix_o[...] = mixed
    tok_o[...] = tok_s[:, here_columns]

    @pl.when(step == pl.num_programs(0) - 1)
    def _():
        full = tok_s[...].astype(f32) + (nn(mix_s[...], wa[...]) + pack[B_ATTN : B_ATTN + 1])
        centre = full - mean_of(full)
        rho = lax.rsqrt(mean_of(centre * centre) + norm_eps)
        normed = centre * rho
        hidden = normed * pack[GAIN_ONE : GAIN_ONE + 1] + pack[SHIFT_ONE : SHIFT_ONE + 1]
        hid_o[...] = hidden.astype(bf16)
        n1_o[...] = normed.astype(bf16)
        rho_o[...] = jnp.broadcast_to(rho, rho_o.shape)


def forward_row(row, rows_here, here, lengths, pieces, pack, w_qkv, w_attn, earlier, weight_us):
    part_len, width = pieces[0].shape
    mixers = len(pieces)
    seq = part_len * mixers
    head_size = width // HEADS
    span = GROUP * head_size
    steps = width // span

    def weight(which):
        return pl.BlockSpec((width, span), lambda g: (0, which * steps + g))

    rows = pack.shape[0]
    column = pl.BlockSpec((rows, span), lambda g: (0, g))
    part = pl.BlockSpec((seq, span), lambda g: (row, g))
    wide = pl.BlockSpec((seq, width), lambda g: (row, 0))
    total = rows_here * seq
    specs = [SMEM_SPEC, SMEM_SPEC] + [whole((part_len, width))] * mixers
    specs += [whole((rows, width)), column, column, weight(0), weight(1), weight(2), whole((width, width))]
    return call(
        functools.partial(forward_kernel, row, rows_here, part_len, mixers, head_size), "forward_row", (steps,),
        specs + [pl.BlockSpec(memory_space=pl.ANY)] * len(earlier),
        [pl.BlockSpec((1, 1, seq, 3 * span), lambda g: (row, g, 0, 0)),
         pl.BlockSpec((1, 1, seq, GROUP * seq), lambda g: (row, g, 0, 0)),
         part, part, wide, wide, pl.BlockSpec((seq, 128), lambda g: (row, 0))],
        [sds((rows_here, steps, seq, 3 * span), bf16), sds((rows_here, steps, seq, GROUP * seq), bf16)]
        + [sds((total, width), bf16)] * 4 + [sds((total, 128), f32)],
        [pltpu.VMEM((seq, width), bf16), pltpu.VMEM((seq, width), bf16), pltpu.VMEM((seq, seq), f32),
         pltpu.VMEM((width, 3 * span), bf16)],
        (weight_us * WORK, 0, 0),
        here, lengths, *pieces, pack, pack, pack, w_qkv, w_qkv, w_qkv, w_attn, *earlier,
        aliases={len(specs) + i: i for i in range(len(earlier))})


def start_spots(here, lengths, r, rows_here, part_len, pairs, seq):
    shift = part_len.bit_length() - 1
    spots = []
    start = jnp.int32(0)
    for k in range(pairs):
        spots.append(r * seq + (((start >> shift) ^ here[0]) << shift) + (start & (part_len - 1)))
        start = start + lengths[k, here[0] * rows_here + r]
    return spots


def feed_kernel(rows_here, part_len, pairs, mixers, send, here, lengths, labels, *refs):
    hid, pack, w_in, w_out, w_pool, w_class, cots = refs[:7]
    act_o, slope_o, out_o, vec_o, sum_o, low_o, send_o = refs[7:14]
    feed_s, normed_s, rho_s, act_s, acc_s = refs[14:]
    step = pl.program_id(0)
    last = pl.num_programs(0) - 1
    tokens, width = hid.shape
    seq = part_len * mixers
    count = tokens // TILE

    @pl.when(step == 0)
    def _():
        feed_s[...] = hid[...].astype(f32) + pack[B_OUT : B_OUT + 1]

    bias = pack[pl.ds(B_IN + step, 1), :]

    def rows(i):
        return slice(i * TILE, (i + 1) * TILE)

    up = nn(hid[rows(0), :], w_in[...])
    before = None
    for i in range(count):
        following = nn(hid[rows(i + 1), :], w_in[...]) if i + 1 < count else None
        up = up + bias
        half = 0.5 * (1.0 + lax.erf(up * inv_root_two))
        act = (up * half).astype(bf16)
        slope_o[rows(i), :] = (half + up * jnp.exp(-0.5 * up * up) * inv_root_tau).astype(bf16)
        turned = act.T
        act_o[:, rows(i)] = turned
        if send:
            blocks = CHUNK // (8 * UNIT)
            act_s[pl.ds(step * blocks, blocks), :, :, :, rows(i)] = turned.reshape(blocks, 2, 2, 2 * UNIT, TILE)
        if before is not None:
            feed_s[rows(i - 1), :] += nn(before, w_out[...])
        before, up = act, following
    feed_s[rows(count - 1), :] += nn(before, w_out[...])

    @pl.when(step == last)
    def _():
        gain = pack[GAIN_TWO : GAIN_TWO + 1]
        for r in range(rows_here):
            for k in range(mixers):
                at = slice(r * seq + k * part_len, r * seq + (k + 1) * part_len)
                full = feed_s[at, :]
                centre = full - mean_of(full)
                rho = lax.rsqrt(mean_of(centre * centre) + norm_eps)
                normed = centre * rho
                out = normed * gain + pack[SHIFT_TWO : SHIFT_TWO + 1]
                feed_s[at, :] = out
                out_o[here[0] ^ k, r] = out.astype(bf16)
                normed_s[at, :] = normed
                rho_s[at, :] = jnp.broadcast_to(rho, (part_len, 128))
        spots = []
        for r in range(rows_here):
            spots += start_spots(here, lengths, r, rows_here, part_len, pairs, seq)
        firsts = jnp.concatenate([feed_s[pl.ds(spot, 1), :] for spot in spots], axis=0)
        sums = [jnp.zeros((1, width), f32)] * 2

        def backward(i, sums):
            r, k = i // mixers, i % mixers
            at = slice(i * part_len, (i + 1) * part_len)
            e = cots[here[0] ^ k, r].astype(f32)
            normed = normed_s[at, :]
            eg = e * gain
            sum_o[at, :] = rho_s[at, 0:1] * (eg - mean_of(eg) - normed * mean_of(eg * normed))
            return [sums[0] + col_sum(e * normed), sums[1] + col_sum(e)]

        tiles = rows_here * mixers
        pool = w_pool[...]
        pool_high = pool.astype(bf16)
        pool_rest = (pool - pool_high.astype(f32)).astype(bf16)
        first_high = firsts.astype(bf16)
        first_rest = (firsts - first_high.astype(f32)).astype(bf16)
        pre = nn(jnp.concatenate([first_high, first_rest], axis=0), pool_high)
        pre = pre[: firsts.shape[0]] + pre[firsts.shape[0] :] + nn(first_high, pool_rest)
        for i in range(tiles // 2):
            sums = backward(i, sums)
        pooled = jnp.tanh(pre + pack[B_POOL : B_POOL + 1])
        classes = w_class.shape[0]
        here_pairs = rows_here * pairs
        class_t = w_class[...]
        lane = lax.broadcasted_iota(jnp.int32, (here_pairs, 128), 1)
        logits = jnp.full((here_pairs, 128), -jnp.inf, f32)
        for c in range(classes):
            logits = jnp.where(lane == c, jnp.sum(pooled * class_t[c : c + 1], axis=1, keepdims=True), logits)
        logits = logits + pack[B_CLASS : B_CLASS + 1, :128]
        top = jnp.max(logits, axis=-1, keepdims=True)
        expo = jnp.exp(logits - top)
        total = jnp.sum(expo, axis=-1, keepdims=True)
        log_total = top + jnp.log(total)
        sub = lax.broadcasted_iota(jnp.int32, (here_pairs, 128), 0)
        label = jnp.zeros((here_pairs, 128), jnp.int32)
        for r in range(rows_here):
            for k in range(pairs):
                label = jnp.where(sub == r * pairs + k, labels[k, here[0] * rows_here + r], label)
        chosen = lane == label
        loss = log_total - jnp.sum(jnp.where(chosen, logits, 0.0), axis=-1, keepdims=True)
        grad_logits = expo / total - chosen.astype(f32)
        grad_pooled = jnp.zeros((here_pairs, width), f32)
        for c in range(classes):
            grad_pooled = grad_pooled + grad_logits[:, c : c + 1] * class_t[c : c + 1]
        grad_pre = grad_pooled * (1.0 - pooled * pooled)
        grad_firsts = nt(grad_pre.astype(bf16), pool_high)
        for i in range(tiles // 2, tiles):
            sums = backward(i, sums)
        normed = jnp.concatenate([normed_s[pl.ds(spot, 1), :] for spot in spots], axis=0)
        rho = jnp.concatenate([rho_s[pl.ds(spot, 1), :] for spot in spots], axis=0)[:, 0:1]
        eg = grad_firsts * gain
        more = rho * (eg - mean_of(eg) - normed * mean_of(eg * normed))
        for i, spot in enumerate(spots):
            sum_o[pl.ds(spot, 1), :] = sum_o[pl.ds(spot, 1), :] + more[i : i + 1, :]
        vec_o[1:2, :] = sums[0] + col_sum(grad_firsts * normed)
        vec_o[2:3, :] = sums[1] + col_sum(grad_firsts)
        vec_o[3:4, :] = col_sum(grad_pre)
        for c in range(classes):
            vec_o[4 + c : 5 + c, :] = col_sum(pooled * grad_logits[:, c : c + 1])
        spread_loss = jnp.where(lane == here[0] * here_pairs + sub, loss, 0.0)
        vec_o[7:8, :] = jnp.concatenate(
            [col_sum(grad_logits), col_sum(spread_loss), jnp.zeros((1, width - 256), f32)], axis=1)
        none = jnp.zeros((16 - here_pairs, width), f32)
        low_o[tokens : tokens + 16, :] = jnp.concatenate([firsts, none], axis=0).astype(bf16)
        low_o[tokens + 16 :, :] = jnp.concatenate([grad_pre, none], axis=0).astype(bf16)
        bias_sum = jnp.zeros((1, width), f32)
        for i in range(count):
            low = sum_o[rows(i), :].astype(bf16)
            low_o[rows(i), :] = low
            bias_sum = bias_sum + col_sum(low.astype(f32))
        vec_o[0:1, :] = bias_sum
        if send:
            dp, upper = here[1], (here[0] >> 1) & 1
            other = 1 - (here[0] & 1)
            for j in range(2):
                acc_s[...] = nn(act_s[:, other, j].reshape(16 * UNIT, tokens), low_o[:tokens, :])
                store_sums([send_o], None, slice(j * 2 * UNIT, (j + 1) * 2 * UNIT), lambda p, y: acc_s[
                    pl.ds(pl.multiple_of((p ^ dp) * 2 * UNIT, 16), 2 * UNIT),
                    pl.ds(pl.multiple_of((upper ^ y) * HALF, 128), HALF)])
        else:
            send_o[...] = jnp.zeros(send_o.shape, bf16)


def feed_forward(part_len, here, lengths, labels, hid, pack, w_in, w_out, w_pool, w_class, cots, send):
    mixers, rows_here = cots.shape[:2]
    tokens, width = hid.shape
    pairs = lengths.shape[0]
    units = w_in.shape[1]
    steps = units // CHUNK
    sent = (16, 4 * UNIT, HALF) if send else (16, 128)
    act_shape = (units // (8 * UNIT), 2, 2, 2 * UNIT, tokens) if send else (8, 128)
    acc_shape = (16 * UNIT, width) if send else (8, 128)
    return call(
        functools.partial(feed_kernel, rows_here, part_len, pairs, mixers, send), "feed_forward", (steps,),
        [SMEM_SPEC] * 3
        + [whole(hid.shape), whole(pack.shape), pl.BlockSpec((width, CHUNK), lambda c: (0, c)),
           pl.BlockSpec((CHUNK, width), lambda c: (c, 0)), whole(w_pool.shape), whole(w_class.shape), whole(cots.shape)],
        [pl.BlockSpec((CHUNK, tokens), lambda c: (c, 0)), pl.BlockSpec((tokens, CHUNK), lambda c: (0, c)),
         whole(cots.shape), whole((8, width)), whole((tokens, width)), whole((tokens + 32, width)), whole(sent)],
        [sds((units, tokens), bf16), sds((tokens, units), bf16), sds(cots.shape, bf16), sds((8, width), f32),
         sds((tokens, width), f32), sds((tokens + 32, width), bf16), sds(sent, bf16)],
        [pltpu.VMEM((tokens, width), f32), pltpu.VMEM((tokens, width), f32), pltpu.VMEM((tokens, 128), f32),
         pltpu.VMEM(act_shape, bf16), pltpu.VMEM(acc_shape, f32)],
        (2 * tokens * width * units, 35e6, 0),
        here, lengths, labels, hid, pack, w_in, w_out, w_pool, w_class, cots)


def back_kernel(low, slope, w_out, w_in, sum_two, ramp, pack, w_attn, n1, rho, up_o, vec_o, att_o, sum_o, mix_o, hid_s):
    step = pl.program_id(0)
    last = pl.num_programs(0) - 1
    count = slope.shape[0] // TILE

    def rows(i):
        return slice(i * TILE, (i + 1) * TILE)

    @pl.when(step == 0)
    def _():
        hid_s[...] = sum_two[...]
        vec_o[7:8, :] = jnp.zeros((1, vec_o.shape[1]), f32)
        vec_o[8:16, :] = ramp[...]

    total = jnp.zeros((1, slope.shape[1]), f32)
    act = nt(low[rows(0), :], w_out[...])
    before = None
    for i in range(count):
        following = nt(low[rows(i + 1), :], w_out[...]) if i + 1 < count else None
        up = (act * slope[rows(i), :].astype(f32)).astype(bf16)
        up_o[rows(i), :] = up
        total = total + col_sum(up.astype(f32))
        if before is not None:
            hid_s[rows(i - 1), :] += nt(before, w_in[...])
        before, act = up, following
    hid_s[rows(count - 1), :] += nt(before, w_in[...])
    vec_o[pl.ds(3 + step, 1), :] = total

    @pl.when(step == last)
    def _():
        width = pack.shape[1]
        sums = [jnp.zeros((1, width), f32)] * 3
        for i in range(count):
            at = rows(i)
            e = hid_s[at, :]
            normed = n1[at, :].astype(f32)
            eg = e * pack[GAIN_ONE : GAIN_ONE + 1]
            grad = rho[at, 0:1] * (eg - mean_of(eg) - normed * mean_of(eg * normed))
            sum_o[at, :] = grad
            att = grad.astype(bf16)
            att_o[at, :] = att
            mix_o[at, :] = nt(att, w_attn[...]).astype(bf16)
            sums = [sums[0] + col_sum(e * normed), sums[1] + col_sum(e), sums[2] + col_sum(att.astype(f32))]
        for i in range(3):
            vec_o[i : i + 1, :] = sums[i]


def feed_backward(low, slope, w_out, w_in, sum_two, n1, rho, ramp, pack, w_attn):
    count, width = n1.shape
    units = slope.shape[1]
    block = pl.BlockSpec((count, CHUNK), lambda j: (0, j))
    return call(
        back_kernel, "feed_backward", (units // CHUNK,),
        [whole(low.shape), block, pl.BlockSpec((CHUNK, width), lambda j: (j, 0)), pl.BlockSpec((width, CHUNK), lambda j: (0, j)),
         whole((count, width)), whole((8, width)), whole(pack.shape), whole((width, width)), whole((count, width)),
         whole((count, 128))],
        [block, whole((16, width))] + [whole((count, width))] * 3,
        [sds((count, units), bf16), sds((16, width), f32), sds((count, width), bf16), sds((count, width), f32),
         sds((count, width), bf16)],
        [pltpu.VMEM((count, width), f32)],
        (2 * count * width * units + count * width * width, 40e6, 0),
        low, slope, w_out, w_in, sum_two, ramp, pack, w_attn, n1, rho)


def attention_back_kernel(
    head_size, part_len, mixers, here, qkv_r, probs_r, mix_r, grad_r, wq, wk, wv, sum_one,
    d_o, vec_o, tok_o, acc_s, w_s, vec_s,
):
    row = pl.program_id(0)
    step = pl.program_id(1)
    last = pl.num_programs(1) - 1
    span = GROUP * head_size
    seq = qkv_r.shape[2]
    qs, keys, values = qkv_r[0, 0, :, :span], qkv_r[0, 0, :, span : 2 * span], qkv_r[0, 0, :, 2 * span :]
    grad = grad_r[...]
    for i, weight in enumerate((wq, wk, wv)):
        w_s[:, i * span : (i + 1) * span] = weight[...]
    prod = grad.T.astype(f32) * mix_r[...].T.astype(f32)
    keys_t = keys.T
    grad_heads = per_head(grad, head_size)
    grad_probs = nt(values, grad_heads)
    parts, dq_t = [], []
    for h in range(GROUP):
        rows = slice(h * head_size, (h + 1) * head_size)
        at = slice(h * seq, (h + 1) * seq)
        part = (probs_r[0, 0, :, at].astype(f32) * (grad_probs[:, at] - col_sum(prod[rows]))).astype(bf16)
        parts.append(part)
        dq_t.append(nn(keys_t[rows], part))
    grad_scores = jnp.concatenate(parts, axis=1)
    dv = nn(probs_r[0, 0], grad_heads).astype(bf16)
    dk = nn(grad_scores, per_head(qs, head_size)).astype(bf16)
    dq = (jnp.concatenate(dq_t, axis=0) * (head_size ** (-0.5))).astype(bf16).T
    all_three = jnp.concatenate([dq, dk, dv], axis=1)
    half = span // 2
    for c in range(2):
        at = slice(c * half, (c + 1) * half)
        d_o[c] = jnp.concatenate([dq[:, at], dk[:, at], dv[:, at]], axis=1)
    vec = jnp.concatenate([col_sum(dq.astype(f32)), col_sum(dv.astype(f32)), jnp.zeros((6, span), f32)], axis=0)

    @pl.when(row == 0)
    def _():
        vec_s[step] = vec

    @pl.when(row > 0)
    def _():
        vec_s[step] += vec

    part = nt(all_three, w_s[...])

    @pl.when(step == 0)
    def _():
        acc_s[...] = sum_one[...] + part

    @pl.when(step > 0)
    def _():
        acc_s[...] += part

    @pl.when(step == last)
    def _():
        steps = vec_s.shape[0]
        for k in range(mixers):
            tok_o[here[0] ^ k, 0] = acc_s[k * part_len : (k + 1) * part_len, :].astype(bf16)
        vec_o[...] = jnp.concatenate([vec_s[g] for g in range(steps)], axis=1)


def attention_backward(here, part_len, qkv, probs, mix, grad_mix, w_qkv, sum_one):
    rows_here, steps, seq, _ = qkv.shape
    total, width = grad_mix.shape
    head_size = width // HEADS
    span = GROUP * head_size
    mixers = seq // part_len
    part = pl.BlockSpec((seq, span), lambda r, g: (r, g))

    def weight(which):
        return pl.BlockSpec((width, span), lambda r, g: (0, which * steps + g))

    return call(
        functools.partial(attention_back_kernel, head_size, part_len, mixers), "attention_backward", (rows_here, steps),
        [SMEM_SPEC, pl.BlockSpec((1, 1, seq, 3 * span), lambda r, g: (r, g, 0, 0)),
         pl.BlockSpec((1, 1, seq, GROUP * seq), lambda r, g: (r, g, 0, 0)), part, part,
         weight(0), weight(1), weight(2), pl.BlockSpec((seq, width), lambda r, g: (r, 0))],
        [pl.BlockSpec((2, seq, 3 * span // 2), lambda r, g: (0, r, g)), whole((8, width)),
         pl.BlockSpec((mixers, 1, part_len, width), lambda r, g: (0, r, 0, 0))],
        [sds((2, total, 3 * width // 2), bf16), sds((8, width), f32), sds((mixers, rows_here, part_len, width), bf16)],
        [pltpu.VMEM((seq, width), f32), pltpu.VMEM((width, 3 * span), bf16), pltpu.VMEM((steps, 8, span), f32)],
        (rows_here * (3 * seq * width * width + 16 * seq * seq * width), 18e6, 0),
        here, qkv, probs, mix, grad_mix, w_qkv, w_qkv, w_qkv, sum_one)


def store_sums(outs, got, rows, read):
    for p in range(8):
        for y in range(2):
            value = read(p, y)
            if got is None:
                outs[0][p * 2 + y, rows, :] = value.astype(bf16)
                continue
            value = (value + got[p * 2 + y, rows, :].astype(f32)).astype(bf16)
            xk, xs, yk, ys = outs
            z2, z1, x = p // 4, p // 2 % 2, p % 2
            if z1 == 0:
                (xk, xs)[x][z2, y, rows, :] = value
            else:
                (yk, ys)[y][z2, x, rows, :] = value


def natural(acc, p, y, dp, upper, columns):
    return acc[pl.ds(pl.multiple_of((p ^ dp) * 2 * UNIT + (y ^ upper) * UNIT, 16), UNIT), columns]


def split_refs(flip, refs):
    return (refs[0], None, refs[1:]) if flip else (refs[1:5], refs[0], refs[5:])


def unit_call(kernel, name, flip, grid, in_specs, rows, step_rows, scratch, work, here, *args, got=None):
    if flip:
        specs, shapes = [pl.BlockSpec((16, step_rows, HALF), lambda j, s: (0, j, 0))], [sds((16, rows, HALF), bf16)]
    else:
        in_specs = in_specs + [pl.BlockSpec((16, step_rows, HALF), lambda j, s: (0, j, 0))]
        args = args + (got,)
        specs = [pl.BlockSpec((2, 2, step_rows, HALF), lambda j, s: (0, 0, j, 0))] * 4
        shapes = [sds((2, 2, rows, HALF), bf16)] * 4
    out = call(kernel, name, (grid,), in_specs, specs, shapes, scratch, work, here, *args, prefetch=1)
    return out[0] if flip else out


def out_units_kernel(flip, here, act, low, *refs):
    outs, got, (acc_s,) = split_refs(flip, refs)
    outs = [outs] if flip else outs
    dp, upper = here[1], (here[0] >> 1) & 1
    count = act.shape[-1]
    acc_s[...] = nn(act[...].reshape(16 * UNIT, count), low[:count])
    at = [pl.multiple_of((upper ^ y) * HALF, 128) for y in range(2)]
    store_sums(outs, got, slice(None), lambda p, y: acc_s[
        pl.ds(pl.multiple_of((p ^ dp) * 2 * UNIT, 16), 2 * UNIT), pl.ds(at[y], HALF)])


def out_units(here, flip, got, act, low):
    width = low.shape[1]
    count = act.shape[-1]
    return unit_call(
        functools.partial(out_units_kernel, flip), "units_out", flip, 2,
        [pl.BlockSpec((8, 1, 2, UNIT, count), lambda j, s: (0, (s[0] & 1) ^ flip, j, 0, 0)), whole(low.shape)],
        4 * UNIT, 2 * UNIT, [pltpu.VMEM((16 * UNIT, width), f32)], (4 * 8 * UNIT * count * width, 5e6, 0),
        here, act, low, got=got)


def in_units_kernel(flip, here, hid, mix, up, att, low, *refs):
    outs, got, (acc_s,) = split_refs(flip, refs)
    outs = [outs] if flip else outs
    step = pl.program_id(0)
    dp = here[1]
    core, upper = (here[0] & 1) ^ flip, (here[0] >> 1) & 1

    @pl.when(step < 2)
    def _():
        acc_s[...] = tn(hid[...], up[...])

    @pl.when(step == 2)
    def _():
        acc_s[:, :HALF] = tn(mix[...], att[...])
        right = low[16:32, :]
        acc_s[:, HALF:] = tn(low[:16, :], jnp.where(core == 0, right[:, :HALF], right[:, HALF:]))

    for u in range(2):
        store_sums(outs, got, slice(u * UNIT, (u + 1) * UNIT), lambda p, y: natural(
            acc_s, p, y, dp, upper, slice(u * HALF, (u + 1) * HALF)))


def in_units(here, flip, got, hid, mix, up, att, low):
    count, width = hid.shape
    return unit_call(
        functools.partial(in_units_kernel, flip), "units_in", flip, 3,
        [whole((count, width))] * 2
        + [pl.BlockSpec((count, 2 * HALF), lambda j, s: (0, ((s[0] & 1) ^ flip) * 2 + jnp.minimum(j, 1))),
           pl.BlockSpec((count, HALF), lambda j, s: (0, (s[0] & 1) ^ flip)),
           pl.BlockSpec((32, width), lambda j, s: (count // 32, 0))],
        6 * UNIT, 2 * UNIT, [pltpu.VMEM((width, 2 * HALF), f32)], (5 * width * HALF * count, 5e6, 0),
        here, hid, mix, up, att, low, got=got)


VEC_ROWS = 16


def qkv_units_kernel(flip, here, tok, grad, back, late, *refs):
    outs, got, (acc_s, tab_s) = split_refs(flip, refs)
    outs = [outs] if flip else outs
    dp, upper = here[1], (here[0] >> 1) & 1
    acc_s[...] = tn(tok[...], grad[0])
    for u in range(3):
        store_sums(outs, got, slice(u * UNIT, (u + 1) * UNIT), lambda p, y: natural(
            acc_s, p, y, dp, upper, slice(u * HALF, (u + 1) * HALF)))
    ramp = back[8:16, :]
    units = jnp.concatenate([back[3 + i : 4 + i, :] for i in range(4)], axis=1)
    short = jnp.concatenate(
        [ramp[0:7], back[0:3, :], late[0:2, :], jnp.zeros((4, ramp.shape[1]), f32)], axis=0)
    share = short.shape[1] // 8
    fill = jnp.zeros((16, 128 - share), f32)
    blank = jnp.zeros((VEC_ROWS - 3, HALF), f32)
    for b in range(8):
        slots = jnp.concatenate([short[:, b * share : (b + 1) * share], fill], axis=1)
        slots = [slots[i : i + 1] for i in range(12)]
        slots += [units[:, b * HALF + i * 128 : b * HALF + (i + 1) * 128] for i in range(3)]
        slots += [ramp[7:8, :128], jnp.where(dp == b, ramp[7:8, 128:256], 0.0), jnp.zeros((1, 128), f32)]
        lines = [jnp.concatenate(slots[i * 3 : i * 3 + 3], axis=1) for i in range(6)]
        for y in range(2):
            tab_s[b, y] = jnp.concatenate(lines[y * 3 : y * 3 + 3] + [blank], axis=0)
    store_sums(outs, got, slice(3 * UNIT, 3 * UNIT + VEC_ROWS), lambda p, y: tab_s[p ^ dp, y ^ upper])


def qkv_units(here, flip, got, tok, grad, back, late):
    count, width = tok.shape
    rows = 3 * UNIT + VEC_ROWS
    wide = 3 * HALF
    return unit_call(
        functools.partial(qkv_units_kernel, flip), "units_qkv", flip, 1,
        [whole((count, width)), pl.BlockSpec((1, count, wide), lambda j, s: ((s[0] & 1) ^ flip, 0, 0)),
         whole((16, width)), whole((8, width))],
        rows, rows, [pltpu.VMEM((width, wide), f32), pltpu.VMEM((8, 2, VEC_ROWS, HALF), f32)],
        (width * wide * count, 5e6, 0), here, tok, grad, back, late, got=got)


def second_kernel(xk, xr, yk, yr, x2k, x2s, y2k, y2s):
    x = xk[0].astype(f32) + xr[0].astype(f32)
    x2k[0] = x[0].astype(bf16)
    x2s[0] = x[1].astype(bf16)
    y = yk[0].astype(f32) + yr[0].astype(f32)
    y2k[0] = y[0].astype(bf16)
    y2s[0] = y[1].astype(bf16)


def add(left, right):
    return (left.astype(f32) + right.astype(f32)).astype(bf16)


def swap(value, axis, bit):
    size = lax.axis_size(axis)
    return lax.ppermute(value, axis, [(i, i ^ bit) for i in range(size)])


def first_swap(stage):
    xk, xs, yk, ys = stage
    return xk, swap(xs, "dp", 1), yk, swap(ys, "mix", 2)


def second_stage(stage, weight):
    rows = stage[0].shape[2]
    block = pl.BlockSpec((1, 2, rows, HALF), lambda z: (z, 0, 0, 0))
    out = pl.BlockSpec((1, rows, HALF), lambda z: (z, 0, 0))
    return call(second_kernel, "stage_two", (2,), [block] * 4, [out] * 4, [sds((2, rows, HALF), bf16)] * 4, [],
                (weight * WORK, 0, 0), *stage)


def second_swap(stage):
    xk, xs, yk, ys = stage
    return xk, swap(xs, "mix", 2), yk, swap(ys, "dp", 1)


def third_stage(stage):
    xk, xr, yk, yr = stage
    return add(xk, xr), add(yk, yr)


def third_kernel(xk, xr, yk, yr, keep, send):
    keep[...] = add(xk[...], xr[...])
    send[...] = add(yk[...], yr[...])


def third_stage_kernel(stage, weight):
    shape = stage[0].shape
    block = pl.BlockSpec((1,) + shape[1:], lambda z: (z, 0, 0))
    return call(third_kernel, "stage_three", (2,), [block] * 4, [block] * 2, [sds(shape, bf16)] * 2, [],
                (weight * WORK, 0, 0), *stage)


def third_swap(stage):
    return stage[0], swap(stage[1], "dp", 2)


def fourth_stage(stage):
    mine, got = stage
    return add(mine[0], got[0]), add(mine[1], got[1])


def fourth_swap(stage):
    return stage[0], swap(stage[1], "dp", 4)


def fifth_stage(stage):
    return add(*stage)


def spread(final):
    other = swap(final, "mix", 2)
    return final, other, swap(final, "mix", 1), swap(other, "mix", 1)


def place_kernel(plan, vec, here, *refs):
    parts, outs = refs[:4], refs[4:]
    core, upper = here[0] & 1, (here[0] >> 1) & 1
    for i, part in enumerate(parts):
        c, y = core ^ (i // 2), upper ^ (i % 2)
        for u, (which, row, row_core, row_y, col_core, col_y, pieces) in enumerate(plan):
            r0 = pl.multiple_of(row + c * row_core + y * row_y, 8)
            at = 0
            for col, size in pieces:
                c0 = pl.multiple_of(col + c * col_core + y * col_y, 128)
                outs[which][pl.ds(r0, UNIT), pl.ds(c0, size)] = part[u * UNIT : (u + 1) * UNIT, at : at + size].astype(f32)
                at += size
    if vec:
        base = len(plan) * UNIT
        mine, other = parts[0][base : base + 8, :].astype(f32), parts[1][base : base + 8, :].astype(f32)
        lines = [jnp.where(upper == 0, mine, other), jnp.where(upper == 0, other, mine)]

        def slot(i):
            return lines[i // 9][i % 9 // 3 : i % 9 // 3 + 1, (i % 3) * 128 : (i % 3 + 1) * 128]

        vec_outs = outs[-13:]
        share = 96
        for i, target in zip((0, 1, 2, 3, 7, 8, 9, 10, 11), vec_outs[:9]):
            target[...] = slot(i)[0, :share]
        vec_outs[9][...] = jnp.concatenate([slot(12), slot(13), slot(14)], axis=1)[0]
        vec_outs[10][...] = jnp.concatenate([slot(4), slot(5), slot(6)], axis=0)[:, :share]
        vec_outs[11][...] = slot(15)[0, :3]
        losses = slot(16)
        pairs, count = vec_outs[12].shape
        lines = [losses[:, r * pairs : (r + 1) * pairs] for r in range(count)]
        lines = jnp.concatenate(lines + [jnp.zeros((8 - count % 8, pairs), f32)] if count % 8 else lines, axis=0)
        vec_outs[12][...] = jnp.concatenate([lines, jnp.zeros((lines.shape[0], 128 - pairs), f32)], axis=1).T[:pairs, :count]


def place_units(here, plan, shapes, parts, vec_shapes=()):
    shape = parts[0].shape
    vm = [whole(s) for s in list(shapes) + list(vec_shapes)]
    return call(
        functools.partial(place_kernel, plan, bool(vec_shapes)), "place_units", (),
        [SMEM_SPEC] + [whole(shape)] * 4, vm, [sds(s, f32) for s in list(shapes) + list(vec_shapes)], [],
        (0.5 * WORK, 0, 0), here, *parts)


def settle_kernel(value, out):
    out[...] = value[...]


def settle(value, weight):
    shape = value.shape
    block = pl.BlockSpec((shape[0] // 2,) + shape[1:], lambda k: (k, 0, 0, 0))
    (out,) = call(settle_kernel, "settle", (2,), [block], [block], [sds(shape, value.dtype)], [], (weight * WORK, 0, 0), value)
    return out.reshape(shape[0] * shape[1], *shape[2:])


def between(value):
    return lax.all_to_all(value, "mix", split_axis=0, concat_axis=0, tiled=True)


def on_device(
    tokens, cotangent, pair_lengths, labels, w_qkv, b_query, b_value, w_attn, b_attn, gain_one, shift_one,
    w_in, b_in, w_out, b_out, gain_two, shift_two, w_pool, b_pool, w_class, b_class,
):
    row_count, part_len, width = tokens.shape
    mixers = lax.axis_size("mix")
    dps = lax.axis_size("dp")
    rows_here = row_count // mixers
    seq = part_len * mixers
    units = w_in.shape[1]
    mix = lax.axis_index("mix").astype(jnp.int32)
    dp = lax.axis_index("dp").astype(jnp.int32)
    here = jnp.stack([mix, dp])
    pairs = pair_lengths.shape[1]
    lengths, classes = pair_lengths.T, labels.T
    quick = dps == 8 and mixers == 4 and width == 768 and units == 3072 and seq * rows_here == 1024 and rows_here == 2

    order = sorted(range(1, mixers), reverse=True)

    def exchange(blocks):
        got = {0: blocks[0]}
        for k in order:
            got[k] = swap(blocks[k], "mix", k)
        return [got[k] for k in range(mixers)]

    pack = jnp.concatenate(
        [b_query, b_value, b_attn, gain_one, shift_one, b_out, gain_two, shift_two, b_pool, b_in, b_class,
         jnp.zeros((3 * width - b_class.shape[0],), f32)]).reshape(16, width)

    def tie(first, second):
        return lax.optimization_barrier((first, second))

    cot = cotangent.reshape(mixers, rows_here, part_len, width)
    rows = ()
    def pieces(array, r):
        return [lax.dynamic_index_in_dim(array, (mix ^ k) * rows_here + r, 0, keepdims=False) for k in range(mixers)]

    blocks = pieces(tokens, 0)
    got = exchange(blocks)
    _, later = tie(blocks[0], tokens)
    for r in range(rows_here):
        if r + 1 < rows_here:
            (got, pack, here), (blocks, cot) = tie((got, pack, here), (pieces(later, r + 1), cot))
            following = exchange(blocks)
            cots = between(cot)
        rows = forward_row(r, rows_here, here, lengths, got, pack, w_qkv, w_attn, rows, (0.0, 15)[r])
        if r + 1 < rows_here:
            rows, got = tie(rows, following)
    qkv, probs, tok, mixture, hid, n1, rho1 = rows
    act, slope, outs, vec_ramp, sum_two, low, send = feed_forward(
        part_len, here, lengths, classes, hid, pack, w_in, w_out, w_pool, w_class.T, cots, quick)
    outs = between(outs)

    if not quick:
        return plain_rest(
            here, part_len, act, slope, outs, low, sum_two, vec_ramp, qkv, probs, tok, mixture, hid, n1, rho1, pack,
            w_qkv, w_attn, w_in, w_out, mix, dp, row_count, units)

    one = first_swap(out_units(here, 0, swap(send, "mix", 1), act.reshape(8, 2, 4, UNIT, rows_here * seq), low))
    _, sum_two = tie(one[0], sum_two)
    grad_up, vec_back, grad_att, sum_one, grad_mix = feed_backward(
        low, slope, w_out, w_in, sum_two, n1, rho1, vec_ramp, pack, w_attn)
    (outs, one), grad_up = tie((outs, one), grad_up)
    args = (hid, mixture, grad_up, grad_att, low)
    send = in_units(here, 1, None, *args)
    _, one = tie(send, one)
    one = second_swap(second_stage(one, 60))
    _, args = tie(one[0], args)
    two = first_swap(in_units(here, 0, swap(send, "mix", 1), *args))
    _, one = tie(two[0], one)
    one = third_swap(third_stage(one))
    _, grad_mix = tie(one[0], grad_mix)

    grad, vec_late, grad_tokens = attention_backward(here, part_len, qkv, probs, mixture, grad_mix, w_qkv, sum_one)
    grad_tokens = between(grad_tokens)
    (one, two), grad = tie((one, two), grad)
    send = qkv_units(here, 1, None, tok, grad, vec_back, vec_late)
    _, two = tie(send, two)
    two = second_swap(second_stage(two, 60))
    _, one = tie(two[0], one)
    one = fourth_swap(fourth_stage(one))
    _, grad = tie(one[0], grad)
    three = first_swap(qkv_units(here, 0, swap(send, "mix", 1), tok, grad, vec_back, vec_late))
    _, outs = tie(three[0], outs)
    output = settle(outs, 1)
    _, one = tie(output, one)
    final = fifth_stage(one)
    _, two = tie(final, two)
    two = third_swap(third_stage_kernel(two, 2))
    (_, grad_tokens), three = tie((two[0], grad_tokens), three)
    three = second_swap(second_stage(three, 60))
    _, two = tie(three[0], two)
    two = fourth_swap(fourth_stage(two))
    _, three = tie(two[0], three)
    three = third_swap(third_stage_kernel(three, 0.2))
    _, grad_tokens = tie(three[0], grad_tokens)
    grad_tokens = settle(grad_tokens, 0.5)
    _, two = tie(grad_tokens, two)
    final = jnp.concatenate([final, fifth_stage(two)], axis=0)
    _, three = tie(final, three)
    three = fourth_swap(fourth_stage(three))
    other = swap(final, "mix", 2)
    final = (final, other, swap(final, "mix", 1), swap(other, "mix", 1))
    other, three = tie(other, three)
    mine = fifth_stage(three)
    other = swap(mine, "mix", 2)
    far = swap(mine, "mix", 1)
    _, final = tie(mine, final)
    grad_w_out, grad_w_in, grad_w_attn, grad_w_pool = place_units(
        here, [(0, j * UNIT, 192, 0, 0, HALF, ((0, HALF),)) for j in range(4)]
        + [(1, 0, 0, UNIT, 4 * HALF, 0, ((j * HALF, HALF),)) for j in range(4)]
        + [(2, 0, 0, UNIT, HALF, 0, ((0, HALF),)), (3, 0, 0, UNIT, HALF, 0, ((0, HALF),))],
        [(384, width), (96, units), (96, width), (96, width)], final)
    _, other = tie(grad_w_in, other)
    three = (mine, other, far, swap(other, "mix", 1))
    share = width // dps
    last = place_units(
        here, [(0, 0, 0, UNIT, 128, 0, tuple((w * width + g * 256, 128) for w in range(3))) for g in range(3)],
        [(96, 3 * width)], three,
        [(share,)] * 9 + [(units // dps,), (w_class.shape[1], share), b_class.shape, (pairs, row_count)])
    (grad_w_qkv, grad_b_out, grad_gain_two, grad_shift_two, grad_b_pool, grad_gain_one, grad_shift_one, grad_b_attn,
     grad_b_query, grad_b_value, grad_b_in, grad_w_class, grad_b_class, pair_loss) = last
    return (
        output, pair_loss.T, grad_tokens, grad_w_qkv, grad_b_query, grad_b_value, grad_w_attn, grad_b_attn,
        grad_gain_one, grad_shift_one, grad_w_in, grad_b_in, grad_w_out, grad_b_out, grad_gain_two, grad_shift_two,
        grad_w_pool, grad_b_pool, grad_w_class.T, grad_b_class,
    )


def plain_rest(
    here, part_len, act, slope, outs, low, sum_two, vec_ramp, qkv, probs, tok, mixture, hid, n1, rho1, pack,
    w_qkv, w_attn, w_in, w_out, mix, dp, row_count, units,
):
    rows_here, _, seq, _ = qkv.shape
    total, width = n1.shape
    dps = lax.axis_size("dp")
    pairs = vec_ramp.shape[0] // rows_here
    grad_up, vec_back, grad_att, sum_one, grad_mix = feed_backward(
        low, slope, w_out, w_in, sum_two, n1, rho1, vec_ramp, pack, w_attn)
    grad, vec_late, grad_tokens = attention_backward(here, part_len, qkv, probs, mixture, grad_mix, w_qkv, sum_one)
    dqkv = grad.reshape(2, total, width // 256, 3, 128).transpose(1, 3, 2, 0, 4).reshape(total, 3 * width)
    output = outs.reshape(row_count, part_len, width)
    grad_tokens = between(grad_tokens).reshape(row_count, part_len, width)
    low, pool = low[:total], low[total:]
    grads = (tn(tok, dqkv), tn(mixture, grad_att), tn(hid, grad_up), nn(act, low), tn(pool[:16], pool[16:]))
    shards = [lax.psum_scatter(g, "dp", scatter_dimension=0, tiled=True) for g in grads]
    shards = [lax.psum(s.astype(bf16), "mix").astype(f32) for s in shards]
    bins = vec_back[3:7]
    vecs = jnp.concatenate([vec_ramp[:7], vec_back[:3], vec_late[:2], bins], axis=0)
    vecs = lax.psum(vecs, ("dp", "mix"))
    class_total = lax.psum(vec_ramp[7, :3], ("dp", "mix"))
    loss = lax.psum(vec_ramp[7, 128 : 128 + row_count * pairs], "mix").reshape(row_count, pairs)
    share = width // dps
    v = lax.dynamic_slice_in_dim(vecs, dp * share, share, axis=1)
    bin_share = lax.dynamic_slice_in_dim(vecs[12:].reshape(-1), dp * (units // dps), units // dps)
    return (
        output, loss, grad_tokens, shards[0], v[10], v[11], shards[1], v[9], v[7], v[8], shards[2], bin_share,
        shards[3], v[0], v[1], v[2], shards[4], v[3], v[4:7].T, class_total,
    )


def solution(mesh):
    wide = P("dp", "mix", None)
    split = P("dp", None)
    in_specs = (wide, wide, split, split) + (P(),) * 17
    out_specs = (
        wide, split, wide,
        split, P("dp"), P("dp"), split, P("dp"), P("dp"), P("dp"),
        split, P("dp"), split, P("dp"), P("dp"), P("dp"),
        split, P("dp"), split, P(),
    )
    return jax.shard_map(on_device, mesh=mesh, in_specs=in_specs, out_specs=out_specs, check_vma=False)
```

```python
import functools

import jax
import jax.numpy as jnp
from jax import lax
from jax.experimental import pallas as pl
from jax.experimental.pallas import tpu as pltpu
from jax.sharding import PartitionSpec as P

HEADS = 12
SCALE = 1.0
WORK = 5.8e8
GROUP = 4
CHUNK = 768
TILE = 256
UNIT = 48
HALF = 384
norm_eps = 1e-06
masked_score = -1000000000.0
inv_root_two = 0.7071067811865476
inv_root_tau = 0.3989422804014327
f32 = jnp.float32
bf16 = jnp.bfloat16
VMEM_LIMIT = 62 * 1024 * 1024
SMALL_LIMIT = 20 * 1024 * 1024
LIMITS = dict.fromkeys(("stage_two", "stage_three", "settle", "place_units"), SMALL_LIMIT)
SMEM_SPEC = pl.BlockSpec(memory_space=pltpu.SMEM)
B_QUERY, B_VALUE, B_ATTN, GAIN_ONE, SHIFT_ONE, B_OUT, GAIN_TWO, SHIFT_TWO, B_POOL, B_IN, B_CLASS = 0, 1, 2, 3, 4, 5, 6, 7, 8, 9, 13


def whole(shape):
    return pl.BlockSpec(shape, lambda *_: (0,) * len(shape))


def sds(shape, dtype):
    return jax.ShapeDtypeStruct(shape, dtype)


def nn(left, right):
    return jnp.dot(left, right, preferred_element_type=f32)


def nt(left, right):
    return lax.dot_general(left, right, (((1,), (1,)), ((), ())), preferred_element_type=f32)


def tn(left, right):
    return lax.dot_general(left, right, (((0,), (0,)), ((), ())), preferred_element_type=f32)


def call(kernel, name, grid, in_specs, out_specs, out_shape, scratch, work, *args, prefetch=0, aliases=None):
    common = dict(
        out_shape=out_shape,
        compiler_params=pltpu.CompilerParams(vmem_limit_bytes=LIMITS.get(name, VMEM_LIMIT)),
        cost_estimate=pl.CostEstimate(flops=int(2 * work[0] * SCALE), bytes_accessed=int(work[1] * SCALE), transcendentals=0),
        name=name,
        input_output_aliases=aliases or {},
    )
    if prefetch:
        spec = pltpu.PrefetchScalarGridSpec(
            num_scalar_prefetch=prefetch, grid=grid, in_specs=in_specs, out_specs=out_specs, scratch_shapes=scratch)
        return pl.pallas_call(kernel, grid_spec=spec, **common)(*args)
    return pl.pallas_call(
        kernel, grid=grid, in_specs=in_specs, out_specs=out_specs, scratch_shapes=scratch, **common)(*args)


def after(value, *earlier):
    return lax.optimization_barrier((value,) + earlier)[0]


def fetch(copies, start, wait):
    copies = [pltpu.make_async_copy(*copy) for copy in copies]

    @pl.when(start)
    def _():
        for copy in copies:
            copy.start()

    @pl.when(wait)
    def _():
        for copy in copies:
            copy.wait()


def mean_of(values):
    return jnp.mean(values, axis=-1, keepdims=True)


def col_sum(values):
    return jnp.sum(values, axis=0, keepdims=True)


def head_only(values, head, size):
    lane = lax.broadcasted_iota(jnp.int32, (1, values.shape[1]), 1) // size
    return jnp.where(lane == head, values, jnp.zeros((), values.dtype))


def per_head(values, size):
    return jnp.concatenate([head_only(values, h, size) for h in range(GROUP)], axis=0)


def segments(places, lengths, row):
    total = jnp.int32(0)
    seg = jnp.zeros(places.shape, jnp.int32)
    for k in range(lengths.shape[0]):
        total = total + lengths[k, row]
        seg = seg + (places >= total).astype(jnp.int32)
    return seg


def forward_kernel(row, rows_here, part_len, mixers, head_size, here, lengths, *refs):
    pieces, refs = refs[:mixers], refs[mixers:]
    pack, packq, packv, wq, wk, wv, wa = refs[:7]
    (qkv_o, probs_o, tok_o, mix_o, hid_o, n1_o, rho_o,
     tok_s, mix_s, bias_s, w_s, wa_s, sems) = refs[-13:]
    step = pl.program_id(0)
    fetch([(wa, wa_s, sems.at[0])], step == 0, step == pl.num_programs(0) - 1)
    seq = part_len * mixers
    shift = part_len.bit_length() - 1
    span = GROUP * head_size

    @pl.when(step == 0)
    def _():
        for i, piece in enumerate(pieces):
            tok_s[i * part_len : (i + 1) * part_len, :] = piece[...]
        mine = here[0]
        down = lax.broadcasted_iota(jnp.int32, (seq, 1), 0)
        across = lax.broadcasted_iota(jnp.int32, (1, seq), 1)

        def place(i):
            return (((i >> shift) ^ mine) << shift) + (i & (part_len - 1))

        number = mine * rows_here + row
        same = segments(place(down), lengths, number) == segments(place(across), lengths, number)
        bias_s[...] = jnp.where(same, 0.0, masked_score)

    for i, weight in enumerate((wq, wk, wv)):
        w_s[:, i * span : (i + 1) * span] = weight[...]
    qkv = nn(tok_s[...], w_s[...])
    qs = (qkv[:, :span] + packq[B_QUERY : B_QUERY + 1]).astype(bf16) * bf16(head_size ** (-0.5))
    keys = qkv[:, span : 2 * span].astype(bf16)
    values = (qkv[:, 2 * span :] + packv[B_VALUE : B_VALUE + 1]).astype(bf16)
    qkv_o[0, 0, :, :span] = qs
    qkv_o[0, 0, :, span : 2 * span] = keys
    qkv_o[0, 0, :, 2 * span :] = values
    scores = nt(keys, per_head(qs, head_size))
    values_t = values.T
    mixed = []
    for h in range(GROUP):
        at = slice(h * seq, (h + 1) * seq)
        part = scores[:, at] + bias_s[...]
        expo = jnp.exp(part - jnp.max(part, axis=0, keepdims=True))
        probs = (expo * (1.0 / col_sum(expo))).astype(bf16)
        probs_o[0, 0, :, at] = probs
        mixed.append(nn(values_t[h * head_size : (h + 1) * head_size], probs))
    mixed = jnp.concatenate(mixed, axis=0).astype(bf16).T
    here_columns = pl.ds(pl.multiple_of(step * span, 128), span)
    mix_s[:, here_columns] = mixed
    mix_o[...] = mixed
    tok_o[...] = tok_s[:, here_columns]

    @pl.when(step == pl.num_programs(0) - 1)
    def _():
        full = tok_s[...].astype(f32) + (nn(mix_s[...], wa_s[...]) + pack[B_ATTN : B_ATTN + 1])
        centre = full - mean_of(full)
        rho = lax.rsqrt(mean_of(centre * centre) + norm_eps)
        normed = centre * rho
        hidden = normed * pack[GAIN_ONE : GAIN_ONE + 1] + pack[SHIFT_ONE : SHIFT_ONE + 1]
        hid_o[...] = hidden.astype(bf16)
        n1_o[...] = normed.astype(bf16)
        rho_o[...] = jnp.broadcast_to(rho, rho_o.shape)


def forward_row(row, rows_here, here, lengths, pieces, pack, w_qkv, w_attn, earlier, weight_us):
    part_len, width = pieces[0].shape
    mixers = len(pieces)
    seq = part_len * mixers
    head_size = width // HEADS
    span = GROUP * head_size
    steps = width // span

    def weight(which):
        return pl.BlockSpec((width, span), lambda g: (0, which * steps + g))

    rows = pack.shape[0]
    column = pl.BlockSpec((rows, span), lambda g: (0, g))
    part = pl.BlockSpec((seq, span), lambda g: (row, g))
    wide = pl.BlockSpec((seq, width), lambda g: (row, 0))
    total = rows_here * seq
    specs = [SMEM_SPEC, SMEM_SPEC] + [whole((part_len, width))] * mixers
    specs += [whole((rows, width)), column, column, weight(0), weight(1), weight(2), pl.BlockSpec(memory_space=pl.ANY)]
    return call(
        functools.partial(forward_kernel, row, rows_here, part_len, mixers, head_size), "forward_row", (steps,),
        specs + [pl.BlockSpec(memory_space=pl.ANY)] * len(earlier),
        [pl.BlockSpec((1, 1, seq, 3 * span), lambda g: (row, g, 0, 0)),
         pl.BlockSpec((1, 1, seq, GROUP * seq), lambda g: (row, g, 0, 0)),
         part, part, wide, wide, pl.BlockSpec((seq, 128), lambda g: (row, 0))],
        [sds((rows_here, steps, seq, 3 * span), bf16), sds((rows_here, steps, seq, GROUP * seq), bf16)]
        + [sds((total, width), bf16)] * 4 + [sds((total, 128), f32)],
        [pltpu.VMEM((seq, width), bf16), pltpu.VMEM((seq, width), bf16), pltpu.VMEM((seq, seq), f32),
         pltpu.VMEM((width, 3 * span), bf16), pltpu.VMEM((width, width), bf16), pltpu.SemaphoreType.DMA((1,))],
        (weight_us * WORK, 0, 0),
        here, lengths, *pieces, pack, pack, pack, w_qkv, w_qkv, w_qkv, w_attn, *earlier,
        aliases={len(specs) + i: i for i in range(len(earlier))})


def start_spots(here, lengths, r, rows_here, part_len, pairs, seq):
    shift = part_len.bit_length() - 1
    spots = []
    start = jnp.int32(0)
    for k in range(pairs):
        spots.append(r * seq + (((start >> shift) ^ here[0]) << shift) + (start & (part_len - 1)))
        start = start + lengths[k, here[0] * rows_here + r]
    return spots


def feed_kernel(rows_here, part_len, pairs, mixers, send, here, lengths, labels, *refs):
    hid, pack, w_in, w_out, w_pool_any, w_class, cots_any = refs[:7]
    act_o, slope_o, out_o, vec_o, sum_o, low_o, send_o = refs[7:14]
    feed_s, normed_s, rho_s, act_s, acc_s, w_pool, cots, sems = refs[14:]
    step = pl.program_id(0)
    last = pl.num_programs(0) - 1
    fetch([(w_pool_any, w_pool, sems.at[0]), (cots_any, cots, sems.at[1])], step == 0, step == last)
    tokens, width = hid.shape
    seq = part_len * mixers
    count = tokens // TILE

    @pl.when(step == 0)
    def _():
        feed_s[...] = hid[...].astype(f32) + pack[B_OUT : B_OUT + 1]

    bias = pack[pl.ds(B_IN + step, 1), :]

    def rows(i):
        return slice(i * TILE, (i + 1) * TILE)

    up = nn(hid[rows(0), :], w_in[...])
    before = None
    for i in range(count):
        following = nn(hid[rows(i + 1), :], w_in[...]) if i + 1 < count else None
        up = up + bias
        half = 0.5 * (1.0 + lax.erf(up * inv_root_two))
        act = (up * half).astype(bf16)
        slope_o[rows(i), :] = (half + up * jnp.exp(-0.5 * up * up) * inv_root_tau).astype(bf16)
        turned = act.T
        act_o[:, rows(i)] = turned
        if send:
            blocks = CHUNK // (8 * UNIT)
            act_s[pl.ds(step * blocks, blocks), :, :, :, rows(i)] = turned.reshape(blocks, 2, 2, 2 * UNIT, TILE)
        if before is not None:
            feed_s[rows(i - 1), :] += nn(before, w_out[...])
        before, up = act, following
    feed_s[rows(count - 1), :] += nn(before, w_out[...])

    @pl.when(step == last)
    def _():
        gain = pack[GAIN_TWO : GAIN_TWO + 1]
        for r in range(rows_here):
            for k in range(mixers):
                at = slice(r * seq + k * part_len, r * seq + (k + 1) * part_len)
                full = feed_s[at, :]
                centre = full - mean_of(full)
                rho = lax.rsqrt(mean_of(centre * centre) + norm_eps)
                normed = centre * rho
                out = normed * gain + pack[SHIFT_TWO : SHIFT_TWO + 1]
                feed_s[at, :] = out
                out_o[here[0] ^ k, r] = out.astype(bf16)
                normed_s[at, :] = normed
                rho_s[at, :] = jnp.broadcast_to(rho, (part_len, 128))
        spots = []
        for r in range(rows_here):
            spots += start_spots(here, lengths, r, rows_here, part_len, pairs, seq)
        firsts = jnp.concatenate([feed_s[pl.ds(spot, 1), :] for spot in spots], axis=0)
        sums = [jnp.zeros((1, width), f32)] * 2

        def backward(i, sums):
            r, k = i // mixers, i % mixers
            at = slice(i * part_len, (i + 1) * part_len)
            e = cots[here[0] ^ k, r].astype(f32)
            normed = normed_s[at, :]
            eg = e * gain
            sum_o[at, :] = rho_s[at, 0:1] * (eg - mean_of(eg) - normed * mean_of(eg * normed))
            return [sums[0] + col_sum(e * normed), sums[1] + col_sum(e)]

        tiles = rows_here * mixers
        pool = w_pool[...]
        pool_high = pool.astype(bf16)
        pool_rest = (pool - pool_high.astype(f32)).astype(bf16)
        first_high = firsts.astype(bf16)
        first_rest = (firsts - first_high.astype(f32)).astype(bf16)
        pre = nn(jnp.concatenate([first_high, first_rest], axis=0), pool_high)
        pre = pre[: firsts.shape[0]] + pre[firsts.shape[0] :] + nn(first_high, pool_rest)
        for i in range(tiles // 2):
            sums = backward(i, sums)
        pooled = jnp.tanh(pre + pack[B_POOL : B_POOL + 1])
        classes = w_class.shape[0]
        here_pairs = rows_here * pairs
        class_t = w_class[...]
        lane = lax.broadcasted_iota(jnp.int32, (here_pairs, 128), 1)
        logits = jnp.full((here_pairs, 128), -jnp.inf, f32)
        for c in range(classes):
            logits = jnp.where(lane == c, jnp.sum(pooled * class_t[c : c + 1], axis=1, keepdims=True), logits)
        logits = logits + pack[B_CLASS : B_CLASS + 1, :128]
        top = jnp.max(logits, axis=-1, keepdims=True)
        expo = jnp.exp(logits - top)
        total = jnp.sum(expo, axis=-1, keepdims=True)
        log_total = top + jnp.log(total)
        sub = lax.broadcasted_iota(jnp.int32, (here_pairs, 128), 0)
        label = jnp.zeros((here_pairs, 128), jnp.int32)
        for r in range(rows_here):
            for k in range(pairs):
                label = jnp.where(sub == r * pairs + k, labels[k, here[0] * rows_here + r], label)
        chosen = lane == label
        loss = log_total - jnp.sum(jnp.where(chosen, logits, 0.0), axis=-1, keepdims=True)
        grad_logits = expo / total - chosen.astype(f32)
        grad_pooled = jnp.zeros((here_pairs, width), f32)
        for c in range(classes):
            grad_pooled = grad_pooled + grad_logits[:, c : c + 1] * class_t[c : c + 1]
        grad_pre = grad_pooled * (1.0 - pooled * pooled)
        grad_firsts = nt(grad_pre.astype(bf16), pool_high)
        for i in range(tiles // 2, tiles):
            sums = backward(i, sums)
        normed = jnp.concatenate([normed_s[pl.ds(spot, 1), :] for spot in spots], axis=0)
        rho = jnp.concatenate([rho_s[pl.ds(spot, 1), :] for spot in spots], axis=0)[:, 0:1]
        eg = grad_firsts * gain
        more = rho * (eg - mean_of(eg) - normed * mean_of(eg * normed))
        for i, spot in enumerate(spots):
            sum_o[pl.ds(spot, 1), :] = sum_o[pl.ds(spot, 1), :] + more[i : i + 1, :]
        vec_o[1:2, :] = sums[0] + col_sum(grad_firsts * normed)
        vec_o[2:3, :] = sums[1] + col_sum(grad_firsts)
        vec_o[3:4, :] = col_sum(grad_pre)
        for c in range(classes):
            vec_o[4 + c : 5 + c, :] = col_sum(pooled * grad_logits[:, c : c + 1])
        spread_loss = jnp.where(lane == here[0] * here_pairs + sub, loss, 0.0)
        vec_o[7:8, :] = jnp.concatenate(
            [col_sum(grad_logits), col_sum(spread_loss), jnp.zeros((1, width - 256), f32)], axis=1)
        none = jnp.zeros((16 - here_pairs, width), f32)
        low_o[tokens : tokens + 16, :] = jnp.concatenate([firsts, none], axis=0).astype(bf16)
        low_o[tokens + 16 :, :] = jnp.concatenate([grad_pre, none], axis=0).astype(bf16)
        bias_sum = jnp.zeros((1, width), f32)
        for i in range(count):
            low = sum_o[rows(i), :].astype(bf16)
            low_o[rows(i), :] = low
            bias_sum = bias_sum + col_sum(low.astype(f32))
        vec_o[0:1, :] = bias_sum
        if send:
            dp, upper = here[1], (here[0] >> 1) & 1
            other = 1 - (here[0] & 1)
            for j in range(2):
                acc_s[...] = nn(act_s[:, other, j].reshape(16 * UNIT, tokens), low_o[:tokens, :])
                store_sums([send_o], None, slice(j * 2 * UNIT, (j + 1) * 2 * UNIT), lambda p, y: acc_s[
                    pl.ds(pl.multiple_of((p ^ dp) * 2 * UNIT, 16), 2 * UNIT),
                    pl.ds(pl.multiple_of((upper ^ y) * HALF, 128), HALF)])
        else:
            send_o[...] = jnp.zeros(send_o.shape, bf16)


def feed_forward(part_len, here, lengths, labels, hid, pack, w_in, w_out, w_pool, w_class, cots, send):
    mixers, rows_here = cots.shape[:2]
    tokens, width = hid.shape
    pairs = lengths.shape[0]
    units = w_in.shape[1]
    steps = units // CHUNK
    sent = (16, 4 * UNIT, HALF) if send else (16, 128)
    act_shape = (units // (8 * UNIT), 2, 2, 2 * UNIT, tokens) if send else (8, 128)
    acc_shape = (16 * UNIT, width) if send else (8, 128)
    return call(
        functools.partial(feed_kernel, rows_here, part_len, pairs, mixers, send), "feed_forward", (steps,),
        [SMEM_SPEC] * 3
        + [whole(hid.shape), whole(pack.shape), pl.BlockSpec((width, CHUNK), lambda c: (0, c)),
           pl.BlockSpec((CHUNK, width), lambda c: (c, 0)), pl.BlockSpec(memory_space=pl.ANY), whole(w_class.shape), pl.BlockSpec(memory_space=pl.ANY)],
        [pl.BlockSpec((CHUNK, tokens), lambda c: (c, 0)), pl.BlockSpec((tokens, CHUNK), lambda c: (0, c)),
         whole(cots.shape), whole((8, width)), whole((tokens, width)), whole((tokens + 32, width)), whole(sent)],
        [sds((units, tokens), bf16), sds((tokens, units), bf16), sds(cots.shape, bf16), sds((8, width), f32),
         sds((tokens, width), f32), sds((tokens + 32, width), bf16), sds(sent, bf16)],
        [pltpu.VMEM((tokens, width), f32), pltpu.VMEM((tokens, width), f32), pltpu.VMEM((tokens, 128), f32),
         pltpu.VMEM(act_shape, bf16), pltpu.VMEM(acc_shape, f32), pltpu.VMEM(w_pool.shape, f32), pltpu.VMEM(cots.shape, bf16),
         pltpu.SemaphoreType.DMA((2,))],
        (2 * tokens * width * units, 35e6, 0),
        here, lengths, labels, hid, pack, w_in, w_out, w_pool, w_class, cots)


def back_kernel(
    low, slope, w_out, w_in, ramp, pack, *refs,
):
    from_any, (up_o, vec_o, att_o, sum_o, mix_o, hid_s), kept, sems = refs[:4], refs[4:10], refs[10:14], refs[14]
    sum_two, w_attn, n1, rho = kept
    step = pl.program_id(0)
    last = pl.num_programs(0) - 1
    fetch([(a, b, sems.at[i]) for i, (a, b) in enumerate(zip(from_any, kept))], step == 0, step == last)
    count = slope.shape[0] // TILE

    def rows(i):
        return slice(i * TILE, (i + 1) * TILE)

    @pl.when(step == 0)
    def _():
        hid_s[...] = jnp.zeros(hid_s.shape, f32)
        vec_o[7:8, :] = jnp.zeros((1, vec_o.shape[1]), f32)
        vec_o[8:16, :] = ramp[...]

    total = jnp.zeros((1, slope.shape[1]), f32)
    act = nt(low[rows(0), :], w_out[...])
    before = None
    for i in range(count):
        following = nt(low[rows(i + 1), :], w_out[...]) if i + 1 < count else None
        up = (act * slope[rows(i), :].astype(f32)).astype(bf16)
        up_o[rows(i), :] = up
        total = total + col_sum(up.astype(f32))
        if before is not None:
            hid_s[rows(i - 1), :] += nt(before, w_in[...])
        before, act = up, following
    hid_s[rows(count - 1), :] += nt(before, w_in[...])
    vec_o[pl.ds(3 + step, 1), :] = total

    @pl.when(step == last)
    def _():
        width = pack.shape[1]
        sums = [jnp.zeros((1, width), f32)] * 3
        for i in range(count):
            at = rows(i)
            e = hid_s[at, :] + sum_two[at, :]
            normed = n1[at, :].astype(f32)
            eg = e * pack[GAIN_ONE : GAIN_ONE + 1]
            grad = rho[at, 0:1] * (eg - mean_of(eg) - normed * mean_of(eg * normed))
            sum_o[at, :] = grad
            att = grad.astype(bf16)
            att_o[at, :] = att
            mix_o[at, :] = nt(att, w_attn[...]).astype(bf16)
            sums = [sums[0] + col_sum(e * normed), sums[1] + col_sum(e), sums[2] + col_sum(att.astype(f32))]
        for i in range(3):
            vec_o[i : i + 1, :] = sums[i]


def feed_backward(low, slope, w_out, w_in, sum_two, n1, rho, ramp, pack, w_attn):
    count, width = n1.shape
    units = slope.shape[1]
    block = pl.BlockSpec((count, CHUNK), lambda j: (0, j))
    late = (sum_two, w_attn, n1, rho)
    return call(
        back_kernel, "feed_backward", (units // CHUNK,),
        [whole(low.shape), block, pl.BlockSpec((CHUNK, width), lambda j: (j, 0)), pl.BlockSpec((width, CHUNK), lambda j: (0, j)),
         whole((8, width)), whole(pack.shape)] + [pl.BlockSpec(memory_space=pl.ANY)] * 4,
        [block, whole((16, width))] + [whole((count, width))] * 3,
        [sds((count, units), bf16), sds((16, width), f32), sds((count, width), bf16), sds((count, width), f32),
         sds((count, width), bf16)],
        [pltpu.VMEM((count, width), f32)] + [pltpu.VMEM(a.shape, a.dtype) for a in late] + [pltpu.SemaphoreType.DMA((4,))],
        (2 * count * width * units + count * width * width, 40e6, 0),
        low, slope, w_out, w_in, ramp, pack, *late)


def attention_back_kernel(
    head_size, part_len, mixers, here, qkv_r, probs_r, mix_r, grad_r, wq, wk, wv, sum_any,
    d_o, vec_o, tok_o, acc_s, w_s, vec_s, sum_one, sems,
):
    row = pl.program_id(0)
    step = pl.program_id(1)
    last = pl.num_programs(1) - 1
    rows_at = pl.ds(pl.multiple_of(row * sum_one.shape[0], 8), sum_one.shape[0])
    fetch([(sum_any.at[rows_at], sum_one, sems.at[0])], step == 0, step == last)
    span = GROUP * head_size
    seq = qkv_r.shape[2]
    qs, keys, values = qkv_r[0, 0, :, :span], qkv_r[0, 0, :, span : 2 * span], qkv_r[0, 0, :, 2 * span :]
    grad = grad_r[...]
    for i, weight in enumerate((wq, wk, wv)):
        w_s[:, i * span : (i + 1) * span] = weight[...]
    prod = grad.T.astype(f32) * mix_r[...].T.astype(f32)
    keys_t = keys.T
    grad_heads = per_head(grad, head_size)
    grad_probs = nt(values, grad_heads)
    parts, dq_t = [], []
    for h in range(GROUP):
        rows = slice(h * head_size, (h + 1) * head_size)
        at = slice(h * seq, (h + 1) * seq)
        part = (probs_r[0, 0, :, at].astype(f32) * (grad_probs[:, at] - col_sum(prod[rows]))).astype(bf16)
        parts.append(part)
        dq_t.append(nn(keys_t[rows], part))
    grad_scores = jnp.concatenate(parts, axis=1)
    dv = nn(probs_r[0, 0], grad_heads).astype(bf16)
    dk = nn(grad_scores, per_head(qs, head_size)).astype(bf16)
    dq = (jnp.concatenate(dq_t, axis=0) * (head_size ** (-0.5))).astype(bf16).T
    all_three = jnp.concatenate([dq, dk, dv], axis=1)
    half = span // 2
    for c in range(2):
        at = slice(c * half, (c + 1) * half)
        d_o[c] = jnp.concatenate([dq[:, at], dk[:, at], dv[:, at]], axis=1)
    vec = jnp.concatenate([col_sum(dq.astype(f32)), col_sum(dv.astype(f32)), jnp.zeros((6, span), f32)], axis=0)

    @pl.when(row == 0)
    def _():
        vec_s[step] = vec

    @pl.when(row > 0)
    def _():
        vec_s[step] += vec

    part = nt(all_three, w_s[...])

    @pl.when(step == 0)
    def _():
        acc_s[...] = part

    @pl.when(step > 0)
    def _():
        acc_s[...] += part

    @pl.when(step == last)
    def _():
        steps = vec_s.shape[0]
        for k in range(mixers):
            tok_o[here[0] ^ k, 0] = (acc_s[k * part_len : (k + 1) * part_len, :] + sum_one[k * part_len : (k + 1) * part_len, :]).astype(bf16)
        vec_o[...] = jnp.concatenate([vec_s[g] for g in range(steps)], axis=1)


def attention_backward(here, part_len, qkv, probs, mix, grad_mix, w_qkv, sum_one):
    rows_here, steps, seq, _ = qkv.shape
    total, width = grad_mix.shape
    head_size = width // HEADS
    span = GROUP * head_size
    mixers = seq // part_len
    part = pl.BlockSpec((seq, span), lambda r, g: (r, g))

    def weight(which):
        return pl.BlockSpec((width, span), lambda r, g: (0, which * steps + g))

    return call(
        functools.partial(attention_back_kernel, head_size, part_len, mixers), "attention_backward", (rows_here, steps),
        [SMEM_SPEC, pl.BlockSpec((1, 1, seq, 3 * span), lambda r, g: (r, g, 0, 0)),
         pl.BlockSpec((1, 1, seq, GROUP * seq), lambda r, g: (r, g, 0, 0)), part, part,
         weight(0), weight(1), weight(2), pl.BlockSpec(memory_space=pl.ANY)],
        [pl.BlockSpec((2, seq, 3 * span // 2), lambda r, g: (0, r, g)), whole((8, width)),
         pl.BlockSpec((mixers, 1, part_len, width), lambda r, g: (0, r, 0, 0))],
        [sds((2, total, 3 * width // 2), bf16), sds((8, width), f32), sds((mixers, rows_here, part_len, width), bf16)],
        [pltpu.VMEM((seq, width), f32), pltpu.VMEM((width, 3 * span), bf16), pltpu.VMEM((steps, 8, span), f32),
         pltpu.VMEM((seq, width), f32), pltpu.SemaphoreType.DMA((1,))],
        (rows_here * (3 * seq * width * width + 16 * seq * seq * width), 18e6, 0),
        here, qkv, probs, mix, grad_mix, w_qkv, w_qkv, w_qkv, sum_one)


def store_sums(outs, got, rows, read):
    for p in range(8):
        for y in range(2):
            value = read(p, y)
            if got is None:
                outs[0][p * 2 + y, rows, :] = value.astype(bf16)
                continue
            value = (value + got[p * 2 + y, rows, :].astype(f32)).astype(bf16)
            xk, xs, yk, ys = outs
            z2, z1, x = p // 4, p // 2 % 2, p % 2
            if z1 == 0:
                (xk, xs)[x][z2, y, rows, :] = value
            else:
                (yk, ys)[y][z2, x, rows, :] = value


def natural(acc, p, y, dp, upper, columns):
    return acc[pl.ds(pl.multiple_of((p ^ dp) * 2 * UNIT + (y ^ upper) * UNIT, 16), UNIT), columns]


def split_refs(flip, refs):
    return (refs[0], None, refs[1:]) if flip else (refs[1:5], refs[0], refs[5:])


def unit_call(kernel, name, flip, grid, in_specs, rows, step_rows, scratch, work, here, *args, got=None):
    if flip:
        specs, shapes = [pl.BlockSpec((16, step_rows, HALF), lambda j, s: (0, j, 0))], [sds((16, rows, HALF), bf16)]
    else:
        in_specs = in_specs + [pl.BlockSpec((16, step_rows, HALF), lambda j, s: (0, j, 0))]
        args = args + (got,)
        specs = [pl.BlockSpec((2, 2, step_rows, HALF), lambda j, s: (0, 0, j, 0))] * 4
        shapes = [sds((2, 2, rows, HALF), bf16)] * 4
    out = call(kernel, name, (grid,), in_specs, specs, shapes, scratch, work, here, *args, prefetch=1)
    return out[0] if flip else out


def out_units_kernel(flip, here, act, low, *refs):
    outs, got, (acc_s,) = split_refs(flip, refs)
    outs = [outs] if flip else outs
    dp, upper = here[1], (here[0] >> 1) & 1
    count = act.shape[-1]
    acc_s[...] = nn(act[...].reshape(16 * UNIT, count), low[:count])
    at = [pl.multiple_of((upper ^ y) * HALF, 128) for y in range(2)]
    store_sums(outs, got, slice(None), lambda p, y: acc_s[
        pl.ds(pl.multiple_of((p ^ dp) * 2 * UNIT, 16), 2 * UNIT), pl.ds(at[y], HALF)])


def out_units(here, flip, got, act, low):
    width = low.shape[1]
    count = act.shape[-1]
    return unit_call(
        functools.partial(out_units_kernel, flip), "units_out", flip, 2,
        [pl.BlockSpec((8, 1, 2, UNIT, count), lambda j, s: (0, (s[0] & 1) ^ flip, j, 0, 0)), whole(low.shape)],
        4 * UNIT, 2 * UNIT, [pltpu.VMEM((16 * UNIT, width), f32)], (4 * 8 * UNIT * count * width, 5e6, 0),
        here, act, low, got=got)


def in_units_kernel(flip, here, hid, mix, up, att, low, *refs):
    outs, got, (acc_s, mix_s, att_s, sems) = split_refs(flip, refs)
    outs = [outs] if flip else outs
    step = pl.program_id(0)
    dp = here[1]
    core, upper = (here[0] & 1) ^ flip, (here[0] >> 1) & 1

    column = pl.ds(pl.multiple_of(core * HALF, 128), HALF)
    copies = [
        pltpu.make_async_copy(mix, mix_s, sems.at[0]),
        pltpu.make_async_copy(att.at[:, column], att_s, sems.at[1]),
    ]

    @pl.when(step == 0)
    def _():
        for copy in copies:
            copy.start()

    @pl.when(step < 2)
    def _():
        acc_s[...] = tn(hid[...], up[...])

    @pl.when(step == 2)
    def _():
        for copy in copies:
            copy.wait()
        acc_s[:, :HALF] = tn(mix_s[...], att_s[...])
        right = low[16:32, :]
        acc_s[:, HALF:] = tn(low[:16, :], jnp.where(core == 0, right[:, :HALF], right[:, HALF:]))

    for u in range(2):
        store_sums(outs, got, slice(u * UNIT, (u + 1) * UNIT), lambda p, y: natural(
            acc_s, p, y, dp, upper, slice(u * HALF, (u + 1) * HALF)))


def in_units(here, flip, got, hid, mix, up, att, low):
    count, width = hid.shape
    return unit_call(
        functools.partial(in_units_kernel, flip), "units_in", flip, 3,
        [whole((count, width)), pl.BlockSpec(memory_space=pl.ANY),
         pl.BlockSpec((count, 2 * HALF), lambda j, s: (0, ((s[0] & 1) ^ flip) * 2 + jnp.minimum(j, 1))),
         pl.BlockSpec(memory_space=pl.ANY), pl.BlockSpec((32, width), lambda j, s: (count // 32, 0))],
        6 * UNIT, 2 * UNIT,
        [pltpu.VMEM((width, 2 * HALF), f32), pltpu.VMEM((count, width), bf16), pltpu.VMEM((count, HALF), bf16),
         pltpu.SemaphoreType.DMA((2,))],
        (5 * width * HALF * count, 5e6, 0),
        here, hid, mix, up, att, low, got=got)


VEC_ROWS = 16


def qkv_units_kernel(flip, here, tok, grad, back, late, *refs):
    outs, got, (acc_s, tab_s) = split_refs(flip, refs)
    outs = [outs] if flip else outs
    dp, upper = here[1], (here[0] >> 1) & 1
    acc_s[...] = tn(tok[...], grad[0])
    for u in range(3):
        store_sums(outs, got, slice(u * UNIT, (u + 1) * UNIT), lambda p, y: natural(
            acc_s, p, y, dp, upper, slice(u * HALF, (u + 1) * HALF)))
    ramp = back[8:16, :]
    units = jnp.concatenate([back[3 + i : 4 + i, :] for i in range(4)], axis=1)
    short = jnp.concatenate(
        [ramp[0:7], back[0:3, :], late[0:2, :], jnp.zeros((4, ramp.shape[1]), f32)], axis=0)
    share = short.shape[1] // 8
    fill = jnp.zeros((16, 128 - share), f32)
    blank = jnp.zeros((VEC_ROWS - 3, HALF), f32)
    for b in range(8):
        slots = jnp.concatenate([short[:, b * share : (b + 1) * share], fill], axis=1)
        slots = [slots[i : i + 1] for i in range(12)]
        slots += [units[:, b * HALF + i * 128 : b * HALF + (i + 1) * 128] for i in range(3)]
        slots += [ramp[7:8, :128], jnp.where(dp == b, ramp[7:8, 128:256], 0.0), jnp.zeros((1, 128), f32)]
        lines = [jnp.concatenate(slots[i * 3 : i * 3 + 3], axis=1) for i in range(6)]
        for y in range(2):
            tab_s[b, y] = jnp.concatenate(lines[y * 3 : y * 3 + 3] + [blank], axis=0)
    store_sums(outs, got, slice(3 * UNIT, 3 * UNIT + VEC_ROWS), lambda p, y: tab_s[p ^ dp, y ^ upper])


def qkv_units(here, flip, got, tok, grad, back, late):
    count, width = tok.shape
    rows = 3 * UNIT + VEC_ROWS
    wide = 3 * HALF
    return unit_call(
        functools.partial(qkv_units_kernel, flip), "units_qkv", flip, 1,
        [whole((count, width)), pl.BlockSpec((1, count, wide), lambda j, s: ((s[0] & 1) ^ flip, 0, 0)),
         whole((16, width)), whole((8, width))],
        rows, rows, [pltpu.VMEM((width, wide), f32), pltpu.VMEM((8, 2, VEC_ROWS, HALF), f32)],
        (width * wide * count, 5e6, 0), here, tok, grad, back, late, got=got)


def second_kernel(xk, xr, yk, yr, x2k, x2s, y2k, y2s):
    x = xk[0].astype(f32) + xr[0].astype(f32)
    x2k[0] = x[0].astype(bf16)
    x2s[0] = x[1].astype(bf16)
    y = yk[0].astype(f32) + yr[0].astype(f32)
    y2k[0] = y[0].astype(bf16)
    y2s[0] = y[1].astype(bf16)


def add(left, right):
    return (left.astype(f32) + right.astype(f32)).astype(bf16)


def swap(value, axis, bit):
    size = lax.axis_size(axis)
    return lax.ppermute(value, axis, [(i, i ^ bit) for i in range(size)])


def first_swap(stage):
    xk, xs, yk, ys = stage
    return xk, swap(xs, "dp", 1), yk, swap(ys, "mix", 2)


def second_stage(stage, weight, name="stage_two"):
    rows = stage[0].shape[2]
    block = pl.BlockSpec((1, 2, rows, HALF), lambda z: (z, 0, 0, 0))
    out = pl.BlockSpec((1, rows, HALF), lambda z: (z, 0, 0))
    return call(second_kernel, name, (2,), [block] * 4, [out] * 4, [sds((2, rows, HALF), bf16)] * 4, [],
                (weight * WORK, 0, 0), *stage)


def second_swap(stage):
    xk, xs, yk, ys = stage
    return xk, swap(xs, "mix", 2), yk, swap(ys, "dp", 1)


def third_stage(stage):
    xk, xr, yk, yr = stage
    return add(xk, xr), add(yk, yr)


def third_kernel(xk, xr, yk, yr, keep, send):
    keep[...] = add(xk[...], xr[...])
    send[...] = add(yk[...], yr[...])


def third_stage_kernel(stage, weight):
    shape = stage[0].shape
    block = pl.BlockSpec((1,) + shape[1:], lambda z: (z, 0, 0))
    return call(third_kernel, "stage_three", (2,), [block] * 4, [block] * 2, [sds(shape, bf16)] * 2, [],
                (weight * WORK, 0, 0), *stage)


def third_swap(stage):
    return stage[0], swap(stage[1], "dp", 2)


def fourth_stage(stage):
    mine, got = stage
    return add(mine[0], got[0]), add(mine[1], got[1])


def fourth_swap(stage):
    return stage[0], swap(stage[1], "dp", 4)


def fifth_stage(stage):
    return add(*stage)


def spread(final):
    other = swap(final, "mix", 2)
    return final, other, swap(final, "mix", 1), swap(other, "mix", 1)


def place_kernel(plan, vec, here, *refs):
    parts, outs = refs[:4], refs[4:]
    core, upper = here[0] & 1, (here[0] >> 1) & 1
    for i, part in enumerate(parts):
        c, y = core ^ (i // 2), upper ^ (i % 2)
        for u, (which, row, row_core, row_y, col_core, col_y, pieces) in enumerate(plan):
            r0 = pl.multiple_of(row + c * row_core + y * row_y, 8)
            at = 0
            for col, size in pieces:
                c0 = pl.multiple_of(col + c * col_core + y * col_y, 128)
                outs[which][pl.ds(r0, UNIT), pl.ds(c0, size)] = part[u * UNIT : (u + 1) * UNIT, at : at + size].astype(f32)
                at += size
    if vec:
        base = len(plan) * UNIT
        mine, other = parts[0][base : base + 8, :].astype(f32), parts[1][base : base + 8, :].astype(f32)
        lines = [jnp.where(upper == 0, mine, other), jnp.where(upper == 0, other, mine)]

        def slot(i):
            return lines[i // 9][i % 9 // 3 : i % 9 // 3 + 1, (i % 3) * 128 : (i % 3 + 1) * 128]

        vec_outs = outs[-13:]
        share = 96
        for i, target in zip((0, 1, 2, 3, 7, 8, 9, 10, 11), vec_outs[:9]):
            target[...] = slot(i)[0, :share]
        vec_outs[9][...] = jnp.concatenate([slot(12), slot(13), slot(14)], axis=1)[0]
        vec_outs[10][...] = jnp.concatenate([slot(4), slot(5), slot(6)], axis=0)[:, :share]
        vec_outs[11][...] = slot(15)[0, :3]
        losses = slot(16)
        pairs, count = vec_outs[12].shape
        lines = [losses[:, r * pairs : (r + 1) * pairs] for r in range(count)]
        lines = jnp.concatenate(lines + [jnp.zeros((8 - count % 8, pairs), f32)] if count % 8 else lines, axis=0)
        vec_outs[12][...] = jnp.concatenate([lines, jnp.zeros((lines.shape[0], 128 - pairs), f32)], axis=1).T[:pairs, :count]


def place_units(here, plan, shapes, parts, vec_shapes=()):
    shape = parts[0].shape
    vm = [whole(s) for s in list(shapes) + list(vec_shapes)]
    return call(
        functools.partial(place_kernel, plan, bool(vec_shapes)), "place_units", (),
        [SMEM_SPEC] + [whole(shape)] * 4, vm, [sds(s, f32) for s in list(shapes) + list(vec_shapes)], [],
        (0.5 * WORK, 0, 0), here, *parts)


def settle_kernel(value, out):
    out[...] = value[...]


def settle(value, weight):
    shape = value.shape
    block = pl.BlockSpec((shape[0] // 2,) + shape[1:], lambda k: (k, 0, 0, 0))
    (out,) = call(settle_kernel, "settle", (2,), [block], [block], [sds(shape, value.dtype)], [], (weight * WORK, 0, 0), value)
    return out.reshape(shape[0] * shape[1], *shape[2:])


def between(value):
    return lax.all_to_all(value, "mix", split_axis=0, concat_axis=0, tiled=True)


def on_device(
    tokens, cotangent, pair_lengths, labels, w_qkv, b_query, b_value, w_attn, b_attn, gain_one, shift_one,
    w_in, b_in, w_out, b_out, gain_two, shift_two, w_pool, b_pool, w_class, b_class,
):
    row_count, part_len, width = tokens.shape
    mixers = lax.axis_size("mix")
    dps = lax.axis_size("dp")
    rows_here = row_count // mixers
    seq = part_len * mixers
    units = w_in.shape[1]
    mix = lax.axis_index("mix").astype(jnp.int32)
    dp = lax.axis_index("dp").astype(jnp.int32)
    here = jnp.stack([mix, dp])
    pairs = pair_lengths.shape[1]
    lengths, classes = pair_lengths.T, labels.T
    quick = dps == 8 and mixers == 4 and width == 768 and units == 3072 and seq * rows_here == 1024 and rows_here == 2

    order = sorted(range(1, mixers), reverse=True)

    def exchange(blocks):
        got = {0: blocks[0]}
        for k in order:
            got[k] = swap(blocks[k], "mix", k)
        return [got[k] for k in range(mixers)]

    pack = jnp.concatenate(
        [b_query, b_value, b_attn, gain_one, shift_one, b_out, gain_two, shift_two, b_pool, b_in, b_class,
         jnp.zeros((3 * width - b_class.shape[0],), f32)]).reshape(16, width)

    def tie(first, second):
        return lax.optimization_barrier((first, second))

    cot = cotangent.reshape(mixers, rows_here, part_len, width)
    rows = ()
    def pieces(array, r):
        return [lax.dynamic_index_in_dim(array, (mix ^ k) * rows_here + r, 0, keepdims=False) for k in range(mixers)]

    blocks = pieces(tokens, 0)
    got = exchange(blocks)
    _, later = tie(blocks[0], tokens)
    for r in range(rows_here):
        if r + 1 < rows_here:
            (got, pack, here), (blocks, cot) = tie((got, pack, here), (pieces(later, r + 1), cot))
            following = exchange(blocks)
            cots = between(cot)
        rows = forward_row(r, rows_here, here, lengths, got, pack, w_qkv, w_attn, rows, (0.0, 15)[r])
        if r + 1 < rows_here:
            rows, got = tie(rows, following)
    qkv, probs, tok, mixture, hid, n1, rho1 = rows
    act, slope, outs, vec_ramp, sum_two, low, send = feed_forward(
        part_len, here, lengths, classes, hid, pack, w_in, w_out, w_pool, w_class.T, cots, quick)
    outs = between(outs)

    if not quick:
        return plain_rest(
            here, part_len, act, slope, outs, low, sum_two, vec_ramp, qkv, probs, tok, mixture, hid, n1, rho1, pack,
            w_qkv, w_attn, w_in, w_out, mix, dp, row_count, units)

    one = first_swap(out_units(here, 0, swap(send, "mix", 1), act.reshape(8, 2, 4, UNIT, rows_here * seq), low))
    _, sum_two = tie(one[0], sum_two)
    grad_up, vec_back, grad_att, sum_one, grad_mix = feed_backward(
        low, slope, w_out, w_in, sum_two, n1, rho1, vec_ramp, pack, w_attn)
    (outs, one), grad_up = tie((outs, one), grad_up)
    args = (hid, mixture, grad_up, grad_att, low)
    send = in_units(here, 1, None, *args)
    _, one = tie(send, one)
    one = second_swap(second_stage(one, 60, "stage_two_wide"))
    _, args = tie(one[0], args)
    two = first_swap(in_units(here, 0, swap(send, "mix", 1), *args))
    _, one = tie(two[0], one)
    one = third_swap(third_stage(one))
    _, grad_mix = tie(one[0], grad_mix)

    grad, vec_late, grad_tokens = attention_backward(here, part_len, qkv, probs, mixture, grad_mix, w_qkv, sum_one)
    grad_tokens = between(grad_tokens)
    (one, two), grad = tie((one, two), grad)
    send = qkv_units(here, 1, None, tok, grad, vec_back, vec_late)
    _, two = tie(send, two)
    two = second_swap(second_stage(two, 60, "stage_two_wide"))
    _, one = tie(two[0], one)
    one = fourth_swap(fourth_stage(one))
    _, grad = tie(one[0], grad)
    three = first_swap(qkv_units(here, 0, swap(send, "mix", 1), tok, grad, vec_back, vec_late))
    _, outs = tie(three[0], outs)
    output = settle(outs, 1)
    _, one = tie(output, one)
    final = fifth_stage(one)
    _, two = tie(final, two)
    two = third_swap(third_stage_kernel(two, 2))
    (_, grad_tokens), three = tie((two[0], grad_tokens), three)
    three = second_swap(second_stage(three, 60))
    _, two = tie(three[0], two)
    two = fourth_swap(fourth_stage(two))
    _, three = tie(two[0], three)
    three = third_swap(third_stage_kernel(three, 0.2))
    _, grad_tokens = tie(three[0], grad_tokens)
    grad_tokens = settle(grad_tokens, 0.5)
    _, two = tie(grad_tokens, two)
    final = jnp.concatenate([final, fifth_stage(two)], axis=0)
    _, three = tie(final, three)
    three = fourth_swap(fourth_stage(three))
    other = swap(final, "mix", 2)
    final = (final, other, swap(final, "mix", 1), swap(other, "mix", 1))
    other, three = tie(other, three)
    mine = fifth_stage(three)
    other = swap(mine, "mix", 2)
    far = swap(mine, "mix", 1)
    _, final = tie(mine, final)
    grad_w_out, grad_w_in, grad_w_attn, grad_w_pool = place_units(
        here, [(0, j * UNIT, 192, 0, 0, HALF, ((0, HALF),)) for j in range(4)]
        + [(1, 0, 0, UNIT, 4 * HALF, 0, ((j * HALF, HALF),)) for j in range(4)]
        + [(2, 0, 0, UNIT, HALF, 0, ((0, HALF),)), (3, 0, 0, UNIT, HALF, 0, ((0, HALF),))],
        [(384, width), (96, units), (96, width), (96, width)], final)
    _, other = tie(grad_w_in, other)
    three = (mine, other, far, swap(other, "mix", 1))
    share = width // dps
    last = place_units(
        here, [(0, 0, 0, UNIT, 128, 0, tuple((w * width + g * 256, 128) for w in range(3))) for g in range(3)],
        [(96, 3 * width)], three,
        [(share,)] * 9 + [(units // dps,), (w_class.shape[1], share), b_class.shape, (pairs, row_count)])
    (grad_w_qkv, grad_b_out, grad_gain_two, grad_shift_two, grad_b_pool, grad_gain_one, grad_shift_one, grad_b_attn,
     grad_b_query, grad_b_value, grad_b_in, grad_w_class, grad_b_class, pair_loss) = last
    return (
        output, pair_loss.T, grad_tokens, grad_w_qkv, grad_b_query, grad_b_value, grad_w_attn, grad_b_attn,
        grad_gain_one, grad_shift_one, grad_w_in, grad_b_in, grad_w_out, grad_b_out, grad_gain_two, grad_shift_two,
        grad_w_pool, grad_b_pool, grad_w_class.T, grad_b_class,
    )


def plain_rest(
    here, part_len, act, slope, outs, low, sum_two, vec_ramp, qkv, probs, tok, mixture, hid, n1, rho1, pack,
    w_qkv, w_attn, w_in, w_out, mix, dp, row_count, units,
):
    rows_here, _, seq, _ = qkv.shape
    total, width = n1.shape
    dps = lax.axis_size("dp")
    pairs = vec_ramp.shape[0] // rows_here
    grad_up, vec_back, grad_att, sum_one, grad_mix = feed_backward(
        low, slope, w_out, w_in, sum_two, n1, rho1, vec_ramp, pack, w_attn)
    grad, vec_late, grad_tokens = attention_backward(here, part_len, qkv, probs, mixture, grad_mix, w_qkv, sum_one)
    dqkv = grad.reshape(2, total, width // 256, 3, 128).transpose(1, 3, 2, 0, 4).reshape(total, 3 * width)
    output = outs.reshape(row_count, part_len, width)
    grad_tokens = between(grad_tokens).reshape(row_count, part_len, width)
    low, pool = low[:total], low[total:]
    grads = (tn(tok, dqkv), tn(mixture, grad_att), tn(hid, grad_up), nn(act, low), tn(pool[:16], pool[16:]))
    shards = [lax.psum_scatter(g, "dp", scatter_dimension=0, tiled=True) for g in grads]
    shards = [lax.psum(s.astype(bf16), "mix").astype(f32) for s in shards]
    bins = vec_back[3:7]
    vecs = jnp.concatenate([vec_ramp[:7], vec_back[:3], vec_late[:2], bins], axis=0)
    vecs = lax.psum(vecs, ("dp", "mix"))
    class_total = lax.psum(vec_ramp[7, :3], ("dp", "mix"))
    loss = lax.psum(vec_ramp[7, 128 : 128 + row_count * pairs], "mix").reshape(row_count, pairs)
    share = width // dps
    v = lax.dynamic_slice_in_dim(vecs, dp * share, share, axis=1)
    bin_share = lax.dynamic_slice_in_dim(vecs[12:].reshape(-1), dp * (units // dps), units // dps)
    return (
        output, loss, grad_tokens, shards[0], v[10], v[11], shards[1], v[9], v[7], v[8], shards[2], bin_share,
        shards[3], v[0], v[1], v[2], shards[4], v[3], v[4:7].T, class_total,
    )


def solution(mesh):
    wide = P("dp", "mix", None)
    split = P("dp", None)
    in_specs = (wide, wide, split, split) + (P(),) * 17
    out_specs = (
        wide, split, wide,
        split, P("dp"), P("dp"), split, P("dp"), P("dp"), P("dp"),
        split, P("dp"), split, P("dp"), P("dp"), P("dp"),
        split, P("dp"), split, P(),
    )
    return jax.shard_map(on_device, mesh=mesh, in_specs=in_specs, out_specs=out_specs, check_vma=False)
```

```python
import functools

import jax
import jax.numpy as jnp
from jax import lax
from jax.experimental import pallas as pl
from jax.experimental.pallas import tpu as pltpu
from jax.sharding import PartitionSpec as P

HEADS = 12
SCALE = 1.0
WORK = 5.8e8
GROUP = 4
CHUNK = 768
TILE = 256
UNIT = 48
HALF = 384
norm_eps = 1e-06
masked_score = -1000000000.0
inv_root_two = 0.7071067811865476
inv_root_tau = 0.3989422804014327
f32 = jnp.float32
bf16 = jnp.bfloat16
VMEM_LIMIT = 62 * 1024 * 1024
SMALL_LIMIT = 20 * 1024 * 1024
LIMITS = dict.fromkeys(("stage_two", "stage_three", "settle", "place_units"), SMALL_LIMIT)
SMEM_SPEC = pl.BlockSpec(memory_space=pltpu.SMEM)
B_QUERY, B_VALUE, B_ATTN, GAIN_ONE, SHIFT_ONE, B_OUT, GAIN_TWO, SHIFT_TWO, B_POOL, B_IN, B_CLASS = 0, 1, 2, 3, 4, 5, 6, 7, 8, 9, 13


def whole(shape):
    return pl.BlockSpec(shape, lambda *_: (0,) * len(shape))


def sds(shape, dtype):
    return jax.ShapeDtypeStruct(shape, dtype)


def nn(left, right):
    return jnp.dot(left, right, preferred_element_type=f32)


def nt(left, right):
    return lax.dot_general(left, right, (((1,), (1,)), ((), ())), preferred_element_type=f32)


def tn(left, right):
    return lax.dot_general(left, right, (((0,), (0,)), ((), ())), preferred_element_type=f32)


def call(kernel, name, grid, in_specs, out_specs, out_shape, scratch, work, *args, prefetch=0, aliases=None):
    common = dict(
        out_shape=out_shape,
        compiler_params=pltpu.CompilerParams(vmem_limit_bytes=LIMITS.get(name, VMEM_LIMIT)),
        cost_estimate=pl.CostEstimate(flops=int(2 * work[0] * SCALE), bytes_accessed=int(work[1] * SCALE), transcendentals=0),
        name=name,
        input_output_aliases=aliases or {},
    )
    if prefetch:
        spec = pltpu.PrefetchScalarGridSpec(
            num_scalar_prefetch=prefetch, grid=grid, in_specs=in_specs, out_specs=out_specs, scratch_shapes=scratch)
        return pl.pallas_call(kernel, grid_spec=spec, **common)(*args)
    return pl.pallas_call(
        kernel, grid=grid, in_specs=in_specs, out_specs=out_specs, scratch_shapes=scratch, **common)(*args)


def after(value, *earlier):
    return lax.optimization_barrier((value,) + earlier)[0]


def fetch(copies, start, wait):
    copies = [pltpu.make_async_copy(*copy) for copy in copies]

    @pl.when(start)
    def _():
        for copy in copies:
            copy.start()

    @pl.when(wait)
    def _():
        for copy in copies:
            copy.wait()


def mean_of(values):
    return jnp.mean(values, axis=-1, keepdims=True)


def col_sum(values):
    return jnp.sum(values, axis=0, keepdims=True)


def head_only(values, head, size):
    lane = lax.broadcasted_iota(jnp.int32, (1, values.shape[1]), 1) // size
    return jnp.where(lane == head, values, jnp.zeros((), values.dtype))


def per_head(values, size):
    return jnp.concatenate([head_only(values, h, size) for h in range(GROUP)], axis=0)


def segments(places, lengths, row):
    total = jnp.int32(0)
    seg = jnp.zeros(places.shape, jnp.int32)
    for k in range(lengths.shape[0]):
        total = total + lengths[k, row]
        seg = seg + (places >= total).astype(jnp.int32)
    return seg


def forward_kernel(row, rows_here, part_len, mixers, head_size, here, lengths, *refs):
    pieces, refs = refs[:mixers], refs[mixers:]
    pack, packq, packv, wq, wk, wv, wa = refs[:7]
    (qkv_o, probs_o, tok_o, mix_o, hid_o, n1_o, rho_o,
     tok_s, mix_s, bias_s, w_s, wa_s, sems) = refs[-13:]
    step = pl.program_id(0)
    fetch([(wa, wa_s, sems.at[0])], step == 0, step == pl.num_programs(0) - 1)
    seq = part_len * mixers
    shift = part_len.bit_length() - 1
    span = GROUP * head_size

    @pl.when(step == 0)
    def _():
        for i, piece in enumerate(pieces):
            tok_s[i * part_len : (i + 1) * part_len, :] = piece[...]
        mine = here[0]
        down = lax.broadcasted_iota(jnp.int32, (seq, 1), 0)
        across = lax.broadcasted_iota(jnp.int32, (1, seq), 1)

        def place(i):
            return (((i >> shift) ^ mine) << shift) + (i & (part_len - 1))

        number = mine * rows_here + row
        same = segments(place(down), lengths, number) == segments(place(across), lengths, number)
        bias_s[...] = jnp.where(same, 0.0, masked_score)

    for i, weight in enumerate((wq, wk, wv)):
        w_s[:, i * span : (i + 1) * span] = weight[...]
    qkv = nn(tok_s[...], w_s[...])
    qs = (qkv[:, :span] + packq[B_QUERY : B_QUERY + 1]).astype(bf16) * bf16(head_size ** (-0.5))
    keys = qkv[:, span : 2 * span].astype(bf16)
    values = (qkv[:, 2 * span :] + packv[B_VALUE : B_VALUE + 1]).astype(bf16)
    qkv_o[0, 0, :, :span] = qs
    qkv_o[0, 0, :, span : 2 * span] = keys
    qkv_o[0, 0, :, 2 * span :] = values
    scores = nt(keys, per_head(qs, head_size))
    values_t = values.T
    mixed = []
    for h in range(GROUP):
        at = slice(h * seq, (h + 1) * seq)
        part = scores[:, at] + bias_s[...]
        expo = jnp.exp(part - jnp.max(part, axis=0, keepdims=True))
        probs = (expo * (1.0 / col_sum(expo))).astype(bf16)
        probs_o[0, 0, :, at] = probs
        mixed.append(nn(values_t[h * head_size : (h + 1) * head_size], probs))
    mixed = jnp.concatenate(mixed, axis=0).astype(bf16).T
    here_columns = pl.ds(pl.multiple_of(step * span, 128), span)
    mix_s[:, here_columns] = mixed
    mix_o[...] = mixed
    tok_o[...] = tok_s[:, here_columns]

    @pl.when(step == pl.num_programs(0) - 1)
    def _():
        full = tok_s[...].astype(f32) + (nn(mix_s[...], wa_s[...]) + pack[B_ATTN : B_ATTN + 1])
        centre = full - mean_of(full)
        rho = lax.rsqrt(mean_of(centre * centre) + norm_eps)
        normed = centre * rho
        hidden = normed * pack[GAIN_ONE : GAIN_ONE + 1] + pack[SHIFT_ONE : SHIFT_ONE + 1]
        hid_o[...] = hidden.astype(bf16)
        n1_o[...] = normed.astype(bf16)
        rho_o[...] = jnp.broadcast_to(rho, rho_o.shape)


def forward_row(row, rows_here, here, lengths, pieces, pack, w_qkv, w_attn, earlier, weight_us):
    part_len, width = pieces[0].shape
    mixers = len(pieces)
    seq = part_len * mixers
    head_size = width // HEADS
    span = GROUP * head_size
    steps = width // span

    def weight(which):
        return pl.BlockSpec((width, span), lambda g: (0, which * steps + g))

    rows = pack.shape[0]
    column = pl.BlockSpec((rows, span), lambda g: (0, g))
    part = pl.BlockSpec((seq, span), lambda g: (row, g))
    wide = pl.BlockSpec((seq, width), lambda g: (row, 0))
    total = rows_here * seq
    specs = [SMEM_SPEC, SMEM_SPEC] + [whole((part_len, width))] * mixers
    specs += [whole((rows, width)), column, column, weight(0), weight(1), weight(2), pl.BlockSpec(memory_space=pl.ANY)]
    return call(
        functools.partial(forward_kernel, row, rows_here, part_len, mixers, head_size), "forward_row", (steps,),
        specs + [pl.BlockSpec(memory_space=pl.ANY)] * len(earlier),
        [pl.BlockSpec((1, 1, seq, 3 * span), lambda g: (row, g, 0, 0)),
         pl.BlockSpec((1, 1, seq, GROUP * seq), lambda g: (row, g, 0, 0)),
         part, part, wide, wide, pl.BlockSpec((seq, 128), lambda g: (row, 0))],
        [sds((rows_here, steps, seq, 3 * span), bf16), sds((rows_here, steps, seq, GROUP * seq), bf16)]
        + [sds((total, width), bf16)] * 4 + [sds((total, 128), f32)],
        [pltpu.VMEM((seq, width), bf16), pltpu.VMEM((seq, width), bf16), pltpu.VMEM((seq, seq), f32),
         pltpu.VMEM((width, 3 * span), bf16), pltpu.VMEM((width, width), bf16), pltpu.SemaphoreType.DMA((1,))],
        (weight_us * WORK, 0, 0),
        here, lengths, *pieces, pack, pack, pack, w_qkv, w_qkv, w_qkv, w_attn, *earlier,
        aliases={len(specs) + i: i for i in range(len(earlier))})


def start_spots(here, lengths, r, rows_here, part_len, pairs, seq):
    shift = part_len.bit_length() - 1
    spots = []
    start = jnp.int32(0)
    for k in range(pairs):
        spots.append(r * seq + (((start >> shift) ^ here[0]) << shift) + (start & (part_len - 1)))
        start = start + lengths[k, here[0] * rows_here + r]
    return spots


def feed_kernel(rows_here, part_len, pairs, mixers, send, here, lengths, labels, *refs):
    hid, pack, w_in, w_out, w_pool_any, w_class, cots_any = refs[:7]
    act_o, slope_o, out_o, vec_o, sum_o, low_o, send_o = refs[7:14]
    feed_s, normed_s, rho_s, act_s, acc_s, w_pool, cots, sems = refs[14:]
    step = pl.program_id(0)
    last = pl.num_programs(0) - 1
    fetch([(w_pool_any, w_pool, sems.at[0]), (cots_any, cots, sems.at[1])], step == 0, step == last)
    tokens, width = hid.shape
    seq = part_len * mixers
    count = tokens // TILE

    @pl.when(step == 0)
    def _():
        feed_s[...] = hid[...].astype(f32) + pack[B_OUT : B_OUT + 1]

    bias = pack[pl.ds(B_IN + step, 1), :]

    def rows(i):
        return slice(i * TILE, (i + 1) * TILE)

    up = nn(hid[rows(0), :], w_in[...])
    before = None
    for i in range(count):
        following = nn(hid[rows(i + 1), :], w_in[...]) if i + 1 < count else None
        up = up + bias
        half = 0.5 * (1.0 + lax.erf(up * inv_root_two))
        act = (up * half).astype(bf16)
        slope_o[rows(i), :] = (half + up * jnp.exp(-0.5 * up * up) * inv_root_tau).astype(bf16)
        turned = act.T
        act_o[:, rows(i)] = turned
        if send:
            blocks = CHUNK // (8 * UNIT)
            act_s[pl.ds(step * blocks, blocks), :, :, :, rows(i)] = turned.reshape(blocks, 2, 2, 2 * UNIT, TILE)
        if before is not None:
            feed_s[rows(i - 1), :] += nn(before, w_out[...])
        before, up = act, following
    feed_s[rows(count - 1), :] += nn(before, w_out[...])

    @pl.when(step == last)
    def _():
        gain = pack[GAIN_TWO : GAIN_TWO + 1]
        for r in range(rows_here):
            for k in range(mixers):
                at = slice(r * seq + k * part_len, r * seq + (k + 1) * part_len)
                full = feed_s[at, :]
                centre = full - mean_of(full)
                rho = lax.rsqrt(mean_of(centre * centre) + norm_eps)
                normed = centre * rho
                out = normed * gain + pack[SHIFT_TWO : SHIFT_TWO + 1]
                feed_s[at, :] = out
                out_o[here[0] ^ k, r] = out.astype(bf16)
                normed_s[at, :] = normed
                rho_s[at, :] = jnp.broadcast_to(rho, (part_len, 128))
        spots = []
        for r in range(rows_here):
            spots += start_spots(here, lengths, r, rows_here, part_len, pairs, seq)
        firsts = jnp.concatenate([feed_s[pl.ds(spot, 1), :] for spot in spots], axis=0)
        sums = [jnp.zeros((1, width), f32)] * 2

        def backward(i, sums):
            r, k = i // mixers, i % mixers
            at = slice(i * part_len, (i + 1) * part_len)
            e = cots[here[0] ^ k, r].astype(f32)
            normed = normed_s[at, :]
            eg = e * gain
            sum_o[at, :] = rho_s[at, 0:1] * (eg - mean_of(eg) - normed * mean_of(eg * normed))
            return [sums[0] + col_sum(e * normed), sums[1] + col_sum(e)]

        tiles = rows_here * mixers
        pool = w_pool[...]
        pool_high = pool.astype(bf16)
        pool_rest = (pool - pool_high.astype(f32)).astype(bf16)
        first_high = firsts.astype(bf16)
        first_rest = (firsts - first_high.astype(f32)).astype(bf16)
        pre = nn(jnp.concatenate([first_high, first_rest], axis=0), pool_high)
        pre = pre[: firsts.shape[0]] + pre[firsts.shape[0] :] + nn(first_high, pool_rest)
        for i in range(tiles // 2):
            sums = backward(i, sums)
        pooled = jnp.tanh(pre + pack[B_POOL : B_POOL + 1])
        classes = w_class.shape[0]
        here_pairs = rows_here * pairs
        class_t = w_class[...]
        lane = lax.broadcasted_iota(jnp.int32, (here_pairs, 128), 1)
        logits = jnp.full((here_pairs, 128), -jnp.inf, f32)
        for c in range(classes):
            logits = jnp.where(lane == c, jnp.sum(pooled * class_t[c : c + 1], axis=1, keepdims=True), logits)
        logits = logits + pack[B_CLASS : B_CLASS + 1, :128]
        top = jnp.max(logits, axis=-1, keepdims=True)
        expo = jnp.exp(logits - top)
        total = jnp.sum(expo, axis=-1, keepdims=True)
        log_total = top + jnp.log(total)
        sub = lax.broadcasted_iota(jnp.int32, (here_pairs, 128), 0)
        label = jnp.zeros((here_pairs, 128), jnp.int32)
        for r in range(rows_here):
            for k in range(pairs):
                label = jnp.where(sub == r * pairs + k, labels[k, here[0] * rows_here + r], label)
        chosen = lane == label
        loss = log_total - jnp.sum(jnp.where(chosen, logits, 0.0), axis=-1, keepdims=True)
        grad_logits = expo / total - chosen.astype(f32)
        grad_pooled = jnp.zeros((here_pairs, width), f32)
        for c in range(classes):
            grad_pooled = grad_pooled + grad_logits[:, c : c + 1] * class_t[c : c + 1]
        grad_pre = grad_pooled * (1.0 - pooled * pooled)
        grad_firsts = nt(grad_pre.astype(bf16), pool_high)
        for i in range(tiles // 2, tiles):
            sums = backward(i, sums)
        normed = jnp.concatenate([normed_s[pl.ds(spot, 1), :] for spot in spots], axis=0)
        rho = jnp.concatenate([rho_s[pl.ds(spot, 1), :] for spot in spots], axis=0)[:, 0:1]
        eg = grad_firsts * gain
        more = rho * (eg - mean_of(eg) - normed * mean_of(eg * normed))
        for i, spot in enumerate(spots):
            sum_o[pl.ds(spot, 1), :] = sum_o[pl.ds(spot, 1), :] + more[i : i + 1, :]
        vec_o[1:2, :] = sums[0] + col_sum(grad_firsts * normed)
        vec_o[2:3, :] = sums[1] + col_sum(grad_firsts)
        vec_o[3:4, :] = col_sum(grad_pre)
        for c in range(classes):
            vec_o[4 + c : 5 + c, :] = col_sum(pooled * grad_logits[:, c : c + 1])
        spread_loss = jnp.where(lane == here[0] * here_pairs + sub, loss, 0.0)
        vec_o[7:8, :] = jnp.concatenate(
            [col_sum(grad_logits), col_sum(spread_loss), jnp.zeros((1, width - 256), f32)], axis=1)
        none = jnp.zeros((16 - here_pairs, width), f32)
        low_o[tokens : tokens + 16, :] = jnp.concatenate([firsts, none], axis=0).astype(bf16)
        low_o[tokens + 16 :, :] = jnp.concatenate([grad_pre, none], axis=0).astype(bf16)
        bias_sum = jnp.zeros((1, width), f32)
        for i in range(count):
            low = sum_o[rows(i), :].astype(bf16)
            low_o[rows(i), :] = low
            bias_sum = bias_sum + col_sum(low.astype(f32))
        vec_o[0:1, :] = bias_sum
        if send:
            dp, upper = here[1], (here[0] >> 1) & 1
            other = 1 - (here[0] & 1)
            for j in range(2):
                acc_s[...] = nn(act_s[:, other, j].reshape(16 * UNIT, tokens), low_o[:tokens, :])
                store_sums([send_o], None, slice(j * 2 * UNIT, (j + 1) * 2 * UNIT), lambda p, y: acc_s[
                    pl.ds(pl.multiple_of((p ^ dp) * 2 * UNIT, 16), 2 * UNIT),
                    pl.ds(pl.multiple_of((upper ^ y) * HALF, 128), HALF)])
        else:
            send_o[...] = jnp.zeros(send_o.shape, bf16)


def feed_forward(part_len, here, lengths, labels, hid, pack, w_in, w_out, w_pool, w_class, cots, send):
    mixers, rows_here = cots.shape[:2]
    tokens, width = hid.shape
    pairs = lengths.shape[0]
    units = w_in.shape[1]
    steps = units // CHUNK
    sent = (16, 4 * UNIT, HALF) if send else (16, 128)
    act_shape = (units // (8 * UNIT), 2, 2, 2 * UNIT, tokens) if send else (8, 128)
    acc_shape = (16 * UNIT, width) if send else (8, 128)
    return call(
        functools.partial(feed_kernel, rows_here, part_len, pairs, mixers, send), "feed_forward", (steps,),
        [SMEM_SPEC] * 3
        + [whole(hid.shape), whole(pack.shape), pl.BlockSpec((width, CHUNK), lambda c: (0, c)),
           pl.BlockSpec((CHUNK, width), lambda c: (c, 0)), pl.BlockSpec(memory_space=pl.ANY), whole(w_class.shape), pl.BlockSpec(memory_space=pl.ANY)],
        [pl.BlockSpec((CHUNK, tokens), lambda c: (c, 0)), pl.BlockSpec((tokens, CHUNK), lambda c: (0, c)),
         whole(cots.shape), whole((8, width)), whole((tokens, width)), whole((tokens + 32, width)), whole(sent)],
        [sds((units, tokens), bf16), sds((tokens, units), bf16), sds(cots.shape, bf16), sds((8, width), f32),
         sds((tokens, width), f32), sds((tokens + 32, width), bf16), sds(sent, bf16)],
        [pltpu.VMEM((tokens, width), f32), pltpu.VMEM((tokens, width), f32), pltpu.VMEM((tokens, 128), f32),
         pltpu.VMEM(act_shape, bf16), pltpu.VMEM(acc_shape, f32), pltpu.VMEM(w_pool.shape, f32), pltpu.VMEM(cots.shape, bf16),
         pltpu.SemaphoreType.DMA((2,))],
        (2 * tokens * width * units, 35e6, 0),
        here, lengths, labels, hid, pack, w_in, w_out, w_pool, w_class, cots)


def back_kernel(
    low, slope, w_out, w_in, ramp, pack, *refs,
):
    from_any, (up_o, vec_o, att_o, sum_o, mix_o, hid_s), kept, sems = refs[:4], refs[4:10], refs[10:14], refs[14]
    sum_two, w_attn, n1, rho = kept
    step = pl.program_id(0)
    last = pl.num_programs(0) - 1
    fetch([(a, b, sems.at[i]) for i, (a, b) in enumerate(zip(from_any, kept))], step == 0, step == last)
    count = slope.shape[0] // TILE

    def rows(i):
        return slice(i * TILE, (i + 1) * TILE)

    @pl.when(step == 0)
    def _():
        hid_s[...] = jnp.zeros(hid_s.shape, f32)
        vec_o[7:8, :] = jnp.zeros((1, vec_o.shape[1]), f32)
        vec_o[8:16, :] = ramp[...]

    total = jnp.zeros((1, slope.shape[1]), f32)
    act = nt(low[rows(0), :], w_out[...])
    before = None
    for i in range(count):
        following = nt(low[rows(i + 1), :], w_out[...]) if i + 1 < count else None
        up = (act * slope[rows(i), :].astype(f32)).astype(bf16)
        up_o[rows(i), :] = up
        total = total + col_sum(up.astype(f32))
        if before is not None:
            hid_s[rows(i - 1), :] += nt(before, w_in[...])
        before, act = up, following
    hid_s[rows(count - 1), :] += nt(before, w_in[...])
    vec_o[pl.ds(3 + step, 1), :] = total

    @pl.when(step == last)
    def _():
        width = pack.shape[1]
        sums = [jnp.zeros((1, width), f32)] * 3
        for i in range(count):
            at = rows(i)
            e = hid_s[at, :] + sum_two[at, :]
            normed = n1[at, :].astype(f32)
            eg = e * pack[GAIN_ONE : GAIN_ONE + 1]
            grad = rho[at, 0:1] * (eg - mean_of(eg) - normed * mean_of(eg * normed))
            sum_o[at, :] = grad
            att = grad.astype(bf16)
            att_o[at, :] = att
            mix_o[at, :] = nt(att, w_attn[...]).astype(bf16)
            sums = [sums[0] + col_sum(e * normed), sums[1] + col_sum(e), sums[2] + col_sum(att.astype(f32))]
        for i in range(3):
            vec_o[i : i + 1, :] = sums[i]


def feed_backward(low, slope, w_out, w_in, sum_two, n1, rho, ramp, pack, w_attn):
    count, width = n1.shape
    units = slope.shape[1]
    block = pl.BlockSpec((count, CHUNK), lambda j: (0, j))
    late = (sum_two, w_attn, n1, rho)
    return call(
        back_kernel, "feed_backward", (units // CHUNK,),
        [whole(low.shape), block, pl.BlockSpec((CHUNK, width), lambda j: (j, 0)), pl.BlockSpec((width, CHUNK), lambda j: (0, j)),
         whole((8, width)), whole(pack.shape)] + [pl.BlockSpec(memory_space=pl.ANY)] * 4,
        [block, whole((16, width))] + [whole((count, width))] * 3,
        [sds((count, units), bf16), sds((16, width), f32), sds((count, width), bf16), sds((count, width), f32),
         sds((count, width), bf16)],
        [pltpu.VMEM((count, width), f32)] + [pltpu.VMEM(a.shape, a.dtype) for a in late] + [pltpu.SemaphoreType.DMA((4,))],
        (2 * count * width * units + count * width * width, 40e6, 0),
        low, slope, w_out, w_in, ramp, pack, *late)


def attention_back_kernel(
    head_size, part_len, mixers, here, qkv_r, probs_r, mix_r, grad_r, wq, wk, wv, sum_any,
    d_o, vec_o, tok_o, acc_s, w_s, vec_s, sum_one, sems,
):
    row = pl.program_id(0)
    step = pl.program_id(1)
    last = pl.num_programs(1) - 1
    rows_at = pl.ds(pl.multiple_of(row * sum_one.shape[0], 8), sum_one.shape[0])
    fetch([(sum_any.at[rows_at], sum_one, sems.at[0])], step == 0, step == last)
    span = GROUP * head_size
    seq = qkv_r.shape[2]
    qs, keys, values = qkv_r[0, 0, :, :span], qkv_r[0, 0, :, span : 2 * span], qkv_r[0, 0, :, 2 * span :]
    grad = grad_r[...]
    for i, weight in enumerate((wq, wk, wv)):
        w_s[:, i * span : (i + 1) * span] = weight[...]
    prod = grad.T.astype(f32) * mix_r[...].T.astype(f32)
    keys_t = keys.T
    grad_heads = per_head(grad, head_size)
    grad_probs = nt(values, grad_heads)
    parts, dq_t = [], []
    for h in range(GROUP):
        rows = slice(h * head_size, (h + 1) * head_size)
        at = slice(h * seq, (h + 1) * seq)
        part = (probs_r[0, 0, :, at].astype(f32) * (grad_probs[:, at] - col_sum(prod[rows]))).astype(bf16)
        parts.append(part)
        dq_t.append(nn(keys_t[rows], part))
    grad_scores = jnp.concatenate(parts, axis=1)
    dv = nn(probs_r[0, 0], grad_heads).astype(bf16)
    dk = nn(grad_scores, per_head(qs, head_size)).astype(bf16)
    dq = (jnp.concatenate(dq_t, axis=0) * (head_size ** (-0.5))).astype(bf16).T
    all_three = jnp.concatenate([dq, dk, dv], axis=1)
    half = span // 2
    for c in range(2):
        at = slice(c * half, (c + 1) * half)
        d_o[c] = jnp.concatenate([dq[:, at], dk[:, at], dv[:, at]], axis=1)
    vec = jnp.concatenate([col_sum(dq.astype(f32)), col_sum(dv.astype(f32)), jnp.zeros((6, span), f32)], axis=0)

    @pl.when(row == 0)
    def _():
        vec_s[step] = vec

    @pl.when(row > 0)
    def _():
        vec_s[step] += vec

    part = nt(all_three, w_s[...])

    @pl.when(step == 0)
    def _():
        acc_s[...] = part

    @pl.when(step > 0)
    def _():
        acc_s[...] += part

    @pl.when(step == last)
    def _():
        steps = vec_s.shape[0]
        for k in range(mixers):
            tok_o[here[0] ^ k, 0] = (acc_s[k * part_len : (k + 1) * part_len, :] + sum_one[k * part_len : (k + 1) * part_len, :]).astype(bf16)
        vec_o[...] = jnp.concatenate([vec_s[g] for g in range(steps)], axis=1)


def attention_backward(here, part_len, qkv, probs, mix, grad_mix, w_qkv, sum_one):
    rows_here, steps, seq, _ = qkv.shape
    total, width = grad_mix.shape
    head_size = width // HEADS
    span = GROUP * head_size
    mixers = seq // part_len
    part = pl.BlockSpec((seq, span), lambda r, g: (r, g))

    def weight(which):
        return pl.BlockSpec((width, span), lambda r, g: (0, which * steps + g))

    return call(
        functools.partial(attention_back_kernel, head_size, part_len, mixers), "attention_backward", (rows_here, steps),
        [SMEM_SPEC, pl.BlockSpec((1, 1, seq, 3 * span), lambda r, g: (r, g, 0, 0)),
         pl.BlockSpec((1, 1, seq, GROUP * seq), lambda r, g: (r, g, 0, 0)), part, part,
         weight(0), weight(1), weight(2), pl.BlockSpec(memory_space=pl.ANY)],
        [pl.BlockSpec((2, seq, 3 * span // 2), lambda r, g: (0, r, g)), whole((8, width)),
         pl.BlockSpec((mixers, 1, part_len, width), lambda r, g: (0, r, 0, 0))],
        [sds((2, total, 3 * width // 2), bf16), sds((8, width), f32), sds((mixers, rows_here, part_len, width), bf16)],
        [pltpu.VMEM((seq, width), f32), pltpu.VMEM((width, 3 * span), bf16), pltpu.VMEM((steps, 8, span), f32),
         pltpu.VMEM((seq, width), f32), pltpu.SemaphoreType.DMA((1,))],
        (rows_here * (3 * seq * width * width + 16 * seq * seq * width), 18e6, 0),
        here, qkv, probs, mix, grad_mix, w_qkv, w_qkv, w_qkv, sum_one)


def store_sums(outs, got, rows, read):
    for p in range(8):
        for y in range(2):
            value = read(p, y)
            if got is None:
                outs[0][p * 2 + y, rows, :] = value.astype(bf16)
                continue
            value = (value + got[p * 2 + y, rows, :].astype(f32)).astype(bf16)
            xk, xs, yk, ys = outs
            z2, z1, x = p // 4, p // 2 % 2, p % 2
            if z1 == 0:
                (xk, xs)[x][z2, y, rows, :] = value
            else:
                (yk, ys)[y][z2, x, rows, :] = value


def natural(acc, p, y, dp, upper, columns):
    return acc[pl.ds(pl.multiple_of((p ^ dp) * 2 * UNIT + (y ^ upper) * UNIT, 16), UNIT), columns]


def split_refs(flip, refs):
    return (refs[0], None, refs[1:]) if flip else (refs[1:5], refs[0], refs[5:])


def unit_call(kernel, name, flip, grid, in_specs, rows, step_rows, scratch, work, here, *args, got=None):
    if flip:
        specs, shapes = [pl.BlockSpec((16, step_rows, HALF), lambda j, s: (0, j, 0))], [sds((16, rows, HALF), bf16)]
    else:
        in_specs = in_specs + [pl.BlockSpec((16, step_rows, HALF), lambda j, s: (0, j, 0))]
        args = args + (got,)
        specs = [pl.BlockSpec((2, 2, step_rows, HALF), lambda j, s: (0, 0, j, 0))] * 4
        shapes = [sds((2, 2, rows, HALF), bf16)] * 4
    out = call(kernel, name, (grid,), in_specs, specs, shapes, scratch, work, here, *args, prefetch=1)
    return out[0] if flip else out


def out_units_kernel(flip, here, act, low, *refs):
    outs, got, (acc_s,) = split_refs(flip, refs)
    outs = [outs] if flip else outs
    dp, upper = here[1], (here[0] >> 1) & 1
    count = act.shape[-1]
    acc_s[...] = nn(act[...].reshape(16 * UNIT, count), low[:count])
    at = [pl.multiple_of((upper ^ y) * HALF, 128) for y in range(2)]
    store_sums(outs, got, slice(None), lambda p, y: acc_s[
        pl.ds(pl.multiple_of((p ^ dp) * 2 * UNIT, 16), 2 * UNIT), pl.ds(at[y], HALF)])


def out_units(here, flip, got, act, low):
    width = low.shape[1]
    count = act.shape[-1]
    return unit_call(
        functools.partial(out_units_kernel, flip), "units_out", flip, 2,
        [pl.BlockSpec((8, 1, 2, UNIT, count), lambda j, s: (0, (s[0] & 1) ^ flip, j, 0, 0)), whole(low.shape)],
        4 * UNIT, 2 * UNIT, [pltpu.VMEM((16 * UNIT, width), f32)], (4 * 8 * UNIT * count * width, 5e6, 0),
        here, act, low, got=got)


def in_units_kernel(flip, here, hid, mix, up, att, low, *refs):
    outs, got, (acc_s, mix_s, att_s, sems) = split_refs(flip, refs)
    outs = [outs] if flip else outs
    step = pl.program_id(0)
    dp = here[1]
    core, upper = (here[0] & 1) ^ flip, (here[0] >> 1) & 1

    column = pl.ds(pl.multiple_of(core * HALF, 128), HALF)
    copies = [
        pltpu.make_async_copy(mix, mix_s, sems.at[0]),
        pltpu.make_async_copy(att.at[:, column], att_s, sems.at[1]),
    ]

    @pl.when(step == 0)
    def _():
        for copy in copies:
            copy.start()

    @pl.when(step < 2)
    def _():
        acc_s[...] = tn(hid[...], up[...])

    @pl.when(step == 2)
    def _():
        for copy in copies:
            copy.wait()
        acc_s[:, :HALF] = tn(mix_s[...], att_s[...])
        right = low[16:32, :]
        acc_s[:, HALF:] = tn(low[:16, :], jnp.where(core == 0, right[:, :HALF], right[:, HALF:]))

    for u in range(2):
        store_sums(outs, got, slice(u * UNIT, (u + 1) * UNIT), lambda p, y: natural(
            acc_s, p, y, dp, upper, slice(u * HALF, (u + 1) * HALF)))


def in_units(here, flip, got, hid, mix, up, att, low):
    count, width = hid.shape
    return unit_call(
        functools.partial(in_units_kernel, flip), "units_in", flip, 3,
        [whole((count, width)), pl.BlockSpec(memory_space=pl.ANY),
         pl.BlockSpec((count, 2 * HALF), lambda j, s: (0, ((s[0] & 1) ^ flip) * 2 + jnp.minimum(j, 1))),
         pl.BlockSpec(memory_space=pl.ANY), pl.BlockSpec((32, width), lambda j, s: (count // 32, 0))],
        6 * UNIT, 2 * UNIT,
        [pltpu.VMEM((width, 2 * HALF), f32), pltpu.VMEM((count, width), bf16), pltpu.VMEM((count, HALF), bf16),
         pltpu.SemaphoreType.DMA((2,))],
        (5 * width * HALF * count, 5e6, 0),
        here, hid, mix, up, att, low, got=got)


VEC_ROWS = 16


DIGITS = 6
CLASSES = 3


def to_digits(values):
    out = jnp.zeros(values.shape, f32)
    rest = values
    for i in range(DIGITS):
        digit = jnp.floor(rest + 0.5)
        rest = (rest - digit) * 8.0
        moved = digit if i == 0 else jnp.concatenate(
            [jnp.zeros((1, i * CLASSES), f32), digit[:, : digit.shape[1] - i * CLASSES]], axis=1)
        out = out + moved
    return out


def from_digits(values):
    return sum(values[:, i * CLASSES : (i + 1) * CLASSES] * (0.125**i) for i in range(DIGITS))


def qkv_units_kernel(flip, here, tok, grad, back, late, *refs):
    outs, got, (acc_s, tab_s) = split_refs(flip, refs)
    outs = [outs] if flip else outs
    dp, upper = here[1], (here[0] >> 1) & 1
    acc_s[...] = tn(tok[...], grad[0])
    for u in range(3):
        store_sums(outs, got, slice(u * UNIT, (u + 1) * UNIT), lambda p, y: natural(
            acc_s, p, y, dp, upper, slice(u * HALF, (u + 1) * HALF)))
    ramp = back[8:16, :]
    units = jnp.concatenate([back[3 + i : 4 + i, :] for i in range(4)], axis=1)
    short = jnp.concatenate(
        [ramp[0:7], back[0:3, :], late[0:2, :], jnp.zeros((4, ramp.shape[1]), f32)], axis=0)
    share = short.shape[1] // 8
    fill = jnp.zeros((16, 128 - share), f32)
    blank = jnp.zeros((VEC_ROWS - 3, HALF), f32)
    class_sums = to_digits(ramp[7:8, :128])
    for b in range(8):
        slots = jnp.concatenate([short[:, b * share : (b + 1) * share], fill], axis=1)
        slots = [slots[i : i + 1] for i in range(12)]
        slots += [units[:, b * HALF + i * 128 : b * HALF + (i + 1) * 128] for i in range(3)]
        slots += [class_sums, jnp.where(dp == b, ramp[7:8, 128:256], 0.0), jnp.zeros((1, 128), f32)]
        lines = [jnp.concatenate(slots[i * 3 : i * 3 + 3], axis=1) for i in range(6)]
        for y in range(2):
            tab_s[b, y] = jnp.concatenate(lines[y * 3 : y * 3 + 3] + [blank], axis=0)
    store_sums(outs, got, slice(3 * UNIT, 3 * UNIT + VEC_ROWS), lambda p, y: tab_s[p ^ dp, y ^ upper])


def qkv_units(here, flip, got, tok, grad, back, late):
    count, width = tok.shape
    rows = 3 * UNIT + VEC_ROWS
    wide = 3 * HALF
    return unit_call(
        functools.partial(qkv_units_kernel, flip), "units_qkv", flip, 1,
        [whole((count, width)), pl.BlockSpec((1, count, wide), lambda j, s: ((s[0] & 1) ^ flip, 0, 0)),
         whole((16, width)), whole((8, width))],
        rows, rows, [pltpu.VMEM((width, wide), f32), pltpu.VMEM((8, 2, VEC_ROWS, HALF), f32)],
        (width * wide * count, 5e6, 0), here, tok, grad, back, late, got=got)


def second_kernel(xk, xr, yk, yr, x2k, x2s, y2k, y2s):
    x = xk[0].astype(f32) + xr[0].astype(f32)
    x2k[0] = x[0].astype(bf16)
    x2s[0] = x[1].astype(bf16)
    y = yk[0].astype(f32) + yr[0].astype(f32)
    y2k[0] = y[0].astype(bf16)
    y2s[0] = y[1].astype(bf16)


def add(left, right):
    return (left.astype(f32) + right.astype(f32)).astype(bf16)


def swap(value, axis, bit):
    size = lax.axis_size(axis)
    return lax.ppermute(value, axis, [(i, i ^ bit) for i in range(size)])


def first_swap(stage):
    xk, xs, yk, ys = stage
    return xk, swap(xs, "dp", 1), yk, swap(ys, "mix", 2)


def second_stage(stage, weight, name="stage_two"):
    rows = stage[0].shape[2]
    block = pl.BlockSpec((1, 2, rows, HALF), lambda z: (z, 0, 0, 0))
    out = pl.BlockSpec((1, rows, HALF), lambda z: (z, 0, 0))
    return call(second_kernel, name, (2,), [block] * 4, [out] * 4, [sds((2, rows, HALF), bf16)] * 4, [],
                (weight * WORK, 0, 0), *stage)


def second_swap(stage):
    xk, xs, yk, ys = stage
    return xk, swap(xs, "mix", 2), yk, swap(ys, "dp", 1)


def third_stage(stage):
    xk, xr, yk, yr = stage
    return add(xk, xr), add(yk, yr)


def third_kernel(xk, xr, yk, yr, keep, send):
    keep[...] = add(xk[...], xr[...])
    send[...] = add(yk[...], yr[...])


def third_stage_kernel(stage, weight):
    shape = stage[0].shape
    block = pl.BlockSpec((1,) + shape[1:], lambda z: (z, 0, 0))
    return call(third_kernel, "stage_three", (2,), [block] * 4, [block] * 2, [sds(shape, bf16)] * 2, [],
                (weight * WORK, 0, 0), *stage)


def third_swap(stage):
    return stage[0], swap(stage[1], "dp", 2)


def fourth_stage(stage):
    mine, got = stage
    return add(mine[0], got[0]), add(mine[1], got[1])


def fourth_swap(stage):
    return stage[0], swap(stage[1], "dp", 4)


def fifth_stage(stage):
    return add(*stage)


def spread(final):
    other = swap(final, "mix", 2)
    return final, other, swap(final, "mix", 1), swap(other, "mix", 1)


def place_kernel(plan, vec, here, *refs):
    parts, outs = refs[:4], refs[4:]
    core, upper = here[0] & 1, (here[0] >> 1) & 1
    for i, part in enumerate(parts):
        c, y = core ^ (i // 2), upper ^ (i % 2)
        for u, (which, row, row_core, row_y, col_core, col_y, pieces) in enumerate(plan):
            r0 = pl.multiple_of(row + c * row_core + y * row_y, 8)
            at = 0
            for col, size in pieces:
                c0 = pl.multiple_of(col + c * col_core + y * col_y, 128)
                outs[which][pl.ds(r0, UNIT), pl.ds(c0, size)] = part[u * UNIT : (u + 1) * UNIT, at : at + size].astype(f32)
                at += size
    if vec:
        base = len(plan) * UNIT
        mine, other = parts[0][base : base + 8, :].astype(f32), parts[1][base : base + 8, :].astype(f32)
        lines = [jnp.where(upper == 0, mine, other), jnp.where(upper == 0, other, mine)]

        def slot(i):
            return lines[i // 9][i % 9 // 3 : i % 9 // 3 + 1, (i % 3) * 128 : (i % 3 + 1) * 128]

        vec_outs = outs[-13:]
        share = 96
        for i, target in zip((0, 1, 2, 3, 7, 8, 9, 10, 11), vec_outs[:9]):
            target[...] = slot(i)[0, :share]
        vec_outs[9][...] = jnp.concatenate([slot(12), slot(13), slot(14)], axis=1)[0]
        vec_outs[10][...] = jnp.concatenate([slot(4), slot(5), slot(6)], axis=0)[:, :share]
        vec_outs[11][...] = from_digits(slot(15))[0]
        losses = slot(16)
        pairs, count = vec_outs[12].shape
        lines = [losses[:, r * pairs : (r + 1) * pairs] for r in range(count)]
        lines = jnp.concatenate(lines + [jnp.zeros((8 - count % 8, pairs), f32)] if count % 8 else lines, axis=0)
        vec_outs[12][...] = jnp.concatenate([lines, jnp.zeros((lines.shape[0], 128 - pairs), f32)], axis=1).T[:pairs, :count]


def place_units(here, plan, shapes, parts, vec_shapes=()):
    shape = parts[0].shape
    vm = [whole(s) for s in list(shapes) + list(vec_shapes)]
    return call(
        functools.partial(place_kernel, plan, bool(vec_shapes)), "place_units", (),
        [SMEM_SPEC] + [whole(shape)] * 4, vm, [sds(s, f32) for s in list(shapes) + list(vec_shapes)], [],
        (0.5 * WORK, 0, 0), here, *parts)


def settle_kernel(value, out):
    out[...] = value[...]


def settle(value, weight):
    shape = value.shape
    block = pl.BlockSpec((shape[0] // 2,) + shape[1:], lambda k: (k, 0, 0, 0))
    (out,) = call(settle_kernel, "settle", (2,), [block], [block], [sds(shape, value.dtype)], [], (weight * WORK, 0, 0), value)
    return out.reshape(shape[0] * shape[1], *shape[2:])


def between(value):
    return lax.all_to_all(value, "mix", split_axis=0, concat_axis=0, tiled=True)


def on_device(
    tokens, cotangent, pair_lengths, labels, w_qkv, b_query, b_value, w_attn, b_attn, gain_one, shift_one,
    w_in, b_in, w_out, b_out, gain_two, shift_two, w_pool, b_pool, w_class, b_class,
):
    row_count, part_len, width = tokens.shape
    mixers = lax.axis_size("mix")
    dps = lax.axis_size("dp")
    rows_here = row_count // mixers
    seq = part_len * mixers
    units = w_in.shape[1]
    mix = lax.axis_index("mix").astype(jnp.int32)
    dp = lax.axis_index("dp").astype(jnp.int32)
    here = jnp.stack([mix, dp])
    pairs = pair_lengths.shape[1]
    lengths, classes = pair_lengths.T, labels.T
    quick = dps == 8 and mixers == 4 and width == 768 and units == 3072 and seq * rows_here == 1024 and rows_here == 2

    order = sorted(range(1, mixers), reverse=True)

    def exchange(blocks):
        got = {0: blocks[0]}
        for k in order:
            got[k] = swap(blocks[k], "mix", k)
        return [got[k] for k in range(mixers)]

    pack = jnp.concatenate(
        [b_query, b_value, b_attn, gain_one, shift_one, b_out, gain_two, shift_two, b_pool, b_in, b_class,
         jnp.zeros((3 * width - b_class.shape[0],), f32)]).reshape(16, width)

    def tie(first, second):
        return lax.optimization_barrier((first, second))

    cot = cotangent.reshape(mixers, rows_here, part_len, width)
    rows = ()
    def pieces(array, r):
        return [lax.dynamic_index_in_dim(array, (mix ^ k) * rows_here + r, 0, keepdims=False) for k in range(mixers)]

    blocks = pieces(tokens, 0)
    got = exchange(blocks)
    _, later = tie(blocks[0], tokens)
    for r in range(rows_here):
        if r + 1 < rows_here:
            (got, pack, here), (blocks, cot) = tie((got, pack, here), (pieces(later, r + 1), cot))
            following = exchange(blocks)
            cots = between(cot)
        rows = forward_row(r, rows_here, here, lengths, got, pack, w_qkv, w_attn, rows, (0.0, 15)[r])
        if r + 1 < rows_here:
            rows, got = tie(rows, following)
    qkv, probs, tok, mixture, hid, n1, rho1 = rows
    act, slope, outs, vec_ramp, sum_two, low, send = feed_forward(
        part_len, here, lengths, classes, hid, pack, w_in, w_out, w_pool, w_class.T, cots, quick)
    outs = between(outs)

    if not quick:
        return plain_rest(
            here, part_len, act, slope, outs, low, sum_two, vec_ramp, qkv, probs, tok, mixture, hid, n1, rho1, pack,
            w_qkv, w_attn, w_in, w_out, mix, dp, row_count, units)

    one = first_swap(out_units(here, 0, swap(send, "mix", 1), act.reshape(8, 2, 4, UNIT, rows_here * seq), low))
    _, sum_two = tie(one[0], sum_two)
    grad_up, vec_back, grad_att, sum_one, grad_mix = feed_backward(
        low, slope, w_out, w_in, sum_two, n1, rho1, vec_ramp, pack, w_attn)
    (outs, one), grad_up = tie((outs, one), grad_up)
    args = (hid, mixture, grad_up, grad_att, low)
    send = in_units(here, 1, None, *args)
    _, one = tie(send, one)
    one = second_swap(second_stage(one, 60, "stage_two_wide"))
    _, args = tie(one[0], args)
    two = first_swap(in_units(here, 0, swap(send, "mix", 1), *args))
    _, one = tie(two[0], one)
    one = third_swap(third_stage(one))
    _, grad_mix = tie(one[0], grad_mix)

    grad, vec_late, grad_tokens = attention_backward(here, part_len, qkv, probs, mixture, grad_mix, w_qkv, sum_one)
    grad_tokens = between(grad_tokens)
    (one, two), grad = tie((one, two), grad)
    send = qkv_units(here, 1, None, tok, grad, vec_back, vec_late)
    _, two = tie(send, two)
    two = second_swap(second_stage(two, 60, "stage_two_wide"))
    _, one = tie(two[0], one)
    one = fourth_swap(fourth_stage(one))
    _, grad = tie(one[0], grad)
    three = first_swap(qkv_units(here, 0, swap(send, "mix", 1), tok, grad, vec_back, vec_late))
    _, outs = tie(three[0], outs)
    output = settle(outs, 1)
    _, one = tie(output, one)
    final = fifth_stage(one)
    _, two = tie(final, two)
    two = third_swap(third_stage_kernel(two, 2))
    (_, grad_tokens), three = tie((two[0], grad_tokens), three)
    three = second_swap(second_stage(three, 60))
    _, two = tie(three[0], two)
    two = fourth_swap(fourth_stage(two))
    _, three = tie(two[0], three)
    three = third_swap(third_stage_kernel(three, 0.2))
    _, grad_tokens = tie(three[0], grad_tokens)
    grad_tokens = settle(grad_tokens, 0.5)
    _, two = tie(grad_tokens, two)
    final = jnp.concatenate([final, fifth_stage(two)], axis=0)
    _, three = tie(final, three)
    three = fourth_swap(fourth_stage(three))
    other = swap(final, "mix", 2)
    final = (final, other, swap(final, "mix", 1), swap(other, "mix", 1))
    other, three = tie(other, three)
    mine = fifth_stage(three)
    other = swap(mine, "mix", 2)
    far = swap(mine, "mix", 1)
    _, final = tie(mine, final)
    grad_w_out, grad_w_in, grad_w_attn, grad_w_pool = place_units(
        here, [(0, j * UNIT, 192, 0, 0, HALF, ((0, HALF),)) for j in range(4)]
        + [(1, 0, 0, UNIT, 4 * HALF, 0, ((j * HALF, HALF),)) for j in range(4)]
        + [(2, 0, 0, UNIT, HALF, 0, ((0, HALF),)), (3, 0, 0, UNIT, HALF, 0, ((0, HALF),))],
        [(384, width), (96, units), (96, width), (96, width)], final)
    _, other = tie(grad_w_in, other)
    three = (mine, other, far, swap(other, "mix", 1))
    share = width // dps
    last = place_units(
        here, [(0, 0, 0, UNIT, 128, 0, tuple((w * width + g * 256, 128) for w in range(3))) for g in range(3)],
        [(96, 3 * width)], three,
        [(share,)] * 9 + [(units // dps,), (w_class.shape[1], share), b_class.shape, (pairs, row_count)])
    (grad_w_qkv, grad_b_out, grad_gain_two, grad_shift_two, grad_b_pool, grad_gain_one, grad_shift_one, grad_b_attn,
     grad_b_query, grad_b_value, grad_b_in, grad_w_class, grad_b_class, pair_loss) = last
    return (
        output, pair_loss.T, grad_tokens, grad_w_qkv, grad_b_query, grad_b_value, grad_w_attn, grad_b_attn,
        grad_gain_one, grad_shift_one, grad_w_in, grad_b_in, grad_w_out, grad_b_out, grad_gain_two, grad_shift_two,
        grad_w_pool, grad_b_pool, grad_w_class.T, grad_b_class,
    )


def plain_rest(
    here, part_len, act, slope, outs, low, sum_two, vec_ramp, qkv, probs, tok, mixture, hid, n1, rho1, pack,
    w_qkv, w_attn, w_in, w_out, mix, dp, row_count, units,
):
    rows_here, _, seq, _ = qkv.shape
    total, width = n1.shape
    dps = lax.axis_size("dp")
    pairs = vec_ramp.shape[0] // rows_here
    grad_up, vec_back, grad_att, sum_one, grad_mix = feed_backward(
        low, slope, w_out, w_in, sum_two, n1, rho1, vec_ramp, pack, w_attn)
    grad, vec_late, grad_tokens = attention_backward(here, part_len, qkv, probs, mixture, grad_mix, w_qkv, sum_one)
    dqkv = grad.reshape(2, total, width // 256, 3, 128).transpose(1, 3, 2, 0, 4).reshape(total, 3 * width)
    output = outs.reshape(row_count, part_len, width)
    grad_tokens = between(grad_tokens).reshape(row_count, part_len, width)
    low, pool = low[:total], low[total:]
    grads = (tn(tok, dqkv), tn(mixture, grad_att), tn(hid, grad_up), nn(act, low), tn(pool[:16], pool[16:]))
    shards = [lax.psum_scatter(g, "dp", scatter_dimension=0, tiled=True) for g in grads]
    shards = [lax.psum(s.astype(bf16), "mix").astype(f32) for s in shards]
    bins = vec_back[3:7]
    vecs = jnp.concatenate([vec_ramp[:7], vec_back[:3], vec_late[:2], bins], axis=0)
    vecs = lax.psum(vecs, ("dp", "mix"))
    class_total = lax.psum(vec_ramp[7, :3], ("dp", "mix"))
    loss = lax.psum(vec_ramp[7, 128 : 128 + row_count * pairs], "mix").reshape(row_count, pairs)
    share = width // dps
    v = lax.dynamic_slice_in_dim(vecs, dp * share, share, axis=1)
    bin_share = lax.dynamic_slice_in_dim(vecs[12:].reshape(-1), dp * (units // dps), units // dps)
    return (
        output, loss, grad_tokens, shards[0], v[10], v[11], shards[1], v[9], v[7], v[8], shards[2], bin_share,
        shards[3], v[0], v[1], v[2], shards[4], v[3], v[4:7].T, class_total,
    )


def solution(mesh):
    wide = P("dp", "mix", None)
    split = P("dp", None)
    in_specs = (wide, wide, split, split) + (P(),) * 17
    out_specs = (
        wide, split, wide,
        split, P("dp"), P("dp"), split, P("dp"), P("dp"), P("dp"),
        split, P("dp"), split, P("dp"), P("dp"), P("dp"),
        split, P("dp"), split, P(),
    )
    return jax.shard_map(on_device, mesh=mesh, in_specs=in_specs, out_specs=out_specs, check_vma=False)
```

```python
import functools

import jax
import jax.numpy as jnp
from jax import lax
from jax.experimental import pallas as pl
from jax.experimental.pallas import tpu as pltpu
from jax.sharding import PartitionSpec as P

HEADS = 12
SCALE = 1.0
WORK = 5.8e8
GROUP = 4
CHUNK = 768
TILE = 256
UNIT = 48
HALF = 384
norm_eps = 1e-06
masked_score = -1000000000.0
inv_root_two = 0.7071067811865476
inv_root_tau = 0.3989422804014327
f32 = jnp.float32
bf16 = jnp.bfloat16
VMEM_LIMIT = 62 * 1024 * 1024
SMALL_LIMIT = 20 * 1024 * 1024
LIMITS = dict.fromkeys(("stage_two", "stage_three", "settle", "place_units"), SMALL_LIMIT)
SMEM_SPEC = pl.BlockSpec(memory_space=pltpu.SMEM)
B_QUERY, B_VALUE, B_ATTN, GAIN_ONE, SHIFT_ONE, B_OUT, GAIN_TWO, SHIFT_TWO, B_POOL, B_IN, B_CLASS = 0, 1, 2, 3, 4, 5, 6, 7, 8, 9, 13


def whole(shape):
    return pl.BlockSpec(shape, lambda *_: (0,) * len(shape))


def sds(shape, dtype):
    return jax.ShapeDtypeStruct(shape, dtype)


def nn(left, right):
    return jnp.dot(left, right, preferred_element_type=f32)


def nt(left, right):
    return lax.dot_general(left, right, (((1,), (1,)), ((), ())), preferred_element_type=f32)


def tn(left, right):
    return lax.dot_general(left, right, (((0,), (0,)), ((), ())), preferred_element_type=f32)


def call(kernel, name, grid, in_specs, out_specs, out_shape, scratch, work, *args, prefetch=0, aliases=None):
    common = dict(
        out_shape=out_shape,
        compiler_params=pltpu.CompilerParams(vmem_limit_bytes=LIMITS.get(name, VMEM_LIMIT)),
        cost_estimate=pl.CostEstimate(flops=int(2 * work[0] * SCALE), bytes_accessed=int(work[1] * SCALE), transcendentals=0),
        name=name,
        input_output_aliases=aliases or {},
    )
    if prefetch:
        spec = pltpu.PrefetchScalarGridSpec(
            num_scalar_prefetch=prefetch, grid=grid, in_specs=in_specs, out_specs=out_specs, scratch_shapes=scratch)
        return pl.pallas_call(kernel, grid_spec=spec, **common)(*args)
    return pl.pallas_call(
        kernel, grid=grid, in_specs=in_specs, out_specs=out_specs, scratch_shapes=scratch, **common)(*args)


def after(value, *earlier):
    return lax.optimization_barrier((value,) + earlier)[0]


def fetch(copies, start, wait):
    copies = [pltpu.make_async_copy(*copy) for copy in copies]

    @pl.when(start)
    def _():
        for copy in copies:
            copy.start()

    @pl.when(wait)
    def _():
        for copy in copies:
            copy.wait()


def mean_of(values):
    return jnp.mean(values, axis=-1, keepdims=True)


def col_sum(values):
    return jnp.sum(values, axis=0, keepdims=True)


def head_only(values, head, size):
    lane = lax.broadcasted_iota(jnp.int32, (1, values.shape[1]), 1) // size
    return jnp.where(lane == head, values, jnp.zeros((), values.dtype))


def per_head(values, size):
    return jnp.concatenate([head_only(values, h, size) for h in range(GROUP)], axis=0)


def segments(places, lengths, row):
    total = jnp.int32(0)
    seg = jnp.zeros(places.shape, jnp.int32)
    for k in range(lengths.shape[0]):
        total = total + lengths[k, row]
        seg = seg + (places >= total).astype(jnp.int32)
    return seg


def forward_kernel(row, rows_here, part_len, mixers, head_size, here, lengths, *refs):
    pieces, refs = refs[:mixers], refs[mixers:]
    pack, packq, packv, wq, wk, wv, wa = refs[:7]
    (qkv_o, probs_o, tok_o, mix_o, hid_o, n1_o, rho_o,
     tok_s, mix_s, bias_s, w_s, wa_s, sems) = refs[-13:]
    step = pl.program_id(0)
    fetch([(wa, wa_s, sems.at[0])], step == 0, step == pl.num_programs(0) - 1)
    seq = part_len * mixers
    shift = part_len.bit_length() - 1
    span = GROUP * head_size

    @pl.when(step == 0)
    def _():
        for i, piece in enumerate(pieces):
            tok_s[i * part_len : (i + 1) * part_len, :] = piece[...]
        mine = here[0]
        down = lax.broadcasted_iota(jnp.int32, (seq, 1), 0)
        across = lax.broadcasted_iota(jnp.int32, (1, seq), 1)

        def place(i):
            return (((i >> shift) ^ mine) << shift) + (i & (part_len - 1))

        number = mine * rows_here + row
        same = segments(place(down), lengths, number) == segments(place(across), lengths, number)
        bias_s[...] = jnp.where(same, 0.0, masked_score)

    for i, weight in enumerate((wq, wk, wv)):
        w_s[:, i * span : (i + 1) * span] = weight[...]
    qkv = nn(tok_s[...], w_s[...])
    qs = (qkv[:, :span] + packq[B_QUERY : B_QUERY + 1]).astype(bf16) * bf16(head_size ** (-0.5))
    keys = qkv[:, span : 2 * span].astype(bf16)
    values = (qkv[:, 2 * span :] + packv[B_VALUE : B_VALUE + 1]).astype(bf16)
    qkv_o[0, 0, :, :span] = qs
    qkv_o[0, 0, :, span : 2 * span] = keys
    qkv_o[0, 0, :, 2 * span :] = values
    scores = nt(keys, per_head(qs, head_size))
    values_t = values.T
    mixed = []
    for h in range(GROUP):
        at = slice(h * seq, (h + 1) * seq)
        part = scores[:, at] + bias_s[...]
        expo = jnp.exp(part - jnp.max(part, axis=0, keepdims=True))
        probs = (expo * (1.0 / col_sum(expo))).astype(bf16)
        probs_o[0, 0, :, at] = probs
        mixed.append(nn(values_t[h * head_size : (h + 1) * head_size], probs))
    mixed = jnp.concatenate(mixed, axis=0).astype(bf16).T
    here_columns = pl.ds(pl.multiple_of(step * span, 128), span)
    mix_s[:, here_columns] = mixed
    mix_o[...] = mixed
    tok_o[...] = tok_s[:, here_columns]

    @pl.when(step == pl.num_programs(0) - 1)
    def _():
        full = tok_s[...].astype(f32) + (nn(mix_s[...], wa_s[...]) + pack[B_ATTN : B_ATTN + 1])
        centre = full - mean_of(full)
        rho = lax.rsqrt(mean_of(centre * centre) + norm_eps)
        normed = centre * rho
        hidden = normed * pack[GAIN_ONE : GAIN_ONE + 1] + pack[SHIFT_ONE : SHIFT_ONE + 1]
        hid_o[...] = hidden.astype(bf16)
        n1_o[...] = normed.astype(bf16)
        rho_o[...] = jnp.broadcast_to(rho, rho_o.shape)


def forward_row(row, rows_here, here, lengths, pieces, pack, w_qkv, w_attn, earlier, weight_us):
    part_len, width = pieces[0].shape
    mixers = len(pieces)
    seq = part_len * mixers
    head_size = width // HEADS
    span = GROUP * head_size
    steps = width // span

    def weight(which):
        return pl.BlockSpec((width, span), lambda g: (0, which * steps + g))

    rows = pack.shape[0]
    column = pl.BlockSpec((rows, span), lambda g: (0, g))
    part = pl.BlockSpec((seq, span), lambda g: (row, g))
    wide = pl.BlockSpec((seq, width), lambda g: (row, 0))
    total = rows_here * seq
    specs = [SMEM_SPEC, SMEM_SPEC] + [whole((part_len, width))] * mixers
    specs += [whole((rows, width)), column, column, weight(0), weight(1), weight(2), pl.BlockSpec(memory_space=pl.ANY)]
    return call(
        functools.partial(forward_kernel, row, rows_here, part_len, mixers, head_size), "forward_row", (steps,),
        specs + [pl.BlockSpec(memory_space=pl.ANY)] * len(earlier),
        [pl.BlockSpec((1, 1, seq, 3 * span), lambda g: (row, g, 0, 0)),
         pl.BlockSpec((1, 1, seq, GROUP * seq), lambda g: (row, g, 0, 0)),
         part, part, wide, wide, pl.BlockSpec((seq, 128), lambda g: (row, 0))],
        [sds((rows_here, steps, seq, 3 * span), bf16), sds((rows_here, steps, seq, GROUP * seq), bf16)]
        + [sds((total, width), bf16)] * 4 + [sds((total, 128), f32)],
        [pltpu.VMEM((seq, width), bf16), pltpu.VMEM((seq, width), bf16), pltpu.VMEM((seq, seq), f32),
         pltpu.VMEM((width, 3 * span), bf16), pltpu.VMEM((width, width), bf16), pltpu.SemaphoreType.DMA((1,))],
        (weight_us * WORK, 0, 0),
        here, lengths, *pieces, pack, pack, pack, w_qkv, w_qkv, w_qkv, w_attn, *earlier,
        aliases={len(specs) + i: i for i in range(len(earlier))})


def start_spots(here, lengths, r, rows_here, part_len, pairs, seq):
    shift = part_len.bit_length() - 1
    spots = []
    start = jnp.int32(0)
    for k in range(pairs):
        spots.append(r * seq + (((start >> shift) ^ here[0]) << shift) + (start & (part_len - 1)))
        start = start + lengths[k, here[0] * rows_here + r]
    return spots


def feed_kernel(rows_here, part_len, pairs, mixers, send, here, lengths, labels, *refs):
    hid, pack, w_in, w_out, w_pool_any, w_class, cots_any = refs[:7]
    act_o, slope_o, out_o, vec_o, sum_o, low_o, send_o = refs[7:14]
    feed_s, normed_s, rho_s, act_s, acc_s, w_pool, cots, sems = refs[14:]
    step = pl.program_id(0)
    last = pl.num_programs(0) - 1
    fetch([(w_pool_any, w_pool, sems.at[0]), (cots_any, cots, sems.at[1])], step == 0, step == last)
    tokens, width = hid.shape
    seq = part_len * mixers
    count = tokens // TILE

    @pl.when(step == 0)
    def _():
        feed_s[...] = hid[...].astype(f32) + pack[B_OUT : B_OUT + 1]

    bias = pack[pl.ds(B_IN + step, 1), :]

    def rows(i):
        return slice(i * TILE, (i + 1) * TILE)

    up = nn(hid[rows(0), :], w_in[...])
    before = None
    for i in range(count):
        following = nn(hid[rows(i + 1), :], w_in[...]) if i + 1 < count else None
        up = up + bias
        half = 0.5 * (1.0 + lax.erf(up * inv_root_two))
        act = (up * half).astype(bf16)
        slope_o[rows(i), :] = (half + up * jnp.exp(-0.5 * up * up) * inv_root_tau).astype(bf16)
        turned = act.T
        act_o[:, rows(i)] = turned
        if send:
            blocks = CHUNK // (8 * UNIT)
            act_s[pl.ds(step * blocks, blocks), :, :, :, rows(i)] = turned.reshape(blocks, 2, 2, 2 * UNIT, TILE)
        if before is not None:
            feed_s[rows(i - 1), :] += nn(before, w_out[...])
        before, up = act, following
    feed_s[rows(count - 1), :] += nn(before, w_out[...])

    @pl.when(step == last)
    def _():
        gain = pack[GAIN_TWO : GAIN_TWO + 1]
        for r in range(rows_here):
            for k in range(mixers):
                at = slice(r * seq + k * part_len, r * seq + (k + 1) * part_len)
                full = feed_s[at, :]
                centre = full - mean_of(full)
                rho = lax.rsqrt(mean_of(centre * centre) + norm_eps)
                normed = centre * rho
                out = normed * gain + pack[SHIFT_TWO : SHIFT_TWO + 1]
                feed_s[at, :] = out
                out_o[here[0] ^ k, r] = out.astype(bf16)
                normed_s[at, :] = normed
                rho_s[at, :] = jnp.broadcast_to(rho, (part_len, 128))
        spots = []
        for r in range(rows_here):
            spots += start_spots(here, lengths, r, rows_here, part_len, pairs, seq)
        firsts = jnp.concatenate([feed_s[pl.ds(spot, 1), :] for spot in spots], axis=0)
        sums = [jnp.zeros((1, width), f32)] * 2

        def backward(i, sums):
            r, k = i // mixers, i % mixers
            at = slice(i * part_len, (i + 1) * part_len)
            e = cots[here[0] ^ k, r].astype(f32)
            normed = normed_s[at, :]
            eg = e * gain
            sum_o[at, :] = rho_s[at, 0:1] * (eg - mean_of(eg) - normed * mean_of(eg * normed))
            return [sums[0] + col_sum(e * normed), sums[1] + col_sum(e)]

        tiles = rows_here * mixers
        pool = w_pool[...]
        pool_high = pool.astype(bf16)
        pool_rest = (pool - pool_high.astype(f32)).astype(bf16)
        first_high = firsts.astype(bf16)
        first_rest = (firsts - first_high.astype(f32)).astype(bf16)
        pre = nn(jnp.concatenate([first_high, first_rest], axis=0), pool_high)
        pre = pre[: firsts.shape[0]] + pre[firsts.shape[0] :] + nn(first_high, pool_rest)
        for i in range(tiles // 2):
            sums = backward(i, sums)
        pooled = jnp.tanh(pre + pack[B_POOL : B_POOL + 1])
        classes = w_class.shape[0]
        here_pairs = rows_here * pairs
        class_t = w_class[...]
        lane = lax.broadcasted_iota(jnp.int32, (here_pairs, 128), 1)
        logits = jnp.full((here_pairs, 128), -jnp.inf, f32)
        for c in range(classes):
            logits = jnp.where(lane == c, jnp.sum(pooled * class_t[c : c + 1], axis=1, keepdims=True), logits)
        logits = logits + pack[B_CLASS : B_CLASS + 1, :128]
        top = jnp.max(logits, axis=-1, keepdims=True)
        expo = jnp.exp(logits - top)
        total = jnp.sum(expo, axis=-1, keepdims=True)
        log_total = top + jnp.log(total)
        sub = lax.broadcasted_iota(jnp.int32, (here_pairs, 128), 0)
        label = jnp.zeros((here_pairs, 128), jnp.int32)
        for r in range(rows_here):
            for k in range(pairs):
                label = jnp.where(sub == r * pairs + k, labels[k, here[0] * rows_here + r], label)
        chosen = lane == label
        loss = log_total - jnp.sum(jnp.where(chosen, logits, 0.0), axis=-1, keepdims=True)
        grad_logits = expo / total - chosen.astype(f32)
        grad_pooled = jnp.zeros((here_pairs, width), f32)
        for c in range(classes):
            grad_pooled = grad_pooled + grad_logits[:, c : c + 1] * class_t[c : c + 1]
        grad_pre = grad_pooled * (1.0 - pooled * pooled)
        grad_firsts = nt(grad_pre.astype(bf16), pool_high)
        for i in range(tiles // 2, tiles):
            sums = backward(i, sums)
        normed = jnp.concatenate([normed_s[pl.ds(spot, 1), :] for spot in spots], axis=0)
        rho = jnp.concatenate([rho_s[pl.ds(spot, 1), :] for spot in spots], axis=0)[:, 0:1]
        eg = grad_firsts * gain
        more = rho * (eg - mean_of(eg) - normed * mean_of(eg * normed))
        for i, spot in enumerate(spots):
            sum_o[pl.ds(spot, 1), :] = sum_o[pl.ds(spot, 1), :] + more[i : i + 1, :]
        vec_o[1:2, :] = sums[0] + col_sum(grad_firsts * normed)
        vec_o[2:3, :] = sums[1] + col_sum(grad_firsts)
        vec_o[3:4, :] = col_sum(grad_pre)
        for c in range(classes):
            vec_o[4 + c : 5 + c, :] = col_sum(pooled * grad_logits[:, c : c + 1])
        spread_loss = jnp.where(lane == here[0] * here_pairs + sub, loss, 0.0)
        vec_o[7:8, :] = jnp.concatenate(
            [col_sum(grad_logits), col_sum(spread_loss), jnp.zeros((1, width - 256), f32)], axis=1)
        none = jnp.zeros((16 - here_pairs, width), f32)
        low_o[tokens : tokens + 16, :] = jnp.concatenate([firsts, none], axis=0).astype(bf16)
        low_o[tokens + 16 :, :] = jnp.concatenate([grad_pre, none], axis=0).astype(bf16)
        bias_sum = jnp.zeros((1, width), f32)
        for i in range(count):
            low = sum_o[rows(i), :].astype(bf16)
            low_o[rows(i), :] = low
            bias_sum = bias_sum + col_sum(low.astype(f32))
        vec_o[0:1, :] = bias_sum
        if send:
            dp, upper = here[1], (here[0] >> 1) & 1
            other = 1 - (here[0] & 1)
            for j in range(2):
                acc_s[...] = nn(act_s[:, other, j].reshape(16 * UNIT, tokens), low_o[:tokens, :])
                store_sums([send_o], None, slice(j * 2 * UNIT, (j + 1) * 2 * UNIT), lambda p, y: acc_s[
                    pl.ds(pl.multiple_of((p ^ dp) * 2 * UNIT, 16), 2 * UNIT),
                    pl.ds(pl.multiple_of((upper ^ y) * HALF, 128), HALF)])
        else:
            send_o[...] = jnp.zeros(send_o.shape, bf16)


def feed_forward(part_len, here, lengths, labels, hid, pack, w_in, w_out, w_pool, w_class, cots, send):
    mixers, rows_here = cots.shape[:2]
    tokens, width = hid.shape
    pairs = lengths.shape[0]
    units = w_in.shape[1]
    steps = units // CHUNK
    sent = (16, 4 * UNIT, HALF) if send else (16, 128)
    act_shape = (units // (8 * UNIT), 2, 2, 2 * UNIT, tokens) if send else (8, 128)
    acc_shape = (16 * UNIT, width) if send else (8, 128)
    return call(
        functools.partial(feed_kernel, rows_here, part_len, pairs, mixers, send), "feed_forward", (steps,),
        [SMEM_SPEC] * 3
        + [whole(hid.shape), whole(pack.shape), pl.BlockSpec((width, CHUNK), lambda c: (0, c)),
           pl.BlockSpec((CHUNK, width), lambda c: (c, 0)), pl.BlockSpec(memory_space=pl.ANY), whole(w_class.shape), pl.BlockSpec(memory_space=pl.ANY)],
        [pl.BlockSpec((CHUNK, tokens), lambda c: (c, 0)), pl.BlockSpec((tokens, CHUNK), lambda c: (0, c)),
         whole(cots.shape), whole((8, width)), whole((tokens, width)), whole((tokens + 32, width)), whole(sent)],
        [sds((units, tokens), bf16), sds((tokens, units), bf16), sds(cots.shape, bf16), sds((8, width), f32),
         sds((tokens, width), f32), sds((tokens + 32, width), bf16), sds(sent, bf16)],
        [pltpu.VMEM((tokens, width), f32), pltpu.VMEM((tokens, width), f32), pltpu.VMEM((tokens, 128), f32),
         pltpu.VMEM(act_shape, bf16), pltpu.VMEM(acc_shape, f32), pltpu.VMEM(w_pool.shape, f32), pltpu.VMEM(cots.shape, bf16),
         pltpu.SemaphoreType.DMA((2,))],
        (2 * tokens * width * units, 35e6, 0),
        here, lengths, labels, hid, pack, w_in, w_out, w_pool, w_class, cots)


def back_kernel(
    low, slope, w_out, w_in, ramp, pack, *refs,
):
    from_any, (up_o, vec_o, att_o, sum_o, mix_o, hid_s), kept, sems = refs[:4], refs[4:10], refs[10:14], refs[14]
    sum_two, w_attn, n1, rho = kept
    step = pl.program_id(0)
    last = pl.num_programs(0) - 1
    fetch([(a, b, sems.at[i]) for i, (a, b) in enumerate(zip(from_any, kept))], step == 0, step == last)
    count = slope.shape[0] // TILE

    def rows(i):
        return slice(i * TILE, (i + 1) * TILE)

    @pl.when(step == 0)
    def _():
        hid_s[...] = jnp.zeros(hid_s.shape, f32)
        vec_o[7:8, :] = jnp.zeros((1, vec_o.shape[1]), f32)
        vec_o[8:16, :] = ramp[...]

    total = jnp.zeros((1, slope.shape[1]), f32)
    act = nt(low[rows(0), :], w_out[...])
    before = None
    for i in range(count):
        following = nt(low[rows(i + 1), :], w_out[...]) if i + 1 < count else None
        up = (act * slope[rows(i), :].astype(f32)).astype(bf16)
        up_o[rows(i), :] = up
        total = total + col_sum(up.astype(f32))
        if before is not None:
            hid_s[rows(i - 1), :] += nt(before, w_in[...])
        before, act = up, following
    hid_s[rows(count - 1), :] += nt(before, w_in[...])
    vec_o[pl.ds(3 + step, 1), :] = total

    @pl.when(step == last)
    def _():
        width = pack.shape[1]
        sums = [jnp.zeros((1, width), f32)] * 3
        for i in range(count):
            at = rows(i)
            e = hid_s[at, :] + sum_two[at, :]
            normed = n1[at, :].astype(f32)
            eg = e * pack[GAIN_ONE : GAIN_ONE + 1]
            grad = rho[at, 0:1] * (eg - mean_of(eg) - normed * mean_of(eg * normed))
            sum_o[at, :] = grad
            att = grad.astype(bf16)
            att_o[at, :] = att
            mix_o[at, :] = nt(att, w_attn[...]).astype(bf16)
            sums = [sums[0] + col_sum(e * normed), sums[1] + col_sum(e), sums[2] + col_sum(att.astype(f32))]
        for i in range(3):
            vec_o[i : i + 1, :] = sums[i]


def feed_backward(low, slope, w_out, w_in, sum_two, n1, rho, ramp, pack, w_attn):
    count, width = n1.shape
    units = slope.shape[1]
    block = pl.BlockSpec((count, CHUNK), lambda j: (0, j))
    late = (sum_two, w_attn, n1, rho)
    return call(
        back_kernel, "feed_backward", (units // CHUNK,),
        [whole(low.shape), block, pl.BlockSpec((CHUNK, width), lambda j: (j, 0)), pl.BlockSpec((width, CHUNK), lambda j: (0, j)),
         whole((8, width)), whole(pack.shape)] + [pl.BlockSpec(memory_space=pl.ANY)] * 4,
        [block, whole((16, width))] + [whole((count, width))] * 3,
        [sds((count, units), bf16), sds((16, width), f32), sds((count, width), bf16), sds((count, width), f32),
         sds((count, width), bf16)],
        [pltpu.VMEM((count, width), f32)] + [pltpu.VMEM(a.shape, a.dtype) for a in late] + [pltpu.SemaphoreType.DMA((4,))],
        (2 * count * width * units + count * width * width, 40e6, 0),
        low, slope, w_out, w_in, ramp, pack, *late)


def attention_back_kernel(
    head_size, part_len, mixers, here, qkv_r, probs_r, mix_r, grad_r, wq, wk, wv, sum_any,
    d_o, vec_o, tok_o, acc_s, w_s, vec_s, sum_one, sems,
):
    row = pl.program_id(0)
    step = pl.program_id(1)
    last = pl.num_programs(1) - 1
    rows_at = pl.ds(pl.multiple_of(row * sum_one.shape[0], 8), sum_one.shape[0])
    fetch([(sum_any.at[rows_at], sum_one, sems.at[0])], step == 0, step == last)
    span = GROUP * head_size
    seq = qkv_r.shape[2]
    qs, keys, values = qkv_r[0, 0, :, :span], qkv_r[0, 0, :, span : 2 * span], qkv_r[0, 0, :, 2 * span :]
    grad = grad_r[...]
    for i, weight in enumerate((wq, wk, wv)):
        w_s[:, i * span : (i + 1) * span] = weight[...]
    prod = grad.T.astype(f32) * mix_r[...].T.astype(f32)
    keys_t = keys.T
    grad_heads = per_head(grad, head_size)
    grad_probs = nt(values, grad_heads)
    parts, dq_t = [], []
    for h in range(GROUP):
        rows = slice(h * head_size, (h + 1) * head_size)
        at = slice(h * seq, (h + 1) * seq)
        part = (probs_r[0, 0, :, at].astype(f32) * (grad_probs[:, at] - col_sum(prod[rows]))).astype(bf16)
        parts.append(part)
        dq_t.append(nn(keys_t[rows], part))
    grad_scores = jnp.concatenate(parts, axis=1)
    dv = nn(probs_r[0, 0], grad_heads).astype(bf16)
    dk = nn(grad_scores, per_head(qs, head_size)).astype(bf16)
    dq = (jnp.concatenate(dq_t, axis=0) * (head_size ** (-0.5))).astype(bf16).T
    all_three = jnp.concatenate([dq, dk, dv], axis=1)
    half = span // 2
    for c in range(2):
        at = slice(c * half, (c + 1) * half)
        d_o[c] = jnp.concatenate([dq[:, at], dk[:, at], dv[:, at]], axis=1)
    vec = jnp.concatenate([col_sum(dq.astype(f32)), col_sum(dv.astype(f32)), jnp.zeros((6, span), f32)], axis=0)

    @pl.when(row == 0)
    def _():
        vec_s[step] = vec

    @pl.when(row > 0)
    def _():
        vec_s[step] += vec

    part = nt(all_three, w_s[...])

    @pl.when(step == 0)
    def _():
        acc_s[...] = part

    @pl.when(step > 0)
    def _():
        acc_s[...] += part

    @pl.when(step == last)
    def _():
        steps = vec_s.shape[0]
        for k in range(mixers):
            tok_o[here[0] ^ k, 0] = (acc_s[k * part_len : (k + 1) * part_len, :] + sum_one[k * part_len : (k + 1) * part_len, :]).astype(bf16)
        vec_o[...] = jnp.concatenate([vec_s[g] for g in range(steps)], axis=1)


def attention_backward(here, part_len, qkv, probs, mix, grad_mix, w_qkv, sum_one):
    rows_here, steps, seq, _ = qkv.shape
    total, width = grad_mix.shape
    head_size = width // HEADS
    span = GROUP * head_size
    mixers = seq // part_len
    part = pl.BlockSpec((seq, span), lambda r, g: (r, g))

    def weight(which):
        return pl.BlockSpec((width, span), lambda r, g: (0, which * steps + g))

    return call(
        functools.partial(attention_back_kernel, head_size, part_len, mixers), "attention_backward", (rows_here, steps),
        [SMEM_SPEC, pl.BlockSpec((1, 1, seq, 3 * span), lambda r, g: (r, g, 0, 0)),
         pl.BlockSpec((1, 1, seq, GROUP * seq), lambda r, g: (r, g, 0, 0)), part, part,
         weight(0), weight(1), weight(2), pl.BlockSpec(memory_space=pl.ANY)],
        [pl.BlockSpec((2, seq, 3 * span // 2), lambda r, g: (0, r, g)), whole((8, width)),
         pl.BlockSpec((mixers, 1, part_len, width), lambda r, g: (0, r, 0, 0))],
        [sds((2, total, 3 * width // 2), bf16), sds((8, width), f32), sds((mixers, rows_here, part_len, width), bf16)],
        [pltpu.VMEM((seq, width), f32), pltpu.VMEM((width, 3 * span), bf16), pltpu.VMEM((steps, 8, span), f32),
         pltpu.VMEM((seq, width), f32), pltpu.SemaphoreType.DMA((1,))],
        (rows_here * (3 * seq * width * width + 16 * seq * seq * width), 18e6, 0),
        here, qkv, probs, mix, grad_mix, w_qkv, w_qkv, w_qkv, sum_one)


def store_sums(outs, got, rows, read):
    for p in range(8):
        for y in range(2):
            value = read(p, y)
            if got is None:
                outs[0][p * 2 + y, rows, :] = value.astype(bf16)
                continue
            value = (value + got[p * 2 + y, rows, :].astype(f32)).astype(bf16)
            xk, xs, yk, ys = outs
            z2, z1, x = p // 4, p // 2 % 2, p % 2
            if z1 == 0:
                (xk, xs)[x][z2, y, rows, :] = value
            else:
                (yk, ys)[y][z2, x, rows, :] = value


def natural(acc, p, y, dp, upper, columns):
    return acc[pl.ds(pl.multiple_of((p ^ dp) * 2 * UNIT + (y ^ upper) * UNIT, 16), UNIT), columns]


def split_refs(flip, refs, step_rows):
    if flip:
        return refs[0], None, refs[1:], lambda: None
    got_any, got_s, sem = refs[0], refs[-2], refs[-1]
    step = pl.program_id(0)
    copy = pltpu.make_async_copy(got_any, got_s, sem.at[0])

    @pl.when(step == 0)
    def _():
        copy.start()

    def ready():
        @pl.when(step == 0)
        def _():
            copy.wait()

    mine = got_s.at[:, pl.ds(pl.multiple_of(step * step_rows, 16), step_rows), :]
    return refs[1:5], mine, refs[5:-2], ready


def unit_call(kernel, name, flip, grid, in_specs, rows, step_rows, scratch, work, here, *args, got=None):
    if flip:
        specs, shapes = [pl.BlockSpec((16, step_rows, HALF), lambda j, s: (0, j, 0))], [sds((16, rows, HALF), bf16)]
    else:
        in_specs = in_specs + [pl.BlockSpec(memory_space=pl.ANY)]
        scratch = scratch + [pltpu.VMEM(got.shape, bf16), pltpu.SemaphoreType.DMA((1,))]
        args = args + (got,)
        specs = [pl.BlockSpec((2, 2, step_rows, HALF), lambda j, s: (0, 0, j, 0))] * 4
        shapes = [sds((2, 2, rows, HALF), bf16)] * 4
    out = call(kernel, name, (grid,), in_specs, specs, shapes, scratch, work, here, *args, prefetch=1)
    return out[0] if flip else out


def out_units_kernel(flip, here, act, low, *refs):
    outs, got, (acc_s,), ready = split_refs(flip, refs, 2 * UNIT)
    outs = [outs] if flip else outs
    dp, upper = here[1], (here[0] >> 1) & 1
    count = act.shape[-1]
    acc_s[...] = nn(act[...].reshape(16 * UNIT, count), low[:count])
    ready()
    at = [pl.multiple_of((upper ^ y) * HALF, 128) for y in range(2)]
    store_sums(outs, got, slice(None), lambda p, y: acc_s[
        pl.ds(pl.multiple_of((p ^ dp) * 2 * UNIT, 16), 2 * UNIT), pl.ds(at[y], HALF)])


def out_units(here, flip, got, act, low):
    width = low.shape[1]
    count = act.shape[-1]
    return unit_call(
        functools.partial(out_units_kernel, flip), "units_out", flip, 2,
        [pl.BlockSpec((8, 1, 2, UNIT, count), lambda j, s: (0, (s[0] & 1) ^ flip, j, 0, 0)), whole(low.shape)],
        4 * UNIT, 2 * UNIT, [pltpu.VMEM((16 * UNIT, width), f32)], (4 * 8 * UNIT * count * width, 5e6, 0),
        here, act, low, got=got)


def in_units_kernel(flip, here, hid, mix, up, att, low, *refs):
    outs, got, (acc_s, mix_s, att_s, sems), ready = split_refs(flip, refs, 2 * UNIT)
    outs = [outs] if flip else outs
    step = pl.program_id(0)
    dp = here[1]
    core, upper = (here[0] & 1) ^ flip, (here[0] >> 1) & 1

    column = pl.ds(pl.multiple_of(core * HALF, 128), HALF)
    copies = [
        pltpu.make_async_copy(mix, mix_s, sems.at[0]),
        pltpu.make_async_copy(att.at[:, column], att_s, sems.at[1]),
    ]

    @pl.when(step == 0)
    def _():
        for copy in copies:
            copy.start()

    @pl.when(step < 2)
    def _():
        acc_s[...] = tn(hid[...], up[...])

    @pl.when(step == 2)
    def _():
        for copy in copies:
            copy.wait()
        acc_s[:, :HALF] = tn(mix_s[...], att_s[...])
        right = low[16:32, :]
        acc_s[:, HALF:] = tn(low[:16, :], jnp.where(core == 0, right[:, :HALF], right[:, HALF:]))

    ready()
    for u in range(2):
        store_sums(outs, got, slice(u * UNIT, (u + 1) * UNIT), lambda p, y: natural(
            acc_s, p, y, dp, upper, slice(u * HALF, (u + 1) * HALF)))


def in_units(here, flip, got, hid, mix, up, att, low):
    count, width = hid.shape
    return unit_call(
        functools.partial(in_units_kernel, flip), "units_in", flip, 3,
        [whole((count, width)), pl.BlockSpec(memory_space=pl.ANY),
         pl.BlockSpec((count, 2 * HALF), lambda j, s: (0, ((s[0] & 1) ^ flip) * 2 + jnp.minimum(j, 1))),
         pl.BlockSpec(memory_space=pl.ANY), pl.BlockSpec((32, width), lambda j, s: (count // 32, 0))],
        6 * UNIT, 2 * UNIT,
        [pltpu.VMEM((width, 2 * HALF), f32), pltpu.VMEM((count, width), bf16), pltpu.VMEM((count, HALF), bf16),
         pltpu.SemaphoreType.DMA((2,))],
        (5 * width * HALF * count, 5e6, 0),
        here, hid, mix, up, att, low, got=got)


VEC_ROWS = 16


DIGITS = 6
CLASSES = 3


def to_digits(values):
    out = jnp.zeros(values.shape, f32)
    rest = values
    for i in range(DIGITS):
        digit = jnp.floor(rest + 0.5)
        rest = (rest - digit) * 8.0
        moved = digit if i == 0 else jnp.concatenate(
            [jnp.zeros((1, i * CLASSES), f32), digit[:, : digit.shape[1] - i * CLASSES]], axis=1)
        out = out + moved
    return out


def from_digits(values):
    return sum(values[:, i * CLASSES : (i + 1) * CLASSES] * (0.125**i) for i in range(DIGITS))


def qkv_units_kernel(flip, here, tok, grad, back, late, *refs):
    outs, got, (acc_s, tab_s), ready = split_refs(flip, refs, 3 * UNIT + VEC_ROWS)
    outs = [outs] if flip else outs
    dp, upper = here[1], (here[0] >> 1) & 1
    acc_s[...] = tn(tok[...], grad[0])
    ready()
    for u in range(3):
        store_sums(outs, got, slice(u * UNIT, (u + 1) * UNIT), lambda p, y: natural(
            acc_s, p, y, dp, upper, slice(u * HALF, (u + 1) * HALF)))
    ramp = back[8:16, :]
    units = jnp.concatenate([back[3 + i : 4 + i, :] for i in range(4)], axis=1)
    short = jnp.concatenate(
        [ramp[0:7], back[0:3, :], late[0:2, :], jnp.zeros((4, ramp.shape[1]), f32)], axis=0)
    share = short.shape[1] // 8
    fill = jnp.zeros((16, 128 - share), f32)
    blank = jnp.zeros((VEC_ROWS - 3, HALF), f32)
    class_sums = to_digits(ramp[7:8, :128])
    for b in range(8):
        slots = jnp.concatenate([short[:, b * share : (b + 1) * share], fill], axis=1)
        slots = [slots[i : i + 1] for i in range(12)]
        slots += [units[:, b * HALF + i * 128 : b * HALF + (i + 1) * 128] for i in range(3)]
        slots += [class_sums, jnp.where(dp == b, ramp[7:8, 128:256], 0.0), jnp.zeros((1, 128), f32)]
        lines = [jnp.concatenate(slots[i * 3 : i * 3 + 3], axis=1) for i in range(6)]
        for y in range(2):
            tab_s[b, y] = jnp.concatenate(lines[y * 3 : y * 3 + 3] + [blank], axis=0)
    store_sums(outs, got, slice(3 * UNIT, 3 * UNIT + VEC_ROWS), lambda p, y: tab_s[p ^ dp, y ^ upper])


def qkv_units(here, flip, got, tok, grad, back, late):
    count, width = tok.shape
    rows = 3 * UNIT + VEC_ROWS
    wide = 3 * HALF
    return unit_call(
        functools.partial(qkv_units_kernel, flip), "units_qkv", flip, 1,
        [whole((count, width)), pl.BlockSpec((1, count, wide), lambda j, s: ((s[0] & 1) ^ flip, 0, 0)),
         whole((16, width)), whole((8, width))],
        rows, rows, [pltpu.VMEM((width, wide), f32), pltpu.VMEM((8, 2, VEC_ROWS, HALF), f32)],
        (width * wide * count, 5e6, 0), here, tok, grad, back, late, got=got)


def second_kernel(xk, xr, yk, yr, x2k, x2s, y2k, y2s):
    x = xk[0].astype(f32) + xr[0].astype(f32)
    x2k[0] = x[0].astype(bf16)
    x2s[0] = x[1].astype(bf16)
    y = yk[0].astype(f32) + yr[0].astype(f32)
    y2k[0] = y[0].astype(bf16)
    y2s[0] = y[1].astype(bf16)


def add(left, right):
    return (left.astype(f32) + right.astype(f32)).astype(bf16)


def swap(value, axis, bit):
    size = lax.axis_size(axis)
    return lax.ppermute(value, axis, [(i, i ^ bit) for i in range(size)])


def first_swap(stage):
    xk, xs, yk, ys = stage
    return xk, swap(xs, "dp", 1), yk, swap(ys, "mix", 2)


def second_stage(stage, weight, name="stage_two"):
    rows = stage[0].shape[2]
    block = pl.BlockSpec((1, 2, rows, HALF), lambda z: (z, 0, 0, 0))
    out = pl.BlockSpec((1, rows, HALF), lambda z: (z, 0, 0))
    return call(second_kernel, name, (2,), [block] * 4, [out] * 4, [sds((2, rows, HALF), bf16)] * 4, [],
                (weight * WORK, 0, 0), *stage)


def second_swap(stage):
    xk, xs, yk, ys = stage
    return xk, swap(xs, "mix", 2), yk, swap(ys, "dp", 1)


def third_stage(stage):
    xk, xr, yk, yr = stage
    return add(xk, xr), add(yk, yr)


def third_kernel(xk, xr, yk, yr, keep, send):
    keep[...] = add(xk[...], xr[...])
    send[...] = add(yk[...], yr[...])


def third_stage_kernel(stage, weight):
    shape = stage[0].shape
    block = pl.BlockSpec((1,) + shape[1:], lambda z: (z, 0, 0))
    return call(third_kernel, "stage_three", (2,), [block] * 4, [block] * 2, [sds(shape, bf16)] * 2, [],
                (weight * WORK, 0, 0), *stage)


def third_swap(stage):
    return stage[0], swap(stage[1], "dp", 2)


def fourth_stage(stage):
    mine, got = stage
    return add(mine[0], got[0]), add(mine[1], got[1])


def fourth_swap(stage):
    return stage[0], swap(stage[1], "dp", 4)


def fifth_stage(stage):
    return add(*stage)


def spread(final):
    other = swap(final, "mix", 2)
    return final, other, swap(final, "mix", 1), swap(other, "mix", 1)


def place_kernel(plan, vec, here, *refs):
    parts, outs = refs[:4], refs[4:]
    core, upper = here[0] & 1, (here[0] >> 1) & 1
    for i, part in enumerate(parts):
        c, y = core ^ (i // 2), upper ^ (i % 2)
        for u, (which, row, row_core, row_y, col_core, col_y, pieces) in enumerate(plan):
            r0 = pl.multiple_of(row + c * row_core + y * row_y, 8)
            at = 0
            for col, size in pieces:
                c0 = pl.multiple_of(col + c * col_core + y * col_y, 128)
                outs[which][pl.ds(r0, UNIT), pl.ds(c0, size)] = part[u * UNIT : (u + 1) * UNIT, at : at + size].astype(f32)
                at += size
    if vec:
        base = len(plan) * UNIT
        mine, other = parts[0][base : base + 8, :].astype(f32), parts[1][base : base + 8, :].astype(f32)
        lines = [jnp.where(upper == 0, mine, other), jnp.where(upper == 0, other, mine)]

        def slot(i):
            return lines[i // 9][i % 9 // 3 : i % 9 // 3 + 1, (i % 3) * 128 : (i % 3 + 1) * 128]

        vec_outs = outs[-13:]
        share = 96
        for i, target in zip((0, 1, 2, 3, 7, 8, 9, 10, 11), vec_outs[:9]):
            target[...] = slot(i)[0, :share]
        vec_outs[9][...] = jnp.concatenate([slot(12), slot(13), slot(14)], axis=1)[0]
        vec_outs[10][...] = jnp.concatenate([slot(4), slot(5), slot(6)], axis=0)[:, :share]
        vec_outs[11][...] = from_digits(slot(15))[0]
        losses = slot(16)
        pairs, count = vec_outs[12].shape
        lines = [losses[:, r * pairs : (r + 1) * pairs] for r in range(count)]
        lines = jnp.concatenate(lines + [jnp.zeros((8 - count % 8, pairs), f32)] if count % 8 else lines, axis=0)
        vec_outs[12][...] = jnp.concatenate([lines, jnp.zeros((lines.shape[0], 128 - pairs), f32)], axis=1).T[:pairs, :count]


def place_units(here, plan, shapes, parts, vec_shapes=()):
    shape = parts[0].shape
    vm = [whole(s) for s in list(shapes) + list(vec_shapes)]
    return call(
        functools.partial(place_kernel, plan, bool(vec_shapes)), "place_units", (),
        [SMEM_SPEC] + [whole(shape)] * 4, vm, [sds(s, f32) for s in list(shapes) + list(vec_shapes)], [],
        (0.5 * WORK, 0, 0), here, *parts)


def settle_kernel(value, out):
    out[...] = value[...]


def settle(value, weight):
    shape = value.shape
    block = pl.BlockSpec((shape[0] // 2,) + shape[1:], lambda k: (k, 0, 0, 0))
    (out,) = call(settle_kernel, "settle", (2,), [block], [block], [sds(shape, value.dtype)], [], (weight * WORK, 0, 0), value)
    return out.reshape(shape[0] * shape[1], *shape[2:])


def between(value):
    return lax.all_to_all(value, "mix", split_axis=0, concat_axis=0, tiled=True)


def on_device(
    tokens, cotangent, pair_lengths, labels, w_qkv, b_query, b_value, w_attn, b_attn, gain_one, shift_one,
    w_in, b_in, w_out, b_out, gain_two, shift_two, w_pool, b_pool, w_class, b_class,
):
    row_count, part_len, width = tokens.shape
    mixers = lax.axis_size("mix")
    dps = lax.axis_size("dp")
    rows_here = row_count // mixers
    seq = part_len * mixers
    units = w_in.shape[1]
    mix = lax.axis_index("mix").astype(jnp.int32)
    dp = lax.axis_index("dp").astype(jnp.int32)
    here = jnp.stack([mix, dp])
    pairs = pair_lengths.shape[1]
    lengths, classes = pair_lengths.T, labels.T
    quick = dps == 8 and mixers == 4 and width == 768 and units == 3072 and seq * rows_here == 1024 and rows_here == 2

    order = sorted(range(1, mixers), reverse=True)

    def exchange(blocks):
        got = {0: blocks[0]}
        for k in order:
            got[k] = swap(blocks[k], "mix", k)
        return [got[k] for k in range(mixers)]

    pack = jnp.concatenate(
        [b_query, b_value, b_attn, gain_one, shift_one, b_out, gain_two, shift_two, b_pool, b_in, b_class,
         jnp.zeros((3 * width - b_class.shape[0],), f32)]).reshape(16, width)

    def tie(first, second):
        return lax.optimization_barrier((first, second))

    cot = cotangent.reshape(mixers, rows_here, part_len, width)
    rows = ()
    def pieces(array, r):
        return [lax.dynamic_index_in_dim(array, (mix ^ k) * rows_here + r, 0, keepdims=False) for k in range(mixers)]

    blocks = pieces(tokens, 0)
    got = exchange(blocks)
    _, later = tie(blocks[0], tokens)
    for r in range(rows_here):
        if r + 1 < rows_here:
            (got, pack, here), (blocks, cot) = tie((got, pack, here), (pieces(later, r + 1), cot))
            following = exchange(blocks)
            cots = between(cot)
        rows = forward_row(r, rows_here, here, lengths, got, pack, w_qkv, w_attn, rows, (0.0, 15)[r])
        if r + 1 < rows_here:
            rows, got = tie(rows, following)
    qkv, probs, tok, mixture, hid, n1, rho1 = rows
    act, slope, outs, vec_ramp, sum_two, low, send = feed_forward(
        part_len, here, lengths, classes, hid, pack, w_in, w_out, w_pool, w_class.T, cots, quick)
    outs = between(outs)

    if not quick:
        return plain_rest(
            here, part_len, act, slope, outs, low, sum_two, vec_ramp, qkv, probs, tok, mixture, hid, n1, rho1, pack,
            w_qkv, w_attn, w_in, w_out, mix, dp, row_count, units)

    one = first_swap(out_units(here, 0, swap(send, "mix", 1), act.reshape(8, 2, 4, UNIT, rows_here * seq), low))
    _, sum_two = tie(one[0], sum_two)
    grad_up, vec_back, grad_att, sum_one, grad_mix = feed_backward(
        low, slope, w_out, w_in, sum_two, n1, rho1, vec_ramp, pack, w_attn)
    (outs, one), grad_up = tie((outs, one), grad_up)
    args = (hid, mixture, grad_up, grad_att, low)
    send = in_units(here, 1, None, *args)
    _, one = tie(send, one)
    one = second_swap(second_stage(one, 60, "stage_two_wide"))
    _, args = tie(one[0], args)
    two = first_swap(in_units(here, 0, swap(send, "mix", 1), *args))
    _, one = tie(two[0], one)
    one = third_swap(third_stage(one))
    _, grad_mix = tie(one[0], grad_mix)

    grad, vec_late, grad_tokens = attention_backward(here, part_len, qkv, probs, mixture, grad_mix, w_qkv, sum_one)
    grad_tokens = between(grad_tokens)
    (one, two), grad = tie((one, two), grad)
    send = qkv_units(here, 1, None, tok, grad, vec_back, vec_late)
    _, two = tie(send, two)
    two = second_swap(second_stage(two, 60, "stage_two_wide"))
    _, one = tie(two[0], one)
    one = fourth_swap(fourth_stage(one))
    _, grad = tie(one[0], grad)
    three = first_swap(qkv_units(here, 0, swap(send, "mix", 1), tok, grad, vec_back, vec_late))
    _, outs = tie(three[0], outs)
    output = settle(outs, 1)
    _, one = tie(output, one)
    final = fifth_stage(one)
    _, two = tie(final, two)
    two = third_swap(third_stage_kernel(two, 2))
    (_, grad_tokens), three = tie((two[0], grad_tokens), three)
    three = second_swap(second_stage(three, 60))
    _, two = tie(three[0], two)
    two = fourth_swap(fourth_stage(two))
    _, three = tie(two[0], three)
    three = third_swap(third_stage_kernel(three, 0.2))
    _, grad_tokens = tie(three[0], grad_tokens)
    grad_tokens = settle(grad_tokens, 0.5)
    _, two = tie(grad_tokens, two)
    final = jnp.concatenate([final, fifth_stage(two)], axis=0)
    _, three = tie(final, three)
    three = fourth_swap(fourth_stage(three))
    other = swap(final, "mix", 2)
    final = (final, other, swap(final, "mix", 1), swap(other, "mix", 1))
    other, three = tie(other, three)
    mine = fifth_stage(three)
    other = swap(mine, "mix", 2)
    far = swap(mine, "mix", 1)
    _, final = tie(mine, final)
    grad_w_out, grad_w_in, grad_w_attn, grad_w_pool = place_units(
        here, [(0, j * UNIT, 192, 0, 0, HALF, ((0, HALF),)) for j in range(4)]
        + [(1, 0, 0, UNIT, 4 * HALF, 0, ((j * HALF, HALF),)) for j in range(4)]
        + [(2, 0, 0, UNIT, HALF, 0, ((0, HALF),)), (3, 0, 0, UNIT, HALF, 0, ((0, HALF),))],
        [(384, width), (96, units), (96, width), (96, width)], final)
    _, other = tie(grad_w_in, other)
    three = (mine, other, far, swap(other, "mix", 1))
    share = width // dps
    last = place_units(
        here, [(0, 0, 0, UNIT, 128, 0, tuple((w * width + g * 256, 128) for w in range(3))) for g in range(3)],
        [(96, 3 * width)], three,
        [(share,)] * 9 + [(units // dps,), (w_class.shape[1], share), b_class.shape, (pairs, row_count)])
    (grad_w_qkv, grad_b_out, grad_gain_two, grad_shift_two, grad_b_pool, grad_gain_one, grad_shift_one, grad_b_attn,
     grad_b_query, grad_b_value, grad_b_in, grad_w_class, grad_b_class, pair_loss) = last
    return (
        output, pair_loss.T, grad_tokens, grad_w_qkv, grad_b_query, grad_b_value, grad_w_attn, grad_b_attn,
        grad_gain_one, grad_shift_one, grad_w_in, grad_b_in, grad_w_out, grad_b_out, grad_gain_two, grad_shift_two,
        grad_w_pool, grad_b_pool, grad_w_class.T, grad_b_class,
    )


def plain_rest(
    here, part_len, act, slope, outs, low, sum_two, vec_ramp, qkv, probs, tok, mixture, hid, n1, rho1, pack,
    w_qkv, w_attn, w_in, w_out, mix, dp, row_count, units,
):
    rows_here, _, seq, _ = qkv.shape
    total, width = n1.shape
    dps = lax.axis_size("dp")
    pairs = vec_ramp.shape[0] // rows_here
    grad_up, vec_back, grad_att, sum_one, grad_mix = feed_backward(
        low, slope, w_out, w_in, sum_two, n1, rho1, vec_ramp, pack, w_attn)
    grad, vec_late, grad_tokens = attention_backward(here, part_len, qkv, probs, mixture, grad_mix, w_qkv, sum_one)
    dqkv = grad.reshape(2, total, width // 256, 3, 128).transpose(1, 3, 2, 0, 4).reshape(total, 3 * width)
    output = outs.reshape(row_count, part_len, width)
    grad_tokens = between(grad_tokens).reshape(row_count, part_len, width)
    low, pool = low[:total], low[total:]
    grads = (tn(tok, dqkv), tn(mixture, grad_att), tn(hid, grad_up), nn(act, low), tn(pool[:16], pool[16:]))
    shards = [lax.psum_scatter(g, "dp", scatter_dimension=0, tiled=True) for g in grads]
    shards = [lax.psum(s.astype(bf16), "mix").astype(f32) for s in shards]
    bins = vec_back[3:7]
    vecs = jnp.concatenate([vec_ramp[:7], vec_back[:3], vec_late[:2], bins], axis=0)
    vecs = lax.psum(vecs, ("dp", "mix"))
    class_total = lax.psum(vec_ramp[7, :3], ("dp", "mix"))
    loss = lax.psum(vec_ramp[7, 128 : 128 + row_count * pairs], "mix").reshape(row_count, pairs)
    share = width // dps
    v = lax.dynamic_slice_in_dim(vecs, dp * share, share, axis=1)
    bin_share = lax.dynamic_slice_in_dim(vecs[12:].reshape(-1), dp * (units // dps), units // dps)
    return (
        output, loss, grad_tokens, shards[0], v[10], v[11], shards[1], v[9], v[7], v[8], shards[2], bin_share,
        shards[3], v[0], v[1], v[2], shards[4], v[3], v[4:7].T, class_total,
    )


def solution(mesh):
    wide = P("dp", "mix", None)
    split = P("dp", None)
    in_specs = (wide, wide, split, split) + (P(),) * 17
    out_specs = (
        wide, split, wide,
        split, P("dp"), P("dp"), split, P("dp"), P("dp"), P("dp"),
        split, P("dp"), split, P("dp"), P("dp"), P("dp"),
        split, P("dp"), split, P(),
    )
    return jax.shard_map(on_device, mesh=mesh, in_specs=in_specs, out_specs=out_specs, check_vma=False)
```
